256 devices in a mesh: die: 2 (over x_lo), row: 16 (over x_hi, y, core), col: 8 (over z).
Axes of the slice: x: 4 (x_hi: 2, x_lo: 2; x = x_hi * 2 + x_lo), y: 4, z: 8, core: 2. Of those that a mesh axis runs over, the one named last changes fastest.
Arguments:
- sheet_res: float32 [4, 2, 1024, 2048], P('die', None, 'row', 'col'), may hold values from 0.5 to 2
- capacity: float32 [4, 1024, 2048], P('die', 'row', 'col'), may hold values from 0.05 to 0.5
- drop_start: float32 [4, 2, 1024, 2048], P('die', None, 'row', 'col'), may hold values from 0 to 1
- load_cell: int32 [4, 128, 256], P('die', 'row', 'col'), may hold values from 0 to 63
- load_current: float32 [2, 4, 2, 128, 256], P(None, 'die', None, 'row', 'col'), may hold values from 1 to 4
- via_cell: int32 [4, 32, 128, 256], P('die', None, 'row', 'col'), may hold values from 0 to 63
- via_current: float32 [2, 4, 2, 32, 128, 256], P(None, 'die', None, None, 'row', 'col'), may hold values from 0.01 to 0.1
- base_sheet: float32 [2, 128, 256], P(None, 'row', 'col'), may hold values from 0.05 to 0.2
- base_start: float32 [2, 128, 256], P(None, 'row', 'col'), may hold values from 0 to 1
- bump_cell: int32 [16, 32], P('row', 'col'), may hold values from 0 to 63
Outputs:
- die_drop: float32 [4, 2, 1024, 2048], P('die', None, 'row', 'col')
- base_drop: float32 [2, 128, 256], P(None, 'row', 'col')
The draws below stay inside these ranges and needn't reach their ends.
Inputs may be any that keep to these rules, and one draw needn't show every extreme that they name: `load_cell`: offset of a cell within its 8 x 8 tile, row-major. `via_cell`: offset of a cell within its 8 x 8 tile, row-major; two vias may share a cell. `bump_cell`: offset of a cell within its 8 x 8 interposer tile, row-major.
All inputs are finite; a program needn't handle non-finite values.
Results may differ from the reference program's by a relative error of at most 0.0003.
Values sent between devices are 32-bit elements; how exact they have to be, the bound alone decides.
No kernel may reach another device: no remote copies, remote signals or barrier semaphores. Data moves between devices by JAX's collectives and lax.ppermute only.
A program may use at most 64 MiB of HBM per device.

```python
import math
import jax
import jax.numpy as jnp
from jax import lax

DIES = 4
VIAS = 32
SWEEPS = 6
STEPS = 2
NX = 1024
NY = 2048
NXC = 128
NYC = 256


def set_ends(result, rng, smallest, top_value):
    extent = result.shape
    spot = [jax.random.randint(jax.random.fold_in(rng, axis), (), 0, extent[axis]) for axis in range(len(extent))]
    result = result.at[tuple(spot)].set(smallest)
    longest = extent.index(max(extent))
    spot[longest] = (spot[longest] + 1) % extent[longest]
    return result.at[tuple(spot)].set(top_value)


def levels(own_key, dims, cuts, least, largest):
    factor_of = 1.0
    for position, blocks in cuts:
        draws = jax.random.uniform(jax.random.fold_in(jax.random.fold_in(own_key, 6), position), (blocks,), jnp.float32, least / len(cuts), largest / len(cuts))
        factor_of = factor_of * jnp.repeat(jnp.exp(draws), dims[position] // blocks).reshape((-1,) + (1,) * (len(dims) - 1 - position))
    return factor_of


def setup_inputs(seed: int = 0) -> dict:
    arg_keys = jax.random.split(jax.random.key(seed), 11)
    return {
        "sheet_res": jnp.clip(jnp.exp(math.log(2.0) - 1.3862944 * jax.random.uniform(arg_keys[0], (DIES, 2, NX, NY), jnp.float32) ** levels(arg_keys[0], (DIES, 2, NX, NY), ((0, 2), (2, 16), (3, 8)), -0.2, 0.2)), 0.5, 2.0),
        "capacity": jnp.clip(jnp.exp(math.log(0.5) - 2.3025851 * jax.random.uniform(arg_keys[1], (DIES, NX, NY), jnp.float32) ** levels(arg_keys[1], (DIES, NX, NY), ((0, 2), (1, 16), (2, 8)), -0.2, 0.2)), 0.05, 0.5),
        "drop_start": jnp.clip(1.0 * jax.random.uniform(arg_keys[2], (DIES, 2, NX, NY), jnp.float32) ** levels(arg_keys[2], (DIES, 2, NX, NY), ((0, 2), (2, 16), (3, 8)), -0.2, 0.2), 0.0, 1.0),
        "load_cell": set_ends(jax.random.randint(arg_keys[3], (DIES, NXC, NYC), 0, 64), jax.random.fold_in(arg_keys[3], 1), 0, 63).astype(jnp.int32),
        "load_current": jnp.clip(jnp.exp(math.log(4.0) - 1.3862944 * jax.random.uniform(arg_keys[4], (STEPS, DIES, 2, NXC, NYC), jnp.float32) ** levels(arg_keys[4], (STEPS, DIES, 2, NXC, NYC), ((1, 2), (3, 16), (4, 8)), -0.2, 0.2)), 1.0, 4.0),
        "via_cell": set_ends(jax.random.randint(arg_keys[5], (DIES, VIAS, NXC, NYC), 0, 64), jax.random.fold_in(arg_keys[5], 1), 0, 63).astype(jnp.int32),
        "via_current": jnp.clip(jnp.exp(math.log(0.1) - 2.3025851 * jax.random.uniform(arg_keys[6], (STEPS, DIES, 2, VIAS, NXC, NYC), jnp.float32) ** levels(arg_keys[6], (STEPS, DIES, 2, VIAS, NXC, NYC), ((1, 2), (4, 16), (5, 8)), -0.2, 0.2)), 0.01, 0.1),
        "base_sheet": jnp.clip(jnp.exp(math.log(0.2) - 1.3862944 * jax.random.uniform(arg_keys[7], (2, NXC, NYC), jnp.float32) ** levels(arg_keys[7], (2, NXC, NYC), ((1, 16), (2, 8)), -0.2, 0.2)), 0.05, 0.2),
        "base_start": jnp.clip(1.0 * jax.random.uniform(arg_keys[8], (2, NXC, NYC), jnp.float32) ** levels(arg_keys[8], (2, NXC, NYC), ((1, 16), (2, 8)), -0.2, 0.2), 0.0, 1.0),
        "bump_cell": set_ends(jax.random.randint(arg_keys[9], (NXC // 8, NYC // 8), 0, 64), jax.random.fold_in(arg_keys[9], 1), 0, 63).astype(jnp.int32),
    }


VIA_CONDUCT = 1.0
VIA_RESIST = 4.0
BUMP_CONDUCT = 50.0
BASE_CAPACITY = 0.1
LOWER_BOUND = 0.1
UPPER_BOUND = 1.9


def tile_offsets(height, breadth):
    row_part = lax.broadcasted_iota(jnp.int32, (height, breadth), 0) % 8
    col_part = lax.broadcasted_iota(jnp.int32, (height, breadth), 1) % 8
    return row_part * 8 + col_part


def place_cells(values, positions, offsets):
    tiles_down, tiles_across = values.shape[-2], values.shape[-1]
    grid = offsets.reshape(tiles_down, 8, tiles_across, 8)
    hit = positions[..., :, None, :, None] == grid
    placed = jnp.where(hit, values[..., :, None, :, None], 0.0)
    return placed.reshape(placed.shape[:-4] + (tiles_down * 8, tiles_across * 8))


def zero_pad(values):
    return jnp.pad(values, [(0, 0)] * (values.ndim - 2) + [(1, 1), (1, 1)])


def link_terms(center, padded):
    def connect(neighbour):
        return jnp.where(neighbour > 0.0, 2.0 / (center + neighbour), 0.0)
    return (connect(padded[..., :-2, 1:-1]), connect(padded[..., 2:, 1:-1]),
            connect(padded[..., 1:-1, :-2]), connect(padded[..., 1:-1, 2:]))


def operate(padded, iterate, couplings):
    link_up, link_down, link_left, link_right, diagonal = couplings
    coupled = link_up * padded[..., :-2, 1:-1] + link_down * padded[..., 2:, 1:-1]
    coupled = coupled + link_left * padded[..., 1:-1, :-2] + link_right * padded[..., 1:-1, 2:]
    return diagonal * iterate - coupled


def chebyshev(initial, source, couplings, inverse, padder):
    middle = 0.5 * (UPPER_BOUND + LOWER_BOUND)
    half_width = 0.5 * (UPPER_BOUND - LOWER_BOUND)
    scaled = middle / half_width
    residual = inverse * (source - operate(padder(initial), initial, couplings))
    update = residual / middle
    iterate = initial
    ratio_now = 1.0 / scaled
    for sweep_index in range(SWEEPS):
        iterate = iterate + update
        if sweep_index + 1 < SWEEPS:
            residual = residual - inverse * operate(padder(update), update, couplings)
            ratio_next = 1.0 / (2.0 * scaled - ratio_now)
            update = (ratio_next * ratio_now) * update + (2.0 * ratio_next / half_width) * residual
            ratio_now = ratio_next
    return iterate


def reference(sheet_res, capacity, drop_start, load_cell, load_current, via_cell, via_current, base_sheet, base_start, bump_cell):
    offsets = tile_offsets(NX, NY)
    base_offsets = tile_offsets(NXC, NYC)
    links = link_terms(sheet_res, zero_pad(sheet_res))

    def via_field(values):
        def add_member(member, total_field):
            positions = lax.dynamic_index_in_dim(via_cell, member, 1, keepdims=False)
            chosen = lax.dynamic_index_in_dim(values, member, 2, keepdims=False)
            return total_field + place_cells(chosen, positions[:, None], offsets)
        return lax.fori_loop(0, VIAS, add_member, jnp.zeros((DIES, 2, NX, NY), jnp.float32))

    counts = via_field(jnp.ones((DIES, 2, VIAS, NXC, NYC), jnp.float32))
    diagonal = capacity[:, None] + links[0] + links[1] + links[2] + links[3] + VIA_CONDUCT * counts
    couplings = links + (diagonal,)
    inverse = 1.0 / diagonal
    base_links = link_terms(base_sheet, zero_pad(base_sheet))
    bumps = place_cells(jnp.ones((NXC // 8, NYC // 8), jnp.float32), bump_cell, base_offsets)
    base_diagonal = BASE_CAPACITY + base_links[0] + base_links[1] + base_links[2] + base_links[3] + BUMP_CONDUCT * bumps
    base_couplings = base_links + (base_diagonal,)
    base_inverse = 1.0 / base_diagonal
    through = jnp.cumsum(via_current, axis=1)
    beneath = jnp.flip(jnp.cumsum(jnp.flip(through, 1), axis=1), 1)
    arriving = jnp.sum(through[:, -1], axis=2)
    die_state, base_state = drop_start, base_start
    for step_index in range(STEPS):
        base_source = BASE_CAPACITY * base_state + arriving[step_index]
        base_state = chebyshev(base_state, base_source, base_couplings, base_inverse, zero_pad)
        bound = base_state[None, :, None] + VIA_RESIST * beneath[step_index]
        loads = place_cells(load_current[step_index], load_cell[:, None], offsets)
        source = capacity[:, None] * die_state + loads + VIA_CONDUCT * via_field(bound)
        die_state = chebyshev(die_state, source, couplings, inverse, zero_pad)
    return die_state, base_state
```

```python
import jax
import jax.numpy as jnp
from jax import lax
from jax.experimental import pallas as pl
from jax.experimental.pallas import tpu as pltpu
from jax.sharding import PartitionSpec as P

SWEEPS = 6
STEPS = 2
VIAS = 32

VIA_CONDUCT = 1.0
VIA_RESIST = 4.0
BUMP_CONDUCT = 50.0
BASE_CAPACITY = 0.1
LOWER_BOUND = 0.1
UPPER_BOUND = 1.9

MIDDLE = 0.5 * (UPPER_BOUND + LOWER_BOUND)
HALF = 0.5 * (UPPER_BOUND - LOWER_BOUND)

GROUPS = 12
F32 = jnp.float32


def sweep_weights():
    scaled = MIDDLE / HALF
    ratio = 1.0 / scaled
    pairs = []
    for _ in range(SWEEPS - 1):
        following = 1.0 / (2.0 * scaled - ratio)
        pairs.append((following * ratio, 2.0 * following / HALF))
        ratio = following
    return pairs


WEIGHTS = sweep_weights()


def lane_iota():
    return lax.broadcasted_iota(jnp.int32, (8, 128), 1)


def sub_iota(width=128):
    return lax.broadcasted_iota(jnp.int32, (8, width), 0)


def roll(x, shift, axis):
    shift = shift % x.shape[axis]
    return pltpu.roll(x, shift, axis) if shift else x


def rows(g):
    return pl.ds(8 * g, 8)


def pack_kernel(die_ref, via_ref, cell_ref, load_ref, load_cell_ref, packed_ref, cells_ref, loads_ref, send_ref):
    later = die_ref[0].astype(F32)

    def one(v, total):
        parts = []
        for d in range(2):
            part = jnp.concatenate([via_ref[t, d, n, v] for t in range(2) for n in range(2)], axis=1)
            packed_ref[d, v] = part
            parts.append(part)
        both = parts[0] + parts[1]
        send_ref[v] = both + later * parts[0]
        return total + both

    send_ref[VIAS] = lax.fori_loop(0, VIAS, one, jnp.zeros((8, 128), F32))

    def four(q, carry):
        for d in range(2):
            cells_ref[d, q] = jnp.concatenate([cell_ref[d, 4 * q + k] for k in range(4)], axis=1)
        return carry

    lax.fori_loop(0, VIAS // 4, four, 0)
    for d in range(2):
        loads_ref[d] = jnp.concatenate([load_ref[t, d, n] for t in range(2) for n in range(2)], axis=1)
    loads_ref[2] = jnp.concatenate([load_cell_ref[0].astype(F32), load_cell_ref[1].astype(F32)] * 2, axis=1)


def shared(first, second, shift):
    return jnp.where(sub_iota() < shift, first, roll(second, shift, 0))


def shared_low(first, second, shift):
    return jnp.where(sub_iota() >= shift, first, roll(second, shift, 0))


def place_kernel(
    die_ref, bump_ref, packed_ref, cells_ref, loads_ref, send_ref, got_ref, sheet_ref, cap_ref, drop_ref, base_sheet_ref,
    base_start_ref, counts_ref, field_ref, up_ref, down_ref, base_ref,
):
    lane = lane_iota()
    sub = sub_iota()
    later = die_ref[0].astype(F32)
    weights = (
        (VIA_RESIST * (4.0 - 2.0 * later), VIA_RESIST * (3.0 - 2.0 * later), VIA_RESIST * (1.0 + later)),
        (VIA_RESIST * (3.0 - 2.0 * later), VIA_RESIST * (3.0 - 2.0 * later), VIA_RESIST),
    )
    within = lane % 8
    for d in range(2):
        for half in range(2):
            spread = half * 16 + lane // 8

            def add(state, cell, values, count):
                code = cell - within
                out = []
                for oi in range(8):
                    hit = code == 8 * oi
                    base = oi * 5
                    for m in range(4):
                        out.append(state[base + m] + jnp.where(hit, values[m], 0.0))
                    out.append(state[base + 4] + jnp.where(hit, 1.0, 0.0) if count else state[base + 4])
                return tuple(out)

            def four(q, state):
                cells = cells_ref[d, q]
                for k in range(4):
                    v = 4 * q + k
                    cell = jnp.take_along_axis(cells, spread + 32 * k, axis=1)
                    mixed = (
                        weights[d][0] * packed_ref[0, v] + weights[d][1] * packed_ref[1, v] + weights[d][2] * got_ref[v]
                    )
                    values = [jnp.take_along_axis(mixed, spread + 32 * m, axis=1) for m in range(4)]
                    state = add(state, cell, values, True)
                return state

            state = tuple(jnp.zeros((8, 128), F32) for _ in range(40))
            state = lax.fori_loop(0, VIAS // 4, four, state)
            load_cell = jnp.take_along_axis(loads_ref[2], spread + 32 * d, axis=1).astype(jnp.int32)
            load = loads_ref[d]
            state = add(
                state, load_cell, [jnp.take_along_axis(load, spread + 32 * m, axis=1) for m in range(4)], False
            )
            for oi in range(8):
                for m in range(4):
                    field_ref[m // 2, d, m % 2, half, pl.ds(oi, 8, stride=8), :] = state[oi * 5 + m]
                counts_ref[d, half, pl.ds(oi, 8, stride=8), :] = state[oi * 5 + 4]

    place = 0

    def put(up, down):
        nonlocal place
        up_ref[rows(place), :] = up
        down_ref[rows(place), :] = down
        place += 1

    def pair(first, second):
        put(first(0), first(7))
        put(second(0), second(7))
        put(shared(first(1), second(1), 4), shared_low(first(6), second(6), 4))

    for d in range(2):
        for half in range(2):
            lanes = pl.ds(half * 128, 128)
            for n in range(2):
                pair(lambda g: sheet_ref[d, n, rows(g), lanes], lambda g: drop_ref[d, n, rows(g), lanes])
                one = lambda g: field_ref[0, d, n, half, rows(g), :]
                two = lambda g: field_ref[1, d, n, half, rows(g), :]
                put(one(0), one(7))
                put(shared(one(1), two(0), 3), shared_low(one(6), two(7), 5))
            pair(lambda g: cap_ref[d, rows(g), lanes], lambda g: counts_ref[d, half, rows(g), :])

    own = (lane % 64 >= 16) & (lane % 64 < 48)
    zeros32 = jnp.zeros((8, 16), F32)

    def spread_nets(first, second):
        return jnp.concatenate([zeros32, first, zeros32, zeros32, second, zeros32], axis=1)

    arriving = send_ref[VIAS] + got_ref[VIAS]
    bump = jnp.zeros((8, 128), F32)
    column = lane % 64 - 16
    for k in range(4):
        bump = jnp.where((column // 8 == k) & (sub * 8 + column % 8 == bump_ref[0, k]), 1.0, bump)
    parts = [
        spread_nets(base_sheet_ref[0], base_sheet_ref[1]),
        spread_nets(base_start_ref[0], base_start_ref[1]),
    ]
    for t in range(2):
        moved = jnp.where(lane < 64, roll(arriving, 16 - 64 * t, 1), roll(arriving, 48 - 64 * t, 1))
        parts.append(jnp.where(own, moved, 0.0))
    parts.append(jnp.where(own, bump, 0.0))
    for part in range(5):
        base_ref[rows(part), :] = parts[part]
        put(parts[part], parts[part])


ROW_GROUPS = 57


def row_place(d, half, n, kind):
    start = (d * 2 + half) * 13
    return start + 10 if kind == 2 else start + 5 * n + 3 * kind


def below_rows(ref, d, half, n, kind, second):
    start = row_place(d, half, n, kind)
    if kind == 1:
        if second:
            return roll(ref[rows(start + 1), :], -3, 0), None
        return ref[rows(start), :], ref[rows(start + 1), :]
    last = ref[rows(start + 2), :]
    if second:
        return ref[rows(start + 1), :], roll(last, -4, 0)
    return ref[rows(start), :], last


def above_rows(ref, d, half, n, kind, second):
    start = row_place(d, half, n, kind)
    if kind == 1:
        if second:
            return roll(ref[rows(start + 1), :], -5, 0), None
        return ref[rows(start), :], ref[rows(start + 1), :]
    last = ref[rows(start + 2), :]
    if second:
        return ref[rows(start + 1), :], roll(last, -4, 0)
    return ref[rows(start), :], last


def column_groups(own, below, above, d, half, n, kind, second):
    low = below_rows(below, d, half, n, kind, second)
    high = above_rows(above, d, half, n, kind, second)
    return [own(g) for g in range(8)] + [low[0], low[1], high[1], high[0]]


BASE_ROWS = (0, 1, 2, 3, 4)


def base_groups(base_ref, below_ref, above_ref, below2_ref, above2_ref, field):
    start = ROW_GROUPS - 5 + field
    return [
        base_ref[rows(field), :], below_ref[rows(start), :], below2_ref[rows(field), :],
        above2_ref[rows(field), :], above_ref[rows(start), :],
    ]


COL_GROUPS = 2 * GROUPS + 10


def strip_kernel(
    sheet_ref, cap_ref, drop_ref, counts_ref, field_ref, base_ref, below_ref, above_ref, below2_ref, above2_ref,
    left_ref, right_ref,
):
    lane = lane_iota()
    within = lane % 16

    def fields(half):
        lanes = pl.ds(half * 128, 128)
        first, second = [], []
        for d in range(2):
            for n in range(2):
                first.append(column_groups(
                    lambda g: sheet_ref[d, n, rows(g), lanes], below_ref, above_ref, d, half, n, 0, False))
        for d in range(2):
            for n in range(2):
                first.append(column_groups(
                    lambda g: drop_ref[d, n, rows(g), lanes], below_ref, above_ref, d, half, n, 0, True))
        for d in range(2):
            second.append(column_groups(
                lambda g: cap_ref[d, rows(g), lanes], below_ref, above_ref, d, half, 0, 2, False))
        for d in range(2):
            second.append(column_groups(
                lambda g: counts_ref[d, half, rows(g), :], below_ref, above_ref, d, half, 0, 2, True))
        for d in range(2):
            for n in range(2):
                one = column_groups(
                    lambda g: field_ref[0, d, n, half, rows(g), :], below_ref, above_ref, d, half, n, 1, False)
                two = column_groups(
                    lambda g: field_ref[1, d, n, half, rows(g), :], below_ref, above_ref, d, half, n, 1, True)
                merged = []
                for a, b in zip(one, two):
                    if b is None:
                        merged.append(a)
                    elif half == 0:
                        merged.append(jnp.where(within < 11, a, roll(b, 11, 1)))
                    else:
                        merged.append(jnp.where(within >= 5, a, roll(b, -11, 1)))
                second.append(merged)
        return first, second

    def join(chunks, origin):
        out = roll(chunks[0], -origin, 1)
        for k in range(1, 8):
            out = jnp.where(lane // 16 == k, roll(chunks[k], 16 * k - origin, 1), out)
        return out

    for half, ref, origin in ((0, left_ref, 0), (1, right_ref, 112)):
        for part, chunks in enumerate(fields(half)):
            for g in range(GROUPS):
                ref[rows(part * GROUPS + g), :] = join([chunk[g] for chunk in chunks], origin)

    start = 2 * GROUPS
    groups = [
        base_groups(base_ref, below_ref, above_ref, below2_ref, above2_ref, field) for field in range(5)
    ]
    quarter = (lane % 64) // 16
    for g in range(5):
        sheet, drop, one, two, bump = [groups[field][g] for field in range(5)]
        left = jnp.where(
            quarter == 1, sheet,
            jnp.where(quarter == 2, roll(drop, 16, 1), jnp.where(quarter == 3, roll(one, 32, 1), roll(two, -16, 1))),
        )
        right = jnp.where(
            quarter == 2, sheet,
            jnp.where(quarter == 3, roll(drop, 16, 1), jnp.where(quarter == 1, roll(two, -16, 1), roll(one, -32, 1))),
        )
        left_ref[rows(start + g), :] = left
        right_ref[rows(start + g), :] = right
        left_ref[rows(start + 5 + g), :] = bump
        right_ref[rows(start + 5 + g), :] = bump


def connect(center, neighbour):
    return jnp.where(neighbour > 0.0, 2.0 / (center + neighbour), 0.0)


def base_solve(fields):
    sheet, start, arriving, bump = fields
    steps = [(1, 0), (-1, 0), (1, 1), (-1, 1)]
    inside = sheet > 0.0
    links = [jnp.where(inside, connect(sheet, roll(sheet, s, a)), 0.0) for s, a in steps]
    diagonal = BASE_CAPACITY + links[0] + links[1] + links[2] + links[3] + BUMP_CONDUCT * bump
    inverse = 1.0 / diagonal
    links = [inverse * link for link in links]

    def coupled(v):
        return (links[0] * roll(v, 1, 0) + links[1] * roll(v, -1, 0)) + (
            links[2] * roll(v, 1, 1) + links[3] * roll(v, -1, 1)
        )

    state, results = start, []
    for t in range(STEPS):
        source = BASE_CAPACITY * state + arriving[t]
        residual = inverse * source - (state - coupled(state))
        update = residual / MIDDLE
        for k in range(SWEEPS):
            state = state + update
            if k + 1 < SWEEPS:
                residual = residual - (update - coupled(update))
                update = WEIGHTS[k][0] * update + WEIGHTS[k][1] * residual
        results.append(state)
    return results


def needed(halo):
    if halo > 8:
        return list(range(GROUPS))
    return list(range(8)) + ([8, 11] if halo > 0 else [])


def solve_kernel(
    sheet_ref, cap_ref, drop_ref, counts_ref, field_ref, base_ref, below_ref, above_ref, below2_ref, above2_ref,
    fromleft_ref, fromright_ref, out_ref, base_out_ref,
    s_ext, x_ext, c_ext, k_ext, f_ext, base_ext, link_up, link_down, link_left, link_right, inv_ext, res, upd,
):
    lane = lane_iota()

    groups = [
        base_groups(base_ref, below_ref, above_ref, below2_ref, above2_ref, field) for field in range(5)
    ]
    start = 2 * GROUPS
    quarter = (lane % 64) // 16
    from_left = [fromleft_ref[rows(start + g), :] for g in range(10)]
    from_right = [fromright_ref[rows(start + g), :] for g in range(10)]
    fields = []
    for field in range(5):
        out = []
        for g in range(5):
            right_shift = (32, 16, 0, 48, 32)[field]
            left_shift = (-32, -48, 0, -16, -32)[field]
            group = g + 5 * (field == 4)
            value = jnp.where(quarter == 3, roll(from_right[group], right_shift, 1), groups[field][g])
            out.append(jnp.where(quarter == 0, roll(from_left[group], left_shift, 1), value))
        fields.append(jnp.concatenate(out, axis=0))
    solved = base_solve((fields[0], fields[1], (fields[2], fields[3]), fields[4]))
    for t in range(STEPS):
        base_ext[t] = solved[t]
    for n in range(2):
        base_out_ref[n] = roll(solved[1][0:8], -(64 * n + 16), 1)[:, 0:32]

    def third(part, chunk, g):
        right = fromright_ref[rows(part * GROUPS + g), :]
        left = fromleft_ref[rows(part * GROUPS + g), :]
        value = jnp.where(lane < 16, roll(right, -16 * chunk, 1), 0.0)
        return jnp.where(lane >= 112, roll(left, 112 - 16 * chunk, 1), value)

    def fill(target, index, own, d, n, kind, second, part, chunk, shift=0):
        for half in range(2):
            for g, value in enumerate(
                column_groups(lambda g: own(half, g), below_ref, above_ref, d, half, n, kind, second)
            ):
                if value is not None:
                    target[index, rows(g), pl.ds(half * 128, 128)] = value
        for g in range(GROUPS):
            if shift and g in (9, 10):
                continue
            value = third(part, chunk, g)
            if shift:
                value = jnp.where(lane < 64, roll(value, -shift, 1), roll(value, shift, 1))
            target[index, rows(g), pl.ds(256, 128)] = value

    for d in range(2):
        fill(c_ext, d, lambda half, g: cap_ref[d, rows(g), pl.ds(half * 128, 128)], d, 0, 2, False, 1, d)
        fill(k_ext, d, lambda half, g: counts_ref[d, half, rows(g), :], d, 0, 2, True, 1, 2 + d)
        for n in range(2):
            i = 2 * d + n
            fill(s_ext, i, lambda half, g: sheet_ref[d, n, rows(g), pl.ds(half * 128, 128)], d, n, 0, False, 0, i)
            fill(x_ext, i, lambda half, g: drop_ref[d, n, rows(g), pl.ds(half * 128, 128)], d, n, 0, True, 0, 4 + i)
            fill(f_ext, i, lambda half, g: field_ref[0, d, n, half, rows(g), :], d, n, 1, False, 1, 4 + i)
            fill(f_ext, 4 + i, lambda half, g: field_ref[1, d, n, half, rows(g), :], d, n, 1, True, 1, 4 + i, 11)

    sub = sub_iota(384)
    tile = [lane // 8 + 16, lane // 8 + 32, jnp.where(lane < 64, lane // 8 + 48, lane // 8 + 14 - 14)]

    def image(i, carry):
        d = i // 2
        n = i % 2

        def get(ref, g):
            return ref[rows(g % GROUPS), :]

        def above(value, before):
            return jnp.where(sub == 0, roll(before, 1, 0), roll(value, 1, 0))

        def below(value, after):
            return jnp.where(sub == 7, roll(after, -1, 0), roll(value, -1, 0))

        for g in range(GROUPS):
            here = s_ext[i, rows(g), :]
            after = s_ext[i, rows((g + 1) % GROUPS), :]
            inside = here > 0.0
            down = jnp.where(inside, connect(here, below(here, after)), 0.0)
            right = jnp.where(inside, connect(here, roll(here, -1, 1)), 0.0)
            link_down[rows(g), :] = down
            link_right[rows(g), :] = right
            link_left[rows(g), :] = roll(right, 1, 1)
        for g in range(GROUPS):
            link_up[rows(g), :] = above(get(link_down, g), get(link_down, g - 1))
        for g in range(GROUPS):
            ups, downs = get(link_up, g), get(link_down, g)
            lefts, rights = get(link_left, g), get(link_right, g)
            diagonal = c_ext[d, rows(g), :] + ups + downs + lefts + rights + VIA_CONDUCT * k_ext[d, rows(g), :]
            inverse = jnp.where(diagonal > 0.0, 1.0 / diagonal, 0.0)
            inv_ext[rows(g), :] = inverse
            link_up[rows(g), :] = inverse * ups
            link_left[rows(g), :] = inverse * lefts
            link_right[rows(g), :] = inverse * rights
        for g in range(GROUPS):
            link_down[rows(g), :] = get(inv_ext, g) * get(link_down, g)

        def apply(read, groups, use):
            values = {}
            for g in groups:
                for near in (g - 1, g, g + 1):
                    if near % GROUPS not in values:
                        values[near % GROUPS] = read(near % GROUPS)
                value = values[g]
                total = get(link_up, g) * above(value, values[(g - 1) % GROUPS])
                total = total + get(link_down, g) * below(value, values[(g + 1) % GROUPS])
                total = total + get(link_left, g) * roll(value, 1, 1) + get(link_right, g) * roll(value, -1, 1)
                use(g, value, total)

        for t in range(STEPS):
            halo = 11 - 6 * t

            def begin(g, value, total):
                row = 2 * n
                spread = base_ext[t, pl.ds(base_row(g), 1), :]
                spread = jnp.broadcast_to(spread, (8, 128))
                pieces = [jnp.take_along_axis(spread, index + 32 * row, axis=1) for index in tile]
                bound = jnp.concatenate(pieces, axis=1)
                source = c_ext[d, rows(g), :] * value + f_ext[4 * t + i, rows(g), :] + k_ext[d, rows(g), :] * bound
                residual = get(inv_ext, g) * source - (value - total)
                res[rows(g), :] = residual
                upd[0, rows(g), :] = residual / MIDDLE

            apply(lambda g: x_ext[i, rows(g), :], needed(halo), begin)
            last = needed(6 - 6 * t)
            for k in range(SWEEPS):
                if k + 1 == SWEEPS:
                    for g in last:
                        value = x_ext[i, rows(g), :] + upd[k % 2, rows(g), :]
                        x_ext[i, rows(g), :] = value
                    break

                def advance(g, value, total):
                    if g in last:
                        x_ext[i, rows(g), :] = x_ext[i, rows(g), :] + value
                    residual = res[rows(g), :] - (value - total)
                    res[rows(g), :] = residual
                    upd[(k + 1) % 2, rows(g), :] = WEIGHTS[k][0] * value + WEIGHTS[k][1] * residual

                apply(lambda g: upd[k % 2, rows(g), :], needed(halo - 1 - k), advance)
        for g in range(8):
            out_ref[d, n, rows(g), :] = x_ext[i, rows(g), pl.ds(0, 256)]
        return carry

    lax.fori_loop(0, 4, image, 0)


def base_row(g):
    return g if g < 10 else 28 + g


def spec(count):
    return [pl.BlockSpec(memory_space=pltpu.VMEM)] * count


def smem():
    return pl.BlockSpec(memory_space=pltpu.SMEM)


def call(kernel, name, outs, ins, scratch=(), limit=24):
    return pl.pallas_call(
        kernel,
        out_shape=outs,
        in_specs=ins,
        out_specs=spec(len(outs)),
        scratch_shapes=list(scratch),
        compiler_params=pltpu.CompilerParams(vmem_limit_bytes=limit * 1024 * 1024),
        name=name,
    )


def arr(*shape, dtype=F32):
    return jax.ShapeDtypeStruct(shape, dtype)


def per_device(
    sheet_res, capacity, drop_start, load_cell, load_current, via_cell, via_current, base_sheet, base_start, bump_cell
):
    die = lax.axis_index("die").astype(jnp.int32).reshape(1)
    row_count = lax.axis_size("row")
    col_count = lax.axis_size("col")

    packed, cells, loads, send = call(
        pack_kernel, "pack_vias",
        (arr(2, VIAS, 8, 128), arr(2, VIAS // 4, 8, 128, dtype=jnp.int32), arr(3, 8, 128), arr(VIAS + 1, 8, 128)),
        [smem()] + spec(4),
    )(die, via_current, via_cell, load_current, load_cell)
    got = lax.ppermute(send, "die", [(0, 1), (1, 0)])

    rows_shape = arr(8 * ROW_GROUPS, 128)
    counts, field, up, down, base = call(
        place_kernel, "place_vias",
        (arr(2, 2, 64, 128), arr(2, 2, 2, 2, 64, 128), rows_shape, rows_shape, arr(40, 128)),
        [smem(), smem()] + spec(10),
    )(die, bump_cell, packed, cells, loads, send, got, sheet_res, capacity, drop_start, base_sheet, base_start)

    below = lax.ppermute(up, "row", [(i + 1, i) for i in range(row_count - 1)])
    above = lax.ppermute(down, "row", [(i, i + 1) for i in range(row_count - 1)])
    below2 = lax.ppermute(base, "row", [(i + 2, i) for i in range(row_count - 2)])
    above2 = lax.ppermute(base, "row", [(i, i + 2) for i in range(row_count - 2)])

    strip_shape = arr(8 * COL_GROUPS, 128)
    left, right = call(strip_kernel, "column_strips", (strip_shape, strip_shape), spec(10))(
        sheet_res, capacity, drop_start, counts, field, base, below, above, below2, above2
    )
    from_right = lax.ppermute(left, "col", [(i + 1, i) for i in range(col_count - 1)])
    from_left = lax.ppermute(right, "col", [(i, i + 1) for i in range(col_count - 1)])

    ext = (96, 384)
    scratch = [
        pltpu.VMEM((4,) + ext, F32), pltpu.VMEM((4,) + ext, F32), pltpu.VMEM((2,) + ext, F32),
        pltpu.VMEM((2,) + ext, F32), pltpu.VMEM((8,) + ext, F32), pltpu.VMEM((2, 40, 128), F32),
    ] + [pltpu.VMEM(ext, F32)] * 6 + [pltpu.VMEM((2,) + ext, F32)]
    return call(
        solve_kernel, "solve", (arr(2, 2, 64, 256), arr(2, 8, 32)), spec(12), scratch,
    )(sheet_res, capacity, drop_start, counts, field, base, below, above, below2, above2, from_left, from_right)


def solution(mesh):
    in_specs = (
        P("die", None, "row", "col"),
        P("die", "row", "col"),
        P("die", None, "row", "col"),
        P("die", "row", "col"),
        P(None, "die", None, "row", "col"),
        P("die", None, "row", "col"),
        P(None, "die", None, None, "row", "col"),
        P(None, "row", "col"),
        P(None, "row", "col"),
        P("row", "col"),
    )
    out_specs = (P("die", None, "row", "col"), P(None, "row", "col"))
    return jax.shard_map(
        per_device, mesh=mesh, in_specs=in_specs, out_specs=out_specs, check_vma=False
    )
```

```python
import jax
import jax.numpy as jnp
from jax import lax
from jax.experimental import pallas as pl
from jax.experimental.pallas import tpu as pltpu
from jax.sharding import PartitionSpec as P

SWEEPS = 6
STEPS = 2
VIAS = 32

VIA_CONDUCT = 1.0
VIA_RESIST = 4.0
BUMP_CONDUCT = 50.0
BASE_CAPACITY = 0.1
LOWER_BOUND = 0.1
UPPER_BOUND = 1.9

MIDDLE = 0.5 * (UPPER_BOUND + LOWER_BOUND)
HALF = 0.5 * (UPPER_BOUND - LOWER_BOUND)

GROUPS = 12
F32 = jnp.float32


def sweep_weights():
    scaled = MIDDLE / HALF
    ratio = 1.0 / scaled
    pairs = []
    for _ in range(SWEEPS - 1):
        following = 1.0 / (2.0 * scaled - ratio)
        pairs.append((following * ratio, 2.0 * following / HALF))
        ratio = following
    return pairs


WEIGHTS = sweep_weights()


def lane_iota():
    return lax.broadcasted_iota(jnp.int32, (8, 128), 1)


def sub_iota(width=128):
    return lax.broadcasted_iota(jnp.int32, (8, width), 0)


def roll(x, shift, axis):
    shift = shift % x.shape[axis]
    return pltpu.roll(x, shift, axis) if shift else x


def rows(g):
    return pl.ds(8 * g, 8)


def spread_nets(ref):
    gap = jnp.zeros((8, 16), F32)
    return jnp.concatenate([gap, ref[0], gap, gap, ref[1], gap], axis=1)


def pack_kernel(place_ref, bump_ref, via_hbm, sheet_hbm, start_hbm, packed_ref, send_ref, far_ref, via_ref, sheet_ref, start_ref, sems):
    copies = [pltpu.make_async_copy(via_hbm.at[t, d], via_ref.at[t, d], sems.at[2 * t + d]) for t in range(2) for d in range(2)]
    copies.append(pltpu.make_async_copy(sheet_hbm, sheet_ref, sems.at[4]))
    copies.append(pltpu.make_async_copy(start_hbm, start_ref, sems.at[5]))
    for copy in copies:
        copy.start()
    later = place_ref[0].astype(F32)
    lane, sub = lane_iota(), sub_iota()
    bump = jnp.zeros((8, 128), F32)
    column = lane % 64 - 16
    for k in range(4):
        bump = jnp.where((column // 8 == k) & (sub * 8 + column % 8 == bump_ref[0, k]), 1.0, bump)
    for copy in copies:
        copy.wait()
    total = jnp.zeros((8, 128), F32)
    for v in range(VIAS):
        parts = []
        for d in range(2):
            part = jnp.concatenate([via_ref[t, d, n, v] for t in range(2) for n in range(2)], axis=1)
            packed_ref[d, v] = part
            parts.append(part)
        both = parts[0] + parts[1]
        send_ref[v] = both + later * parts[0]
        total = total + both
    send_ref[VIAS] = total
    far_ref[rows(0), :] = spread_nets(sheet_ref)
    far_ref[rows(1), :] = spread_nets(start_ref)
    far_ref[rows(2), :] = bump
    far_ref[rows(3), :] = total


def spread_matrix(height, width):
    row = lax.broadcasted_iota(jnp.int32, (height, width), 0) % 128
    column = lax.broadcasted_iota(jnp.int32, (height, width), 1)
    return jnp.where(row == column // 8, 1.0, 0.0).astype(jnp.bfloat16)


def halves(value):
    high = value.astype(jnp.bfloat16)
    low = (value - high.astype(F32)).astype(jnp.bfloat16)
    return jnp.concatenate([high, low], axis=1)


def prepare_kernel(cell_ref, load_cell_ref, load_ref, cells_ref, load_cells_ref, loads_ref, spread_ref, counts_ref):
    within = (lane_iota() % 8).astype(F32)
    spread = spread_matrix(32, 256)
    for d in range(2):
        cells = cell_ref[d].reshape(8 * VIAS, 32).astype(F32).astype(jnp.bfloat16)
        wide = jnp.dot(cells, spread, preferred_element_type=F32)
        load_cell = load_cell_ref[d].astype(F32).astype(jnp.bfloat16)
        load_cell = jnp.dot(load_cell, spread, preferred_element_type=F32)
        for half in range(2):
            lanes = slice(128 * half, 128 * half + 128)
            for v in range(VIAS):
                cells_ref[2 * d + half, v] = wide[8 * v : 8 * v + 8, lanes] - within
            load_cells_ref[2 * d + half] = load_cell[:, lanes] - within
    spread_ref[...] = spread_matrix(256, 1024)
    loads = jnp.concatenate([load_ref[t, d, n] for d in range(2) for t in range(2) for n in range(2)], axis=0)
    high = loads.astype(jnp.bfloat16)
    low = (loads - high.astype(F32)).astype(jnp.bfloat16)
    wide = jnp.dot(high, spread, preferred_element_type=F32) + jnp.dot(low, spread, preferred_element_type=F32)
    for d in range(2):
        for half in range(2):
            for m in range(4):
                loads_ref[2 * d + half, m] = wide[32 * d + 8 * m : 32 * d + 8 * m + 8, 128 * half : 128 * half + 128]

    def count(i, carry):
        state = [jnp.zeros((8, 128), F32) for _ in range(8)]
        for v in range(VIAS):
            cell = cells_ref[i, v]
            for oi in range(8):
                state[oi] = state[oi] + jnp.where(cell == 8.0 * oi, 1.0, 0.0)
        for oi in range(8):
            counts_ref[i, pl.ds(oi, 8, stride=8), :] = state[oi]
        return carry

    lax.fori_loop(0, 4, count, 0)


def shared(first, second, shift):
    return jnp.where(sub_iota() < shift, first, roll(second, shift, 0))


def shared_low(first, second, shift):
    return jnp.where(sub_iota() >= shift, first, roll(second, shift, 0))


def place_kernel(
    place_ref, packed_ref, send_ref, got_ref, cells_ref, load_cells_ref, loads_ref, spread_ref, counts_ref, far_ref,
    sheet_ref, cap_ref, drop_ref, field_ref, even_ref, odd_ref, base_ref, values_ref,
):
    lane = lane_iota()
    later = place_ref[0].astype(F32)
    even = place_ref[1] % 2 == 0
    weights = (
        (VIA_RESIST * (4.0 - 2.0 * later), VIA_RESIST * (3.0 - 2.0 * later), VIA_RESIST * (1.0 + later)),
        (VIA_RESIST * (3.0 - 2.0 * later), VIA_RESIST * (3.0 - 2.0 * later), VIA_RESIST),
    )
    size = (8 * VIAS, 128)
    first, second, got = packed_ref[0].reshape(size), packed_ref[1].reshape(size), got_ref[0:VIAS].reshape(size)
    for d in range(2):
        mixed = weights[d][0] * first + weights[d][1] * second + weights[d][2] * got
        wide = jnp.dot(halves(mixed), spread_ref[...], preferred_element_type=F32)
        for half in range(2):
            for m in range(4):
                start = 256 * m + 128 * half
                values_ref[2 * d + half, m] = wide[:, start : start + 128].reshape(VIAS, 8, 128)

    def add(i, carry):
        cell = load_cells_ref[i]
        loads = [loads_ref[i, m] for m in range(4)]
        state = []
        for oi in range(8):
            hit = cell == 8.0 * oi
            state.append([jnp.where(hit, load, 0.0) for load in loads])
        for v in range(VIAS):
            cell = cells_ref[i, v]
            values = [values_ref[i, m, v] for m in range(4)]
            for oi in range(8):
                hit = cell == 8.0 * oi
                state[oi] = [old + jnp.where(hit, value, 0.0) for old, value in zip(state[oi], values)]
        for oi in range(8):
            for m in range(4):
                field_ref[m, i, pl.ds(oi, 8, stride=8), :] = state[oi][m]
        return carry

    lax.fori_loop(0, 4, add, 0)

    place = 0

    def put(up, down):
        nonlocal place
        even_ref[rows(place), :] = jnp.where(even, down, up)
        odd_ref[rows(place), :] = jnp.where(even, up, down)
        place += 1

    def pair(first, second):
        put(first(0), first(7))
        put(second(0), second(7))
        put(shared(first(1), second(1), 4), shared_low(first(6), second(6), 4))

    for d in range(2):
        for half in range(2):
            lanes = pl.ds(half * 128, 128)
            for n in range(2):
                pair(lambda g: sheet_ref[d, n, rows(g), lanes], lambda g: drop_ref[d, n, rows(g), lanes])
                one = lambda g: field_ref[n, 2 * d + half, rows(g), :]
                two = lambda g: field_ref[2 + n, 2 * d + half, rows(g), :]
                put(one(0), one(7))
                put(shared(one(1), two(0), 3), shared_low(one(6), two(7), 5))
            pair(lambda g: cap_ref[d, rows(g), lanes], lambda g: counts_ref[2 * d + half, rows(g), :])

    parts = [far_ref[rows(0), :], far_ref[rows(1), :], far_ref[rows(2), :], send_ref[VIAS] + got_ref[VIAS]]
    for part in range(4):
        base_ref[rows(part), :] = parts[part]
        put(parts[part], parts[part])


BASE = 4
ROW_GROUPS = 52 + BASE


def row_place(d, half, n, kind):
    start = (d * 2 + half) * 13
    return start + 10 if kind == 2 else start + 5 * n + 3 * kind


def below_rows(ref, d, half, n, kind, second):
    start = row_place(d, half, n, kind)
    if kind == 1:
        if second:
            return roll(ref[rows(start + 1), :], -3, 0), None
        return ref[rows(start), :], ref[rows(start + 1), :]
    last = ref[rows(start + 2), :]
    if second:
        return ref[rows(start + 1), :], roll(last, -4, 0)
    return ref[rows(start), :], last


def above_rows(ref, d, half, n, kind, second):
    start = row_place(d, half, n, kind)
    if kind == 1:
        if second:
            return roll(ref[rows(start + 1), :], -5, 0), None
        return ref[rows(start), :], ref[rows(start + 1), :]
    last = ref[rows(start + 2), :]
    if second:
        return ref[rows(start + 1), :], roll(last, -4, 0)
    return ref[rows(start), :], last


def column_groups(own, below, above, d, half, n, kind, second):
    low = below_rows(below, d, half, n, kind, second)
    high = above_rows(above, d, half, n, kind, second)
    return [own(g) for g in range(8)] + [low[0], low[1], high[1], high[0]]


COL_GROUPS = 2 * GROUPS + 10


def strip_kernel(
    place_ref, sheet_ref, cap_ref, drop_ref, counts_ref, field_ref, base_ref, even_ref, odd_ref, near_ref, next_ref, far_ref,
    left_ref, right_ref, below_ref, above_ref, wide_ref,
):
    lane = lane_iota()
    within = lane % 16
    row, last = place_ref[1], place_ref[3]
    even, low = row % 2 == 0, row % 4 < 2

    def pick(flag, yes, no, inside):
        return jnp.where(inside, jnp.where(flag, yes, no), 0.0)

    for g in range(ROW_GROUPS):
        a, b = even_ref[rows(g), :], odd_ref[rows(g), :]
        below_ref[rows(g), :] = pick(even, a, b, row < last)
        above_ref[rows(g), :] = pick(even, b, a, row > 0)

    own = (lane % 64 >= 16) & (lane % 64 < 48)

    def spread_steps(value):
        out = []
        for t in range(2):
            moved = jnp.where(lane < 64, roll(value, 16 - 64 * t, 1), roll(value, 48 - 64 * t, 1))
            out.append(jnp.where(own, moved, 0.0))
        return out

    groups = []
    for g in range(5):
        if g == 0:
            parts = [base_ref[rows(f), :] for f in range(BASE)]
        elif g in (1, 4):
            ref = below_ref if g == 1 else above_ref
            parts = [ref[rows(ROW_GROUPS - BASE + f), :] for f in range(BASE)]
        else:
            inside = row + 2 <= last if g == 2 else row >= 2
            flag = low if g == 2 else jnp.logical_not(low)
            parts = [pick(flag, near_ref[rows(f), :], next_ref[rows(f), :], inside) for f in range(BASE)]
            parts[3] = parts[3] + pick(flag, far_ref[rows(0), :], far_ref[rows(1), :], inside)
        one, two = spread_steps(parts[3])
        groups.append([parts[0], parts[1], one, two, parts[2]])
        for f in range(5):
            wide_ref[rows(5 * f + g), :] = groups[g][f]

    def fields(half):
        lanes = pl.ds(half * 128, 128)
        first, second = [], []
        for d in range(2):
            for n in range(2):
                first.append(column_groups(
                    lambda g: sheet_ref[d, n, rows(g), lanes], below_ref, above_ref, d, half, n, 0, False))
        for d in range(2):
            for n in range(2):
                first.append(column_groups(
                    lambda g: drop_ref[d, n, rows(g), lanes], below_ref, above_ref, d, half, n, 0, True))
        for d in range(2):
            second.append(column_groups(
                lambda g: cap_ref[d, rows(g), lanes], below_ref, above_ref, d, half, 0, 2, False))
        for d in range(2):
            second.append(column_groups(
                lambda g: counts_ref[2 * d + half, rows(g), :], below_ref, above_ref, d, half, 0, 2, True))
        for d in range(2):
            for n in range(2):
                one = column_groups(
                    lambda g: field_ref[n, 2 * d + half, rows(g), :], below_ref, above_ref, d, half, n, 1, False)
                two = column_groups(
                    lambda g: field_ref[2 + n, 2 * d + half, rows(g), :], below_ref, above_ref, d, half, n, 1, True)
                merged = []
                for a, b in zip(one, two):
                    if b is None:
                        merged.append(a)
                    elif half == 0:
                        merged.append(jnp.where(within < 11, a, roll(b, 11, 1)))
                    else:
                        merged.append(jnp.where(within >= 5, a, roll(b, -11, 1)))
                second.append(merged)
        return first, second

    def join(chunks, origin):
        out = roll(chunks[0], -origin, 1)
        for k in range(1, 8):
            out = jnp.where(lane // 16 == k, roll(chunks[k], 16 * k - origin, 1), out)
        return out

    for half, ref, origin in ((0, left_ref, 0), (1, right_ref, 112)):
        for part, chunks in enumerate(fields(half)):
            for g in range(GROUPS):
                ref[rows(part * GROUPS + g), :] = join([chunk[g] for chunk in chunks], origin)

    start = 2 * GROUPS
    quarter = (lane % 64) // 16
    for g in range(5):
        sheet, drop, one, two, bump = groups[g]
        left = jnp.where(
            quarter == 1, sheet,
            jnp.where(quarter == 2, roll(drop, 16, 1), jnp.where(quarter == 3, roll(one, 32, 1), roll(two, -16, 1))),
        )
        right = jnp.where(
            quarter == 2, sheet,
            jnp.where(quarter == 3, roll(drop, 16, 1), jnp.where(quarter == 1, roll(two, -16, 1), roll(one, -32, 1))),
        )
        left_ref[rows(start + g), :] = left
        right_ref[rows(start + g), :] = right
        left_ref[rows(start + 5 + g), :] = bump
        right_ref[rows(start + 5 + g), :] = bump


def connect(center, neighbour):
    return jnp.where(neighbour > 0.0, 2.0 / (center + neighbour), 0.0)


def three_terms(k):
    if k == 0:
        return 1.0 - 1.0 / MIDDLE, 0.0, 1.0 / MIDDLE
    a, b = WEIGHTS[k - 1]
    return 1.0 + a - b, -a, b


def advance(k, value, previous, total):
    fore, back, gain = three_terms(k)
    out = total if gain == 1.0 else gain * total
    if fore != 0.0:
        out = out + fore * value
    return out + back * previous() if k else out


def base_solve(fields):
    sheet, state, arriving, bump = fields
    steps = [(1, 0), (-1, 0), (1, 1), (-1, 1)]
    inside = sheet > 0.0
    links = [jnp.where(inside, connect(sheet, roll(sheet, s, a)), 0.0) for s, a in steps]
    diagonal = BASE_CAPACITY + links[0] + links[1] + links[2] + links[3] + BUMP_CONDUCT * bump
    inverse = 1.0 / diagonal
    links = [inverse * link for link in links]
    results = []
    for t in range(STEPS):
        source = inverse * (BASE_CAPACITY * state + arriving[t])
        previous = None
        for k in range(SWEEPS):
            total = (links[0] * roll(state, 1, 0) + links[1] * roll(state, -1, 0)) + (
                links[2] * roll(state, 1, 1) + links[3] * roll(state, -1, 1)
            ) + source
            state, previous = advance(k, state, lambda: previous, total), state
        results.append(state)
    return results


def needed(halo):
    if halo > 8:
        return list(range(GROUPS))
    return list(range(8)) + ([8, 11] if halo > 0 else [])


def solve_kernel(
    place_ref, sheet_ref, cap_ref, drop_ref, counts_ref, field_ref, wide_ref, below_ref, above_ref,
    fromleft_ref, fromright_ref, out_ref, base_out_ref,
    s_ext, x_ext, c_ext, k_ext, f_ext, base_ext, link_up, link_down, link_left, link_right, inv_ext, src, alt,
):
    lane = lane_iota()
    has_left, has_right = place_ref[2] > 0, place_ref[2] < place_ref[4]

    start = 2 * GROUPS
    quarter = (lane % 64) // 16
    take_left, take_right = (quarter == 0) & has_left, (quarter == 3) & has_right
    from_left = [fromleft_ref[rows(start + g), :] for g in range(10)]
    from_right = [fromright_ref[rows(start + g), :] for g in range(10)]
    fields = []
    for field in range(5):
        out = []
        for g in range(5):
            right_shift = (32, 16, 0, 48, 32)[field]
            left_shift = (-32, -48, 0, -16, -32)[field]
            group = g + 5 * (field == 4)
            value = jnp.where(take_right, roll(from_right[group], right_shift, 1), wide_ref[rows(5 * field + g), :])
            out.append(jnp.where(take_left, roll(from_left[group], left_shift, 1), value))
        fields.append(jnp.concatenate(out, axis=0))
    solved = base_solve((fields[0], fields[1], (fields[2], fields[3]), fields[4]))
    for t in range(STEPS):
        base_ext[t] = solved[t]
    for n in range(2):
        base_out_ref[n] = roll(solved[1][0:8], -(64 * n + 16), 1)[:, 0:32]

    at_left, at_right = (lane >= 112) & has_left, (lane < 16) & has_right

    def third(part, chunk, g):
        right = fromright_ref[rows(part * GROUPS + g), :]
        left = fromleft_ref[rows(part * GROUPS + g), :]
        value = jnp.where(at_right, roll(right, -16 * chunk, 1), 0.0)
        return jnp.where(at_left, roll(left, 112 - 16 * chunk, 1), value)

    def fill(target, index, own, d, n, kind, second, part, chunk, shift=0):
        for half in range(2):
            for g, value in enumerate(
                column_groups(lambda g: own(half, g), below_ref, above_ref, d, half, n, kind, second)
            ):
                if value is not None:
                    target[index, rows(g), pl.ds(half * 128, 128)] = value
        for g in range(GROUPS):
            if shift and g in (9, 10):
                continue
            value = third(part, chunk, g)
            if shift:
                value = jnp.where(lane < 64, roll(value, -shift, 1), roll(value, shift, 1))
            target[index, rows(g), pl.ds(256, 128)] = value

    for d in range(2):
        fill(c_ext, d, lambda half, g: cap_ref[d, rows(g), pl.ds(half * 128, 128)], d, 0, 2, False, 1, d)
        fill(k_ext, d, lambda half, g: counts_ref[2 * d + half, rows(g), :], d, 0, 2, True, 1, 2 + d)
        for n in range(2):
            i = 2 * d + n
            fill(s_ext, i, lambda half, g: sheet_ref[d, n, rows(g), pl.ds(half * 128, 128)], d, n, 0, False, 0, i)
            fill(x_ext, i, lambda half, g: drop_ref[d, n, rows(g), pl.ds(half * 128, 128)], d, n, 0, True, 0, 4 + i)
            fill(f_ext, i, lambda half, g: field_ref[n, 2 * d + half, rows(g), :], d, n, 1, False, 1, 4 + i)
            fill(f_ext, 4 + i, lambda half, g: field_ref[2 + n, 2 * d + half, rows(g), :], d, n, 1, True, 1, 4 + i, 11)

    sub = sub_iota(384)
    tile = [lane // 8 + 16, lane // 8 + 32, jnp.where(lane < 64, lane // 8 + 48, lane // 8)]

    def image(i, carry):
        d = i // 2
        n = i % 2

        def get(ref, g):
            return ref[rows(g % GROUPS), :]

        def above(value, before):
            return jnp.where(sub == 0, roll(before, 1, 0), roll(value, 1, 0))

        def below(value, after):
            return jnp.where(sub == 7, roll(after, -1, 0), roll(value, -1, 0))

        for g in range(GROUPS):
            here = s_ext[i, rows(g), :]
            after = s_ext[i, rows((g + 1) % GROUPS), :]
            inside = here > 0.0
            down = jnp.where(inside, connect(here, below(here, after)), 0.0)
            right = jnp.where(inside, connect(here, roll(here, -1, 1)), 0.0)
            link_down[rows(g), :] = down
            link_right[rows(g), :] = right
            link_left[rows(g), :] = roll(right, 1, 1)
        for g in range(GROUPS):
            link_up[rows(g), :] = above(get(link_down, g), get(link_down, g - 1))
        for g in range(GROUPS):
            ups, downs = get(link_up, g), get(link_down, g)
            lefts, rights = get(link_left, g), get(link_right, g)
            diagonal = c_ext[d, rows(g), :] + ups + downs + lefts + rights + VIA_CONDUCT * k_ext[d, rows(g), :]
            inverse = jnp.where(diagonal > 0.0, 1.0 / diagonal, 0.0)
            inv_ext[rows(g), :] = inverse
            link_up[rows(g), :] = inverse * ups
            link_left[rows(g), :] = inverse * lefts
            link_right[rows(g), :] = inverse * rights
        for g in range(GROUPS):
            link_down[rows(g), :] = get(inv_ext, g) * get(link_down, g)

        for t in range(STEPS):
            for k in range(SWEEPS):
                for g in needed(11 - 6 * t - k):
                    def read(near):
                        near = near % GROUPS
                        return alt[rows(near), :] if k % 2 else x_ext[i, rows(near), :]

                    value = read(g)
                    total = get(link_up, g) * above(value, read(g - 1)) + get(link_down, g) * below(value, read(g + 1))
                    total = total + (get(link_left, g) * roll(value, 1, 1) + get(link_right, g) * roll(value, -1, 1))
                    if k == 0:
                        spread = jnp.broadcast_to(base_ext[t, pl.ds(base_row(g), 1), :], (8, 128))
                        pieces = [jnp.take_along_axis(spread, index + 64 * n, axis=1) for index in tile]
                        source = c_ext[d, rows(g), :] * value + f_ext[4 * t + i, rows(g), :]
                        source = source + k_ext[d, rows(g), :] * jnp.concatenate(pieces, axis=1)
                        source = get(inv_ext, g) * source
                        src[rows(g), :] = source
                    else:
                        source = get(src, g)
                    total = total + source
                    if k % 2:
                        x_ext[i, rows(g), :] = advance(k, value, lambda: x_ext[i, rows(g), :], total)
                    else:
                        alt[rows(g), :] = advance(k, value, lambda: alt[rows(g), :], total)
        for g in range(8):
            out_ref[d, n, rows(g), :] = x_ext[i, rows(g), pl.ds(0, 256)]
        return carry

    lax.fori_loop(0, 4, image, 0)


def base_row(g):
    return g if g < 10 else 28 + g


def spec(count):
    return [pl.BlockSpec(memory_space=pltpu.VMEM)] * count


def smem():
    return pl.BlockSpec(memory_space=pltpu.SMEM)


def hbm():
    return pl.BlockSpec(memory_space=pltpu.HBM)


def call(kernel, name, outs, ins, scratch=(), limit=24):
    return pl.pallas_call(
        kernel,
        out_shape=outs,
        in_specs=ins,
        out_specs=spec(len(outs)),
        scratch_shapes=list(scratch),
        compiler_params=pltpu.CompilerParams(vmem_limit_bytes=limit * 1024 * 1024),
        name=name,
    )


def arr(*shape, dtype=F32):
    return jax.ShapeDtypeStruct(shape, dtype)


def swaps(count, offset, distance=1):
    pairs = []
    for i in range(count):
        if ((i - offset) // distance) % 2 == 0:
            j = (i + distance) % count
            pairs += [(i, j), (j, i)]
    return pairs


def per_device(
    sheet_res, capacity, drop_start, load_cell, load_current, via_cell, via_current, base_sheet, base_start, bump_cell
):
    row_count = lax.axis_size("row")
    col_count = lax.axis_size("col")
    place = jnp.stack(
        [lax.axis_index("die"), lax.axis_index("row"), lax.axis_index("col"), row_count - 1, col_count - 1]
    ).astype(jnp.int32)
    others = [(0, 1), (1, 0)]

    packed, send, far = call(
        pack_kernel, "pack_vias", (arr(2, VIAS, 8, 128), arr(VIAS + 1, 8, 128), arr(8 * BASE, 128)),
        [smem(), smem(), hbm(), hbm(), hbm()],
        [pltpu.VMEM((2, 2, 2, VIAS, 8, 32), F32), pltpu.VMEM((2, 8, 32), F32), pltpu.VMEM((2, 8, 32), F32),
         pltpu.SemaphoreType.DMA((6,))],
    )(place, bump_cell, via_current, base_sheet, base_start)
    got = lax.ppermute(send, "die", others)
    near = lax.ppermute(far, "row", swaps(row_count, 0, 2))
    after = lax.ppermute(far, "row", swaps(row_count, 2, 2))

    cells, load_cells, loads, spread, counts = call(
        prepare_kernel, "spread_cells",
        (arr(4, VIAS, 8, 128), arr(4, 8, 128), arr(4, 4, 8, 128), arr(256, 1024, dtype=jnp.bfloat16), arr(4, 64, 128)),
        spec(3),
    )(via_cell, load_cell, load_current)

    rows_shape = arr(8 * ROW_GROUPS, 128)
    field, even, odd, base = call(
        place_kernel, "place_vias", (arr(4, 4, 64, 128), rows_shape, rows_shape, arr(8 * BASE, 128)),
        [smem()] + spec(12), [pltpu.VMEM((4, 4, VIAS, 8, 128), F32)],
    )(place, packed, send, got, cells, load_cells, loads, spread, counts, far, sheet_res, capacity, drop_start)

    even = lax.ppermute(even, "row", swaps(row_count, 0))
    odd = lax.ppermute(odd, "row", swaps(row_count, 1))
    shares = jnp.concatenate([near[24:32], after[24:32]], axis=0)
    shares = lax.ppermute(shares, "die", others)

    strip_shape = arr(8 * COL_GROUPS, 128)
    left, right, below, above, wide = call(
        strip_kernel, "column_strips", (strip_shape, strip_shape, rows_shape, rows_shape, arr(200, 128)), [smem()] + spec(11)
    )(place, sheet_res, capacity, drop_start, counts, field, base, even, odd, near, after, shares)
    from_right = lax.ppermute(left, "col", [(i, (i - 1) % col_count) for i in range(col_count)])
    from_left = lax.ppermute(right, "col", [(i, (i + 1) % col_count) for i in range(col_count)])

    ext = (96, 384)
    scratch = [
        pltpu.VMEM((4,) + ext, F32), pltpu.VMEM((4,) + ext, F32), pltpu.VMEM((2,) + ext, F32),
        pltpu.VMEM((2,) + ext, F32), pltpu.VMEM((8,) + ext, F32), pltpu.VMEM((2, 40, 128), F32),
    ] + [pltpu.VMEM(ext, F32)] * 7
    return call(
        solve_kernel, "solve", (arr(2, 2, 64, 256), arr(2, 8, 32)), [smem()] + spec(10), scratch,
    )(place, sheet_res, capacity, drop_start, counts, field, wide, below, above, from_left, from_right)


def solution(mesh):
    in_specs = (
        P("die", None, "row", "col"),
        P("die", "row", "col"),
        P("die", None, "row", "col"),
        P("die", "row", "col"),
        P(None, "die", None, "row", "col"),
        P("die", None, "row", "col"),
        P(None, "die", None, None, "row", "col"),
        P(None, "row", "col"),
        P(None, "row", "col"),
        P("row", "col"),
    )
    out_specs = (P("die", None, "row", "col"), P(None, "row", "col"))
    return jax.shard_map(
        per_device, mesh=mesh, in_specs=in_specs, out_specs=out_specs, check_vma=False
    )
```

```python
import jax
import jax.numpy as jnp
from jax import lax
from jax.experimental import pallas as pl
from jax.experimental.pallas import tpu as pltpu
from jax.sharding import PartitionSpec as P

SWEEPS = 6
STEPS = 2
VIAS = 32

VIA_CONDUCT = 1.0
VIA_RESIST = 4.0
BUMP_CONDUCT = 50.0
BASE_CAPACITY = 0.1
LOWER_BOUND = 0.1
UPPER_BOUND = 1.9

MIDDLE = 0.5 * (UPPER_BOUND + LOWER_BOUND)
HALF = 0.5 * (UPPER_BOUND - LOWER_BOUND)

GROUPS = 12
F32 = jnp.float32


def sweep_weights():
    scaled = MIDDLE / HALF
    ratio = 1.0 / scaled
    pairs = []
    for _ in range(SWEEPS - 1):
        following = 1.0 / (2.0 * scaled - ratio)
        pairs.append((following * ratio, 2.0 * following / HALF))
        ratio = following
    return pairs


WEIGHTS = sweep_weights()


def lane_iota():
    return lax.broadcasted_iota(jnp.int32, (8, 128), 1)


def sub_iota(width=128):
    return lax.broadcasted_iota(jnp.int32, (8, width), 0)


def roll(x, shift, axis):
    shift = shift % x.shape[axis]
    return pltpu.roll(x, shift, axis) if shift else x


def rows(g):
    return pl.ds(8 * g, 8)


def pack_kernel(place_ref, via_ref, packed_ref, send_ref):
    later = place_ref[0].astype(F32)
    total = jnp.zeros((8, 128), F32)
    for v in range(VIAS):
        parts = []
        for d in range(2):
            part = jnp.concatenate([via_ref[t, d, n, v] for t in range(2) for n in range(2)], axis=1)
            packed_ref[d, v] = part
            parts.append(part)
        both = parts[0] + parts[1]
        send_ref[v] = both + later * parts[0]
        total = total + both
    send_ref[VIAS] = total


def spread_nets(ref):
    gap = jnp.zeros((8, 16), F32)
    return jnp.concatenate([gap, ref[0], gap, gap, ref[1], gap], axis=1)


def base_kernel(bump_ref, sheet_ref, start_ref, send_ref, far_ref):
    lane, sub = lane_iota(), sub_iota()
    bump = jnp.zeros((8, 128), F32)
    column = lane % 64 - 16
    for k in range(4):
        bump = jnp.where((column // 8 == k) & (sub * 8 + column % 8 == bump_ref[0, k]), 1.0, bump)
    far_ref[rows(0), :] = spread_nets(sheet_ref)
    far_ref[rows(1), :] = spread_nets(start_ref)
    far_ref[rows(2), :] = bump
    far_ref[rows(3), :] = send_ref[VIAS]


def spread_matrix(height, width):
    row = lax.broadcasted_iota(jnp.int32, (height, width), 0) % 128
    column = lax.broadcasted_iota(jnp.int32, (height, width), 1)
    return jnp.where(row == column // 8, 1.0, 0.0).astype(jnp.bfloat16)


def halves(value):
    high = value.astype(jnp.bfloat16)
    low = (value - high.astype(F32)).astype(jnp.bfloat16)
    return jnp.concatenate([high, low], axis=1)


def prepare_kernel(cell_ref, load_cell_ref, load_ref, cells_ref, load_cells_ref, loads_ref, spread_ref, counts_ref):
    within = (lane_iota() % 8).astype(F32)
    spread = spread_matrix(32, 256)
    for d in range(2):
        cells = cell_ref[d].reshape(8 * VIAS, 32).astype(F32).astype(jnp.bfloat16)
        wide = jnp.dot(cells, spread, preferred_element_type=F32)
        load_cell = load_cell_ref[d].astype(F32).astype(jnp.bfloat16)
        load_cell = jnp.dot(load_cell, spread, preferred_element_type=F32)
        for half in range(2):
            lanes = slice(128 * half, 128 * half + 128)
            for v in range(VIAS):
                cells_ref[2 * d + half, v] = wide[8 * v : 8 * v + 8, lanes] - within
            load_cells_ref[2 * d + half] = load_cell[:, lanes] - within
    spread_ref[...] = spread_matrix(256, 1024)
    loads = jnp.concatenate([load_ref[t, d, n] for d in range(2) for t in range(2) for n in range(2)], axis=0)
    high = loads.astype(jnp.bfloat16)
    low = (loads - high.astype(F32)).astype(jnp.bfloat16)
    wide = jnp.dot(high, spread, preferred_element_type=F32) + jnp.dot(low, spread, preferred_element_type=F32)
    for d in range(2):
        for half in range(2):
            for m in range(4):
                loads_ref[2 * d + half, m] = wide[32 * d + 8 * m : 32 * d + 8 * m + 8, 128 * half : 128 * half + 128]

    def count(i, carry):
        state = [jnp.zeros((8, 128), F32) for _ in range(8)]
        for v in range(VIAS):
            cell = cells_ref[i, v]
            for oi in range(8):
                state[oi] = state[oi] + jnp.where(cell == 8.0 * oi, 1.0, 0.0)
        for oi in range(8):
            counts_ref[i, pl.ds(oi, 8, stride=8), :] = state[oi]
        return carry

    lax.fori_loop(0, 4, count, 0)


def shared(first, second, shift):
    return jnp.where(sub_iota() < shift, first, roll(second, shift, 0))


def shared_low(first, second, shift):
    return jnp.where(sub_iota() >= shift, first, roll(second, shift, 0))


def place_kernel(
    place_ref, packed_ref, send_ref, got_ref, cells_ref, load_cells_ref, loads_ref, spread_ref, counts_ref, far_ref,
    near_ref, next_ref, sheet_ref, cap_ref, drop_ref, field_ref, even_ref, odd_ref, base_ref, shares_ref, values_ref,
):
    lane = lane_iota()
    later = place_ref[0].astype(F32)
    even = place_ref[1] % 2 == 0
    weights = (
        (VIA_RESIST * (4.0 - 2.0 * later), VIA_RESIST * (3.0 - 2.0 * later), VIA_RESIST * (1.0 + later)),
        (VIA_RESIST * (3.0 - 2.0 * later), VIA_RESIST * (3.0 - 2.0 * later), VIA_RESIST),
    )
    size = (8 * VIAS, 128)
    first, second, got = packed_ref[0].reshape(size), packed_ref[1].reshape(size), got_ref[0:VIAS].reshape(size)
    for d in range(2):
        mixed = weights[d][0] * first + weights[d][1] * second + weights[d][2] * got
        wide = jnp.dot(halves(mixed), spread_ref[...], preferred_element_type=F32)
        for half in range(2):
            for m in range(4):
                start = 256 * m + 128 * half
                values_ref[2 * d + half, m] = wide[:, start : start + 128].reshape(VIAS, 8, 128)

    def add(i, carry):
        cell = load_cells_ref[i]
        loads = [loads_ref[i, m] for m in range(4)]
        state = []
        for oi in range(8):
            hit = cell == 8.0 * oi
            state.append([jnp.where(hit, load, 0.0) for load in loads])
        for v in range(VIAS):
            cell = cells_ref[i, v]
            values = [values_ref[i, m, v] for m in range(4)]
            for oi in range(8):
                hit = cell == 8.0 * oi
                state[oi] = [old + jnp.where(hit, value, 0.0) for old, value in zip(state[oi], values)]
        for oi in range(8):
            for m in range(4):
                field_ref[m, i, pl.ds(oi, 8, stride=8), :] = state[oi][m]
        return carry

    lax.fori_loop(0, 4, add, 0)

    shares_ref[rows(0), :] = near_ref[rows(3), :]
    shares_ref[rows(1), :] = next_ref[rows(3), :]

    place = 0

    def put(up, down):
        nonlocal place
        even_ref[rows(place), :] = jnp.where(even, down, up)
        odd_ref[rows(place), :] = jnp.where(even, up, down)
        place += 1

    def pair(first, second):
        put(first(0), first(7))
        put(second(0), second(7))
        put(shared(first(1), second(1), 4), shared_low(first(6), second(6), 4))

    for d in range(2):
        for half in range(2):
            lanes = pl.ds(half * 128, 128)
            for n in range(2):
                pair(lambda g: sheet_ref[d, n, rows(g), lanes], lambda g: drop_ref[d, n, rows(g), lanes])
                one = lambda g: field_ref[n, 2 * d + half, rows(g), :]
                two = lambda g: field_ref[2 + n, 2 * d + half, rows(g), :]
                put(one(0), one(7))
                put(shared(one(1), two(0), 3), shared_low(one(6), two(7), 5))
            pair(lambda g: cap_ref[d, rows(g), lanes], lambda g: counts_ref[2 * d + half, rows(g), :])

    parts = [far_ref[rows(0), :], far_ref[rows(1), :], far_ref[rows(2), :], send_ref[VIAS] + got_ref[VIAS]]
    for part in range(4):
        base_ref[rows(part), :] = parts[part]
        put(parts[part], parts[part])


BASE = 4
ROW_GROUPS = 52 + BASE


def row_place(d, half, n, kind):
    start = (d * 2 + half) * 13
    return start + 10 if kind == 2 else start + 5 * n + 3 * kind


def near_rows(read, d, half, n, kind, second, upper):
    start = row_place(d, half, n, kind)
    if kind == 1:
        if second:
            return roll(read(start + 1), -5 if upper else -3, 0), None
        return read(start), read(start + 1)
    last = read(start + 2)
    if second:
        return read(start + 1), roll(last, -4, 0)
    return read(start), last


def column_groups(own, below, above, d, half, n, kind, second):
    low = near_rows(below, d, half, n, kind, second, False)
    high = near_rows(above, d, half, n, kind, second, True)
    return [own(g) for g in range(8)] + [low[0], low[1], high[1], high[0]]


COL_GROUPS = 2 * GROUPS + 10


def strip_kernel(
    place_ref, sheet_ref, cap_ref, drop_ref, counts_ref, field_ref, base_ref, even_ref, odd_ref, near_ref, next_ref, far_ref,
    left_ref, right_ref, wide_ref,
):
    lane = lane_iota()
    within = lane % 16
    row, last = place_ref[1], place_ref[3]
    even, low = row % 2 == 0, row % 4 < 2

    def below(g):
        return jnp.where(even, even_ref[rows(g), :], odd_ref[rows(g), :])

    def above(g):
        return jnp.where(even, odd_ref[rows(g), :], even_ref[rows(g), :])

    own = (lane % 64 >= 16) & (lane % 64 < 48)

    def spread_steps(value):
        out = []
        for t in range(2):
            moved = jnp.where(lane < 64, roll(value, 16 - 64 * t, 1), roll(value, 48 - 64 * t, 1))
            out.append(jnp.where(own, moved, 0.0))
        return out

    groups = []
    for g in range(5):
        if g == 0:
            parts = [base_ref[rows(f), :] for f in range(BASE)]
        elif g in (1, 4):
            read, inside = (below, row < last) if g == 1 else (above, row > 0)
            parts = [jnp.where(inside, read(ROW_GROUPS - BASE + f), 0.0) for f in range(BASE)]
        else:
            inside = row + 2 <= last if g == 2 else row >= 2
            flag = low if g == 2 else jnp.logical_not(low)
            parts = [jnp.where(flag, near_ref[rows(f), :], next_ref[rows(f), :]) for f in range(BASE)]
            parts[3] = parts[3] + jnp.where(flag, far_ref[rows(0), :], far_ref[rows(1), :])
            parts = [jnp.where(inside, part, 0.0) for part in parts]
        one, two = spread_steps(parts[3])
        groups.append([parts[0], parts[1], one, two, parts[2]])
        for f in range(5):
            wide_ref[rows(5 * f + g), :] = groups[g][f]

    def fields(half):
        lanes = pl.ds(half * 128, 128)
        first, second = [], []
        for d in range(2):
            for n in range(2):
                first.append(column_groups(lambda g: sheet_ref[d, n, rows(g), lanes], below, above, d, half, n, 0, False))
        for d in range(2):
            for n in range(2):
                first.append(column_groups(lambda g: drop_ref[d, n, rows(g), lanes], below, above, d, half, n, 0, True))
        for d in range(2):
            second.append(column_groups(lambda g: cap_ref[d, rows(g), lanes], below, above, d, half, 0, 2, False))
        for d in range(2):
            second.append(
                column_groups(lambda g: counts_ref[2 * d + half, rows(g), :], below, above, d, half, 0, 2, True))
        for d in range(2):
            for n in range(2):
                one = column_groups(
                    lambda g: field_ref[n, 2 * d + half, rows(g), :], below, above, d, half, n, 1, False)
                two = column_groups(
                    lambda g: field_ref[2 + n, 2 * d + half, rows(g), :], below, above, d, half, n, 1, True)
                merged = []
                for a, b in zip(one, two):
                    if b is None:
                        merged.append(a)
                    elif half == 0:
                        merged.append(jnp.where(within < 11, a, roll(b, 11, 1)))
                    else:
                        merged.append(jnp.where(within >= 5, a, roll(b, -11, 1)))
                second.append(merged)
        return first, second

    for half, ref in ((0, left_ref), (1, right_ref)):
        for part, chunks in enumerate(fields(half)):
            for g in range(GROUPS):
                out = chunks[0][g]
                for k in range(1, 8):
                    out = jnp.where((lane // 16 + half) % 8 == k, roll(chunks[k][g], 16 * k, 1), out)
                ref[rows(part * GROUPS + g), :] = out

    start = 2 * GROUPS
    quarter = (lane % 64) // 16
    for g in range(5):
        sheet, drop, one, two, bump = groups[g]
        left = jnp.where(
            quarter == 1, sheet,
            jnp.where(quarter == 2, roll(drop, 16, 1), jnp.where(quarter == 3, roll(one, 32, 1), roll(two, -16, 1))),
        )
        right = jnp.where(
            quarter == 2, sheet,
            jnp.where(quarter == 3, roll(drop, 16, 1), jnp.where(quarter == 1, roll(two, -16, 1), roll(one, -32, 1))),
        )
        left_ref[rows(start + g), :] = left
        right_ref[rows(start + g), :] = right
        left_ref[rows(start + 5 + g), :] = bump
        right_ref[rows(start + 5 + g), :] = bump


def assemble_kernel(
    place_ref, sheet_ref, cap_ref, drop_ref, counts_ref, field_ref, even_ref, odd_ref,
    s_ref, x_ref, c_ref, k_ref, one_ref, two_ref, up_ref, down_ref, left_ref, right_ref, diag_ref, spread_ref,
):
    row, last = place_ref[1], place_ref[3]
    even = row % 2 == 0
    sub, lane = sub_iota(256), lax.broadcasted_iota(jnp.int32, (8, 256), 1)

    def below(g):
        return jnp.where(row < last, jnp.where(even, even_ref[rows(g), :], odd_ref[rows(g), :]), 0.0)

    def above(g):
        return jnp.where(row > 0, jnp.where(even, odd_ref[rows(g), :], even_ref[rows(g), :]), 0.0)

    def both(own, d, n, kind, second):
        sides = [column_groups(lambda g: own(half, g), below, above, d, half, n, kind, second) for half in range(2)]
        return [None if a is None else jnp.concatenate([a, b], axis=1) for a, b in zip(*sides)]

    for d in range(2):
        caps = both(lambda half, g: cap_ref[d, rows(g), pl.ds(half * 128, 128)], d, 0, 2, False)
        counts = both(lambda half, g: counts_ref[2 * d + half, rows(g), :], d, 0, 2, True)
        for g in range(GROUPS):
            c_ref[d, rows(g), :] = caps[g]
            k_ref[d, rows(g), :] = counts[g]
        for n in range(2):
            i = 2 * d + n
            sheets = both(lambda half, g: sheet_ref[d, n, rows(g), pl.ds(half * 128, 128)], d, n, 0, False)
            drops = both(lambda half, g: drop_ref[d, n, rows(g), pl.ds(half * 128, 128)], d, n, 0, True)
            ones = both(lambda half, g: field_ref[n, 2 * d + half, rows(g), :], d, n, 1, False)
            twos = both(lambda half, g: field_ref[2 + n, 2 * d + half, rows(g), :], d, n, 1, True)
            for g in range(GROUPS):
                s_ref[i, rows(g), :] = sheets[g]
                x_ref[i, rows(g), :] = drops[g]
                one_ref[i, rows(g), :] = c_ref[d, rows(g), :] * drops[g] + ones[g]
                if twos[g] is not None:
                    two_ref[i, rows(g), :] = twos[g]
            for g in range(GROUPS):
                here, after = s_ref[i, rows(g), :], s_ref[i, rows((g + 1) % GROUPS), :]
                under = jnp.where(sub == 7, roll(after, -1, 0), roll(here, -1, 0))
                inside = here > 0.0
                down_ref[i, rows(g), :] = jnp.where(inside, connect(here, under), 0.0)
                right = jnp.where(inside & (lane < 255), connect(here, roll(here, -1, 1)), 0.0)
                right_ref[i, rows(g), :] = right
                left_ref[i, rows(g), :] = roll(right, 1, 1)
            for g in range(GROUPS):
                here, before = down_ref[i, rows(g), :], down_ref[i, rows((g - 1) % GROUPS), :]
                up = jnp.where(sub == 0, roll(before, 1, 0), roll(here, 1, 0))
                up_ref[i, rows(g), :] = up
                diag = c_ref[d, rows(g), :] + up + here + left_ref[i, rows(g), :] + right_ref[i, rows(g), :]
                diag_ref[i, rows(g), :] = diag + VIA_CONDUCT * k_ref[d, rows(g), :]
    source = lax.broadcasted_iota(jnp.int32, (256, 384), 0) % 128
    column = lax.broadcasted_iota(jnp.int32, (256, 384), 1)
    column = jnp.where(column < 256, 16 + column // 8, jnp.where(column < 320, 48, 0) + (column - 256) // 8)
    for n in range(2):
        spread_ref[n] = jnp.where(source == column + 64 * n, 1.0, 0.0).astype(jnp.bfloat16)


def connect(center, neighbour):
    return jnp.where(neighbour > 0.0, 2.0 / (center + neighbour), 0.0)


def three_terms(k):
    if k == 0:
        return 1.0 - 1.0 / MIDDLE, 0.0, 1.0 / MIDDLE
    a, b = WEIGHTS[k - 1]
    return 1.0 + a - b, -a, b


def advance(k, value, previous, total):
    fore, back, gain = three_terms(k)
    out = total if gain == 1.0 else gain * total
    if fore != 0.0:
        out = out + fore * value
    return out + back * previous() if k else out


def base_solve(fields):
    sheet, state, arriving, bump = fields
    steps = [(1, 0), (-1, 0), (1, 1), (-1, 1)]
    inside = sheet > 0.0
    links = [jnp.where(inside, connect(sheet, roll(sheet, s, a)), 0.0) for s, a in steps]
    diagonal = BASE_CAPACITY + links[0] + links[1] + links[2] + links[3] + BUMP_CONDUCT * bump
    inverse = 1.0 / diagonal
    links = [inverse * link for link in links]
    results = []
    for t in range(STEPS):
        source = inverse * (BASE_CAPACITY * state + arriving[t])
        previous = None
        for k in range(SWEEPS):
            total = (links[0] * roll(state, 1, 0) + links[1] * roll(state, -1, 0)) + (
                links[2] * roll(state, 1, 1) + links[3] * roll(state, -1, 1)
            ) + source
            state, previous = advance(k, state, lambda: previous, total), state
        results.append(state)
    return results


def needed(halo):
    if halo > 8:
        return list(range(GROUPS))
    return list(range(8)) + ([8, 11] if halo > 0 else [])


def solve_kernel(
    place_ref, s_ref, x_ref, c_ref, k_ref, one_ref, two_ref, up_ref, down_ref, left_ref, right_ref, diag_ref, spread_ref,
    wide_ref, fromleft_ref, fromright_ref, out_ref, base_out_ref,
    c_ext, k_ext, f_ext, bound, link_up, link_down, link_left, link_right, inv_ext, src, state, alt,
):
    lane = lane_iota()
    row, col = place_ref[1], place_ref[2]
    has_left, has_right = col > 0, col < place_ref[4]

    start = 2 * GROUPS
    quarter = (lane % 64) // 16
    take_left, take_right = (quarter == 0) & has_left, (quarter == 3) & has_right
    from_left = [fromleft_ref[rows(start + g), :] for g in range(10)]
    from_right = [fromright_ref[rows(start + g), :] for g in range(10)]
    fields = []
    for field in range(5):
        out = []
        for g in range(5):
            right_shift = (32, 16, 0, 48, 32)[field]
            left_shift = (-32, -48, 0, -16, -32)[field]
            group = g + 5 * (field == 4)
            value = jnp.where(take_right, roll(from_right[group], right_shift, 1), wide_ref[rows(5 * field + g), :])
            out.append(jnp.where(take_left, roll(from_left[group], left_shift, 1), value))
        fields.append(jnp.concatenate(out, axis=0))
    solved = base_solve((fields[0], fields[1], (fields[2], fields[3]), fields[4]))
    for t in range(STEPS):
        pieces = halves(solved[t])
        for n in range(2):
            bound[2 * t + n] = jnp.dot(pieces, spread_ref[n], preferred_element_type=F32)
    for n in range(2):
        base_out_ref[n] = roll(solved[1][0:8], -(64 * n + 16), 1)[:, 0:32]

    def third(part, chunk, g):
        right_ok, left_ok = has_right, has_left
        if g in (8, 9):
            right_ok, left_ok = right_ok & (row < place_ref[3]), left_ok & (row < place_ref[3])
        if g in (10, 11):
            right_ok, left_ok = right_ok & (row > 0), left_ok & (row > 0)
        right = jnp.where((lane // 16 == chunk) & right_ok, fromright_ref[rows(part * GROUPS + g), :], 0.0)
        value = jnp.where((lane // 16 == (chunk + 7) % 8) & left_ok, fromleft_ref[rows(part * GROUPS + g), :], right)
        return roll(value, -16 * chunk, 1)

    sub, sub3 = sub_iota(), sub_iota(384)

    def above(value, before, index):
        return jnp.where(index == 0, roll(before, 1, 0), roll(value, 1, 0))

    def below(value, after, index):
        return jnp.where(index == 7, roll(after, -1, 0), roll(value, -1, 0))

    for i in range(4):
        d, n = i // 2, i % 2

        def wide(ref, g, extra, index=i):
            return jnp.concatenate([ref[index, rows(g), :], extra], axis=1)

        if n == 0:
            for g in range(GROUPS):
                c_ext[rows(g), :] = wide(c_ref, g, third(1, d, g), d)
                k_ext[rows(g), :] = wide(k_ref, g, third(1, 2 + d, g), d)
        sheets = [third(0, i, g) for g in range(GROUPS)]
        for g in range(GROUPS):
            here = sheets[g]
            inside = here > 0.0
            low, high = s_ref[i, rows(g), pl.ds(0, 128)], s_ref[i, rows(g), pl.ds(128, 128)]
            after = jnp.where(lane == 127, roll(low, -1, 1), roll(here, -1, 1))
            before = jnp.where(lane == 0, roll(high, 1, 1), roll(here, 1, 1))
            right = jnp.where(inside, connect(here, after), 0.0)
            left = jnp.where(inside, connect(here, before), 0.0)
            down = jnp.where(inside, connect(here, below(here, sheets[(g + 1) % GROUPS], sub)), 0.0)
            up = jnp.where(inside, connect(here, above(here, sheets[(g - 1) % GROUPS], sub)), 0.0)
            first = jnp.where(lane == 0, roll(right, 1, 1), 0.0)
            final = jnp.where(lane == 127, roll(left, -1, 1), 0.0)
            diag = wide(diag_ref, g, 0.0 * here) + jnp.concatenate(
                [first, final, c_ext[rows(g), pl.ds(256, 128)] + up + down + left + right
                 + VIA_CONDUCT * k_ext[rows(g), pl.ds(256, 128)]], axis=1)
            inverse = jnp.where(diag > 0.0, 1.0 / diag, 0.0)
            inv_ext[rows(g), :] = inverse
            zero = jnp.zeros_like(first)
            link_up[rows(g), :] = inverse * wide(up_ref, g, up)
            link_down[rows(g), :] = inverse * wide(down_ref, g, down)
            link_left[rows(g), :] = inverse * (wide(left_ref, g, left) + jnp.concatenate([first, zero, zero], axis=1))
            link_right[rows(g), :] = inverse * (wide(right_ref, g, right) + jnp.concatenate([zero, final, zero], axis=1))
            drop = third(0, 4 + i, g)
            state[rows(g), :] = wide(x_ref, g, drop)
            one = third(1, 4 + i, g)
            f_ext[0, rows(g), :] = wide(one_ref, g, c_ext[rows(g), pl.ds(256, 128)] * drop + one)
            if g not in (9, 10):
                two = jnp.where(lane < 64, roll(one, -11, 1), roll(one, 11, 1))
                f_ext[1, rows(g), :] = wide(two_ref, g, two)

        for t in range(STEPS):
            for k in range(SWEEPS):
                now, then = (alt, state) if k % 2 else (state, alt)
                for g in needed(11 - 6 * t - k):
                    value = now[rows(g), :]
                    total = link_up[rows(g), :] * above(value, now[rows((g - 1) % GROUPS), :], sub3)
                    total = total + link_down[rows(g), :] * below(value, now[rows((g + 1) % GROUPS), :], sub3)
                    total = total + (
                        link_left[rows(g), :] * roll(value, 1, 1) + link_right[rows(g), :] * roll(value, -1, 1))
                    if k == 0:
                        spread = jnp.broadcast_to(bound[2 * t + n, pl.ds(base_row(g), 1), :], (8, 384))
                        source = f_ext[t, rows(g), :] + k_ext[rows(g), :] * spread
                        if t:
                            source = source + c_ext[rows(g), :] * value
                        source = inv_ext[rows(g), :] * source
                        src[rows(g), :] = source
                    else:
                        source = src[rows(g), :]
                    then[rows(g), :] = advance(k, value, lambda: then[rows(g), :], total + source)
        for g in range(8):
            out_ref[d, n, rows(g), :] = state[rows(g), pl.ds(0, 256)]


def base_row(g):
    return g if g < 10 else 28 + g


def spec(count):
    return [pl.BlockSpec(memory_space=pltpu.VMEM)] * count


def smem():
    return pl.BlockSpec(memory_space=pltpu.SMEM)


def call(kernel, name, outs, ins, scratch=(), limit=24):
    return pl.pallas_call(
        kernel,
        out_shape=outs,
        in_specs=ins,
        out_specs=spec(len(outs)),
        scratch_shapes=list(scratch),
        compiler_params=pltpu.CompilerParams(vmem_limit_bytes=limit * 1024 * 1024),
        name=name,
    )


def arr(*shape, dtype=F32):
    return jax.ShapeDtypeStruct(shape, dtype)


def swaps(count, offset, distance=1):
    pairs = []
    for i in range(count):
        if ((i - offset) // distance) % 2 == 0:
            j = (i + distance) % count
            pairs += [(i, j), (j, i)]
    return pairs


def per_device(
    sheet_res, capacity, drop_start, load_cell, load_current, via_cell, via_current, base_sheet, base_start, bump_cell
):
    row_count = lax.axis_size("row")
    col_count = lax.axis_size("col")
    place = jnp.stack(
        [lax.axis_index("die"), lax.axis_index("row"), lax.axis_index("col"), row_count - 1, col_count - 1]
    ).astype(jnp.int32)
    others = [(0, 1), (1, 0)]

    packed, send = call(pack_kernel, "pack_vias", (arr(2, VIAS, 8, 128), arr(VIAS + 1, 8, 128)), [smem()] + spec(1))(
        place, via_current
    )
    got = lax.ppermute(send, "die", others)
    far = call(base_kernel, "pack_base", (arr(8 * BASE, 128),), [smem()] + spec(3))(
        bump_cell, base_sheet, base_start, send
    )[0]
    near = lax.ppermute(far, "row", swaps(row_count, 0, 2))
    after = lax.ppermute(far, "row", swaps(row_count, 2, 2))

    cells, load_cells, loads, spread, counts = call(
        prepare_kernel, "spread_cells",
        (arr(4, VIAS, 8, 128), arr(4, 8, 128), arr(4, 4, 8, 128), arr(256, 1024, dtype=jnp.bfloat16), arr(4, 64, 128)),
        spec(3),
    )(via_cell, load_cell, load_current)

    rows_shape = arr(8 * ROW_GROUPS, 128)
    field, even, odd, base, shares = call(
        place_kernel, "place_vias", (arr(4, 4, 64, 128), rows_shape, rows_shape, arr(8 * BASE, 128), arr(16, 128)),
        [smem()] + spec(14), [pltpu.VMEM((4, 4, VIAS, 8, 128), F32)],
    )(place, packed, send, got, cells, load_cells, loads, spread, counts, far, near, after, sheet_res, capacity, drop_start)

    even = lax.ppermute(even, "row", swaps(row_count, 0))
    odd = lax.ppermute(odd, "row", swaps(row_count, 1))
    shares = lax.ppermute(shares, "die", others)

    strip_shape = arr(8 * COL_GROUPS, 128)
    left, right, wide = call(
        strip_kernel, "column_strips", (strip_shape, strip_shape, arr(200, 128)), [smem()] + spec(11)
    )(place, sheet_res, capacity, drop_start, counts, field, base, even, odd, near, after, shares)
    from_right = lax.ppermute(left, "col", [(i, (i - 1) % col_count) for i in range(col_count)])
    from_left = lax.ppermute(right, "col", [(i, (i + 1) % col_count) for i in range(col_count)])

    image, pair = arr(4, 96, 256), arr(2, 96, 256)
    parts = call(
        assemble_kernel, "assemble",
        (image, image, pair, pair) + (image,) * 7 + (arr(2, 256, 384, dtype=jnp.bfloat16),), [smem()] + spec(7),
    )(place, sheet_res, capacity, drop_start, counts, field, even, odd)

    ext = pltpu.VMEM((96, 384), F32)
    scratch = [ext, ext, pltpu.VMEM((2, 96, 384), F32), pltpu.VMEM((4, 40, 384), F32)] + [ext] * 8
    return call(solve_kernel, "solve", (arr(2, 2, 64, 256), arr(2, 8, 32)), [smem()] + spec(15), scratch)(
        place, *parts, wide, from_left, from_right
    )


def solution(mesh):
    in_specs = (
        P("die", None, "row", "col"),
        P("die", "row", "col"),
        P("die", None, "row", "col"),
        P("die", "row", "col"),
        P(None, "die", None, "row", "col"),
        P("die", None, "row", "col"),
        P(None, "die", None, None, "row", "col"),
        P(None, "row", "col"),
        P(None, "row", "col"),
        P("row", "col"),
    )
    out_specs = (P("die", None, "row", "col"), P(None, "row", "col"))
    return jax.shard_map(
        per_device, mesh=mesh, in_specs=in_specs, out_specs=out_specs, check_vma=False
    )
```

```python
import jax
import jax.numpy as jnp
from jax import lax
from jax.experimental import pallas as pl
from jax.experimental.pallas import tpu as pltpu
from jax.sharding import PartitionSpec as P

SWEEPS = 6
STEPS = 2
VIAS = 32

VIA_CONDUCT = 1.0
VIA_RESIST = 4.0
BUMP_CONDUCT = 50.0
BASE_CAPACITY = 0.1
LOWER_BOUND = 0.1
UPPER_BOUND = 1.9

MIDDLE = 0.5 * (UPPER_BOUND + LOWER_BOUND)
HALF = 0.5 * (UPPER_BOUND - LOWER_BOUND)

GROUPS = 12
F32 = jnp.float32


def sweep_weights():
    scaled = MIDDLE / HALF
    ratio = 1.0 / scaled
    pairs = []
    for _ in range(SWEEPS - 1):
        following = 1.0 / (2.0 * scaled - ratio)
        pairs.append((following * ratio, 2.0 * following / HALF))
        ratio = following
    return pairs


WEIGHTS = sweep_weights()


def lane_iota():
    return lax.broadcasted_iota(jnp.int32, (8, 128), 1)


def sub_iota(width=128):
    return lax.broadcasted_iota(jnp.int32, (8, width), 0)


def roll(x, shift, axis):
    shift = shift % x.shape[axis]
    return pltpu.roll(x, shift, axis) if shift else x


def rows(g):
    return pl.ds(8 * g, 8)


def pack_kernel(place_ref, via_ref, packed_ref, send_ref):
    later = place_ref[0].astype(F32)
    total = jnp.zeros((8, 128), F32)
    for v in range(VIAS):
        parts = []
        for d in range(2):
            part = jnp.concatenate([via_ref[t, d, n, v] for t in range(2) for n in range(2)], axis=1)
            packed_ref[d, v] = part
            parts.append(part)
        both = parts[0] + parts[1]
        send_ref[v] = both + later * parts[0]
        total = total + both
    send_ref[VIAS] = total


def spread_nets(ref):
    gap = jnp.zeros((8, 16), F32)
    return jnp.concatenate([gap, ref[0], gap, gap, ref[1], gap], axis=1)


def base_kernel(bump_ref, sheet_ref, start_ref, send_ref, far_ref):
    lane, sub = lane_iota(), sub_iota()
    bump = jnp.zeros((8, 128), F32)
    column = lane % 64 - 16
    for k in range(4):
        bump = jnp.where((column // 8 == k) & (sub * 8 + column % 8 == bump_ref[0, k]), 1.0, bump)
    far_ref[rows(0), :] = spread_nets(sheet_ref)
    far_ref[rows(1), :] = spread_nets(start_ref)
    far_ref[rows(2), :] = bump
    far_ref[rows(3), :] = send_ref[VIAS]


def spread_matrix(height, width):
    row = lax.broadcasted_iota(jnp.int32, (height, width), 0) % 128
    column = lax.broadcasted_iota(jnp.int32, (height, width), 1)
    return jnp.where(row == column // 8, 1.0, 0.0).astype(jnp.bfloat16)


def halves(value):
    high = value.astype(jnp.bfloat16)
    low = (value - high.astype(F32)).astype(jnp.bfloat16)
    return jnp.concatenate([high, low], axis=1)


def prepare_kernel(cell_ref, load_cell_ref, load_ref, cells_ref, load_cells_ref, loads_ref, spread_ref, counts_ref):
    within = (lane_iota() % 8).astype(F32)
    spread = spread_matrix(32, 256)
    for d in range(2):
        cells = cell_ref[d].reshape(8 * VIAS, 32).astype(F32).astype(jnp.bfloat16)
        wide = jnp.dot(cells, spread, preferred_element_type=F32)
        load_cell = load_cell_ref[d].astype(F32).astype(jnp.bfloat16)
        load_cell = jnp.dot(load_cell, spread, preferred_element_type=F32)
        for half in range(2):
            lanes = slice(128 * half, 128 * half + 128)
            for v in range(VIAS):
                cells_ref[2 * d + half, v] = wide[8 * v : 8 * v + 8, lanes] - within
            load_cells_ref[2 * d + half] = load_cell[:, lanes] - within
    spread_ref[...] = spread_matrix(256, 1024)
    loads = jnp.concatenate([load_ref[t, d, n] for d in range(2) for t in range(2) for n in range(2)], axis=0)
    high = loads.astype(jnp.bfloat16)
    low = (loads - high.astype(F32)).astype(jnp.bfloat16)
    wide = jnp.dot(high, spread, preferred_element_type=F32) + jnp.dot(low, spread, preferred_element_type=F32)
    for d in range(2):
        for half in range(2):
            for m in range(4):
                loads_ref[2 * d + half, m] = wide[32 * d + 8 * m : 32 * d + 8 * m + 8, 128 * half : 128 * half + 128]

    def count(i, carry):
        state = [jnp.zeros((8, 128), F32) for _ in range(8)]
        for v in range(VIAS):
            cell = cells_ref[i, v]
            for oi in range(8):
                state[oi] = state[oi] + jnp.where(cell == 8.0 * oi, 1.0, 0.0)
        for oi in range(8):
            counts_ref[i, pl.ds(oi, 8, stride=8), :] = state[oi]
        return carry

    lax.fori_loop(0, 4, count, 0)


def shared(first, second, shift):
    return jnp.where(sub_iota() < shift, first, roll(second, shift, 0))


def shared_low(first, second, shift):
    return jnp.where(sub_iota() >= shift, first, roll(second, shift, 0))


def place_kernel(
    place_ref, packed_ref, send_ref, got_ref, cells_ref, load_cells_ref, loads_ref, spread_ref, counts_ref, far_ref,
    near_ref, next_ref, sheet_ref, cap_ref, drop_ref, field_ref, even_ref, odd_ref, base_ref, shares_ref, values_ref,
):
    lane = lane_iota()
    later = place_ref[0].astype(F32)
    even = place_ref[1] % 2 == 0
    weights = (
        (VIA_RESIST * (4.0 - 2.0 * later), VIA_RESIST * (3.0 - 2.0 * later), VIA_RESIST * (1.0 + later)),
        (VIA_RESIST * (3.0 - 2.0 * later), VIA_RESIST * (3.0 - 2.0 * later), VIA_RESIST),
    )
    size = (8 * VIAS, 128)
    first, second, got = packed_ref[0].reshape(size), packed_ref[1].reshape(size), got_ref[0:VIAS].reshape(size)
    for d in range(2):
        mixed = weights[d][0] * first + weights[d][1] * second + weights[d][2] * got
        wide = jnp.dot(halves(mixed), spread_ref[...], preferred_element_type=F32)
        for half in range(2):
            for m in range(4):
                start = 256 * m + 128 * half
                values_ref[2 * d + half, m] = wide[:, start : start + 128].reshape(VIAS, 8, 128)

    def add(i, carry):
        cell = load_cells_ref[i]
        loads = [loads_ref[i, m] for m in range(4)]
        state = []
        for oi in range(8):
            hit = cell == 8.0 * oi
            state.append([jnp.where(hit, load, 0.0) for load in loads])
        for v in range(VIAS):
            cell = cells_ref[i, v]
            values = [values_ref[i, m, v] for m in range(4)]
            for oi in range(8):
                hit = cell == 8.0 * oi
                state[oi] = [old + jnp.where(hit, value, 0.0) for old, value in zip(state[oi], values)]
        for oi in range(8):
            for m in range(4):
                field_ref[m, i, pl.ds(oi, 8, stride=8), :] = state[oi][m]
        return carry

    lax.fori_loop(0, 4, add, 0)

    shares_ref[rows(0), :] = near_ref[rows(3), :]
    shares_ref[rows(1), :] = next_ref[rows(3), :]

    place = 0

    def put(up, down):
        nonlocal place
        even_ref[rows(place), :] = jnp.where(even, down, up)
        odd_ref[rows(place), :] = jnp.where(even, up, down)
        place += 1

    def pair(first, second):
        put(first(0), first(7))
        put(second(0), second(7))
        put(shared(first(1), second(1), 4), shared_low(first(6), second(6), 4))

    for d in range(2):
        for half in range(2):
            lanes = pl.ds(half * 128, 128)
            for n in range(2):
                pair(lambda g: sheet_ref[d, n, rows(g), lanes], lambda g: drop_ref[d, n, rows(g), lanes])
                one = lambda g: field_ref[n, 2 * d + half, rows(g), :]
                two = lambda g: field_ref[2 + n, 2 * d + half, rows(g), :]
                put(one(0), one(7))
                put(shared(one(1), two(0), 3), shared_low(one(6), two(7), 5))
            pair(lambda g: cap_ref[d, rows(g), lanes], lambda g: counts_ref[2 * d + half, rows(g), :])

    parts = [far_ref[rows(0), :], far_ref[rows(1), :], far_ref[rows(2), :], send_ref[VIAS] + got_ref[VIAS]]
    for part in range(4):
        base_ref[rows(part), :] = parts[part]
        put(parts[part], parts[part])


BASE = 4
ROW_GROUPS = 52 + BASE


def row_place(d, half, n, kind):
    start = (d * 2 + half) * 13
    return start + 10 if kind == 2 else start + 5 * n + 3 * kind


def near_rows(read, d, half, n, kind, second, upper):
    start = row_place(d, half, n, kind)
    if kind == 1:
        if second:
            return roll(read(start + 1), -5 if upper else -3, 0), None
        return read(start), read(start + 1)
    last = read(start + 2)
    if second:
        return read(start + 1), roll(last, -4, 0)
    return read(start), last


def column_groups(own, below, above, d, half, n, kind, second):
    low = near_rows(below, d, half, n, kind, second, False)
    high = near_rows(above, d, half, n, kind, second, True)
    return [own(g) for g in range(8)] + [low[0], low[1], high[1], high[0]]


COL_GROUPS = 2 * GROUPS + 10


def strip_kernel(
    place_ref, sheet_ref, cap_ref, drop_ref, counts_ref, field_ref, base_ref, even_ref, odd_ref, near_ref, next_ref, far_ref,
    left_ref, right_ref, wide_ref,
):
    lane = lane_iota()
    within = lane % 16
    row, last = place_ref[1], place_ref[3]
    even, low = row % 2 == 0, row % 4 < 2

    def below(g):
        return jnp.where(even, even_ref[rows(g), :], odd_ref[rows(g), :])

    def above(g):
        return jnp.where(even, odd_ref[rows(g), :], even_ref[rows(g), :])

    own = (lane % 64 >= 16) & (lane % 64 < 48)

    def spread_steps(value):
        out = []
        for t in range(2):
            moved = jnp.where(lane < 64, roll(value, 16 - 64 * t, 1), roll(value, 48 - 64 * t, 1))
            out.append(jnp.where(own, moved, 0.0))
        return out

    groups = []
    for g in range(5):
        if g == 0:
            parts = [base_ref[rows(f), :] for f in range(BASE)]
        elif g in (1, 4):
            read, inside = (below, row < last) if g == 1 else (above, row > 0)
            parts = [jnp.where(inside, read(ROW_GROUPS - BASE + f), 0.0) for f in range(BASE)]
        else:
            inside = row + 2 <= last if g == 2 else row >= 2
            flag = low if g == 2 else jnp.logical_not(low)
            parts = [jnp.where(flag, near_ref[rows(f), :], next_ref[rows(f), :]) for f in range(BASE)]
            parts[3] = parts[3] + jnp.where(flag, far_ref[rows(0), :], far_ref[rows(1), :])
            parts = [jnp.where(inside, part, 0.0) for part in parts]
        one, two = spread_steps(parts[3])
        groups.append([parts[0], parts[1], one, two, parts[2]])
        for f in range(5):
            wide_ref[rows(5 * f + g), :] = groups[g][f]

    def fields(half):
        lanes = pl.ds(half * 128, 128)
        first, second = [], []
        for d in range(2):
            for n in range(2):
                first.append(column_groups(lambda g: sheet_ref[d, n, rows(g), lanes], below, above, d, half, n, 0, False))
        for d in range(2):
            for n in range(2):
                first.append(column_groups(lambda g: drop_ref[d, n, rows(g), lanes], below, above, d, half, n, 0, True))
        for d in range(2):
            second.append(column_groups(lambda g: cap_ref[d, rows(g), lanes], below, above, d, half, 0, 2, False))
        for d in range(2):
            second.append(
                column_groups(lambda g: counts_ref[2 * d + half, rows(g), :], below, above, d, half, 0, 2, True))
        for d in range(2):
            for n in range(2):
                one = column_groups(
                    lambda g: field_ref[n, 2 * d + half, rows(g), :], below, above, d, half, n, 1, False)
                two = column_groups(
                    lambda g: field_ref[2 + n, 2 * d + half, rows(g), :], below, above, d, half, n, 1, True)
                merged = []
                for a, b in zip(one, two):
                    if b is None:
                        merged.append(a)
                    elif half == 0:
                        merged.append(jnp.where(within < 11, a, roll(b, 11, 1)))
                    else:
                        merged.append(jnp.where(within >= 5, a, roll(b, -11, 1)))
                second.append(merged)
        return first, second

    for half, ref in ((0, left_ref), (1, right_ref)):
        for part, chunks in enumerate(fields(half)):
            for g in range(GROUPS):
                out = chunks[0][g]
                for k in range(1, 8):
                    out = jnp.where((lane // 16 + half) % 8 == k, roll(chunks[k][g], 16 * k, 1), out)
                ref[rows(part * GROUPS + g), :] = out

    start = 2 * GROUPS
    quarter = (lane % 64) // 16
    for g in range(5):
        sheet, drop, one, two, bump = groups[g]
        left = jnp.where(
            quarter == 1, sheet,
            jnp.where(quarter == 2, roll(drop, 16, 1), jnp.where(quarter == 3, roll(one, 32, 1), roll(two, -16, 1))),
        )
        right = jnp.where(
            quarter == 2, sheet,
            jnp.where(quarter == 3, roll(drop, 16, 1), jnp.where(quarter == 1, roll(two, -16, 1), roll(one, -32, 1))),
        )
        left_ref[rows(start + g), :] = left
        right_ref[rows(start + g), :] = right
        left_ref[rows(start + 5 + g), :] = bump
        right_ref[rows(start + 5 + g), :] = bump


def assemble_kernel(
    place_ref, sheet_ref, cap_ref, drop_ref, counts_ref, field_ref, even_ref, odd_ref,
    s_ref, x_ref, c_ref, k_ref, one_ref, two_ref, up_ref, down_ref, left_ref, right_ref, diag_ref, spread_ref,
):
    row, last = place_ref[1], place_ref[3]
    even = row % 2 == 0
    sub, lane = sub_iota(256), lax.broadcasted_iota(jnp.int32, (8, 256), 1)

    def below(g):
        return jnp.where(row < last, jnp.where(even, even_ref[rows(g), :], odd_ref[rows(g), :]), 0.0)

    def above(g):
        return jnp.where(row > 0, jnp.where(even, odd_ref[rows(g), :], even_ref[rows(g), :]), 0.0)

    def both(own, d, n, kind, second):
        sides = [column_groups(lambda g: own(half, g), below, above, d, half, n, kind, second) for half in range(2)]
        return [None if a is None else jnp.concatenate([a, b], axis=1) for a, b in zip(*sides)]

    for d in range(2):
        caps = both(lambda half, g: cap_ref[d, rows(g), pl.ds(half * 128, 128)], d, 0, 2, False)
        counts = both(lambda half, g: counts_ref[2 * d + half, rows(g), :], d, 0, 2, True)
        for g in range(GROUPS):
            c_ref[d, rows(g), :] = caps[g]
            k_ref[d, rows(g), :] = counts[g]
        for n in range(2):
            i = 2 * d + n
            sheets = both(lambda half, g: sheet_ref[d, n, rows(g), pl.ds(half * 128, 128)], d, n, 0, False)
            drops = both(lambda half, g: drop_ref[d, n, rows(g), pl.ds(half * 128, 128)], d, n, 0, True)
            ones = both(lambda half, g: field_ref[n, 2 * d + half, rows(g), :], d, n, 1, False)
            twos = both(lambda half, g: field_ref[2 + n, 2 * d + half, rows(g), :], d, n, 1, True)
            for g in range(GROUPS):
                s_ref[i, rows(g), :] = sheets[g]
                x_ref[i, rows(g), :] = drops[g]
                one_ref[i, rows(g), :] = c_ref[d, rows(g), :] * drops[g] + ones[g]
                if twos[g] is not None:
                    two_ref[i, rows(g), :] = twos[g]
            for g in range(GROUPS):
                here, after = s_ref[i, rows(g), :], s_ref[i, rows((g + 1) % GROUPS), :]
                under = jnp.where(sub == 7, roll(after, -1, 0), roll(here, -1, 0))
                inside = here > 0.0
                down_ref[i, rows(g), :] = jnp.where(inside, connect(here, under), 0.0)
                right = jnp.where(inside & (lane < 255), connect(here, roll(here, -1, 1)), 0.0)
                right_ref[i, rows(g), :] = right
                left_ref[i, rows(g), :] = roll(right, 1, 1)
            for g in range(GROUPS):
                here, before = down_ref[i, rows(g), :], down_ref[i, rows((g - 1) % GROUPS), :]
                up = jnp.where(sub == 0, roll(before, 1, 0), roll(here, 1, 0))
                up_ref[i, rows(g), :] = up
                diag = c_ref[d, rows(g), :] + up + here + left_ref[i, rows(g), :] + right_ref[i, rows(g), :]
                diag_ref[i, rows(g), :] = diag + VIA_CONDUCT * k_ref[d, rows(g), :]
    source = lax.broadcasted_iota(jnp.int32, (256, 384), 0) % 128
    column = lax.broadcasted_iota(jnp.int32, (256, 384), 1)
    column = jnp.where(column < 256, 16 + column // 8, jnp.where(column < 320, 48, 0) + (column - 256) // 8)
    for n in range(2):
        spread_ref[n] = jnp.where(source == column + 64 * n, 1.0, 0.0).astype(jnp.bfloat16)


def connect(center, neighbour):
    return jnp.where(neighbour > 0.0, 2.0 / (center + neighbour), 0.0)


def three_terms(k):
    if k == 0:
        return 1.0 - 1.0 / MIDDLE, 0.0, 1.0 / MIDDLE
    a, b = WEIGHTS[k - 1]
    return 1.0 + a - b, -a, b


def advance(k, value, previous, total):
    fore, back, gain = three_terms(k)
    out = total if gain == 1.0 else gain * total
    if fore != 0.0:
        out = out + fore * value
    return out + back * previous() if k else out


def base_solve(fields):
    sheet, state, arriving, bump = fields
    steps = [(1, 0), (-1, 0), (1, 1), (-1, 1)]
    inside = sheet > 0.0
    links = [jnp.where(inside, connect(sheet, roll(sheet, s, a)), 0.0) for s, a in steps]
    diagonal = BASE_CAPACITY + links[0] + links[1] + links[2] + links[3] + BUMP_CONDUCT * bump
    inverse = 1.0 / diagonal
    links = [inverse * link for link in links]
    results = []
    for t in range(STEPS):
        source = inverse * (BASE_CAPACITY * state + arriving[t])
        previous = None
        for k in range(SWEEPS):
            total = (links[0] * roll(state, 1, 0) + links[1] * roll(state, -1, 0)) + (
                links[2] * roll(state, 1, 1) + links[3] * roll(state, -1, 1)
            ) + source
            state, previous = advance(k, state, lambda: previous, total), state
        results.append(state)
    return results


def needed(halo):
    if halo > 8:
        return list(range(GROUPS))
    return list(range(8)) + ([8, 11] if halo > 0 else [])


def solve_kernel(
    place_ref, s_ref, x_ref, c_ref, k_ref, one_ref, two_ref, up_ref, down_ref, left_ref, right_ref, diag_ref, spread_ref,
    wide_ref, fromleft_ref, fromright_ref, out_ref, base_out_ref,
    c_ext, k_ext, f_ext, bound, link_up, link_down, link_left, link_right, inv_ext, src, state, alt,
):
    lane = lane_iota()
    row, col = place_ref[1], place_ref[2]
    has_left, has_right = col > 0, col < place_ref[4]

    start = 2 * GROUPS
    quarter = (lane % 64) // 16
    take_left, take_right = (quarter == 0) & has_left, (quarter == 3) & has_right
    from_left = [fromleft_ref[rows(start + g), :] for g in range(10)]
    from_right = [fromright_ref[rows(start + g), :] for g in range(10)]
    fields = []
    for field in range(5):
        out = []
        for g in range(5):
            right_shift = (32, 16, 0, 48, 32)[field]
            left_shift = (-32, -48, 0, -16, -32)[field]
            group = g + 5 * (field == 4)
            value = jnp.where(take_right, roll(from_right[group], right_shift, 1), wide_ref[rows(5 * field + g), :])
            out.append(jnp.where(take_left, roll(from_left[group], left_shift, 1), value))
        fields.append(jnp.concatenate(out, axis=0))
    solved = base_solve((fields[0], fields[1], (fields[2], fields[3]), fields[4]))
    for t in range(STEPS):
        pieces = halves(solved[t])
        for n in range(2):
            bound[2 * t + n] = jnp.dot(pieces, spread_ref[n], preferred_element_type=F32)
    for n in range(2):
        base_out_ref[n] = roll(solved[1][0:8], -(64 * n + 16), 1)[:, 0:32]

    def third(part, chunk, g):
        right_ok, left_ok = has_right, has_left
        if g in (8, 9):
            right_ok, left_ok = right_ok & (row < place_ref[3]), left_ok & (row < place_ref[3])
        if g in (10, 11):
            right_ok, left_ok = right_ok & (row > 0), left_ok & (row > 0)
        right = jnp.where((lane // 16 == chunk) & right_ok, fromright_ref[rows(part * GROUPS + g), :], 0.0)
        value = jnp.where((lane // 16 == (chunk + 7) % 8) & left_ok, fromleft_ref[rows(part * GROUPS + g), :], right)
        return roll(value, -16 * chunk, 1)

    sub, sub3 = sub_iota(), sub_iota(384)

    def above(value, before, index):
        return jnp.where(index == 0, roll(before, 1, 0), roll(value, 1, 0))

    def below(value, after, index):
        return jnp.where(index == 7, roll(after, -1, 0), roll(value, -1, 0))

    for i in range(4):
        d, n = i // 2, i % 2

        def wide(ref, g, extra, index=i):
            return jnp.concatenate([ref[index, rows(g), :], extra], axis=1)

        if n == 0:
            for g in range(GROUPS):
                c_ext[rows(g), :] = wide(c_ref, g, third(1, d, g), d)
                k_ext[rows(g), :] = wide(k_ref, g, third(1, 2 + d, g), d)
        @pl.when(place_ref[3] >= 0)
        def _():
            sheets = [third(0, i, g) for g in range(GROUPS)]
            for g in range(GROUPS):
                here = sheets[g]
                inside = here > 0.0
                low, high = s_ref[i, rows(g), pl.ds(0, 128)], s_ref[i, rows(g), pl.ds(128, 128)]
                after = roll(jnp.where(lane == 0, low, here), -1, 1)
                before = roll(jnp.where(lane == 127, high, here), 1, 1)
                right = jnp.where(inside, connect(here, after), 0.0)
                left = jnp.where(inside, connect(here, before), 0.0)
                down = jnp.where(inside, connect(here, below(here, sheets[(g + 1) % GROUPS], sub)), 0.0)
                up = jnp.where(inside, connect(here, above(here, sheets[(g - 1) % GROUPS], sub)), 0.0)
                first = jnp.where(lane == 0, roll(right, 1, 1), 0.0)
                final = jnp.where(lane == 127, roll(left, -1, 1), 0.0)
                diag = wide(diag_ref, g, 0.0 * here) + jnp.concatenate(
                    [first, final, c_ext[rows(g), pl.ds(256, 128)] + up + down + left + right
                     + VIA_CONDUCT * k_ext[rows(g), pl.ds(256, 128)]], axis=1)
                inverse = jnp.where(diag > 0.0, 1.0 / diag, 0.0)
                inv_ext[rows(g), :] = inverse
                zero = jnp.zeros_like(first)
                link_up[rows(g), :] = inverse * wide(up_ref, g, up)
                link_down[rows(g), :] = inverse * wide(down_ref, g, down)
                link_left[rows(g), :] = inverse * (wide(left_ref, g, left) + jnp.concatenate([first, zero, zero], axis=1))
                link_right[rows(g), :] = inverse * (wide(right_ref, g, right) + jnp.concatenate([zero, final, zero], axis=1))
                drop = third(0, 4 + i, g)
                state[rows(g), :] = wide(x_ref, g, drop)
                one = third(1, 4 + i, g)
                f_ext[0, rows(g), :] = wide(one_ref, g, c_ext[rows(g), pl.ds(256, 128)] * drop + one)
                if g not in (9, 10):
                    two = jnp.where(lane < 64, roll(one, -11, 1), roll(one, 11, 1))
                    f_ext[1, rows(g), :] = wide(two_ref, g, two)

        @pl.when(place_ref[3] >= 0)
        def _():
            for t in range(STEPS):
                for k in range(SWEEPS):
                    now, then = (alt, state) if k % 2 else (state, alt)
                    for g in needed(11 - 6 * t - k):
                        value = now[rows(g), :]
                        total = link_up[rows(g), :] * above(value, now[rows((g - 1) % GROUPS), :], sub3)
                        total = total + link_down[rows(g), :] * below(value, now[rows((g + 1) % GROUPS), :], sub3)
                        total = total + (
                            link_left[rows(g), :] * roll(value, 1, 1) + link_right[rows(g), :] * roll(value, -1, 1))
                        if k == 0:
                            spread = jnp.broadcast_to(bound[2 * t + n, pl.ds(base_row(g), 1), :], (8, 384))
                            source = f_ext[t, rows(g), :] + k_ext[rows(g), :] * spread
                            if t:
                                source = source + c_ext[rows(g), :] * value
                            source = inv_ext[rows(g), :] * source
                            src[rows(g), :] = source
                        else:
                            source = src[rows(g), :]
                        then[rows(g), :] = advance(k, value, lambda: then[rows(g), :], total + source)

        for g in range(8):
            out_ref[d, n, rows(g), :] = state[rows(g), pl.ds(0, 256)]


def base_row(g):
    return g if g < 10 else 28 + g


def spec(count):
    return [pl.BlockSpec(memory_space=pltpu.VMEM)] * count


def smem():
    return pl.BlockSpec(memory_space=pltpu.SMEM)


def call(kernel, name, outs, ins, scratch=(), limit=24):
    return pl.pallas_call(
        kernel,
        out_shape=outs,
        in_specs=ins,
        out_specs=spec(len(outs)),
        scratch_shapes=list(scratch),
        compiler_params=pltpu.CompilerParams(vmem_limit_bytes=limit * 1024 * 1024),
        name=name,
    )


def arr(*shape, dtype=F32):
    return jax.ShapeDtypeStruct(shape, dtype)


def swaps(count, offset, distance=1):
    pairs = []
    for i in range(count):
        if ((i - offset) // distance) % 2 == 0:
            j = (i + distance) % count
            pairs += [(i, j), (j, i)]
    return pairs


def per_device(
    sheet_res, capacity, drop_start, load_cell, load_current, via_cell, via_current, base_sheet, base_start, bump_cell
):
    row_count = lax.axis_size("row")
    col_count = lax.axis_size("col")
    place = jnp.stack(
        [lax.axis_index("die"), lax.axis_index("row"), lax.axis_index("col"), row_count - 1, col_count - 1]
    ).astype(jnp.int32)
    others = [(0, 1), (1, 0)]

    packed, send = call(pack_kernel, "pack_vias", (arr(2, VIAS, 8, 128), arr(VIAS + 1, 8, 128)), [smem()] + spec(1))(
        place, via_current
    )
    got = lax.ppermute(send, "die", others)
    far = call(base_kernel, "pack_base", (arr(8 * BASE, 128),), [smem()] + spec(3))(
        bump_cell, base_sheet, base_start, send
    )[0]
    near = lax.ppermute(far, "row", swaps(row_count, 0, 2))
    after = lax.ppermute(far, "row", swaps(row_count, 2, 2))

    cells, load_cells, loads, spread, counts = call(
        prepare_kernel, "spread_cells",
        (arr(4, VIAS, 8, 128), arr(4, 8, 128), arr(4, 4, 8, 128), arr(256, 1024, dtype=jnp.bfloat16), arr(4, 64, 128)),
        spec(3),
    )(via_cell, load_cell, load_current)

    rows_shape = arr(8 * ROW_GROUPS, 128)
    field, even, odd, base, shares = call(
        place_kernel, "place_vias", (arr(4, 4, 64, 128), rows_shape, rows_shape, arr(8 * BASE, 128), arr(16, 128)),
        [smem()] + spec(14), [pltpu.VMEM((4, 4, VIAS, 8, 128), F32)],
    )(place, packed, send, got, cells, load_cells, loads, spread, counts, far, near, after, sheet_res, capacity, drop_start)

    even = lax.ppermute(even, "row", swaps(row_count, 0))
    odd = lax.ppermute(odd, "row", swaps(row_count, 1))
    shares = lax.ppermute(shares, "die", others)

    strip_shape = arr(8 * COL_GROUPS, 128)
    left, right, wide = call(
        strip_kernel, "column_strips", (strip_shape, strip_shape, arr(200, 128)), [smem()] + spec(11)
    )(place, sheet_res, capacity, drop_start, counts, field, base, even, odd, near, after, shares)
    from_right = lax.ppermute(left, "col", [(i, (i - 1) % col_count) for i in range(col_count)])
    from_left = lax.ppermute(right, "col", [(i, (i + 1) % col_count) for i in range(col_count)])

    image, pair = arr(4, 96, 256), arr(2, 96, 256)
    parts = call(
        assemble_kernel, "assemble",
        (image, image, pair, pair) + (image,) * 7 + (arr(2, 256, 384, dtype=jnp.bfloat16),), [smem()] + spec(7),
    )(place, sheet_res, capacity, drop_start, counts, field, even, odd)

    ext = pltpu.VMEM((96, 384), F32)
    scratch = [ext, ext, pltpu.VMEM((2, 96, 384), F32), pltpu.VMEM((4, 40, 384), F32)] + [ext] * 8
    return call(solve_kernel, "solve", (arr(2, 2, 64, 256), arr(2, 8, 32)), [smem()] + spec(15), scratch)(
        place, *parts, wide, from_left, from_right
    )


def solution(mesh):
    in_specs = (
        P("die", None, "row", "col"),
        P("die", "row", "col"),
        P("die", None, "row", "col"),
        P("die", "row", "col"),
        P(None, "die", None, "row", "col"),
        P("die", None, "row", "col"),
        P(None, "die", None, None, "row", "col"),
        P(None, "row", "col"),
        P(None, "row", "col"),
        P("row", "col"),
    )
    out_specs = (P("die", None, "row", "col"), P(None, "row", "col"))
    return jax.shard_map(
        per_device, mesh=mesh, in_specs=in_specs, out_specs=out_specs, check_vma=False
    )
```

```python
import jax
import jax.numpy as jnp
from jax import lax
from jax.experimental import pallas as pl
from jax.experimental.pallas import tpu as pltpu
from jax.sharding import PartitionSpec as P

SWEEPS = 6
STEPS = 2
VIAS = 32

VIA_CONDUCT = 1.0
VIA_RESIST = 4.0
BUMP_CONDUCT = 50.0
BASE_CAPACITY = 0.1
LOWER_BOUND = 0.1
UPPER_BOUND = 1.9

MIDDLE = 0.5 * (UPPER_BOUND + LOWER_BOUND)
HALF = 0.5 * (UPPER_BOUND - LOWER_BOUND)

GROUPS = 12
F32 = jnp.float32


def sweep_weights():
    scaled = MIDDLE / HALF
    ratio = 1.0 / scaled
    pairs = []
    for _ in range(SWEEPS - 1):
        following = 1.0 / (2.0 * scaled - ratio)
        pairs.append((following * ratio, 2.0 * following / HALF))
        ratio = following
    return pairs


WEIGHTS = sweep_weights()


def lane_iota():
    return lax.broadcasted_iota(jnp.int32, (8, 128), 1)


def sub_iota(width=128):
    return lax.broadcasted_iota(jnp.int32, (8, width), 0)


def roll(x, shift, axis):
    shift = shift % x.shape[axis]
    return pltpu.roll(x, shift, axis) if shift else x


def rows(g):
    return pl.ds(8 * g, 8)


def pack_kernel(place_ref, via_ref, packed_ref, send_ref):
    later = place_ref[0].astype(F32)
    total = jnp.zeros((8, 128), F32)
    for v in range(VIAS):
        parts = []
        for d in range(2):
            part = jnp.concatenate([via_ref[t, d, n, v] for t in range(2) for n in range(2)], axis=1)
            packed_ref[d, v] = part
            parts.append(part)
        both = parts[0] + parts[1]
        send_ref[v] = both + later * parts[0]
        total = total + both
    send_ref[VIAS] = total


def spread_nets(ref):
    gap = jnp.zeros((8, 16), F32)
    return jnp.concatenate([gap, ref[0], gap, gap, ref[1], gap], axis=1)


def shared(first, second, shift):
    return jnp.where(sub_iota() < shift, first, roll(second, shift, 0))


def shared_low(first, second, shift):
    return jnp.where(sub_iota() >= shift, first, roll(second, shift, 0))


class RowSender:
    def __init__(self, even, even_ref, odd_ref):
        self.even, self.even_ref, self.odd_ref, self.place = even, even_ref, odd_ref, 0

    def put(self, up, down):
        self.even_ref[rows(self.place), :] = jnp.where(self.even, down, up)
        self.odd_ref[rows(self.place), :] = jnp.where(self.even, up, down)
        self.place += 1

    def pair(self, first, second):
        self.put(first(0), first(7))
        self.put(second(0), second(7))
        self.put(shared(first(1), second(1), 4), shared_low(first(6), second(6), 4))


BASE = 4
EARLY = 30
LATE = 22


def early_kernel(
    place_ref, bump_ref, base_sheet_ref, base_start_ref, send_ref, sheet_ref, cap_ref, drop_ref, even_ref, odd_ref, base_ref
):
    lane, sub = lane_iota(), sub_iota()
    bump = jnp.zeros((8, 128), F32)
    column = lane % 64 - 16
    for k in range(4):
        bump = jnp.where((column // 8 == k) & (sub * 8 + column % 8 == bump_ref[0, k]), 1.0, bump)
    for part, value in enumerate([spread_nets(base_sheet_ref), spread_nets(base_start_ref), bump, send_ref[VIAS]]):
        base_ref[rows(part), :] = value
        even_ref[rows(EARLY + part), :] = value
    sender = RowSender(place_ref[1] % 2 == 0, even_ref, odd_ref)
    for d in range(2):
        for half in range(2):
            lanes = pl.ds(half * 128, 128)
            for n in range(2):
                sender.pair(lambda g: sheet_ref[d, n, rows(g), lanes], lambda g: drop_ref[d, n, rows(g), lanes])
        sender.pair(lambda g: cap_ref[d, rows(g), pl.ds(0, 128)], lambda g: cap_ref[d, rows(g), pl.ds(128, 128)])


def chip_kernel(place_ref, odd_ref, base_ref, got_ref, between_ref, far_ref):
    even = place_ref[1] % 2 == 0
    for g in range(EARLY):
        between_ref[rows(g), :] = odd_ref[rows(g), :]
    for part in range(BASE):
        own, got = base_ref[rows(part), :], got_ref[rows(EARLY + part), :]
        for slot, value in enumerate([jnp.where(even, own, got), jnp.where(even, got, own)]):
            between_ref[rows(EARLY + BASE * slot + part), :] = value
            far_ref[rows(BASE * slot + part), :] = value


def shares_kernel(after_ref, first_ref, between_ref, far_ref, shares_ref):
    shares_ref[rows(0), :] = first_ref[rows(EARLY + 3), :]
    for slot in range(2):
        shares_ref[rows(1 + slot), :] = between_ref[rows(EARLY + BASE * slot + 3), :]
        shares_ref[rows(3 + slot), :] = far_ref[rows(BASE * slot + 3), :]


def spread_matrix(height, width):
    row = lax.broadcasted_iota(jnp.int32, (height, width), 0) % 128
    column = lax.broadcasted_iota(jnp.int32, (height, width), 1)
    return jnp.where(row == column // 8, 1.0, 0.0).astype(jnp.bfloat16)


def halves(value):
    high = value.astype(jnp.bfloat16)
    low = (value - high.astype(F32)).astype(jnp.bfloat16)
    return jnp.concatenate([high, low], axis=1)


def prepare_kernel(cell_ref, load_cell_ref, load_ref, cells_ref, load_cells_ref, loads_ref, spread_ref, counts_ref):
    within = (lane_iota() % 8).astype(F32)
    spread = spread_matrix(32, 256)
    for d in range(2):
        cells = cell_ref[d].reshape(8 * VIAS, 32).astype(F32).astype(jnp.bfloat16)
        wide = jnp.dot(cells, spread, preferred_element_type=F32)
        load_cell = load_cell_ref[d].astype(F32).astype(jnp.bfloat16)
        load_cell = jnp.dot(load_cell, spread, preferred_element_type=F32)
        for half in range(2):
            lanes = slice(128 * half, 128 * half + 128)
            for v in range(VIAS):
                cells_ref[2 * d + half, v] = wide[8 * v : 8 * v + 8, lanes] - within
            load_cells_ref[2 * d + half] = load_cell[:, lanes] - within
    spread_ref[...] = spread_matrix(256, 1024)
    loads = jnp.concatenate([load_ref[t, d, n] for d in range(2) for t in range(2) for n in range(2)], axis=0)
    high = loads.astype(jnp.bfloat16)
    low = (loads - high.astype(F32)).astype(jnp.bfloat16)
    wide = jnp.dot(high, spread, preferred_element_type=F32) + jnp.dot(low, spread, preferred_element_type=F32)
    for d in range(2):
        for half in range(2):
            for m in range(4):
                loads_ref[2 * d + half, m] = wide[32 * d + 8 * m : 32 * d + 8 * m + 8, 128 * half : 128 * half + 128]

    def count(i, carry):
        state = [jnp.zeros((8, 128), F32) for _ in range(8)]
        for v in range(VIAS):
            cell = cells_ref[i, v]
            for oi in range(8):
                state[oi] = state[oi] + jnp.where(cell == 8.0 * oi, 1.0, 0.0)
        for oi in range(8):
            counts_ref[i, pl.ds(oi, 8, stride=8), :] = state[oi]
        return carry

    lax.fori_loop(0, 4, count, 0)


def place_kernel(
    place_ref, packed_ref, send_ref, got_ref, cells_ref, load_cells_ref, loads_ref, spread_ref, counts_ref, _,
    field_ref, even_ref, odd_ref, arriving_ref, values_ref,
):
    lane = lane_iota()
    later = place_ref[0].astype(F32)
    even = place_ref[1] % 2 == 0
    weights = (
        (VIA_RESIST * (4.0 - 2.0 * later), VIA_RESIST * (3.0 - 2.0 * later), VIA_RESIST * (1.0 + later)),
        (VIA_RESIST * (3.0 - 2.0 * later), VIA_RESIST * (3.0 - 2.0 * later), VIA_RESIST),
    )
    size = (8 * VIAS, 128)
    first, second, got = packed_ref[0].reshape(size), packed_ref[1].reshape(size), got_ref[0:VIAS].reshape(size)
    for d in range(2):
        mixed = weights[d][0] * first + weights[d][1] * second + weights[d][2] * got
        wide = jnp.dot(halves(mixed), spread_ref[...], preferred_element_type=F32)
        for half in range(2):
            for m in range(4):
                start = 256 * m + 128 * half
                values_ref[2 * d + half, m] = wide[:, start : start + 128].reshape(VIAS, 8, 128)

    def add(i, carry):
        cell = load_cells_ref[i]
        loads = [loads_ref[i, m] for m in range(4)]
        state = []
        for oi in range(8):
            hit = cell == 8.0 * oi
            state.append([jnp.where(hit, load, 0.0) for load in loads])
        for v in range(VIAS):
            cell = cells_ref[i, v]
            values = [values_ref[i, m, v] for m in range(4)]
            for oi in range(8):
                hit = cell == 8.0 * oi
                state[oi] = [old + jnp.where(hit, value, 0.0) for old, value in zip(state[oi], values)]
        for oi in range(8):
            for m in range(4):
                field_ref[m, i, pl.ds(oi, 8, stride=8), :] = state[oi][m]
        return carry

    lax.fori_loop(0, 4, add, 0)

    arriving_ref[...] = send_ref[VIAS] + got_ref[VIAS]
    sender = RowSender(even, even_ref, odd_ref)
    for d in range(2):
        for half in range(2):
            for n in range(2):
                one = lambda g: field_ref[n, 2 * d + half, rows(g), :]
                two = lambda g: field_ref[2 + n, 2 * d + half, rows(g), :]
                sender.put(one(0), one(7))
                sender.put(shared(one(1), two(0), 3), shared_low(one(6), two(7), 5))
        sender.pair(lambda g: counts_ref[2 * d, rows(g), :], lambda g: counts_ref[2 * d + 1, rows(g), :])


SHEET, DROP, CAPACITY, COUNTS, FIRST, SECOND = range(6)


def near_rows(read, kind, d, half, n, upper):
    early, late = read
    if kind in (FIRST, SECOND):
        start = 11 * d + 4 * half + 2 * n
        if kind == SECOND:
            return roll(late(start + 1), -5 if upper else -3, 0), None
        return late(start), late(start + 1)
    if kind in (SHEET, DROP):
        take, start, second = early, 15 * d + 6 * half + 3 * n, kind == DROP
    elif kind == CAPACITY:
        take, start, second = early, 15 * d + 12, half == 1
    else:
        take, start, second = late, 11 * d + 8, half == 1
    last = take(start + 2)
    return (take(start + 1), roll(last, -4, 0)) if second else (take(start), last)


def column_groups(own, below, above, kind, d, half, n):
    low = near_rows(below, kind, d, half, n, False)
    high = near_rows(above, kind, d, half, n, True)
    return [own(g) for g in range(8)] + [low[0], low[1], high[1], high[0]]


def readers(even, below, above, first_ref, between_ref, even_ref, odd_ref):
    def make(inside, flag, a_ref, b_ref):
        def read(g):
            value = jnp.where(flag, a_ref[rows(g), :], b_ref[rows(g), :])
            return value if inside is None else jnp.where(inside, value, 0.0)
        return read

    odd = jnp.logical_not(even)
    return (
        (make(below, even, first_ref, between_ref), make(below, even, even_ref, odd_ref)),
        (make(above, odd, first_ref, between_ref), make(above, odd, even_ref, odd_ref)),
    )


COL_GROUPS = 2 * GROUPS + 10


def strip_kernel(
    place_ref, sheet_ref, cap_ref, drop_ref, counts_ref, field_ref, base_ref, arriving_ref, first_ref, between_ref, far_ref,
    even_ref, odd_ref, shares_ref, left_ref, right_ref, wide_ref,
):
    lane = lane_iota()
    within = lane % 16
    row, last = place_ref[1], place_ref[3]
    even = row % 2 == 0
    below, above = readers(even, None, None, first_ref, between_ref, even_ref, odd_ref)

    own = (lane % 64 >= 16) & (lane % 64 < 48)

    def spread_steps(value):
        out = []
        for t in range(2):
            moved = jnp.where(lane < 64, roll(value, 16 - 64 * t, 1), roll(value, 48 - 64 * t, 1))
            out.append(jnp.where(own, moved, 0.0))
        return out

    def block(ref, start, share):
        parts = [ref[rows(start + f), :] for f in range(BASE)]
        parts[3] = parts[3] + shares_ref[rows(share), :]
        return parts

    def choose(a, b, inside):
        return [jnp.where(inside, jnp.where(even, x, y), 0.0) for x, y in zip(a, b)]

    partner = block(first_ref, EARLY, 0)
    between = [block(between_ref, EARLY + BASE * slot, 1 + slot) for slot in range(2)]
    far = [block(far_ref, BASE * slot, 3 + slot) for slot in range(2)]
    groups = []
    for g, parts in enumerate([
        [base_ref[rows(f), :] for f in range(3)] + [arriving_ref[...]],
        choose(partner, between[0], row < last),
        choose(far[0], between[1], row + 2 <= last),
        choose(between[0], far[1], row >= 2),
        choose(between[1], partner, row > 0),
    ]):
        one, two = spread_steps(parts[3])
        groups.append([parts[0], parts[1], one, two, parts[2]])
        for f in range(5):
            wide_ref[rows(5 * f + g), :] = groups[g][f]

    def fields(part, half):
        lanes = pl.ds(half * 128, 128)
        images = [(d, n) for d in range(2) for n in range(2)]
        if part == 0:
            return [
                column_groups(lambda g: ref[d, n, rows(g), lanes], below, above, kind, d, half, n)
                for kind, ref in ((SHEET, sheet_ref), (DROP, drop_ref)) for d, n in images
            ]
        out = [column_groups(lambda g: cap_ref[d, rows(g), lanes], below, above, CAPACITY, d, half, 0) for d in range(2)]
        out += [
            column_groups(lambda g: counts_ref[2 * d + half, rows(g), :], below, above, COUNTS, d, half, 0)
            for d in range(2)
        ]
        for d, n in images:
            one = column_groups(lambda g: field_ref[n, 2 * d + half, rows(g), :], below, above, FIRST, d, half, n)
            two = column_groups(lambda g: field_ref[2 + n, 2 * d + half, rows(g), :], below, above, SECOND, d, half, n)
            merged = []
            for a, b in zip(one, two):
                if b is None:
                    merged.append(a)
                elif half == 0:
                    merged.append(jnp.where(within < 11, a, roll(b, 11, 1)))
                else:
                    merged.append(jnp.where(within >= 5, a, roll(b, -11, 1)))
            out.append(merged)
        return out

    for half, ref in ((0, left_ref), (1, right_ref)):
        for part in range(2):
            @pl.when(place_ref[3] >= 0)
            def _():
                chunks = fields(part, half)
                for g in range(GROUPS):
                    out = chunks[0][g]
                    for k in range(1, 8):
                        out = jnp.where((lane // 16 + half) % 8 == k, roll(chunks[k][g], 16 * k, 1), out)
                    ref[rows(part * GROUPS + g), :] = out

    start = 2 * GROUPS
    quarter = (lane % 64) // 16
    for g in range(5):
        sheet, drop, one, two, bump = groups[g]
        left = jnp.where(
            quarter == 1, sheet,
            jnp.where(quarter == 2, roll(drop, 16, 1), jnp.where(quarter == 3, roll(one, 32, 1), roll(two, -16, 1))),
        )
        right = jnp.where(
            quarter == 2, sheet,
            jnp.where(quarter == 3, roll(drop, 16, 1), jnp.where(quarter == 1, roll(two, -16, 1), roll(one, -32, 1))),
        )
        left_ref[rows(start + g), :] = left
        right_ref[rows(start + g), :] = right
        left_ref[rows(start + 5 + g), :] = bump
        right_ref[rows(start + 5 + g), :] = bump


def assemble_kernel(
    place_ref, sheet_ref, cap_ref, drop_ref, counts_ref, field_ref, first_ref, between_ref, even_ref, odd_ref,
    s_ref, x_ref, c_ref, k_ref, one_ref, two_ref, up_ref, down_ref, left_ref, right_ref, diag_ref, spread_ref,
):
    row, last = place_ref[1], place_ref[3]
    sub, lane = sub_iota(256), lax.broadcasted_iota(jnp.int32, (8, 256), 1)
    below, above = readers(row % 2 == 0, row < last, row > 0, first_ref, between_ref, even_ref, odd_ref)

    def both(own, kind, d, n):
        sides = [column_groups(lambda g: own(half, g), below, above, kind, d, half, n) for half in range(2)]
        return [None if a is None else jnp.concatenate([a, b], axis=1) for a, b in zip(*sides)]

    for d in range(2):
        caps = both(lambda half, g: cap_ref[d, rows(g), pl.ds(half * 128, 128)], CAPACITY, d, 0)
        counts = both(lambda half, g: counts_ref[2 * d + half, rows(g), :], COUNTS, d, 0)
        for g in range(GROUPS):
            c_ref[d, rows(g), :] = caps[g]
            k_ref[d, rows(g), :] = counts[g]
        for n in range(2):
            i = 2 * d + n
            sheets = both(lambda half, g: sheet_ref[d, n, rows(g), pl.ds(half * 128, 128)], SHEET, d, n)
            drops = both(lambda half, g: drop_ref[d, n, rows(g), pl.ds(half * 128, 128)], DROP, d, n)
            ones = both(lambda half, g: field_ref[n, 2 * d + half, rows(g), :], FIRST, d, n)
            twos = both(lambda half, g: field_ref[2 + n, 2 * d + half, rows(g), :], SECOND, d, n)
            for g in range(GROUPS):
                s_ref[i, rows(g), :] = sheets[g]
                x_ref[i, rows(g), :] = drops[g]
                one_ref[i, rows(g), :] = c_ref[d, rows(g), :] * drops[g] + ones[g]
                if twos[g] is not None:
                    two_ref[i, rows(g), :] = twos[g]
            for g in range(GROUPS):
                here, after = s_ref[i, rows(g), :], s_ref[i, rows((g + 1) % GROUPS), :]
                under = jnp.where(sub == 7, roll(after, -1, 0), roll(here, -1, 0))
                inside = here > 0.0
                down_ref[i, rows(g), :] = jnp.where(inside, connect(here, under), 0.0)
                right = jnp.where(inside & (lane < 255), connect(here, roll(here, -1, 1)), 0.0)
                right_ref[i, rows(g), :] = right
                left_ref[i, rows(g), :] = roll(right, 1, 1)
            for g in range(GROUPS):
                here, before = down_ref[i, rows(g), :], down_ref[i, rows((g - 1) % GROUPS), :]
                up = jnp.where(sub == 0, roll(before, 1, 0), roll(here, 1, 0))
                up_ref[i, rows(g), :] = up
                diag = c_ref[d, rows(g), :] + up + here + left_ref[i, rows(g), :] + right_ref[i, rows(g), :]
                diag_ref[i, rows(g), :] = diag + VIA_CONDUCT * k_ref[d, rows(g), :]
    source = lax.broadcasted_iota(jnp.int32, (256, 384), 0) % 128
    column = lax.broadcasted_iota(jnp.int32, (256, 384), 1)
    column = jnp.where(column < 256, 16 + column // 8, jnp.where(column < 320, 48, 0) + (column - 256) // 8)
    for n in range(2):
        spread_ref[n] = jnp.where(source == column + 64 * n, 1.0, 0.0).astype(jnp.bfloat16)


def connect(center, neighbour):
    return jnp.where(neighbour > 0.0, 2.0 / (center + neighbour), 0.0)


def three_terms(k):
    if k == 0:
        return 1.0 - 1.0 / MIDDLE, 0.0, 1.0 / MIDDLE
    a, b = WEIGHTS[k - 1]
    return 1.0 + a - b, -a, b


def advance(k, value, previous, total):
    fore, back, gain = three_terms(k)
    out = total if gain == 1.0 else gain * total
    if fore != 0.0:
        out = out + fore * value
    return out + back * previous() if k else out


def base_solve(fields):
    sheet, state, arriving, bump = fields
    steps = [(1, 0), (-1, 0), (1, 1), (-1, 1)]
    inside = sheet > 0.0
    links = [jnp.where(inside, connect(sheet, roll(sheet, s, a)), 0.0) for s, a in steps]
    diagonal = BASE_CAPACITY + links[0] + links[1] + links[2] + links[3] + BUMP_CONDUCT * bump
    inverse = 1.0 / diagonal
    links = [inverse * link for link in links]
    results = []
    for t in range(STEPS):
        source = inverse * (BASE_CAPACITY * state + arriving[t])
        previous = None
        for k in range(SWEEPS):
            total = (links[0] * roll(state, 1, 0) + links[1] * roll(state, -1, 0)) + (
                links[2] * roll(state, 1, 1) + links[3] * roll(state, -1, 1)
            ) + source
            state, previous = advance(k, state, lambda: previous, total), state
        results.append(state)
    return results


def needed(halo):
    if halo > 8:
        return list(range(GROUPS))
    return list(range(8)) + ([8, 11] if halo > 0 else [])


def solve_kernel(
    place_ref, s_ref, x_ref, c_ref, k_ref, one_ref, two_ref, up_ref, down_ref, left_ref, right_ref, diag_ref, spread_ref,
    wide_ref, fromleft_ref, fromright_ref, out_ref, base_out_ref,
    c_ext, k_ext, f_ext, bound, link_up, link_down, link_left, link_right, inv_ext, src, state, alt,
):
    lane = lane_iota()
    row, col = place_ref[1], place_ref[2]
    has_left, has_right = col > 0, col < place_ref[4]

    start = 2 * GROUPS
    quarter = (lane % 64) // 16
    take_left, take_right = (quarter == 0) & has_left, (quarter == 3) & has_right
    from_left = [fromleft_ref[rows(start + g), :] for g in range(10)]
    from_right = [fromright_ref[rows(start + g), :] for g in range(10)]
    fields = []
    for field in range(5):
        out = []
        for g in range(5):
            right_shift = (32, 16, 0, 48, 32)[field]
            left_shift = (-32, -48, 0, -16, -32)[field]
            group = g + 5 * (field == 4)
            value = jnp.where(take_right, roll(from_right[group], right_shift, 1), wide_ref[rows(5 * field + g), :])
            out.append(jnp.where(take_left, roll(from_left[group], left_shift, 1), value))
        fields.append(jnp.concatenate(out, axis=0))
    solved = base_solve((fields[0], fields[1], (fields[2], fields[3]), fields[4]))
    for t in range(STEPS):
        pieces = halves(solved[t])
        for n in range(2):
            bound[2 * t + n] = jnp.dot(pieces, spread_ref[n], preferred_element_type=F32)
    for n in range(2):
        base_out_ref[n] = roll(solved[1][0:8], -(64 * n + 16), 1)[:, 0:32]

    def third(part, chunk, g):
        right_ok, left_ok = has_right, has_left
        if g in (8, 9):
            right_ok, left_ok = right_ok & (row < place_ref[3]), left_ok & (row < place_ref[3])
        if g in (10, 11):
            right_ok, left_ok = right_ok & (row > 0), left_ok & (row > 0)
        right = jnp.where((lane // 16 == chunk) & right_ok, fromright_ref[rows(part * GROUPS + g), :], 0.0)
        value = jnp.where((lane // 16 == (chunk + 7) % 8) & left_ok, fromleft_ref[rows(part * GROUPS + g), :], right)
        return roll(value, -16 * chunk, 1)

    sub, sub3 = sub_iota(), sub_iota(384)

    def above(value, before, index):
        return jnp.where(index == 0, roll(before, 1, 0), roll(value, 1, 0))

    def below(value, after, index):
        return jnp.where(index == 7, roll(after, -1, 0), roll(value, -1, 0))

    for i in range(4):
        d, n = i // 2, i % 2

        def wide(ref, g, extra, index=i):
            return jnp.concatenate([ref[index, rows(g), :], extra], axis=1)

        if n == 0:
            for g in range(GROUPS):
                c_ext[rows(g), :] = wide(c_ref, g, third(1, d, g), d)
                k_ext[rows(g), :] = wide(k_ref, g, third(1, 2 + d, g), d)
        @pl.when(place_ref[3] >= 0)
        def _():
            sheets = [third(0, i, g) for g in range(GROUPS)]
            for g in range(GROUPS):
                here = sheets[g]
                inside = here > 0.0
                low, high = s_ref[i, rows(g), pl.ds(0, 128)], s_ref[i, rows(g), pl.ds(128, 128)]
                after = roll(jnp.where(lane == 0, low, here), -1, 1)
                before = roll(jnp.where(lane == 127, high, here), 1, 1)
                right = jnp.where(inside, connect(here, after), 0.0)
                left = jnp.where(inside, connect(here, before), 0.0)
                down = jnp.where(inside, connect(here, below(here, sheets[(g + 1) % GROUPS], sub)), 0.0)
                up = jnp.where(inside, connect(here, above(here, sheets[(g - 1) % GROUPS], sub)), 0.0)
                first = jnp.where(lane == 0, roll(right, 1, 1), 0.0)
                final = jnp.where(lane == 127, roll(left, -1, 1), 0.0)
                diag = wide(diag_ref, g, 0.0 * here) + jnp.concatenate(
                    [first, final, c_ext[rows(g), pl.ds(256, 128)] + up + down + left + right
                     + VIA_CONDUCT * k_ext[rows(g), pl.ds(256, 128)]], axis=1)
                inverse = jnp.where(diag > 0.0, 1.0 / diag, 0.0)
                inv_ext[rows(g), :] = inverse
                zero = jnp.zeros_like(first)
                link_up[rows(g), :] = inverse * wide(up_ref, g, up)
                link_down[rows(g), :] = inverse * wide(down_ref, g, down)
                link_left[rows(g), :] = inverse * (wide(left_ref, g, left) + jnp.concatenate([first, zero, zero], axis=1))
                link_right[rows(g), :] = inverse * (wide(right_ref, g, right) + jnp.concatenate([zero, final, zero], axis=1))
                drop = third(0, 4 + i, g)
                state[rows(g), :] = wide(x_ref, g, drop)
                one = third(1, 4 + i, g)
                f_ext[0, rows(g), :] = wide(one_ref, g, c_ext[rows(g), pl.ds(256, 128)] * drop + one)
                if g not in (9, 10):
                    two = jnp.where(lane < 64, roll(one, -11, 1), roll(one, 11, 1))
                    f_ext[1, rows(g), :] = wide(two_ref, g, two)

        @pl.when(place_ref[3] >= 0)
        def _():
            for t in range(STEPS):
                for k in range(SWEEPS):
                    now, then = (alt, state) if k % 2 else (state, alt)
                    for g in needed(11 - 6 * t - k):
                        value = now[rows(g), :]
                        total = link_up[rows(g), :] * above(value, now[rows((g - 1) % GROUPS), :], sub3)
                        total = total + link_down[rows(g), :] * below(value, now[rows((g + 1) % GROUPS), :], sub3)
                        total = total + (
                            link_left[rows(g), :] * roll(value, 1, 1) + link_right[rows(g), :] * roll(value, -1, 1))
                        if k == 0:
                            spread = jnp.broadcast_to(bound[2 * t + n, pl.ds(base_row(g), 1), :], (8, 384))
                            source = f_ext[t, rows(g), :] + k_ext[rows(g), :] * spread
                            if t:
                                source = source + c_ext[rows(g), :] * value
                            source = inv_ext[rows(g), :] * source
                            src[rows(g), :] = source
                        else:
                            source = src[rows(g), :]
                        then[rows(g), :] = advance(k, value, lambda: then[rows(g), :], total + source)

        for g in range(8):
            out_ref[d, n, rows(g), :] = state[rows(g), pl.ds(0, 256)]


def base_row(g):
    return g if g < 10 else 28 + g


def spec(count):
    return [pl.BlockSpec(memory_space=pltpu.VMEM)] * count


def smem():
    return pl.BlockSpec(memory_space=pltpu.SMEM)


def call(kernel, name, outs, ins, scratch=(), limit=24):
    return pl.pallas_call(
        kernel,
        out_shape=outs,
        in_specs=ins,
        out_specs=spec(len(outs)),
        scratch_shapes=list(scratch),
        compiler_params=pltpu.CompilerParams(vmem_limit_bytes=limit * 1024 * 1024),
        name=name,
    )


def arr(*shape, dtype=F32):
    return jax.ShapeDtypeStruct(shape, dtype)


def swaps(count, offset, distance=1):
    pairs = []
    for i in range(count):
        if ((i - offset) // distance) % 2 == 0:
            j = (i + distance) % count
            pairs += [(i, j), (j, i)]
    return pairs


def per_device(
    sheet_res, capacity, drop_start, load_cell, load_current, via_cell, via_current, base_sheet, base_start, bump_cell
):
    row_count = lax.axis_size("row")
    col_count = lax.axis_size("col")
    place = jnp.stack(
        [lax.axis_index("die"), lax.axis_index("row"), lax.axis_index("col"), row_count - 1, col_count - 1]
    ).astype(jnp.int32)
    others = [(0, 1), (1, 0)]

    packed, send = call(pack_kernel, "pack_vias", (arr(2, VIAS, 8, 128), arr(VIAS + 1, 8, 128)), [smem()] + spec(1))(
        place, via_current
    )
    got = lax.ppermute(send, "die", others)
    def buffer(count):
        return arr(8 * count, 128)

    even, odd, base = call(
        early_kernel, "pack_early", (buffer(EARLY + BASE), buffer(EARLY), buffer(BASE)), [smem(), smem()] + spec(6)
    )(place, bump_cell, base_sheet, base_start, send, sheet_res, capacity, drop_start)
    first = lax.ppermute(even, "row", swaps(row_count, 0))
    cells, load_cells, loads, spread, counts = call(
        prepare_kernel, "spread_cells",
        (arr(4, VIAS, 8, 128), arr(4, 8, 128), arr(4, 4, 8, 128), arr(256, 1024, dtype=jnp.bfloat16), arr(4, 64, 128)),
        spec(3),
    )(via_cell, load_cell, load_current)
    between, far = call(chip_kernel, "pack_chip", (buffer(EARLY + 2 * BASE), buffer(2 * BASE)), [smem()] + spec(3))(
        place, odd, base, first
    )
    far = lax.ppermute(
        far, "row", [(i, (i + 3 if i % 2 == 0 else i - 3) % row_count) for i in range(row_count)]
    )
    between = lax.ppermute(between, "row", swaps(row_count, 1))

    field, even, odd, arriving = call(
        place_kernel, "place_vias", (arr(4, 4, 64, 128), buffer(LATE), buffer(LATE), buffer(1)),
        [smem()] + spec(9), [pltpu.VMEM((4, 4, VIAS, 8, 128), F32)],
    )(place, packed, send, got, cells, load_cells, loads, spread, counts, far)

    even = lax.ppermute(even, "row", swaps(row_count, 0))
    odd = lax.ppermute(odd, "row", swaps(row_count, 1))
    shares = call(shares_kernel, "pack_shares", (buffer(5),), spec(4))(arriving, first, between, far)[0]
    shares = lax.ppermute(shares, "die", others)

    strip_shape = arr(8 * COL_GROUPS, 128)
    left, right, wide = call(
        strip_kernel, "column_strips", (strip_shape, strip_shape, arr(200, 128)), [smem()] + spec(13)
    )(place, sheet_res, capacity, drop_start, counts, field, base, arriving, first, between, far, even, odd, shares)
    from_right = lax.ppermute(left, "col", [(i, (i - 1) % col_count) for i in range(col_count)])
    from_left = lax.ppermute(right, "col", [(i, (i + 1) % col_count) for i in range(col_count)])

    image, pair = arr(4, 96, 256), arr(2, 96, 256)
    parts = call(
        assemble_kernel, "assemble",
        (image, image, pair, pair) + (image,) * 7 + (arr(2, 256, 384, dtype=jnp.bfloat16),), [smem()] + spec(9),
    )(place, sheet_res, capacity, drop_start, counts, field, first, between, even, odd)

    ext = pltpu.VMEM((96, 384), F32)
    scratch = [ext, ext, pltpu.VMEM((2, 96, 384), F32), pltpu.VMEM((4, 40, 384), F32)] + [ext] * 8
    return call(solve_kernel, "solve", (arr(2, 2, 64, 256), arr(2, 8, 32)), [smem()] + spec(15), scratch)(
        place, *parts, wide, from_left, from_right
    )


def solution(mesh):
    in_specs = (
        P("die", None, "row", "col"),
        P("die", "row", "col"),
        P("die", None, "row", "col"),
        P("die", "row", "col"),
        P(None, "die", None, "row", "col"),
        P("die", None, "row", "col"),
        P(None, "die", None, None, "row", "col"),
        P(None, "row", "col"),
        P(None, "row", "col"),
        P("row", "col"),
    )
    out_specs = (P("die", None, "row", "col"), P(None, "row", "col"))
    return jax.shard_map(
        per_device, mesh=mesh, in_specs=in_specs, out_specs=out_specs, check_vma=False
    )
```

```python
import jax
import jax.numpy as jnp
from jax import lax
from jax.experimental import pallas as pl
from jax.experimental.pallas import tpu as pltpu
from jax.sharding import PartitionSpec as P

SWEEPS = 6
STEPS = 2
VIAS = 32

VIA_CONDUCT = 1.0
VIA_RESIST = 4.0
BUMP_CONDUCT = 50.0
BASE_CAPACITY = 0.1
LOWER_BOUND = 0.1
UPPER_BOUND = 1.9

MIDDLE = 0.5 * (UPPER_BOUND + LOWER_BOUND)
HALF = 0.5 * (UPPER_BOUND - LOWER_BOUND)

GROUPS = 12
F32 = jnp.float32


def sweep_weights():
    scaled = MIDDLE / HALF
    ratio = 1.0 / scaled
    pairs = []
    for _ in range(SWEEPS - 1):
        following = 1.0 / (2.0 * scaled - ratio)
        pairs.append((following * ratio, 2.0 * following / HALF))
        ratio = following
    return pairs


WEIGHTS = sweep_weights()


def lane_iota():
    return lax.broadcasted_iota(jnp.int32, (8, 128), 1)


def sub_iota(width=128):
    return lax.broadcasted_iota(jnp.int32, (8, width), 0)


def roll(x, shift, axis):
    shift = shift % x.shape[axis]
    return pltpu.roll(x, shift, axis) if shift else x


def rows(g):
    return pl.ds(8 * g, 8)


def pack_kernel(place_ref, via_ref, packed_ref, send_ref):
    later = place_ref[0].astype(F32)
    total = jnp.zeros((8, 128), F32)
    for v in range(VIAS):
        parts = []
        for d in range(2):
            part = jnp.concatenate([via_ref[t, d, n, v] for t in range(2) for n in range(2)], axis=1)
            packed_ref[d, v] = part
            parts.append(part)
        both = parts[0] + parts[1]
        send_ref[v] = both + later * parts[0]
        total = total + both
    send_ref[VIAS] = total


def spread_nets(ref):
    gap = jnp.zeros((8, 16), F32)
    return jnp.concatenate([gap, ref[0], gap, gap, ref[1], gap], axis=1)


def shared(first, second, shift):
    return jnp.where(sub_iota() < shift, first, roll(second, shift, 0))


def shared_low(first, second, shift):
    return jnp.where(sub_iota() >= shift, first, roll(second, shift, 0))


class RowSender:
    def __init__(self, even, even_ref, odd_ref):
        self.even, self.even_ref, self.odd_ref, self.place = even, even_ref, odd_ref, 0

    def put(self, up, down):
        self.even_ref[rows(self.place), :] = jnp.where(self.even, down, up)
        self.odd_ref[rows(self.place), :] = jnp.where(self.even, up, down)
        self.place += 1

    def pair(self, first, second):
        self.put(first(0), first(7))
        self.put(second(0), second(7))
        self.put(shared(first(1), second(1), 4), shared_low(first(6), second(6), 4))


BASE = 4
EARLY = 30
LATE = 22


def base_kernel(bump_ref, sheet_ref, start_ref, send_ref, base_ref):
    lane, sub = lane_iota(), sub_iota()
    bump = jnp.zeros((8, 128), F32)
    column = lane % 64 - 16
    for k in range(4):
        bump = jnp.where((column // 8 == k) & (sub * 8 + column % 8 == bump_ref[0, k]), 1.0, bump)
    for part, value in enumerate([spread_nets(sheet_ref), spread_nets(start_ref), bump, send_ref[VIAS]]):
        base_ref[rows(part), :] = value


def chip_kernel(place_ref, base_ref, got_ref, sheet_ref, cap_ref, drop_ref, within_ref, between_ref):
    even = place_ref[1] % 2 == 0
    sender = RowSender(even, within_ref, between_ref)
    for d in range(2):
        for half in range(2):
            lanes = pl.ds(half * 128, 128)
            for n in range(2):
                sender.pair(lambda g: sheet_ref[d, n, rows(g), lanes], lambda g: drop_ref[d, n, rows(g), lanes])
        sender.pair(lambda g: cap_ref[d, rows(g), pl.ds(0, 128)], lambda g: cap_ref[d, rows(g), pl.ds(128, 128)])
    for part in range(BASE):
        own, got = base_ref[rows(part), :], got_ref[rows(part), :]
        for slot, value in enumerate([jnp.where(even, own, got), jnp.where(even, got, own)]):
            between_ref[rows(EARLY + BASE * slot + part), :] = value


def relay_kernel(place_ref, between_ref, relay_ref):
    even = place_ref[1] % 2 == 0
    for part in range(BASE):
        a, b = between_ref[rows(EARLY + part), :], between_ref[rows(EARLY + BASE + part), :]
        relay_ref[rows(part), :] = jnp.where(even, b, a)


def shares_kernel(first_ref, between_ref, relayed_ref, shares_ref):
    shares_ref[rows(0), :] = first_ref[rows(3), :]
    for slot in range(2):
        shares_ref[rows(1 + slot), :] = between_ref[rows(EARLY + BASE * slot + 3), :]
    shares_ref[rows(3), :] = relayed_ref[rows(3), :]


def spread_matrix(height, width):
    row = lax.broadcasted_iota(jnp.int32, (height, width), 0) % 128
    column = lax.broadcasted_iota(jnp.int32, (height, width), 1)
    return jnp.where(row == column // 8, 1.0, 0.0).astype(jnp.bfloat16)


def halves(value):
    high = value.astype(jnp.bfloat16)
    low = (value - high.astype(F32)).astype(jnp.bfloat16)
    return jnp.concatenate([high, low], axis=1)


def prepare_kernel(cell_ref, load_cell_ref, load_ref, cells_ref, load_cells_ref, loads_ref, spread_ref, counts_ref):
    within = (lane_iota() % 8).astype(F32)
    spread = spread_matrix(32, 256)
    for d in range(2):
        cells = cell_ref[d].reshape(8 * VIAS, 32).astype(F32).astype(jnp.bfloat16)
        wide = jnp.dot(cells, spread, preferred_element_type=F32)
        load_cell = load_cell_ref[d].astype(F32).astype(jnp.bfloat16)
        load_cell = jnp.dot(load_cell, spread, preferred_element_type=F32)
        for half in range(2):
            lanes = slice(128 * half, 128 * half + 128)
            for v in range(VIAS):
                cells_ref[2 * d + half, v] = wide[8 * v : 8 * v + 8, lanes] - within
            load_cells_ref[2 * d + half] = load_cell[:, lanes] - within
    spread_ref[...] = spread_matrix(256, 1024)
    loads = jnp.concatenate([load_ref[t, d, n] for d in range(2) for t in range(2) for n in range(2)], axis=0)
    high = loads.astype(jnp.bfloat16)
    low = (loads - high.astype(F32)).astype(jnp.bfloat16)
    wide = jnp.dot(high, spread, preferred_element_type=F32) + jnp.dot(low, spread, preferred_element_type=F32)
    for d in range(2):
        for half in range(2):
            for m in range(4):
                loads_ref[2 * d + half, m] = wide[32 * d + 8 * m : 32 * d + 8 * m + 8, 128 * half : 128 * half + 128]

    def count(i, carry):
        state = [jnp.zeros((8, 128), F32) for _ in range(8)]
        for v in range(VIAS):
            cell = cells_ref[i, v]
            for oi in range(8):
                state[oi] = state[oi] + jnp.where(cell == 8.0 * oi, 1.0, 0.0)
        for oi in range(8):
            counts_ref[i, pl.ds(oi, 8, stride=8), :] = state[oi]
        return carry

    lax.fori_loop(0, 4, count, 0)


def place_kernel(
    place_ref, packed_ref, send_ref, got_ref, cells_ref, load_cells_ref, loads_ref, spread_ref, counts_ref, early_ref,
    field_ref, even_ref, odd_ref, arriving_ref, values_ref,
):
    lane = lane_iota()
    later = place_ref[0].astype(F32)
    even = place_ref[1] % 2 == 0
    weights = (
        (VIA_RESIST * (4.0 - 2.0 * later), VIA_RESIST * (3.0 - 2.0 * later), VIA_RESIST * (1.0 + later)),
        (VIA_RESIST * (3.0 - 2.0 * later), VIA_RESIST * (3.0 - 2.0 * later), VIA_RESIST),
    )
    size = (8 * VIAS, 128)
    first, second, got = packed_ref[0].reshape(size), packed_ref[1].reshape(size), got_ref[0:VIAS].reshape(size)
    for d in range(2):
        mixed = weights[d][0] * first + weights[d][1] * second + weights[d][2] * got
        wide = jnp.dot(halves(mixed), spread_ref[...], preferred_element_type=F32)
        for half in range(2):
            for m in range(4):
                start = 256 * m + 128 * half
                values_ref[2 * d + half, m] = wide[:, start : start + 128].reshape(VIAS, 8, 128)

    def add(i, carry):
        cell = load_cells_ref[i]
        loads = [loads_ref[i, m] for m in range(4)]
        state = []
        for oi in range(8):
            hit = cell == 8.0 * oi
            state.append([jnp.where(hit, load, 0.0) for load in loads])
        for v in range(VIAS):
            cell = cells_ref[i, v]
            values = [values_ref[i, m, v] for m in range(4)]
            for oi in range(8):
                hit = cell == 8.0 * oi
                state[oi] = [old + jnp.where(hit, value, 0.0) for old, value in zip(state[oi], values)]
        for oi in range(8):
            for m in range(4):
                field_ref[m, i, pl.ds(oi, 8, stride=8), :] = state[oi][m]
        return carry

    lax.fori_loop(0, 4, add, 0)

    arriving_ref[...] = send_ref[VIAS] + got_ref[VIAS]
    for g in range(EARLY):
        even_ref[rows(LATE + g), :] = early_ref[rows(g), :]
    sender = RowSender(even, even_ref, odd_ref)
    for d in range(2):
        for half in range(2):
            for n in range(2):
                one = lambda g: field_ref[n, 2 * d + half, rows(g), :]
                two = lambda g: field_ref[2 + n, 2 * d + half, rows(g), :]
                sender.put(one(0), one(7))
                sender.put(shared(one(1), two(0), 3), shared_low(one(6), two(7), 5))
        sender.pair(lambda g: counts_ref[2 * d, rows(g), :], lambda g: counts_ref[2 * d + 1, rows(g), :])


SHEET, DROP, CAPACITY, COUNTS, FIRST, SECOND = range(6)


def near_rows(read, kind, d, half, n, upper):
    early, late = read
    if kind in (FIRST, SECOND):
        start = 11 * d + 4 * half + 2 * n
        if kind == SECOND:
            return roll(late(start + 1), -5 if upper else -3, 0), None
        return late(start), late(start + 1)
    if kind in (SHEET, DROP):
        take, start, second = early, 15 * d + 6 * half + 3 * n, kind == DROP
    elif kind == CAPACITY:
        take, start, second = early, 15 * d + 12, half == 1
    else:
        take, start, second = late, 11 * d + 8, half == 1
    last = take(start + 2)
    return (take(start + 1), roll(last, -4, 0)) if second else (take(start), last)


def column_groups(own, below, above, kind, d, half, n):
    low = near_rows(below, kind, d, half, n, False)
    high = near_rows(above, kind, d, half, n, True)
    return [own(g) for g in range(8)] + [low[0], low[1], high[1], high[0]]


def readers(even, below, above, within_ref, between_ref, late_ref):
    def make(inside, near, skip, far_ref):
        def read(g):
            value = jnp.where(near, within_ref[rows(skip + g), :], far_ref[rows(g), :])
            return value if inside is None else jnp.where(inside, value, 0.0)
        return read

    odd = jnp.logical_not(even)
    return tuple(
        (make(inside, near, LATE, between_ref), make(inside, near, 0, late_ref)) for inside, near in ((below, even), (above, odd))
    )


COL_GROUPS = 2 * GROUPS + 10


def strip_kernel(
    place_ref, sheet_ref, cap_ref, drop_ref, counts_ref, field_ref, base_ref, arriving_ref, first_ref, between_ref,
    within_ref, late_ref, relayed_ref, shares_ref, even_ref, odd_ref, wide_ref,
):
    lane = lane_iota()
    within = lane % 16
    row, last = place_ref[1], place_ref[3]
    even = row % 2 == 0
    below, above = readers(even, None, None, within_ref, between_ref, late_ref)
    even_col = place_ref[2] % 2 == 0

    own = (lane % 64 >= 16) & (lane % 64 < 48)

    def spread_steps(value):
        out = []
        for t in range(2):
            moved = jnp.where(lane < 64, roll(value, 16 - 64 * t, 1), roll(value, 48 - 64 * t, 1))
            out.append(jnp.where(own, moved, 0.0))
        return out

    def block(ref, start, share):
        parts = [ref[rows(start + f), :] for f in range(BASE)]
        parts[3] = parts[3] + shares_ref[rows(share), :]
        return parts

    def choose(a, b, inside):
        return [jnp.where(inside, jnp.where(even, x, y), 0.0) for x, y in zip(a, b)]

    partner = block(first_ref, 0, 0)
    between = [block(between_ref, EARLY + BASE * slot, 1 + slot) for slot in range(2)]
    relayed = block(relayed_ref, 0, 3)
    groups = []
    for g, parts in enumerate([
        [base_ref[rows(f), :] for f in range(3)] + [arriving_ref[...]],
        choose(partner, between[0], row < last),
        choose(relayed, between[1], row + 2 <= last),
        choose(between[0], relayed, row >= 2),
        choose(between[1], partner, row > 0),
    ]):
        one, two = spread_steps(parts[3])
        groups.append([parts[0], parts[1], one, two, parts[2]])
        for f in range(5):
            wide_ref[rows(5 * f + g), :] = groups[g][f]

    def fields(part, half):
        lanes = pl.ds(half * 128, 128)
        images = [(d, n) for d in range(2) for n in range(2)]
        if part == 0:
            return [
                column_groups(lambda g: ref[d, n, rows(g), lanes], below, above, kind, d, half, n)
                for kind, ref in ((SHEET, sheet_ref), (DROP, drop_ref)) for d, n in images
            ]
        out = [column_groups(lambda g: cap_ref[d, rows(g), lanes], below, above, CAPACITY, d, half, 0) for d in range(2)]
        out += [
            column_groups(lambda g: counts_ref[2 * d + half, rows(g), :], below, above, COUNTS, d, half, 0)
            for d in range(2)
        ]
        for d, n in images:
            one = column_groups(lambda g: field_ref[n, 2 * d + half, rows(g), :], below, above, FIRST, d, half, n)
            two = column_groups(lambda g: field_ref[2 + n, 2 * d + half, rows(g), :], below, above, SECOND, d, half, n)
            merged = []
            for a, b in zip(one, two):
                if b is None:
                    merged.append(a)
                elif half == 0:
                    merged.append(jnp.where(within < 11, a, roll(b, 11, 1)))
                else:
                    merged.append(jnp.where(within >= 5, a, roll(b, -11, 1)))
            out.append(merged)
        return out

    def put(place, left, right):
        even_ref[rows(place), :] = jnp.where(even_col, right, left)
        odd_ref[rows(place), :] = jnp.where(even_col, left, right)

    for part in range(2):
        sides = [fields(part, half) for half in range(2)]
        for g in range(GROUPS):
            out = []
            for half, chunks in enumerate(sides):
                value = chunks[0][g]
                for k in range(1, 8):
                    value = jnp.where((lane // 16 + half) % 8 == k, roll(chunks[k][g], 16 * k, 1), value)
                out.append(value)
            put(part * GROUPS + g, *out)

    start = 2 * GROUPS
    quarter = (lane % 64) // 16
    for g in range(5):
        sheet, drop, one, two, bump = groups[g]
        left = jnp.where(
            quarter == 1, sheet,
            jnp.where(quarter == 2, roll(drop, 16, 1), jnp.where(quarter == 3, roll(one, 32, 1), roll(two, -16, 1))),
        )
        right = jnp.where(
            quarter == 2, sheet,
            jnp.where(quarter == 3, roll(drop, 16, 1), jnp.where(quarter == 1, roll(two, -16, 1), roll(one, -32, 1))),
        )
        put(start + g, left, right)
        put(start + 5 + g, bump, bump)


def assemble_kernel(
    place_ref, sheet_ref, cap_ref, drop_ref, counts_ref, field_ref, within_ref, between_ref, late_ref,
    s_ref, x_ref, c_ref, k_ref, one_ref, two_ref, up_ref, down_ref, left_ref, right_ref, diag_ref, spread_ref,
):
    row, last = place_ref[1], place_ref[3]
    sub, lane = sub_iota(256), lax.broadcasted_iota(jnp.int32, (8, 256), 1)
    below, above = readers(row % 2 == 0, row < last, row > 0, within_ref, between_ref, late_ref)

    def both(own, kind, d, n):
        sides = [column_groups(lambda g: own(half, g), below, above, kind, d, half, n) for half in range(2)]
        return [None if a is None else jnp.concatenate([a, b], axis=1) for a, b in zip(*sides)]

    for d in range(2):
        caps = both(lambda half, g: cap_ref[d, rows(g), pl.ds(half * 128, 128)], CAPACITY, d, 0)
        counts = both(lambda half, g: counts_ref[2 * d + half, rows(g), :], COUNTS, d, 0)
        for g in range(GROUPS):
            c_ref[d, rows(g), :] = caps[g]
            k_ref[d, rows(g), :] = counts[g]
        for n in range(2):
            i = 2 * d + n
            sheets = both(lambda half, g: sheet_ref[d, n, rows(g), pl.ds(half * 128, 128)], SHEET, d, n)
            drops = both(lambda half, g: drop_ref[d, n, rows(g), pl.ds(half * 128, 128)], DROP, d, n)
            ones = both(lambda half, g: field_ref[n, 2 * d + half, rows(g), :], FIRST, d, n)
            twos = both(lambda half, g: field_ref[2 + n, 2 * d + half, rows(g), :], SECOND, d, n)
            for g in range(GROUPS):
                s_ref[i, rows(g), :] = sheets[g]
                x_ref[i, rows(g), :] = drops[g]
                one_ref[i, rows(g), :] = c_ref[d, rows(g), :] * drops[g] + ones[g]
                if twos[g] is not None:
                    two_ref[i, rows(g), :] = twos[g]
            for g in range(GROUPS):
                here, after = s_ref[i, rows(g), :], s_ref[i, rows((g + 1) % GROUPS), :]
                under = jnp.where(sub == 7, roll(after, -1, 0), roll(here, -1, 0))
                inside = here > 0.0
                down_ref[i, rows(g), :] = jnp.where(inside, connect(here, under), 0.0)
                right = jnp.where(inside & (lane < 255), connect(here, roll(here, -1, 1)), 0.0)
                right_ref[i, rows(g), :] = right
                left_ref[i, rows(g), :] = roll(right, 1, 1)
            for g in range(GROUPS):
                here, before = down_ref[i, rows(g), :], down_ref[i, rows((g - 1) % GROUPS), :]
                up = jnp.where(sub == 0, roll(before, 1, 0), roll(here, 1, 0))
                up_ref[i, rows(g), :] = up
                diag = c_ref[d, rows(g), :] + up + here + left_ref[i, rows(g), :] + right_ref[i, rows(g), :]
                diag_ref[i, rows(g), :] = diag + VIA_CONDUCT * k_ref[d, rows(g), :]
    source = lax.broadcasted_iota(jnp.int32, (256, 384), 0) % 128
    column = lax.broadcasted_iota(jnp.int32, (256, 384), 1)
    column = jnp.where(column < 256, 16 + column // 8, jnp.where(column < 320, 48, 0) + (column - 256) // 8)
    for n in range(2):
        spread_ref[n] = jnp.where(source == column + 64 * n, 1.0, 0.0).astype(jnp.bfloat16)


def connect(center, neighbour):
    return jnp.where(neighbour > 0.0, 2.0 / (center + neighbour), 0.0)


def three_terms(k):
    if k == 0:
        return 1.0 - 1.0 / MIDDLE, 0.0, 1.0 / MIDDLE
    a, b = WEIGHTS[k - 1]
    return 1.0 + a - b, -a, b


def advance(k, value, previous, total):
    fore, back, gain = three_terms(k)
    out = total if gain == 1.0 else gain * total
    if fore != 0.0:
        out = out + fore * value
    return out + back * previous() if k else out


def base_solve(fields):
    sheet, state, arriving, bump = fields
    steps = [(1, 0), (-1, 0), (1, 1), (-1, 1)]
    inside = sheet > 0.0
    links = [jnp.where(inside, connect(sheet, roll(sheet, s, a)), 0.0) for s, a in steps]
    diagonal = BASE_CAPACITY + links[0] + links[1] + links[2] + links[3] + BUMP_CONDUCT * bump
    inverse = 1.0 / diagonal
    links = [inverse * link for link in links]
    results = []
    for t in range(STEPS):
        source = inverse * (BASE_CAPACITY * state + arriving[t])
        previous = None
        for k in range(SWEEPS):
            total = (links[0] * roll(state, 1, 0) + links[1] * roll(state, -1, 0)) + (
                links[2] * roll(state, 1, 1) + links[3] * roll(state, -1, 1)
            ) + source
            state, previous = advance(k, state, lambda: previous, total), state
        results.append(state)
    return results


def needed(halo):
    if halo > 8:
        return list(range(GROUPS))
    return list(range(8)) + ([8, 11] if halo > 0 else [])


def solve_kernel(
    place_ref, s_ref, x_ref, c_ref, k_ref, one_ref, two_ref, up_ref, down_ref, left_ref, right_ref, diag_ref, spread_ref,
    wide_ref, even_ref, odd_ref, out_ref, base_out_ref,
    c_ext, k_ext, f_ext, bound, link_up, link_down, link_left, link_right, inv_ext, src, state, alt,
):
    lane = lane_iota()
    row, col = place_ref[1], place_ref[2]
    has_left, has_right = col > 0, col < place_ref[4]
    even_col = col % 2 == 0

    def from_left(g):
        return jnp.where(even_col, odd_ref[rows(g), :], even_ref[rows(g), :])

    def from_right(g):
        return jnp.where(even_col, even_ref[rows(g), :], odd_ref[rows(g), :])

    start = 2 * GROUPS
    quarter = (lane % 64) // 16
    take_left, take_right = (quarter == 0) & has_left, (quarter == 3) & has_right
    fields = []
    for field in range(5):
        out = []
        for g in range(5):
            right_shift = (32, 16, 0, 48, 32)[field]
            left_shift = (-32, -48, 0, -16, -32)[field]
            group = g + 5 * (field == 4)
            value = jnp.where(take_right, roll(from_right(start + group), right_shift, 1), wide_ref[rows(5 * field + g), :])
            out.append(jnp.where(take_left, roll(from_left(start + group), left_shift, 1), value))
        fields.append(jnp.concatenate(out, axis=0))
    solved = base_solve((fields[0], fields[1], (fields[2], fields[3]), fields[4]))
    for t in range(STEPS):
        pieces = halves(solved[t])
        for n in range(2):
            bound[2 * t + n] = jnp.dot(pieces, spread_ref[n], preferred_element_type=F32)
    for n in range(2):
        base_out_ref[n] = roll(solved[1][0:8], -(64 * n + 16), 1)[:, 0:32]

    def third(part, chunk, g):
        right_ok, left_ok = has_right, has_left
        if g in (8, 9):
            right_ok, left_ok = right_ok & (row < place_ref[3]), left_ok & (row < place_ref[3])
        if g in (10, 11):
            right_ok, left_ok = right_ok & (row > 0), left_ok & (row > 0)
        right = jnp.where((lane // 16 == chunk) & right_ok, from_right(part * GROUPS + g), 0.0)
        value = jnp.where((lane // 16 == (chunk + 7) % 8) & left_ok, from_left(part * GROUPS + g), right)
        return roll(value, -16 * chunk, 1)

    sub, sub3 = sub_iota(), sub_iota(384)

    def above(value, before, index):
        return jnp.where(index == 0, roll(before, 1, 0), roll(value, 1, 0))

    def below(value, after, index):
        return jnp.where(index == 7, roll(after, -1, 0), roll(value, -1, 0))

    for i in range(4):
        d, n = i // 2, i % 2

        def wide(ref, g, extra, index=i):
            return jnp.concatenate([ref[index, rows(g), :], extra], axis=1)

        if n == 0:
            for g in range(GROUPS):
                c_ext[rows(g), :] = wide(c_ref, g, third(1, d, g), d)
                k_ext[rows(g), :] = wide(k_ref, g, third(1, 2 + d, g), d)
        @pl.when(place_ref[3] >= 0)
        def _():
            sheets = [third(0, i, g) for g in range(GROUPS)]
            for g in range(GROUPS):
                here = sheets[g]
                inside = here > 0.0
                low, high = s_ref[i, rows(g), pl.ds(0, 128)], s_ref[i, rows(g), pl.ds(128, 128)]
                after = roll(jnp.where(lane == 0, low, here), -1, 1)
                before = roll(jnp.where(lane == 127, high, here), 1, 1)
                right = jnp.where(inside, connect(here, after), 0.0)
                left = jnp.where(inside, connect(here, before), 0.0)
                down = jnp.where(inside, connect(here, below(here, sheets[(g + 1) % GROUPS], sub)), 0.0)
                up = jnp.where(inside, connect(here, above(here, sheets[(g - 1) % GROUPS], sub)), 0.0)
                first = jnp.where(lane == 0, roll(right, 1, 1), 0.0)
                final = jnp.where(lane == 127, roll(left, -1, 1), 0.0)
                diag = wide(diag_ref, g, 0.0 * here) + jnp.concatenate(
                    [first, final, c_ext[rows(g), pl.ds(256, 128)] + up + down + left + right
                     + VIA_CONDUCT * k_ext[rows(g), pl.ds(256, 128)]], axis=1)
                inverse = jnp.where(diag > 0.0, 1.0 / diag, 0.0)
                inv_ext[rows(g), :] = inverse
                zero = jnp.zeros_like(first)
                link_up[rows(g), :] = inverse * wide(up_ref, g, up)
                link_down[rows(g), :] = inverse * wide(down_ref, g, down)
                link_left[rows(g), :] = inverse * (wide(left_ref, g, left) + jnp.concatenate([first, zero, zero], axis=1))
                link_right[rows(g), :] = inverse * (wide(right_ref, g, right) + jnp.concatenate([zero, final, zero], axis=1))
                drop = third(0, 4 + i, g)
                state[rows(g), :] = wide(x_ref, g, drop)
                one = third(1, 4 + i, g)
                f_ext[0, rows(g), :] = wide(one_ref, g, c_ext[rows(g), pl.ds(256, 128)] * drop + one)
                if g not in (9, 10):
                    two = jnp.where(lane < 64, roll(one, -11, 1), roll(one, 11, 1))
                    f_ext[1, rows(g), :] = wide(two_ref, g, two)

        @pl.when(place_ref[3] >= 0)
        def _():
            for t in range(STEPS):
                for k in range(SWEEPS):
                    now, then = (alt, state) if k % 2 else (state, alt)
                    for g in needed(11 - 6 * t - k):
                        value = now[rows(g), :]
                        total = link_up[rows(g), :] * above(value, now[rows((g - 1) % GROUPS), :], sub3)
                        total = total + link_down[rows(g), :] * below(value, now[rows((g + 1) % GROUPS), :], sub3)
                        total = total + (
                            link_left[rows(g), :] * roll(value, 1, 1) + link_right[rows(g), :] * roll(value, -1, 1))
                        if k == 0:
                            spread = jnp.broadcast_to(bound[2 * t + n, pl.ds(base_row(g), 1), :], (8, 384))
                            source = f_ext[t, rows(g), :] + k_ext[rows(g), :] * spread
                            if t:
                                source = source + c_ext[rows(g), :] * value
                            source = inv_ext[rows(g), :] * source
                            src[rows(g), :] = source
                        else:
                            source = src[rows(g), :]
                        then[rows(g), :] = advance(k, value, lambda: then[rows(g), :], total + source)

        for g in range(8):
            out_ref[d, n, rows(g), :] = state[rows(g), pl.ds(0, 256)]


def base_row(g):
    return g if g < 10 else 28 + g


def spec(count):
    return [pl.BlockSpec(memory_space=pltpu.VMEM)] * count


def smem():
    return pl.BlockSpec(memory_space=pltpu.SMEM)


def call(kernel, name, outs, ins, scratch=(), limit=24):
    return pl.pallas_call(
        kernel,
        out_shape=outs,
        in_specs=ins,
        out_specs=spec(len(outs)),
        scratch_shapes=list(scratch),
        compiler_params=pltpu.CompilerParams(vmem_limit_bytes=limit * 1024 * 1024),
        name=name,
        cost_estimate=HINTS.get(name),
    )


LONG = pl.CostEstimate(flops=10**9, bytes_accessed=10**7, transcendentals=0)
NONE = pl.CostEstimate(flops=0, bytes_accessed=0, transcendentals=0)
HINTS = {"spread_cells": NONE, "pack_early": NONE, "place_vias": LONG, "pack_relay": LONG}


def arr(*shape, dtype=F32):
    return jax.ShapeDtypeStruct(shape, dtype)


def swaps(count, offset):
    partner = list(range(count))
    for i in range(offset, count - 1, 2):
        partner[i], partner[i + 1] = i + 1, i
    return list(enumerate(partner))


def per_device(
    sheet_res, capacity, drop_start, load_cell, load_current, via_cell, via_current, base_sheet, base_start, bump_cell
):
    row_count = lax.axis_size("row")
    col_count = lax.axis_size("col")
    place = jnp.stack(
        [lax.axis_index("die"), lax.axis_index("row"), lax.axis_index("col"), row_count - 1, col_count - 1]
    ).astype(jnp.int32)
    others = [(0, 1), (1, 0)]

    packed, send = call(pack_kernel, "pack_vias", (arr(2, VIAS, 8, 128), arr(VIAS + 1, 8, 128)), [smem()] + spec(1))(
        place, via_current
    )
    got = lax.ppermute(send, "die", others)
    def buffer(count):
        return arr(8 * count, 128)

    base = call(base_kernel, "pack_base", (buffer(BASE),), [smem()] + spec(3))(bump_cell, base_sheet, base_start, send)[0]
    first = lax.ppermute(base, "row", swaps(row_count, 0))
    early, between = call(chip_kernel, "pack_early", (buffer(EARLY), buffer(EARLY + 2 * BASE)), [smem()] + spec(5))(
        place, base, first, sheet_res, capacity, drop_start
    )
    between = lax.ppermute(between, "row", swaps(row_count, 1))
    cells, load_cells, loads, spread, counts = call(
        prepare_kernel, "spread_cells",
        (arr(4, VIAS, 8, 128), arr(4, 8, 128), arr(4, 4, 8, 128), arr(256, 1024, dtype=jnp.bfloat16), arr(4, 64, 128)),
        spec(3),
    )(via_cell, load_cell, load_current)

    field, even, odd, arriving = call(
        place_kernel, "place_vias", (arr(4, 4, 64, 128), buffer(LATE + EARLY), buffer(LATE), buffer(1)),
        [smem()] + spec(9), [pltpu.VMEM((4, 4, VIAS, 8, 128), F32)],
    )(place, packed, send, got, cells, load_cells, loads, spread, counts, early)

    late = lax.ppermute(odd, "row", swaps(row_count, 1))
    within = lax.ppermute(even, "row", swaps(row_count, 0))
    relay = call(relay_kernel, "pack_relay", (buffer(BASE),), [smem()] + spec(1))(place, between)[0]
    relayed = lax.ppermute(relay, "row", swaps(row_count, 0))
    shares = call(shares_kernel, "pack_shares", (buffer(4),), spec(3))(first, between, relayed)[0]
    shares = lax.ppermute(shares, "die", others)

    even, odd, wide = call(
        strip_kernel, "column_strips", (buffer(COL_GROUPS), buffer(COL_GROUPS), arr(200, 128)), [smem()] + spec(13)
    )(place, sheet_res, capacity, drop_start, counts, field, base, arriving, first, between, within, late, relayed, shares)
    even = lax.ppermute(even, "col", swaps(col_count, 0))
    odd = lax.ppermute(odd, "col", swaps(col_count, 1))

    image, pair = arr(4, 96, 256), arr(2, 96, 256)
    parts = call(
        assemble_kernel, "assemble",
        (image, image, pair, pair) + (image,) * 7 + (arr(2, 256, 384, dtype=jnp.bfloat16),), [smem()] + spec(8),
    )(place, sheet_res, capacity, drop_start, counts, field, within, between, late)

    ext = pltpu.VMEM((96, 384), F32)
    scratch = [ext, ext, pltpu.VMEM((2, 96, 384), F32), pltpu.VMEM((4, 40, 384), F32)] + [ext] * 8
    return call(solve_kernel, "solve", (arr(2, 2, 64, 256), arr(2, 8, 32)), [smem()] + spec(15), scratch)(
        place, *parts, wide, even, odd
    )


def solution(mesh):
    in_specs = (
        P("die", None, "row", "col"),
        P("die", "row", "col"),
        P("die", None, "row", "col"),
        P("die", "row", "col"),
        P(None, "die", None, "row", "col"),
        P("die", None, "row", "col"),
        P(None, "die", None, None, "row", "col"),
        P(None, "row", "col"),
        P(None, "row", "col"),
        P("row", "col"),
    )
    out_specs = (P("die", None, "row", "col"), P(None, "row", "col"))
    return jax.shard_map(
        per_device, mesh=mesh, in_specs=in_specs, out_specs=out_specs, check_vma=False
    )
```

```python
import jax
import jax.numpy as jnp
from jax import lax
from jax.experimental import pallas as pl
from jax.experimental.pallas import tpu as pltpu
from jax.sharding import PartitionSpec as P

SWEEPS = 6
STEPS = 2
VIAS = 32

VIA_CONDUCT = 1.0
VIA_RESIST = 4.0
BUMP_CONDUCT = 50.0
BASE_CAPACITY = 0.1
LOWER_BOUND = 0.1
UPPER_BOUND = 1.9

MIDDLE = 0.5 * (UPPER_BOUND + LOWER_BOUND)
HALF = 0.5 * (UPPER_BOUND - LOWER_BOUND)

GROUPS = 12
F32 = jnp.float32


def sweep_weights():
    scaled = MIDDLE / HALF
    ratio = 1.0 / scaled
    pairs = []
    for _ in range(SWEEPS - 1):
        following = 1.0 / (2.0 * scaled - ratio)
        pairs.append((following * ratio, 2.0 * following / HALF))
        ratio = following
    return pairs


WEIGHTS = sweep_weights()


def lane_iota():
    return lax.broadcasted_iota(jnp.int32, (8, 128), 1)


def sub_iota(width=128):
    return lax.broadcasted_iota(jnp.int32, (8, width), 0)


def roll(x, shift, axis):
    shift = shift % x.shape[axis]
    return pltpu.roll(x, shift, axis) if shift else x


def rows(g):
    return pl.ds(8 * g, 8)


def pack_kernel(via_ref, packed_ref, send_ref):
    later = lax.axis_index("die").astype(F32)
    total = jnp.zeros((8, 128), F32)
    for v in range(VIAS):
        parts = []
        for d in range(2):
            part = jnp.concatenate([via_ref[t, d, n, v] for t in range(2) for n in range(2)], axis=1)
            packed_ref[d, v] = part
            parts.append(part)
        both = parts[0] + parts[1]
        send_ref[v] = both + later * parts[0]
        total = total + both
    send_ref[VIAS] = total


def spread_nets(ref):
    gap = jnp.zeros((8, 16), F32)
    return jnp.concatenate([gap, ref[0], gap, gap, ref[1], gap], axis=1)


def shared(first, second, shift):
    return jnp.where(sub_iota() < shift, first, roll(second, shift, 0))


def shared_low(first, second, shift):
    return jnp.where(sub_iota() >= shift, first, roll(second, shift, 0))


class RowSender:
    def __init__(self, even, even_ref, odd_ref):
        self.even, self.even_ref, self.odd_ref, self.place = even, even_ref, odd_ref, 0

    def put(self, up, down):
        self.even_ref[rows(self.place), :] = jnp.where(self.even, down, up)
        self.odd_ref[rows(self.place), :] = jnp.where(self.even, up, down)
        self.place += 1

    def pair(self, first, second):
        self.put(first(0), first(7))
        self.put(second(0), second(7))
        self.put(shared(first(1), second(1), 4), shared_low(first(6), second(6), 4))


BASE = 4
EARLY = 30
LATE = 22


def base_kernel(bump_ref, sheet_ref, start_ref, send_ref, base_ref):
    lane, sub = lane_iota(), sub_iota()
    bump = jnp.zeros((8, 128), F32)
    column = lane % 64 - 16
    for k in range(4):
        bump = jnp.where((column // 8 == k) & (sub * 8 + column % 8 == bump_ref[0:1, k : k + 1]), 1.0, bump)
    for part, value in enumerate([spread_nets(sheet_ref), spread_nets(start_ref), bump, send_ref[VIAS]]):
        base_ref[rows(part), :] = value


def chip_kernel(base_ref, got_ref, sheet_ref, cap_ref, drop_ref, within_ref, between_ref):
    even = lax.axis_index("row") % 2 == 0
    sender = RowSender(even, within_ref, between_ref)
    for d in range(2):
        for half in range(2):
            lanes = pl.ds(half * 128, 128)
            for n in range(2):
                sender.pair(lambda g: sheet_ref[d, n, rows(g), lanes], lambda g: drop_ref[d, n, rows(g), lanes])
        sender.pair(lambda g: cap_ref[d, rows(g), pl.ds(0, 128)], lambda g: cap_ref[d, rows(g), pl.ds(128, 128)])
    for part in range(BASE):
        own, got = base_ref[rows(part), :], got_ref[rows(part), :]
        for slot, value in enumerate([jnp.where(even, own, got), jnp.where(even, got, own)]):
            between_ref[rows(EARLY + BASE * slot + part), :] = value


def relay_kernel(between_ref, relay_ref):
    even = lax.axis_index("row") % 2 == 0
    for part in range(BASE):
        a, b = between_ref[rows(EARLY + part), :], between_ref[rows(EARLY + BASE + part), :]
        relay_ref[rows(part), :] = jnp.where(even, b, a)


def shares_kernel(first_ref, between_ref, relayed_ref, shares_ref):
    shares_ref[rows(0), :] = first_ref[rows(3), :]
    for slot in range(2):
        shares_ref[rows(1 + slot), :] = between_ref[rows(EARLY + BASE * slot + 3), :]
    shares_ref[rows(3), :] = relayed_ref[rows(3), :]


def spread_matrix(height, width):
    row = lax.broadcasted_iota(jnp.int32, (height, width), 0) % 128
    column = lax.broadcasted_iota(jnp.int32, (height, width), 1)
    return jnp.where(row == column // 8, 1.0, 0.0).astype(jnp.bfloat16)


def halves(value):
    high = value.astype(jnp.bfloat16)
    low = (value - high.astype(F32)).astype(jnp.bfloat16)
    return jnp.concatenate([high, low], axis=1)


def prepare_kernel(cell_ref, load_cell_ref, load_ref, cells_ref, load_cells_ref, loads_ref, spread_ref, counts_ref):
    within = (lane_iota() % 8).astype(F32)
    spread = spread_matrix(32, 256)
    for d in range(2):
        cells = cell_ref[d].reshape(8 * VIAS, 32).astype(F32).astype(jnp.bfloat16)
        wide = jnp.dot(cells, spread, preferred_element_type=F32)
        load_cell = load_cell_ref[d].astype(F32).astype(jnp.bfloat16)
        load_cell = jnp.dot(load_cell, spread, preferred_element_type=F32)
        for half in range(2):
            lanes = slice(128 * half, 128 * half + 128)
            for v in range(VIAS):
                cells_ref[2 * d + half, v] = wide[8 * v : 8 * v + 8, lanes] - within
            load_cells_ref[2 * d + half] = load_cell[:, lanes] - within
    spread_ref[...] = spread_matrix(256, 1024)
    loads = jnp.concatenate([load_ref[t, d, n] for d in range(2) for t in range(2) for n in range(2)], axis=0)
    high = loads.astype(jnp.bfloat16)
    low = (loads - high.astype(F32)).astype(jnp.bfloat16)
    wide = jnp.dot(high, spread, preferred_element_type=F32) + jnp.dot(low, spread, preferred_element_type=F32)
    for d in range(2):
        for half in range(2):
            for m in range(4):
                loads_ref[2 * d + half, m] = wide[32 * d + 8 * m : 32 * d + 8 * m + 8, 128 * half : 128 * half + 128]

    def count(i, carry):
        state = [jnp.zeros((8, 128), F32) for _ in range(8)]
        for v in range(VIAS):
            cell = cells_ref[i, v]
            for oi in range(8):
                state[oi] = state[oi] + jnp.where(cell == 8.0 * oi, 1.0, 0.0)
        for oi in range(8):
            counts_ref[i, pl.ds(oi, 8, stride=8), :] = state[oi]
        return carry

    lax.fori_loop(0, 4, count, 0)


def place_kernel(
    packed_ref, send_ref, got_ref, cells_ref, load_cells_ref, loads_ref, spread_ref, counts_ref, early_ref,
    field_ref, even_ref, odd_ref, arriving_ref, values_ref,
):
    lane = lane_iota()
    later = lax.axis_index("die").astype(F32)
    even = lax.axis_index("row") % 2 == 0
    weights = (
        (VIA_RESIST * (4.0 - 2.0 * later), VIA_RESIST * (3.0 - 2.0 * later), VIA_RESIST * (1.0 + later)),
        (VIA_RESIST * (3.0 - 2.0 * later), VIA_RESIST * (3.0 - 2.0 * later), VIA_RESIST),
    )
    size = (8 * VIAS, 128)
    first, second, got = packed_ref[0].reshape(size), packed_ref[1].reshape(size), got_ref[0:VIAS].reshape(size)
    for d in range(2):
        mixed = weights[d][0] * first + weights[d][1] * second + weights[d][2] * got
        wide = jnp.dot(halves(mixed), spread_ref[...], preferred_element_type=F32)
        for half in range(2):
            for m in range(4):
                start = 256 * m + 128 * half
                values_ref[2 * d + half, m] = wide[:, start : start + 128].reshape(VIAS, 8, 128)

    def add(i, carry):
        cell = load_cells_ref[i]
        loads = [loads_ref[i, m] for m in range(4)]
        state = []
        for oi in range(8):
            hit = cell == 8.0 * oi
            state.append([jnp.where(hit, load, 0.0) for load in loads])
        for v in range(VIAS):
            cell = cells_ref[i, v]
            values = [values_ref[i, m, v] for m in range(4)]
            for oi in range(8):
                hit = cell == 8.0 * oi
                state[oi] = [old + jnp.where(hit, value, 0.0) for old, value in zip(state[oi], values)]
        for oi in range(8):
            for m in range(4):
                field_ref[m, i, pl.ds(oi, 8, stride=8), :] = state[oi][m]
        return carry

    lax.fori_loop(0, 4, add, 0)

    arriving_ref[...] = send_ref[VIAS] + got_ref[VIAS]
    for g in range(EARLY):
        even_ref[rows(LATE + g), :] = early_ref[rows(g), :]
    sender = RowSender(even, even_ref, odd_ref)
    for d in range(2):
        for half in range(2):
            for n in range(2):
                one = lambda g: field_ref[n, 2 * d + half, rows(g), :]
                two = lambda g: field_ref[2 + n, 2 * d + half, rows(g), :]
                sender.put(one(0), one(7))
                sender.put(shared(one(1), two(0), 3), shared_low(one(6), two(7), 5))
        sender.pair(lambda g: counts_ref[2 * d, rows(g), :], lambda g: counts_ref[2 * d + 1, rows(g), :])


SHEET, DROP, CAPACITY, COUNTS, FIRST, SECOND = range(6)


def near_rows(read, kind, d, half, n, upper):
    early, late = read
    if kind in (FIRST, SECOND):
        start = 11 * d + 4 * half + 2 * n
        if kind == SECOND:
            return roll(late(start + 1), -5 if upper else -3, 0), None
        return late(start), late(start + 1)
    if kind in (SHEET, DROP):
        take, start, second = early, 15 * d + 6 * half + 3 * n, kind == DROP
    elif kind == CAPACITY:
        take, start, second = early, 15 * d + 12, half == 1
    else:
        take, start, second = late, 11 * d + 8, half == 1
    last = take(start + 2)
    return (take(start + 1), roll(last, -4, 0)) if second else (take(start), last)


def column_groups(own, below, above, kind, d, half, n):
    low = near_rows(below, kind, d, half, n, False)
    high = near_rows(above, kind, d, half, n, True)
    return [own(g) for g in range(8)] + [low[0], low[1], high[1], high[0]]


def readers(even, below, above, within_ref, between_ref, late_ref):
    def make(inside, near, skip, far_ref):
        def read(g):
            value = jnp.where(near, within_ref[rows(skip + g), :], far_ref[rows(g), :])
            return value if inside is None else jnp.where(inside, value, 0.0)
        return read

    odd = jnp.logical_not(even)
    return tuple(
        (make(inside, near, LATE, between_ref), make(inside, near, 0, late_ref)) for inside, near in ((below, even), (above, odd))
    )


COL_GROUPS = 2 * GROUPS + 10


def strip_kernel(
    sheet_ref, cap_ref, drop_ref, counts_ref, field_ref, base_ref, arriving_ref, first_ref, between_ref,
    within_ref, late_ref, relayed_ref, shares_ref, even_ref, odd_ref, wide_ref,
):
    lane = lane_iota()
    within = lane % 16
    row, last = lax.axis_index("row"), (lax.axis_size("row") - 1)
    even = row % 2 == 0
    below, above = readers(even, None, None, within_ref, between_ref, late_ref)
    even_col = lax.axis_index("col") % 2 == 0

    own = (lane % 64 >= 16) & (lane % 64 < 48)

    def spread_steps(value):
        out = []
        for t in range(2):
            moved = jnp.where(lane < 64, roll(value, 16 - 64 * t, 1), roll(value, 48 - 64 * t, 1))
            out.append(jnp.where(own, moved, 0.0))
        return out

    def block(ref, start, share):
        parts = [ref[rows(start + f), :] for f in range(BASE)]
        parts[3] = parts[3] + shares_ref[rows(share), :]
        return parts

    def choose(a, b, inside):
        return [jnp.where(inside, jnp.where(even, x, y), 0.0) for x, y in zip(a, b)]

    partner = block(first_ref, 0, 0)
    between = [block(between_ref, EARLY + BASE * slot, 1 + slot) for slot in range(2)]
    relayed = block(relayed_ref, 0, 3)
    groups = []
    for g, parts in enumerate([
        [base_ref[rows(f), :] for f in range(3)] + [arriving_ref[...]],
        choose(partner, between[0], row < last),
        choose(relayed, between[1], row + 2 <= last),
        choose(between[0], relayed, row >= 2),
        choose(between[1], partner, row > 0),
    ]):
        one, two = spread_steps(parts[3])
        groups.append([parts[0], parts[1], one, two, parts[2]])
        for f in range(5):
            wide_ref[rows(5 * f + g), :] = groups[g][f]

    def fields(part, half):
        lanes = pl.ds(half * 128, 128)
        images = [(d, n) for d in range(2) for n in range(2)]
        if part == 0:
            return [
                column_groups(lambda g: ref[d, n, rows(g), lanes], below, above, kind, d, half, n)
                for kind, ref in ((SHEET, sheet_ref), (DROP, drop_ref)) for d, n in images
            ]
        out = [column_groups(lambda g: cap_ref[d, rows(g), lanes], below, above, CAPACITY, d, half, 0) for d in range(2)]
        out += [
            column_groups(lambda g: counts_ref[2 * d + half, rows(g), :], below, above, COUNTS, d, half, 0)
            for d in range(2)
        ]
        for d, n in images:
            one = column_groups(lambda g: field_ref[n, 2 * d + half, rows(g), :], below, above, FIRST, d, half, n)
            two = column_groups(lambda g: field_ref[2 + n, 2 * d + half, rows(g), :], below, above, SECOND, d, half, n)
            merged = []
            for a, b in zip(one, two):
                if b is None:
                    merged.append(a)
                elif half == 0:
                    merged.append(jnp.where(within < 11, a, roll(b, 11, 1)))
                else:
                    merged.append(jnp.where(within >= 5, a, roll(b, -11, 1)))
            out.append(merged)
        return out

    def put(index, left, right):
        even_ref[rows(index), :] = jnp.where(even_col, right, left)
        odd_ref[rows(index), :] = jnp.where(even_col, left, right)

    for part in range(2):
        sides = [fields(part, half) for half in range(2)]
        for g in range(GROUPS):
            out = []
            for half, chunks in enumerate(sides):
                value = chunks[0][g]
                for k in range(1, 8):
                    value = jnp.where((lane // 16 + half) % 8 == k, roll(chunks[k][g], 16 * k, 1), value)
                out.append(value)
            put(part * GROUPS + g, *out)

    start = 2 * GROUPS
    quarter = (lane % 64) // 16
    for g in range(5):
        sheet, drop, one, two, bump = groups[g]
        left = jnp.where(
            quarter == 1, sheet,
            jnp.where(quarter == 2, roll(drop, 16, 1), jnp.where(quarter == 3, roll(one, 32, 1), roll(two, -16, 1))),
        )
        right = jnp.where(
            quarter == 2, sheet,
            jnp.where(quarter == 3, roll(drop, 16, 1), jnp.where(quarter == 1, roll(two, -16, 1), roll(one, -32, 1))),
        )
        put(start + g, left, right)
        put(start + 5 + g, bump, bump)


def assemble_kernel(
    sheet_ref, cap_ref, drop_ref, counts_ref, field_ref, within_ref, between_ref, late_ref,
    s_ref, x_ref, c_ref, k_ref, one_ref, two_ref, up_ref, down_ref, left_ref, right_ref, diag_ref, spread_ref,
):
    row, last = lax.axis_index("row"), (lax.axis_size("row") - 1)
    sub, lane = sub_iota(256), lax.broadcasted_iota(jnp.int32, (8, 256), 1)
    below, above = readers(row % 2 == 0, row < last, row > 0, within_ref, between_ref, late_ref)

    def both(own, kind, d, n):
        sides = [column_groups(lambda g: own(half, g), below, above, kind, d, half, n) for half in range(2)]
        return [None if a is None else jnp.concatenate([a, b], axis=1) for a, b in zip(*sides)]

    for d in range(2):
        caps = both(lambda half, g: cap_ref[d, rows(g), pl.ds(half * 128, 128)], CAPACITY, d, 0)
        counts = both(lambda half, g: counts_ref[2 * d + half, rows(g), :], COUNTS, d, 0)
        for g in range(GROUPS):
            c_ref[d, rows(g), :] = caps[g]
            k_ref[d, rows(g), :] = counts[g]
        for n in range(2):
            i = 2 * d + n
            sheets = both(lambda half, g: sheet_ref[d, n, rows(g), pl.ds(half * 128, 128)], SHEET, d, n)
            drops = both(lambda half, g: drop_ref[d, n, rows(g), pl.ds(half * 128, 128)], DROP, d, n)
            ones = both(lambda half, g: field_ref[n, 2 * d + half, rows(g), :], FIRST, d, n)
            twos = both(lambda half, g: field_ref[2 + n, 2 * d + half, rows(g), :], SECOND, d, n)
            for g in range(GROUPS):
                s_ref[i, rows(g), :] = sheets[g]
                x_ref[i, rows(g), :] = drops[g]
                one_ref[i, rows(g), :] = c_ref[d, rows(g), :] * drops[g] + ones[g]
                if twos[g] is not None:
                    two_ref[i, rows(g), :] = twos[g]
            for g in range(GROUPS):
                here, after = s_ref[i, rows(g), :], s_ref[i, rows((g + 1) % GROUPS), :]
                under = jnp.where(sub == 7, roll(after, -1, 0), roll(here, -1, 0))
                inside = here > 0.0
                down_ref[i, rows(g), :] = jnp.where(inside, connect(here, under), 0.0)
                right = jnp.where(inside & (lane < 255), connect(here, roll(here, -1, 1)), 0.0)
                right_ref[i, rows(g), :] = right
                left_ref[i, rows(g), :] = roll(right, 1, 1)
            for g in range(GROUPS):
                here, before = down_ref[i, rows(g), :], down_ref[i, rows((g - 1) % GROUPS), :]
                up = jnp.where(sub == 0, roll(before, 1, 0), roll(here, 1, 0))
                up_ref[i, rows(g), :] = up
                diag = c_ref[d, rows(g), :] + up + here + left_ref[i, rows(g), :] + right_ref[i, rows(g), :]
                diag_ref[i, rows(g), :] = diag + VIA_CONDUCT * k_ref[d, rows(g), :]
    source = lax.broadcasted_iota(jnp.int32, (256, 384), 0) % 128
    column = lax.broadcasted_iota(jnp.int32, (256, 384), 1)
    column = jnp.where(column < 256, 16 + column // 8, jnp.where(column < 320, 48, 0) + (column - 256) // 8)
    for n in range(2):
        spread_ref[n] = jnp.where(source == column + 64 * n, 1.0, 0.0).astype(jnp.bfloat16)


def connect(center, neighbour):
    return jnp.where(neighbour > 0.0, 2.0 / (center + neighbour), 0.0)


def three_terms(k):
    if k == 0:
        return 1.0 - 1.0 / MIDDLE, 0.0, 1.0 / MIDDLE
    a, b = WEIGHTS[k - 1]
    return 1.0 + a - b, -a, b


def advance(k, value, previous, total):
    fore, back, gain = three_terms(k)
    out = total if gain == 1.0 else gain * total
    if fore != 0.0:
        out = out + fore * value
    return out + back * previous() if k else out


def base_solve(fields):
    sheet, state, arriving, bump = fields
    steps = [(1, 0), (-1, 0), (1, 1), (-1, 1)]
    inside = sheet > 0.0
    links = [jnp.where(inside, connect(sheet, roll(sheet, s, a)), 0.0) for s, a in steps]
    diagonal = BASE_CAPACITY + links[0] + links[1] + links[2] + links[3] + BUMP_CONDUCT * bump
    inverse = 1.0 / diagonal
    links = [inverse * link for link in links]
    results = []
    for t in range(STEPS):
        source = inverse * (BASE_CAPACITY * state + arriving[t])
        previous = None
        for k in range(SWEEPS):
            total = (links[0] * roll(state, 1, 0) + links[1] * roll(state, -1, 0)) + (
                links[2] * roll(state, 1, 1) + links[3] * roll(state, -1, 1)
            ) + source
            state, previous = advance(k, state, lambda: previous, total), state
        results.append(state)
    return results


def needed(halo):
    if halo > 8:
        return list(range(GROUPS))
    return list(range(8)) + ([8, 11] if halo > 0 else [])


def solve_kernel(
    s_ref, x_ref, c_ref, k_ref, one_ref, two_ref, up_ref, down_ref, left_ref, right_ref, diag_ref, spread_ref,
    wide_ref, even_ref, odd_ref, out_ref, base_out_ref,
    c_ext, k_ext, f_ext, bound, link_up, link_down, link_left, link_right, inv_ext, src, state, alt,
):
    lane = lane_iota()
    row, col = lax.axis_index("row"), lax.axis_index("col")
    has_left, has_right = col > 0, col < (lax.axis_size("col") - 1)
    even_col = col % 2 == 0

    def from_left(g):
        return jnp.where(even_col, odd_ref[rows(g), :], even_ref[rows(g), :])

    def from_right(g):
        return jnp.where(even_col, even_ref[rows(g), :], odd_ref[rows(g), :])

    start = 2 * GROUPS
    quarter = (lane % 64) // 16
    take_left, take_right = (quarter == 0) & has_left, (quarter == 3) & has_right
    fields = []
    for field in range(5):
        out = []
        for g in range(5):
            right_shift = (32, 16, 0, 48, 32)[field]
            left_shift = (-32, -48, 0, -16, -32)[field]
            group = g + 5 * (field == 4)
            value = jnp.where(take_right, roll(from_right(start + group), right_shift, 1), wide_ref[rows(5 * field + g), :])
            out.append(jnp.where(take_left, roll(from_left(start + group), left_shift, 1), value))
        fields.append(jnp.concatenate(out, axis=0))
    solved = base_solve((fields[0], fields[1], (fields[2], fields[3]), fields[4]))
    for t in range(STEPS):
        pieces = halves(solved[t])
        for n in range(2):
            bound[2 * t + n] = jnp.dot(pieces, spread_ref[n], preferred_element_type=F32)
    for n in range(2):
        base_out_ref[n] = roll(solved[1][0:8], -(64 * n + 16), 1)[:, 0:32]

    def third(part, chunk, g):
        right_ok, left_ok = has_right, has_left
        if g in (8, 9):
            right_ok, left_ok = right_ok & (row < (lax.axis_size("row") - 1)), left_ok & (row < (lax.axis_size("row") - 1))
        if g in (10, 11):
            right_ok, left_ok = right_ok & (row > 0), left_ok & (row > 0)
        right = jnp.where((lane // 16 == chunk) & right_ok, from_right(part * GROUPS + g), 0.0)
        value = jnp.where((lane // 16 == (chunk + 7) % 8) & left_ok, from_left(part * GROUPS + g), right)
        return roll(value, -16 * chunk, 1)

    sub, sub3 = sub_iota(), sub_iota(384)

    def above(value, before, index):
        return jnp.where(index == 0, roll(before, 1, 0), roll(value, 1, 0))

    def below(value, after, index):
        return jnp.where(index == 7, roll(after, -1, 0), roll(value, -1, 0))

    for i in range(4):
        d, n = i // 2, i % 2

        def wide(ref, g, extra, index=i):
            return jnp.concatenate([ref[index, rows(g), :], extra], axis=1)

        if n == 0:
            for g in range(GROUPS):
                c_ext[rows(g), :] = wide(c_ref, g, third(1, d, g), d)
                k_ext[rows(g), :] = wide(k_ref, g, third(1, 2 + d, g), d)
        @pl.when(row >= 0)
        def _():
            sheets = [third(0, i, g) for g in range(GROUPS)]
            for g in range(GROUPS):
                here = sheets[g]
                inside = here > 0.0
                low, high = s_ref[i, rows(g), pl.ds(0, 128)], s_ref[i, rows(g), pl.ds(128, 128)]
                after = roll(jnp.where(lane == 0, low, here), -1, 1)
                before = roll(jnp.where(lane == 127, high, here), 1, 1)
                right = jnp.where(inside, connect(here, after), 0.0)
                left = jnp.where(inside, connect(here, before), 0.0)
                down = jnp.where(inside, connect(here, below(here, sheets[(g + 1) % GROUPS], sub)), 0.0)
                up = jnp.where(inside, connect(here, above(here, sheets[(g - 1) % GROUPS], sub)), 0.0)
                first = jnp.where(lane == 0, roll(right, 1, 1), 0.0)
                final = jnp.where(lane == 127, roll(left, -1, 1), 0.0)
                diag = wide(diag_ref, g, 0.0 * here) + jnp.concatenate(
                    [first, final, c_ext[rows(g), pl.ds(256, 128)] + up + down + left + right
                     + VIA_CONDUCT * k_ext[rows(g), pl.ds(256, 128)]], axis=1)
                inverse = jnp.where(diag > 0.0, 1.0 / diag, 0.0)
                inv_ext[rows(g), :] = inverse
                zero = jnp.zeros_like(first)
                link_up[rows(g), :] = inverse * wide(up_ref, g, up)
                link_down[rows(g), :] = inverse * wide(down_ref, g, down)
                link_left[rows(g), :] = inverse * (wide(left_ref, g, left) + jnp.concatenate([first, zero, zero], axis=1))
                link_right[rows(g), :] = inverse * (wide(right_ref, g, right) + jnp.concatenate([zero, final, zero], axis=1))
                drop = third(0, 4 + i, g)
                state[rows(g), :] = wide(x_ref, g, drop)
                one = third(1, 4 + i, g)
                f_ext[0, rows(g), :] = wide(one_ref, g, c_ext[rows(g), pl.ds(256, 128)] * drop + one)
                if g not in (9, 10):
                    two = jnp.where(lane < 64, roll(one, -11, 1), roll(one, 11, 1))
                    f_ext[1, rows(g), :] = wide(two_ref, g, two)

        @pl.when(row >= 0)
        def _():
            for t in range(STEPS):
                for k in range(SWEEPS):
                    now, then = (alt, state) if k % 2 else (state, alt)
                    for g in needed(11 - 6 * t - k):
                        value = now[rows(g), :]
                        total = link_up[rows(g), :] * above(value, now[rows((g - 1) % GROUPS), :], sub3)
                        total = total + link_down[rows(g), :] * below(value, now[rows((g + 1) % GROUPS), :], sub3)
                        total = total + (
                            link_left[rows(g), :] * roll(value, 1, 1) + link_right[rows(g), :] * roll(value, -1, 1))
                        if k == 0:
                            spread = jnp.broadcast_to(bound[2 * t + n, pl.ds(base_row(g), 1), :], (8, 384))
                            source = f_ext[t, rows(g), :] + k_ext[rows(g), :] * spread
                            if t:
                                source = source + c_ext[rows(g), :] * value
                            source = inv_ext[rows(g), :] * source
                            src[rows(g), :] = source
                        else:
                            source = src[rows(g), :]
                        then[rows(g), :] = advance(k, value, lambda: then[rows(g), :], total + source)

        for g in range(8):
            out_ref[d, n, rows(g), :] = state[rows(g), pl.ds(0, 256)]


def base_row(g):
    return g if g < 10 else 28 + g


def spec(count):
    return [pl.BlockSpec(memory_space=pltpu.VMEM)] * count


def call(kernel, name, outs, ins, scratch=(), limit=24):
    return pl.pallas_call(
        kernel,
        out_shape=outs,
        in_specs=ins,
        out_specs=spec(len(outs)),
        scratch_shapes=list(scratch),
        compiler_params=pltpu.CompilerParams(vmem_limit_bytes=limit * 1024 * 1024),
        name=name,
        cost_estimate=HINTS.get(name),
    )


LONG = pl.CostEstimate(flops=10**9, bytes_accessed=10**7, transcendentals=0)
NONE = pl.CostEstimate(flops=0, bytes_accessed=0, transcendentals=0)
HINTS = {"spread_cells": NONE, "pack_early": NONE, "place_vias": LONG, "pack_relay": LONG}


def arr(*shape, dtype=F32):
    return jax.ShapeDtypeStruct(shape, dtype)


def swaps(count, offset):
    partner = list(range(count))
    for i in range(offset, count - 1, 2):
        partner[i], partner[i + 1] = i + 1, i
    return list(enumerate(partner))


def per_device(
    sheet_res, capacity, drop_start, load_cell, load_current, via_cell, via_current, base_sheet, base_start, bump_cell
):
    row_count = lax.axis_size("row")
    col_count = lax.axis_size("col")
    others = [(0, 1), (1, 0)]

    packed, send = call(pack_kernel, "pack_vias", (arr(2, VIAS, 8, 128), arr(VIAS + 1, 8, 128)), spec(1))(via_current)
    got = lax.ppermute(send, "die", others)
    def buffer(count):
        return arr(8 * count, 128)

    base = call(base_kernel, "pack_base", (buffer(BASE),), spec(4))(bump_cell, base_sheet, base_start, send)[0]
    first = lax.ppermute(base, "row", swaps(row_count, 0))
    early, between = call(chip_kernel, "pack_early", (buffer(EARLY), buffer(EARLY + 2 * BASE)), spec(5))(
        base, first, sheet_res, capacity, drop_start
    )
    between = lax.ppermute(between, "row", swaps(row_count, 1))
    cells, load_cells, loads, spread, counts = call(
        prepare_kernel, "spread_cells",
        (arr(4, VIAS, 8, 128), arr(4, 8, 128), arr(4, 4, 8, 128), arr(256, 1024, dtype=jnp.bfloat16), arr(4, 64, 128)),
        spec(3),
    )(via_cell, load_cell, load_current)

    field, even, odd, arriving = call(
        place_kernel, "place_vias", (arr(4, 4, 64, 128), buffer(LATE + EARLY), buffer(LATE), buffer(1)),
        spec(9), [pltpu.VMEM((4, 4, VIAS, 8, 128), F32)],
    )(packed, send, got, cells, load_cells, loads, spread, counts, early)

    late = lax.ppermute(odd, "row", swaps(row_count, 1))
    within = lax.ppermute(even, "row", swaps(row_count, 0))
    relay = call(relay_kernel, "pack_relay", (buffer(BASE),), spec(1))(between)[0]
    relayed = lax.ppermute(relay, "row", swaps(row_count, 0))
    shares = call(shares_kernel, "pack_shares", (buffer(4),), spec(3))(first, between, relayed)[0]
    shares = lax.ppermute(shares, "die", others)

    even, odd, wide = call(
        strip_kernel, "column_strips", (buffer(COL_GROUPS), buffer(COL_GROUPS), arr(200, 128)), spec(13)
    )(sheet_res, capacity, drop_start, counts, field, base, arriving, first, between, within, late, relayed, shares)
    even = lax.ppermute(even, "col", swaps(col_count, 0))
    odd = lax.ppermute(odd, "col", swaps(col_count, 1))

    image, pair = arr(4, 96, 256), arr(2, 96, 256)
    parts = call(
        assemble_kernel, "assemble",
        (image, image, pair, pair) + (image,) * 7 + (arr(2, 256, 384, dtype=jnp.bfloat16),), spec(8),
    )(sheet_res, capacity, drop_start, counts, field, within, between, late)

    ext = pltpu.VMEM((96, 384), F32)
    scratch = [ext, ext, pltpu.VMEM((2, 96, 384), F32), pltpu.VMEM((4, 40, 384), F32)] + [ext] * 8
    return call(solve_kernel, "solve", (arr(2, 2, 64, 256), arr(2, 8, 32)), spec(15), scratch)(
        *parts, wide, even, odd
    )


def solution(mesh):
    in_specs = (
        P("die", None, "row", "col"),
        P("die", "row", "col"),
        P("die", None, "row", "col"),
        P("die", "row", "col"),
        P(None, "die", None, "row", "col"),
        P("die", None, "row", "col"),
        P(None, "die", None, None, "row", "col"),
        P(None, "row", "col"),
        P(None, "row", "col"),
        P("row", "col"),
    )
    out_specs = (P("die", None, "row", "col"), P(None, "row", "col"))
    return jax.shard_map(
        per_device, mesh=mesh, in_specs=in_specs, out_specs=out_specs, check_vma=False
    )
```

```python
import jax
import jax.numpy as jnp
from jax import lax
from jax.experimental import pallas as pl
from jax.experimental.pallas import tpu as pltpu
from jax.sharding import PartitionSpec as P

SWEEPS = 6
STEPS = 2
VIAS = 32

VIA_CONDUCT = 1.0
VIA_RESIST = 4.0
BUMP_CONDUCT = 50.0
BASE_CAPACITY = 0.1
LOWER_BOUND = 0.1
UPPER_BOUND = 1.9

MIDDLE = 0.5 * (UPPER_BOUND + LOWER_BOUND)
HALF = 0.5 * (UPPER_BOUND - LOWER_BOUND)

GROUPS = 12
F32 = jnp.float32


def sweep_weights():
    scaled = MIDDLE / HALF
    ratio = 1.0 / scaled
    pairs = []
    for _ in range(SWEEPS - 1):
        following = 1.0 / (2.0 * scaled - ratio)
        pairs.append((following * ratio, 2.0 * following / HALF))
        ratio = following
    return pairs


WEIGHTS = sweep_weights()


def lane_iota():
    return lax.broadcasted_iota(jnp.int32, (8, 128), 1)


def sub_iota(width=128):
    return lax.broadcasted_iota(jnp.int32, (8, width), 0)


def roll(x, shift, axis):
    shift = shift % x.shape[axis]
    return pltpu.roll(x, shift, axis) if shift else x


def rows(g):
    return pl.ds(8 * g, 8)


def pack_kernel(via_ref, packed_ref, send_ref, total_ref):
    later = lax.axis_index("die").astype(F32)
    total = jnp.zeros((8, 128), F32)
    for v in range(VIAS):
        parts = []
        for d in range(2):
            part = jnp.concatenate([via_ref[t, d, n, v] for t in range(2) for n in range(2)], axis=1)
            packed_ref[d, v] = part
            parts.append(part)
        both = parts[0] + parts[1]
        send_ref[v] = both + later * parts[0]
        total = total + both
    total_ref[...] = total


def spread_nets(ref):
    gap = jnp.zeros((8, 16), F32)
    return jnp.concatenate([gap, ref[0], gap, gap, ref[1], gap], axis=1)


def shared(first, second, shift):
    return jnp.where(sub_iota() < shift, first, roll(second, shift, 0))


def shared_low(first, second, shift):
    return jnp.where(sub_iota() >= shift, first, roll(second, shift, 0))


class RowSender:
    def __init__(self, even, even_ref, odd_ref):
        self.even, self.even_ref, self.odd_ref, self.place = even, even_ref, odd_ref, 0

    def put(self, up, down):
        self.even_ref[rows(self.place), :] = jnp.where(self.even, down, up)
        self.odd_ref[rows(self.place), :] = jnp.where(self.even, up, down)
        self.place += 1

    def pair(self, first, second):
        self.put(first(0), first(7))
        self.put(second(0), second(7))
        self.put(shared(first(1), second(1), 4), shared_low(first(6), second(6), 4))


BASE = 4
EARLY = 30
LATE = 22


def base_kernel(bump_ref, sheet_ref, start_ref, total_ref, got_ref, base_ref):
    lane, sub = lane_iota(), sub_iota()
    bump = jnp.zeros((8, 128), F32)
    column = lane % 64 - 16
    for k in range(4):
        bump = jnp.where((column // 8 == k) & (sub * 8 + column % 8 == bump_ref[0:1, k : k + 1]), 1.0, bump)
    for part, value in enumerate([spread_nets(sheet_ref), spread_nets(start_ref), bump, total_ref[...] + got_ref[...]]):
        base_ref[rows(part), :] = value


def chip_kernel(base_ref, got_ref, sheet_ref, cap_ref, drop_ref, within_ref, between_ref):
    even = lax.axis_index("row") % 2 == 0
    sender = RowSender(even, within_ref, between_ref)
    for d in range(2):
        for half in range(2):
            lanes = pl.ds(half * 128, 128)
            for n in range(2):
                sender.pair(lambda g: sheet_ref[d, n, rows(g), lanes], lambda g: drop_ref[d, n, rows(g), lanes])
        sender.pair(lambda g: cap_ref[d, rows(g), pl.ds(0, 128)], lambda g: cap_ref[d, rows(g), pl.ds(128, 128)])
    for part in range(BASE):
        own, got = base_ref[rows(part), :], got_ref[rows(part), :]
        for slot, value in enumerate([jnp.where(even, own, got), jnp.where(even, got, own)]):
            between_ref[rows(EARLY + BASE * slot + part), :] = value


def relay_kernel(between_ref, relay_ref):
    even = lax.axis_index("row") % 2 == 0
    for part in range(BASE):
        a, b = between_ref[rows(EARLY + part), :], between_ref[rows(EARLY + BASE + part), :]
        relay_ref[rows(part), :] = jnp.where(even, b, a)


def spread_matrix(height, width):
    row = lax.broadcasted_iota(jnp.int32, (height, width), 0) % 128
    column = lax.broadcasted_iota(jnp.int32, (height, width), 1)
    return jnp.where(row == column // 8, 1.0, 0.0).astype(jnp.bfloat16)


def halves(value):
    high = value.astype(jnp.bfloat16)
    low = (value - high.astype(F32)).astype(jnp.bfloat16)
    return jnp.concatenate([high, low], axis=1)


def prepare_kernel(cell_ref, load_cell_ref, load_ref, cells_ref, load_cells_ref, loads_ref, spread_ref, counts_ref):
    within = (lane_iota() % 8).astype(F32)
    spread = spread_matrix(32, 256)
    for d in range(2):
        cells = cell_ref[d].reshape(8 * VIAS, 32).astype(F32).astype(jnp.bfloat16)
        wide = jnp.dot(cells, spread, preferred_element_type=F32)
        load_cell = load_cell_ref[d].astype(F32).astype(jnp.bfloat16)
        load_cell = jnp.dot(load_cell, spread, preferred_element_type=F32)
        for half in range(2):
            lanes = slice(128 * half, 128 * half + 128)
            for v in range(VIAS):
                cells_ref[2 * d + half, v] = wide[8 * v : 8 * v + 8, lanes] - within
            load_cells_ref[2 * d + half] = load_cell[:, lanes] - within
    spread_ref[...] = spread_matrix(256, 1024)
    loads = jnp.concatenate([load_ref[t, d, n] for d in range(2) for t in range(2) for n in range(2)], axis=0)
    high = loads.astype(jnp.bfloat16)
    low = (loads - high.astype(F32)).astype(jnp.bfloat16)
    wide = jnp.dot(high, spread, preferred_element_type=F32) + jnp.dot(low, spread, preferred_element_type=F32)
    for d in range(2):
        for half in range(2):
            for m in range(4):
                loads_ref[2 * d + half, m] = wide[32 * d + 8 * m : 32 * d + 8 * m + 8, 128 * half : 128 * half + 128]

    def count(i, carry):
        state = [jnp.zeros((8, 128), F32) for _ in range(8)]
        for v in range(VIAS):
            cell = cells_ref[i, v]
            for oi in range(8):
                state[oi] = state[oi] + jnp.where(cell == 8.0 * oi, 1.0, 0.0)
        for oi in range(8):
            counts_ref[i, pl.ds(oi, 8, stride=8), :] = state[oi]
        return carry

    lax.fori_loop(0, 4, count, 0)


def place_kernel(
    packed_ref, got_ref, cells_ref, load_cells_ref, loads_ref, spread_ref, counts_ref,
    field_ref, even_ref, odd_ref, values_ref,
):
    lane = lane_iota()
    later = lax.axis_index("die").astype(F32)
    even = lax.axis_index("row") % 2 == 0
    weights = (
        (VIA_RESIST * (4.0 - 2.0 * later), VIA_RESIST * (3.0 - 2.0 * later), VIA_RESIST * (1.0 + later)),
        (VIA_RESIST * (3.0 - 2.0 * later), VIA_RESIST * (3.0 - 2.0 * later), VIA_RESIST),
    )
    size = (8 * VIAS, 128)
    first, second, got = packed_ref[0].reshape(size), packed_ref[1].reshape(size), got_ref[...].reshape(size)
    for d in range(2):
        mixed = weights[d][0] * first + weights[d][1] * second + weights[d][2] * got
        wide = jnp.dot(halves(mixed), spread_ref[...], preferred_element_type=F32)
        for half in range(2):
            for m in range(4):
                start = 256 * m + 128 * half
                values_ref[2 * d + half, m] = wide[:, start : start + 128].reshape(VIAS, 8, 128)

    def add(i, carry):
        cell = load_cells_ref[i]
        loads = [loads_ref[i, m] for m in range(4)]
        state = []
        for oi in range(8):
            hit = cell == 8.0 * oi
            state.append([jnp.where(hit, load, 0.0) for load in loads])
        for v in range(VIAS):
            cell = cells_ref[i, v]
            values = [values_ref[i, m, v] for m in range(4)]
            for oi in range(8):
                hit = cell == 8.0 * oi
                state[oi] = [old + jnp.where(hit, value, 0.0) for old, value in zip(state[oi], values)]
        for oi in range(8):
            for m in range(4):
                field_ref[m, i, pl.ds(oi, 8, stride=8), :] = state[oi][m]
        return carry

    lax.fori_loop(0, 4, add, 0)

    sender = RowSender(even, even_ref, odd_ref)
    for d in range(2):
        for half in range(2):
            for n in range(2):
                one = lambda g: field_ref[n, 2 * d + half, rows(g), :]
                two = lambda g: field_ref[2 + n, 2 * d + half, rows(g), :]
                sender.put(one(0), one(7))
                sender.put(shared(one(1), two(0), 3), shared_low(one(6), two(7), 5))
        sender.pair(lambda g: counts_ref[2 * d, rows(g), :], lambda g: counts_ref[2 * d + 1, rows(g), :])


SHEET, DROP, CAPACITY, COUNTS, FIRST, SECOND = range(6)


def near_rows(read, kind, d, half, n, upper):
    early, late = read
    if kind in (FIRST, SECOND):
        start = 11 * d + 4 * half + 2 * n
        if kind == SECOND:
            return roll(late(start + 1), -5 if upper else -3, 0), None
        return late(start), late(start + 1)
    if kind in (SHEET, DROP):
        take, start, second = early, 15 * d + 6 * half + 3 * n, kind == DROP
    elif kind == CAPACITY:
        take, start, second = early, 15 * d + 12, half == 1
    else:
        take, start, second = late, 11 * d + 8, half == 1
    last = take(start + 2)
    return (take(start + 1), roll(last, -4, 0)) if second else (take(start), last)


def column_groups(own, below, above, kind, d, half, n):
    low = near_rows(below, kind, d, half, n, False)
    high = near_rows(above, kind, d, half, n, True)
    return [own(g) for g in range(8)] + [low[0], low[1], high[1], high[0]]


def readers(even, below, above, early_ref, between_ref, within_ref, late_ref):
    def make(inside, near, near_ref, far_ref):
        def read(g):
            value = jnp.where(near, near_ref[rows(g), :], far_ref[rows(g), :])
            return value if inside is None else jnp.where(inside, value, 0.0)
        return read

    odd = jnp.logical_not(even)
    return tuple(
        (make(inside, near, early_ref, between_ref), make(inside, near, within_ref, late_ref))
        for inside, near in ((below, even), (above, odd))
    )


COL_GROUPS = 2 * GROUPS + 10


def strip_kernel(
    sheet_ref, cap_ref, drop_ref, counts_ref, field_ref, base_ref, first_ref, early_ref, between_ref,
    within_ref, late_ref, relayed_ref, even_ref, odd_ref, wide_ref,
):
    lane = lane_iota()
    within = lane % 16
    row, last = lax.axis_index("row"), (lax.axis_size("row") - 1)
    even = row % 2 == 0
    below, above = readers(even, None, None, early_ref, between_ref, within_ref, late_ref)
    even_col = lax.axis_index("col") % 2 == 0

    own = (lane % 64 >= 16) & (lane % 64 < 48)

    def spread_steps(value):
        out = []
        for t in range(2):
            moved = jnp.where(lane < 64, roll(value, 16 - 64 * t, 1), roll(value, 48 - 64 * t, 1))
            out.append(jnp.where(own, moved, 0.0))
        return out

    def block(ref, start):
        return [ref[rows(start + f), :] for f in range(BASE)]

    def choose(a, b, inside):
        return [jnp.where(inside, jnp.where(even, x, y), 0.0) for x, y in zip(a, b)]

    partner = block(first_ref, 0)
    between = [block(between_ref, EARLY + BASE * slot) for slot in range(2)]
    relayed = block(relayed_ref, 0)
    groups = []
    for g, parts in enumerate([
        block(base_ref, 0),
        choose(partner, between[0], row < last),
        choose(relayed, between[1], row + 2 <= last),
        choose(between[0], relayed, row >= 2),
        choose(between[1], partner, row > 0),
    ]):
        one, two = spread_steps(parts[3])
        groups.append([parts[0], parts[1], one, two, parts[2]])
        for f in range(5):
            wide_ref[rows(5 * f + g), :] = groups[g][f]

    def fields(part, half):
        lanes = pl.ds(half * 128, 128)
        images = [(d, n) for d in range(2) for n in range(2)]
        if part == 0:
            return [
                column_groups(lambda g: ref[d, n, rows(g), lanes], below, above, kind, d, half, n)
                for kind, ref in ((SHEET, sheet_ref), (DROP, drop_ref)) for d, n in images
            ]
        out = [column_groups(lambda g: cap_ref[d, rows(g), lanes], below, above, CAPACITY, d, half, 0) for d in range(2)]
        out += [
            column_groups(lambda g: counts_ref[2 * d + half, rows(g), :], below, above, COUNTS, d, half, 0)
            for d in range(2)
        ]
        for d, n in images:
            one = column_groups(lambda g: field_ref[n, 2 * d + half, rows(g), :], below, above, FIRST, d, half, n)
            two = column_groups(lambda g: field_ref[2 + n, 2 * d + half, rows(g), :], below, above, SECOND, d, half, n)
            merged = []
            for a, b in zip(one, two):
                if b is None:
                    merged.append(a)
                elif half == 0:
                    merged.append(jnp.where(within < 11, a, roll(b, 11, 1)))
                else:
                    merged.append(jnp.where(within >= 5, a, roll(b, -11, 1)))
            out.append(merged)
        return out

    def put(index, left, right):
        even_ref[rows(index), :] = jnp.where(even_col, right, left)
        odd_ref[rows(index), :] = jnp.where(even_col, left, right)

    for part in range(2):
        sides = [fields(part, half) for half in range(2)]
        for g in range(GROUPS):
            out = []
            for half, chunks in enumerate(sides):
                value = chunks[0][g]
                for k in range(1, 8):
                    value = jnp.where((lane // 16 + half) % 8 == k, roll(chunks[k][g], 16 * k, 1), value)
                out.append(value)
            put(part * GROUPS + g, *out)

    start = 2 * GROUPS
    quarter = (lane % 64) // 16
    for g in range(5):
        sheet, drop, one, two, bump = groups[g]
        left = jnp.where(
            quarter == 1, sheet,
            jnp.where(quarter == 2, roll(drop, 16, 1), jnp.where(quarter == 3, roll(one, 32, 1), roll(two, -16, 1))),
        )
        right = jnp.where(
            quarter == 2, sheet,
            jnp.where(quarter == 3, roll(drop, 16, 1), jnp.where(quarter == 1, roll(two, -16, 1), roll(one, -32, 1))),
        )
        put(start + g, left, right)
        put(start + 5 + g, bump, bump)


def assemble_kernel(
    sheet_ref, cap_ref, drop_ref, counts_ref, field_ref, early_ref, between_ref, within_ref, late_ref,
    s_ref, x_ref, c_ref, k_ref, one_ref, two_ref, up_ref, down_ref, left_ref, right_ref, diag_ref, spread_ref,
):
    row, last = lax.axis_index("row"), (lax.axis_size("row") - 1)
    sub, lane = sub_iota(256), lax.broadcasted_iota(jnp.int32, (8, 256), 1)
    below, above = readers(row % 2 == 0, row < last, row > 0, early_ref, between_ref, within_ref, late_ref)

    def both(own, kind, d, n):
        sides = [column_groups(lambda g: own(half, g), below, above, kind, d, half, n) for half in range(2)]
        return [None if a is None else jnp.concatenate([a, b], axis=1) for a, b in zip(*sides)]

    for d in range(2):
        caps = both(lambda half, g: cap_ref[d, rows(g), pl.ds(half * 128, 128)], CAPACITY, d, 0)
        counts = both(lambda half, g: counts_ref[2 * d + half, rows(g), :], COUNTS, d, 0)
        for g in range(GROUPS):
            c_ref[d, rows(g), :] = caps[g]
            k_ref[d, rows(g), :] = counts[g]
        for n in range(2):
            i = 2 * d + n
            sheets = both(lambda half, g: sheet_ref[d, n, rows(g), pl.ds(half * 128, 128)], SHEET, d, n)
            drops = both(lambda half, g: drop_ref[d, n, rows(g), pl.ds(half * 128, 128)], DROP, d, n)
            ones = both(lambda half, g: field_ref[n, 2 * d + half, rows(g), :], FIRST, d, n)
            twos = both(lambda half, g: field_ref[2 + n, 2 * d + half, rows(g), :], SECOND, d, n)
            for g in range(GROUPS):
                s_ref[i, rows(g), :] = sheets[g]
                x_ref[i, rows(g), :] = drops[g]
                one_ref[i, rows(g), :] = c_ref[d, rows(g), :] * drops[g] + ones[g]
                if twos[g] is not None:
                    two_ref[i, rows(g), :] = twos[g]
            for g in range(GROUPS):
                here, after = s_ref[i, rows(g), :], s_ref[i, rows((g + 1) % GROUPS), :]
                under = jnp.where(sub == 7, roll(after, -1, 0), roll(here, -1, 0))
                inside = here > 0.0
                down_ref[i, rows(g), :] = jnp.where(inside, connect(here, under), 0.0)
                right = jnp.where(inside & (lane < 255), connect(here, roll(here, -1, 1)), 0.0)
                right_ref[i, rows(g), :] = right
                left_ref[i, rows(g), :] = roll(right, 1, 1)
            for g in range(GROUPS):
                here, before = down_ref[i, rows(g), :], down_ref[i, rows((g - 1) % GROUPS), :]
                up = jnp.where(sub == 0, roll(before, 1, 0), roll(here, 1, 0))
                up_ref[i, rows(g), :] = up
                diag = c_ref[d, rows(g), :] + up + here + left_ref[i, rows(g), :] + right_ref[i, rows(g), :]
                diag_ref[i, rows(g), :] = diag + VIA_CONDUCT * k_ref[d, rows(g), :]
    source = lax.broadcasted_iota(jnp.int32, (256, 384), 0) % 128
    column = lax.broadcasted_iota(jnp.int32, (256, 384), 1)
    column = jnp.where(column < 256, 16 + column // 8, jnp.where(column < 320, 48, 0) + (column - 256) // 8)
    for n in range(2):
        spread_ref[n] = jnp.where(source == column + 64 * n, 1.0, 0.0).astype(jnp.bfloat16)


def connect(center, neighbour):
    return jnp.where(neighbour > 0.0, 2.0 / (center + neighbour), 0.0)


def three_terms(k):
    if k == 0:
        return 1.0 - 1.0 / MIDDLE, 0.0, 1.0 / MIDDLE
    a, b = WEIGHTS[k - 1]
    return 1.0 + a - b, -a, b


def advance(k, value, previous, total):
    fore, back, gain = three_terms(k)
    out = total if gain == 1.0 else gain * total
    if fore != 0.0:
        out = out + fore * value
    return out + back * previous() if k else out


def base_solve(fields):
    sheet, state, arriving, bump = fields
    steps = [(1, 0), (-1, 0), (1, 1), (-1, 1)]
    inside = sheet > 0.0
    links = [jnp.where(inside, connect(sheet, roll(sheet, s, a)), 0.0) for s, a in steps]
    diagonal = BASE_CAPACITY + links[0] + links[1] + links[2] + links[3] + BUMP_CONDUCT * bump
    inverse = 1.0 / diagonal
    links = [inverse * link for link in links]
    results = []
    for t in range(STEPS):
        source = inverse * (BASE_CAPACITY * state + arriving[t])
        previous = None
        for k in range(SWEEPS):
            total = (links[0] * roll(state, 1, 0) + links[1] * roll(state, -1, 0)) + (
                links[2] * roll(state, 1, 1) + links[3] * roll(state, -1, 1)
            ) + source
            state, previous = advance(k, state, lambda: previous, total), state
        results.append(state)
    return results


def needed(halo):
    if halo > 8:
        return list(range(GROUPS))
    return list(range(8)) + ([8, 11] if halo > 0 else [])


def solve_kernel(
    s_ref, x_ref, c_ref, k_ref, one_ref, two_ref, up_ref, down_ref, left_ref, right_ref, diag_ref, spread_ref,
    wide_ref, even_ref, odd_ref, out_ref, base_out_ref,
    c_ext, k_ext, f_ext, bound, link_up, link_down, link_left, link_right, inv_ext, src, state, alt,
):
    lane = lane_iota()
    row, col = lax.axis_index("row"), lax.axis_index("col")
    has_left, has_right = col > 0, col < (lax.axis_size("col") - 1)
    even_col = col % 2 == 0

    def from_left(g):
        return jnp.where(even_col, odd_ref[rows(g), :], even_ref[rows(g), :])

    def from_right(g):
        return jnp.where(even_col, even_ref[rows(g), :], odd_ref[rows(g), :])

    start = 2 * GROUPS
    quarter = (lane % 64) // 16
    take_left, take_right = (quarter == 0) & has_left, (quarter == 3) & has_right
    fields = []
    for field in range(5):
        out = []
        for g in range(5):
            right_shift = (32, 16, 0, 48, 32)[field]
            left_shift = (-32, -48, 0, -16, -32)[field]
            group = g + 5 * (field == 4)
            value = jnp.where(take_right, roll(from_right(start + group), right_shift, 1), wide_ref[rows(5 * field + g), :])
            out.append(jnp.where(take_left, roll(from_left(start + group), left_shift, 1), value))
        fields.append(jnp.concatenate(out, axis=0))
    solved = base_solve((fields[0], fields[1], (fields[2], fields[3]), fields[4]))
    for t in range(STEPS):
        pieces = halves(solved[t])
        for n in range(2):
            bound[2 * t + n] = jnp.dot(pieces, spread_ref[n], preferred_element_type=F32)
    for n in range(2):
        base_out_ref[n] = roll(solved[1][0:8], -(64 * n + 16), 1)[:, 0:32]

    def third(part, chunk, g):
        right_ok, left_ok = has_right, has_left
        if g in (8, 9):
            right_ok, left_ok = right_ok & (row < (lax.axis_size("row") - 1)), left_ok & (row < (lax.axis_size("row") - 1))
        if g in (10, 11):
            right_ok, left_ok = right_ok & (row > 0), left_ok & (row > 0)
        right = jnp.where((lane // 16 == chunk) & right_ok, from_right(part * GROUPS + g), 0.0)
        value = jnp.where((lane // 16 == (chunk + 7) % 8) & left_ok, from_left(part * GROUPS + g), right)
        return roll(value, -16 * chunk, 1)

    sub, sub3 = sub_iota(), sub_iota(384)

    def above(value, before, index):
        return jnp.where(index == 0, roll(before, 1, 0), roll(value, 1, 0))

    def below(value, after, index):
        return jnp.where(index == 7, roll(after, -1, 0), roll(value, -1, 0))

    for i in range(4):
        d, n = i // 2, i % 2

        def wide(ref, g, extra, index=i):
            return jnp.concatenate([ref[index, rows(g), :], extra], axis=1)

        if n == 0:
            for g in range(GROUPS):
                c_ext[rows(g), :] = wide(c_ref, g, third(1, d, g), d)
                k_ext[rows(g), :] = wide(k_ref, g, third(1, 2 + d, g), d)
        @pl.when(row >= 0)
        def _():
            sheets = [third(0, i, g) for g in range(GROUPS)]
            for g in range(GROUPS):
                here = sheets[g]
                inside = here > 0.0
                low, high = s_ref[i, rows(g), pl.ds(0, 128)], s_ref[i, rows(g), pl.ds(128, 128)]
                after = roll(jnp.where(lane == 0, low, here), -1, 1)
                before = roll(jnp.where(lane == 127, high, here), 1, 1)
                right = jnp.where(inside, connect(here, after), 0.0)
                left = jnp.where(inside, connect(here, before), 0.0)
                down = jnp.where(inside, connect(here, below(here, sheets[(g + 1) % GROUPS], sub)), 0.0)
                up = jnp.where(inside, connect(here, above(here, sheets[(g - 1) % GROUPS], sub)), 0.0)
                first = jnp.where(lane == 0, roll(right, 1, 1), 0.0)
                final = jnp.where(lane == 127, roll(left, -1, 1), 0.0)
                diag = wide(diag_ref, g, 0.0 * here) + jnp.concatenate(
                    [first, final, c_ext[rows(g), pl.ds(256, 128)] + up + down + left + right
                     + VIA_CONDUCT * k_ext[rows(g), pl.ds(256, 128)]], axis=1)
                inverse = jnp.where(diag > 0.0, 1.0 / diag, 0.0)
                inv_ext[rows(g), :] = inverse
                zero = jnp.zeros_like(first)
                link_up[rows(g), :] = inverse * wide(up_ref, g, up)
                link_down[rows(g), :] = inverse * wide(down_ref, g, down)
                link_left[rows(g), :] = inverse * (wide(left_ref, g, left) + jnp.concatenate([first, zero, zero], axis=1))
                link_right[rows(g), :] = inverse * (wide(right_ref, g, right) + jnp.concatenate([zero, final, zero], axis=1))
                drop = third(0, 4 + i, g)
                state[rows(g), :] = wide(x_ref, g, drop)
                one = third(1, 4 + i, g)
                f_ext[0, rows(g), :] = wide(one_ref, g, c_ext[rows(g), pl.ds(256, 128)] * drop + one)
                if g not in (9, 10):
                    two = jnp.where(lane < 64, roll(one, -11, 1), roll(one, 11, 1))
                    f_ext[1, rows(g), :] = wide(two_ref, g, two)

        @pl.when(row >= 0)
        def _():
            for t in range(STEPS):
                for k in range(SWEEPS):
                    now, then = (alt, state) if k % 2 else (state, alt)
                    for g in needed(11 - 6 * t - k):
                        value = now[rows(g), :]
                        total = link_up[rows(g), :] * above(value, now[rows((g - 1) % GROUPS), :], sub3)
                        total = total + link_down[rows(g), :] * below(value, now[rows((g + 1) % GROUPS), :], sub3)
                        total = total + (
                            link_left[rows(g), :] * roll(value, 1, 1) + link_right[rows(g), :] * roll(value, -1, 1))
                        if k == 0:
                            spread = jnp.broadcast_to(bound[2 * t + n, pl.ds(base_row(g), 1), :], (8, 384))
                            source = f_ext[t, rows(g), :] + k_ext[rows(g), :] * spread
                            if t:
                                source = source + c_ext[rows(g), :] * value
                            source = inv_ext[rows(g), :] * source
                            src[rows(g), :] = source
                        else:
                            source = src[rows(g), :]
                        then[rows(g), :] = advance(k, value, lambda: then[rows(g), :], total + source)

        for g in range(8):
            out_ref[d, n, rows(g), :] = state[rows(g), pl.ds(0, 256)]


def base_row(g):
    return g if g < 10 else 28 + g


def spec(count):
    return [pl.BlockSpec(memory_space=pltpu.VMEM)] * count


def call(kernel, name, outs, ins, scratch=(), limit=24):
    return pl.pallas_call(
        kernel,
        out_shape=outs,
        in_specs=ins,
        out_specs=spec(len(outs)),
        scratch_shapes=list(scratch),
        compiler_params=pltpu.CompilerParams(vmem_limit_bytes=limit * 1024 * 1024),
        name=name,
        cost_estimate=HINTS.get(name),
    )


LONG = pl.CostEstimate(flops=10**9, bytes_accessed=10**7, transcendentals=0)
NONE = pl.CostEstimate(flops=0, bytes_accessed=0, transcendentals=0)
HINTS = {"spread_cells": NONE, "pack_early": NONE, "place_vias": LONG, "pack_relay": LONG, "pack_base": LONG}


def arr(*shape, dtype=F32):
    return jax.ShapeDtypeStruct(shape, dtype)


def swaps(count, offset):
    partner = list(range(count))
    for i in range(offset, count - 1, 2):
        partner[i], partner[i + 1] = i + 1, i
    return list(enumerate(partner))


def per_device(
    sheet_res, capacity, drop_start, load_cell, load_current, via_cell, via_current, base_sheet, base_start, bump_cell
):
    row_count = lax.axis_size("row")
    col_count = lax.axis_size("col")
    others = [(0, 1), (1, 0)]

    def buffer(count):
        return arr(8 * count, 128)

    packed, send, total = call(pack_kernel, "pack_vias", (arr(2, VIAS, 8, 128), arr(VIAS, 8, 128), buffer(1)), spec(1))(via_current)
    other = lax.ppermute(total, "die", others)
    got = lax.ppermute(send, "die", others)
    base = call(base_kernel, "pack_base", (buffer(BASE),), spec(5))(bump_cell, base_sheet, base_start, total, other)[0]
    first = lax.ppermute(base, "row", swaps(row_count, 0))
    early, between = call(chip_kernel, "pack_early", (buffer(EARLY), buffer(EARLY + 2 * BASE)), spec(5))(
        base, first, sheet_res, capacity, drop_start
    )
    between = lax.ppermute(between, "row", swaps(row_count, 1))
    early = lax.ppermute(early, "row", swaps(row_count, 0))
    cells, load_cells, loads, spread, counts = call(
        prepare_kernel, "spread_cells",
        (arr(4, VIAS, 8, 128), arr(4, 8, 128), arr(4, 4, 8, 128), arr(256, 1024, dtype=jnp.bfloat16), arr(4, 64, 128)),
        spec(3),
    )(via_cell, load_cell, load_current)

    field, even, odd = call(
        place_kernel, "place_vias", (arr(4, 4, 64, 128), buffer(LATE), buffer(LATE)),
        spec(7), [pltpu.VMEM((4, 4, VIAS, 8, 128), F32)],
    )(packed, got, cells, load_cells, loads, spread, counts)

    late = lax.ppermute(odd, "row", swaps(row_count, 1))
    within = lax.ppermute(even, "row", swaps(row_count, 0))
    relay = call(relay_kernel, "pack_relay", (buffer(BASE),), spec(1))(between)[0]
    relayed = lax.ppermute(relay, "row", swaps(row_count, 0))

    even, odd, wide = call(
        strip_kernel, "column_strips", (buffer(COL_GROUPS), buffer(COL_GROUPS), arr(200, 128)), spec(12)
    )(sheet_res, capacity, drop_start, counts, field, base, first, early, between, within, late, relayed)
    even = lax.ppermute(even, "col", swaps(col_count, 0))
    odd = lax.ppermute(odd, "col", swaps(col_count, 1))

    image, pair = arr(4, 96, 256), arr(2, 96, 256)
    parts = call(
        assemble_kernel, "assemble",
        (image, image, pair, pair) + (image,) * 7 + (arr(2, 256, 384, dtype=jnp.bfloat16),), spec(9),
    )(sheet_res, capacity, drop_start, counts, field, early, between, within, late)

    ext = pltpu.VMEM((96, 384), F32)
    scratch = [ext, ext, pltpu.VMEM((2, 96, 384), F32), pltpu.VMEM((4, 40, 384), F32)] + [ext] * 8
    return call(solve_kernel, "solve", (arr(2, 2, 64, 256), arr(2, 8, 32)), spec(15), scratch)(
        *parts, wide, even, odd
    )


def solution(mesh):
    in_specs = (
        P("die", None, "row", "col"),
        P("die", "row", "col"),
        P("die", None, "row", "col"),
        P("die", "row", "col"),
        P(None, "die", None, "row", "col"),
        P("die", None, "row", "col"),
        P(None, "die", None, None, "row", "col"),
        P(None, "row", "col"),
        P(None, "row", "col"),
        P("row", "col"),
    )
    out_specs = (P("die", None, "row", "col"), P(None, "row", "col"))
    return jax.shard_map(
        per_device, mesh=mesh, in_specs=in_specs, out_specs=out_specs, check_vma=False
    )
```

```python
import jax
import jax.numpy as jnp
from jax import lax
from jax.experimental import pallas as pl
from jax.experimental.pallas import tpu as pltpu
from jax.sharding import PartitionSpec as P

SWEEPS = 6
STEPS = 2
VIAS = 32

VIA_CONDUCT = 1.0
VIA_RESIST = 4.0
BUMP_CONDUCT = 50.0
BASE_CAPACITY = 0.1
LOWER_BOUND = 0.1
UPPER_BOUND = 1.9

MIDDLE = 0.5 * (UPPER_BOUND + LOWER_BOUND)
HALF = 0.5 * (UPPER_BOUND - LOWER_BOUND)

GROUPS = 12
F32 = jnp.float32


def sweep_weights():
    scaled = MIDDLE / HALF
    ratio = 1.0 / scaled
    pairs = []
    for _ in range(SWEEPS - 1):
        following = 1.0 / (2.0 * scaled - ratio)
        pairs.append((following * ratio, 2.0 * following / HALF))
        ratio = following
    return pairs


WEIGHTS = sweep_weights()


def lane_iota():
    return lax.broadcasted_iota(jnp.int32, (8, 128), 1)


def sub_iota(width=128):
    return lax.broadcasted_iota(jnp.int32, (8, width), 0)


def roll(x, shift, axis):
    shift = shift % x.shape[axis]
    return pltpu.roll(x, shift, axis) if shift else x


def rows(g):
    return pl.ds(8 * g, 8)


def pack_kernel(via_ref, packed_ref, send_ref):
    later = lax.axis_index("die").astype(F32)
    total = jnp.zeros((8, 128), F32)
    for v in range(VIAS):
        parts = []
        for d in range(2):
            part = jnp.concatenate([via_ref[t, d, n, v] for t in range(2) for n in range(2)], axis=1)
            packed_ref[d, v] = part
            parts.append(part)
        both = parts[0] + parts[1]
        send_ref[v] = both + later * parts[0]
        total = total + both
    send_ref[VIAS] = total


def spread_nets(ref):
    gap = jnp.zeros((8, 16), F32)
    return jnp.concatenate([gap, ref[0], gap, gap, ref[1], gap], axis=1)


def shared(first, second, shift):
    return jnp.where(sub_iota() < shift, first, roll(second, shift, 0))


def shared_low(first, second, shift):
    return jnp.where(sub_iota() >= shift, first, roll(second, shift, 0))


class RowSender:
    def __init__(self, even, even_ref, odd_ref):
        self.even, self.even_ref, self.odd_ref, self.place = even, even_ref, odd_ref, 0

    def put(self, up, down):
        self.even_ref[rows(self.place), :] = jnp.where(self.even, down, up)
        self.odd_ref[rows(self.place), :] = jnp.where(self.even, up, down)
        self.place += 1

    def pair(self, first, second):
        self.put(first(0), first(7))
        self.put(second(0), second(7))
        self.put(shared(first(1), second(1), 4), shared_low(first(6), second(6), 4))


BASE = 4
EARLY = 30
LATE = 22


def base_kernel(bump_ref, sheet_ref, start_ref, send_ref, base_ref):
    lane, sub = lane_iota(), sub_iota()
    bump = jnp.zeros((8, 128), F32)
    column = lane % 64 - 16
    for k in range(4):
        bump = jnp.where((column // 8 == k) & (sub * 8 + column % 8 == bump_ref[0:1, k : k + 1]), 1.0, bump)
    for part, value in enumerate([spread_nets(sheet_ref), spread_nets(start_ref), bump, send_ref[VIAS]]):
        base_ref[rows(part), :] = value


def chip_kernel(base_ref, got_ref, sheet_ref, cap_ref, drop_ref, within_ref, between_ref):
    even = lax.axis_index("row") % 2 == 0
    sender = RowSender(even, within_ref, between_ref)
    for d in range(2):
        for half in range(2):
            lanes = pl.ds(half * 128, 128)
            for n in range(2):
                sender.pair(lambda g: sheet_ref[d, n, rows(g), lanes], lambda g: drop_ref[d, n, rows(g), lanes])
        sender.pair(lambda g: cap_ref[d, rows(g), pl.ds(0, 128)], lambda g: cap_ref[d, rows(g), pl.ds(128, 128)])
    for part in range(BASE):
        own, got = base_ref[rows(part), :], got_ref[rows(part), :]
        for slot, value in enumerate([jnp.where(even, own, got), jnp.where(even, got, own)]):
            between_ref[rows(EARLY + BASE * slot + part), :] = value


def relay_kernel(between_ref, relay_ref):
    even = lax.axis_index("row") % 2 == 0
    for part in range(BASE):
        a, b = between_ref[rows(EARLY + part), :], between_ref[rows(EARLY + BASE + part), :]
        relay_ref[rows(part), :] = jnp.where(even, b, a)


def shares_kernel(first_ref, between_ref, relayed_ref, shares_ref):
    shares_ref[rows(0), :] = first_ref[rows(3), :]
    for slot in range(2):
        shares_ref[rows(1 + slot), :] = between_ref[rows(EARLY + BASE * slot + 3), :]
    shares_ref[rows(3), :] = relayed_ref[rows(3), :]


def spread_matrix(height, width):
    row = lax.broadcasted_iota(jnp.int32, (height, width), 0) % 128
    column = lax.broadcasted_iota(jnp.int32, (height, width), 1)
    return jnp.where(row == column // 8, 1.0, 0.0).astype(jnp.bfloat16)


def halves(value):
    high = value.astype(jnp.bfloat16)
    low = (value - high.astype(F32)).astype(jnp.bfloat16)
    return jnp.concatenate([high, low], axis=1)


def prepare_kernel(cell_ref, load_cell_ref, load_ref, cells_ref, load_cells_ref, loads_ref, spread_ref, counts_ref):
    within = (lane_iota() % 8).astype(F32)
    spread = spread_matrix(32, 256)
    for d in range(2):
        cells = cell_ref[d].reshape(8 * VIAS, 32).astype(F32).astype(jnp.bfloat16)
        wide = jnp.dot(cells, spread, preferred_element_type=F32)
        load_cell = load_cell_ref[d].astype(F32).astype(jnp.bfloat16)
        load_cell = jnp.dot(load_cell, spread, preferred_element_type=F32)
        for half in range(2):
            lanes = slice(128 * half, 128 * half + 128)
            for v in range(VIAS):
                cells_ref[2 * d + half, v] = wide[8 * v : 8 * v + 8, lanes] - within
            load_cells_ref[2 * d + half] = load_cell[:, lanes] - within
    spread_ref[...] = spread_matrix(256, 1024)
    loads = jnp.concatenate([load_ref[t, d, n] for d in range(2) for t in range(2) for n in range(2)], axis=0)
    high = loads.astype(jnp.bfloat16)
    low = (loads - high.astype(F32)).astype(jnp.bfloat16)
    wide = jnp.dot(high, spread, preferred_element_type=F32) + jnp.dot(low, spread, preferred_element_type=F32)
    for d in range(2):
        for half in range(2):
            for m in range(4):
                loads_ref[2 * d + half, m] = wide[32 * d + 8 * m : 32 * d + 8 * m + 8, 128 * half : 128 * half + 128]

    def count(i, carry):
        state = [jnp.zeros((8, 128), F32) for _ in range(8)]
        for v in range(VIAS):
            cell = cells_ref[i, v]
            for oi in range(8):
                state[oi] = state[oi] + jnp.where(cell == 8.0 * oi, 1.0, 0.0)
        for oi in range(8):
            counts_ref[i, pl.ds(oi, 8, stride=8), :] = state[oi]
        return carry

    lax.fori_loop(0, 4, count, 0)


def place_kernel(
    packed_ref, send_ref, got_ref, cells_ref, load_cells_ref, loads_ref, spread_ref, counts_ref, early_ref,
    field_ref, even_ref, odd_ref, arriving_ref, values_ref,
):
    lane = lane_iota()
    later = lax.axis_index("die").astype(F32)
    even = lax.axis_index("row") % 2 == 0
    weights = (
        (VIA_RESIST * (4.0 - 2.0 * later), VIA_RESIST * (3.0 - 2.0 * later), VIA_RESIST * (1.0 + later)),
        (VIA_RESIST * (3.0 - 2.0 * later), VIA_RESIST * (3.0 - 2.0 * later), VIA_RESIST),
    )
    size = (8 * VIAS, 128)
    first, second, got = packed_ref[0].reshape(size), packed_ref[1].reshape(size), got_ref[0:VIAS].reshape(size)
    for d in range(2):
        mixed = weights[d][0] * first + weights[d][1] * second + weights[d][2] * got
        wide = jnp.dot(halves(mixed), spread_ref[...], preferred_element_type=F32)
        for half in range(2):
            for m in range(4):
                start = 256 * m + 128 * half
                values_ref[2 * d + half, m] = wide[:, start : start + 128].reshape(VIAS, 8, 128)

    def add(i, carry):
        cell = load_cells_ref[i]
        loads = [loads_ref[i, m] for m in range(4)]
        state = []
        for oi in range(8):
            hit = cell == 8.0 * oi
            state.append([jnp.where(hit, load, 0.0) for load in loads])
        for v in range(VIAS):
            cell = cells_ref[i, v]
            values = [values_ref[i, m, v] for m in range(4)]
            for oi in range(8):
                hit = cell == 8.0 * oi
                state[oi] = [old + jnp.where(hit, value, 0.0) for old, value in zip(state[oi], values)]
        for oi in range(8):
            for m in range(4):
                field_ref[m, i, pl.ds(oi, 8, stride=8), :] = state[oi][m]
        return carry

    lax.fori_loop(0, 4, add, 0)

    arriving_ref[...] = send_ref[VIAS] + got_ref[VIAS]
    for g in range(EARLY):
        even_ref[rows(LATE + g), :] = early_ref[rows(g), :]
    sender = RowSender(even, even_ref, odd_ref)
    for d in range(2):
        for half in range(2):
            for n in range(2):
                one = lambda g: field_ref[n, 2 * d + half, rows(g), :]
                two = lambda g: field_ref[2 + n, 2 * d + half, rows(g), :]
                sender.put(one(0), one(7))
                sender.put(shared(one(1), two(0), 3), shared_low(one(6), two(7), 5))
        sender.pair(lambda g: counts_ref[2 * d, rows(g), :], lambda g: counts_ref[2 * d + 1, rows(g), :])


SHEET, DROP, CAPACITY, COUNTS, FIRST, SECOND = range(6)


def near_rows(read, kind, d, half, n, upper):
    early, late = read
    if kind in (FIRST, SECOND):
        start = 11 * d + 4 * half + 2 * n
        if kind == SECOND:
            return roll(late(start + 1), -5 if upper else -3, 0), None
        return late(start), late(start + 1)
    if kind in (SHEET, DROP):
        take, start, second = early, 15 * d + 6 * half + 3 * n, kind == DROP
    elif kind == CAPACITY:
        take, start, second = early, 15 * d + 12, half == 1
    else:
        take, start, second = late, 11 * d + 8, half == 1
    last = take(start + 2)
    return (take(start + 1), roll(last, -4, 0)) if second else (take(start), last)


def column_groups(own, below, above, kind, d, half, n):
    low = near_rows(below, kind, d, half, n, False)
    high = near_rows(above, kind, d, half, n, True)
    return [own(g) for g in range(8)] + [low[0], low[1], high[1], high[0]]


def readers(even, below, above, within_ref, between_ref, late_ref):
    def make(inside, near, skip, far_ref):
        def read(g):
            value = jnp.where(near, within_ref[rows(skip + g), :], far_ref[rows(g), :])
            return value if inside is None else jnp.where(inside, value, 0.0)
        return read

    odd = jnp.logical_not(even)
    return tuple(
        (make(inside, near, LATE, between_ref), make(inside, near, 0, late_ref)) for inside, near in ((below, even), (above, odd))
    )


COL_GROUPS = 2 * GROUPS + 10


def strip_kernel(
    sheet_ref, cap_ref, drop_ref, counts_ref, field_ref, base_ref, arriving_ref, first_ref, between_ref,
    within_ref, late_ref, relayed_ref, shares_ref, even_ref, odd_ref, wide_ref,
):
    lane = lane_iota()
    within = lane % 16
    row, last = lax.axis_index("row"), (lax.axis_size("row") - 1)
    even = row % 2 == 0
    below, above = readers(even, None, None, within_ref, between_ref, late_ref)
    even_col = lax.axis_index("col") % 2 == 0

    own = (lane % 64 >= 16) & (lane % 64 < 48)

    def spread_steps(value):
        out = []
        for t in range(2):
            moved = jnp.where(lane < 64, roll(value, 16 - 64 * t, 1), roll(value, 48 - 64 * t, 1))
            out.append(jnp.where(own, moved, 0.0))
        return out

    def block(ref, start, share):
        parts = [ref[rows(start + f), :] for f in range(BASE)]
        parts[3] = parts[3] + shares_ref[rows(share), :]
        return parts

    def choose(a, b, inside):
        return [jnp.where(inside, jnp.where(even, x, y), 0.0) for x, y in zip(a, b)]

    partner = block(first_ref, 0, 0)
    between = [block(between_ref, EARLY + BASE * slot, 1 + slot) for slot in range(2)]
    relayed = block(relayed_ref, 0, 3)
    groups = []
    for g, parts in enumerate([
        [base_ref[rows(f), :] for f in range(3)] + [arriving_ref[...]],
        choose(partner, between[0], row < last),
        choose(relayed, between[1], row + 2 <= last),
        choose(between[0], relayed, row >= 2),
        choose(between[1], partner, row > 0),
    ]):
        one, two = spread_steps(parts[3])
        groups.append([parts[0], parts[1], one, two, parts[2]])
        for f in range(5):
            wide_ref[rows(5 * f + g), :] = groups[g][f]

    def fields(part, half):
        lanes = pl.ds(half * 128, 128)
        images = [(d, n) for d in range(2) for n in range(2)]
        if part == 0:
            return [
                column_groups(lambda g: ref[d, n, rows(g), lanes], below, above, kind, d, half, n)
                for kind, ref in ((SHEET, sheet_ref), (DROP, drop_ref)) for d, n in images
            ]
        out = [column_groups(lambda g: cap_ref[d, rows(g), lanes], below, above, CAPACITY, d, half, 0) for d in range(2)]
        out += [
            column_groups(lambda g: counts_ref[2 * d + half, rows(g), :], below, above, COUNTS, d, half, 0)
            for d in range(2)
        ]
        for d, n in images:
            one = column_groups(lambda g: field_ref[n, 2 * d + half, rows(g), :], below, above, FIRST, d, half, n)
            two = column_groups(lambda g: field_ref[2 + n, 2 * d + half, rows(g), :], below, above, SECOND, d, half, n)
            merged = []
            for a, b in zip(one, two):
                if b is None:
                    merged.append(a)
                elif half == 0:
                    merged.append(jnp.where(within < 11, a, roll(b, 11, 1)))
                else:
                    merged.append(jnp.where(within >= 5, a, roll(b, -11, 1)))
            out.append(merged)
        return out

    def put(index, left, right):
        even_ref[rows(index), :] = jnp.where(even_col, right, left)
        odd_ref[rows(index), :] = jnp.where(even_col, left, right)

    for part in range(2):
        sides = [fields(part, half) for half in range(2)]
        for g in range(GROUPS):
            out = []
            for half, chunks in enumerate(sides):
                value = chunks[0][g]
                for k in range(1, 8):
                    value = jnp.where((lane // 16 + half) % 8 == k, roll(chunks[k][g], 16 * k, 1), value)
                out.append(value)
            put(part * GROUPS + g, *out)

    start = 2 * GROUPS
    quarter = (lane % 64) // 16
    for g in range(5):
        sheet, drop, one, two, bump = groups[g]
        left = jnp.where(
            quarter == 1, sheet,
            jnp.where(quarter == 2, roll(drop, 16, 1), jnp.where(quarter == 3, roll(one, 32, 1), roll(two, -16, 1))),
        )
        right = jnp.where(
            quarter == 2, sheet,
            jnp.where(quarter == 3, roll(drop, 16, 1), jnp.where(quarter == 1, roll(two, -16, 1), roll(one, -32, 1))),
        )
        put(start + g, left, right)
        put(start + 5 + g, bump, bump)


def assemble_kernel(
    sheet_ref, cap_ref, drop_ref, counts_ref, field_ref, within_ref, between_ref, late_ref,
    s_ref, x_ref, c_ref, k_ref, one_ref, two_ref, up_ref, down_ref, left_ref, right_ref, diag_ref, spread_ref,
):
    row, last = lax.axis_index("row"), (lax.axis_size("row") - 1)
    sub, lane = sub_iota(256), lax.broadcasted_iota(jnp.int32, (8, 256), 1)
    below, above = readers(row % 2 == 0, row < last, row > 0, within_ref, between_ref, late_ref)

    def both(own, kind, d, n):
        sides = [column_groups(lambda g: own(half, g), below, above, kind, d, half, n) for half in range(2)]
        return [None if a is None else jnp.concatenate([a, b], axis=1) for a, b in zip(*sides)]

    for d in range(2):
        caps = both(lambda half, g: cap_ref[d, rows(g), pl.ds(half * 128, 128)], CAPACITY, d, 0)
        counts = both(lambda half, g: counts_ref[2 * d + half, rows(g), :], COUNTS, d, 0)
        for g in range(GROUPS):
            c_ref[d, rows(g), :] = caps[g]
            k_ref[d, rows(g), :] = counts[g]
        for n in range(2):
            i = 2 * d + n
            sheets = both(lambda half, g: sheet_ref[d, n, rows(g), pl.ds(half * 128, 128)], SHEET, d, n)
            drops = both(lambda half, g: drop_ref[d, n, rows(g), pl.ds(half * 128, 128)], DROP, d, n)
            ones = both(lambda half, g: field_ref[n, 2 * d + half, rows(g), :], FIRST, d, n)
            twos = both(lambda half, g: field_ref[2 + n, 2 * d + half, rows(g), :], SECOND, d, n)
            for g in range(GROUPS):
                s_ref[i, rows(g), :] = sheets[g]
                x_ref[i, rows(g), :] = drops[g]
                one_ref[i, rows(g), :] = c_ref[d, rows(g), :] * drops[g] + ones[g]
                if twos[g] is not None:
                    two_ref[i, rows(g), :] = twos[g]
            for g in range(GROUPS):
                here, after = s_ref[i, rows(g), :], s_ref[i, rows((g + 1) % GROUPS), :]
                under = jnp.where(sub == 7, roll(after, -1, 0), roll(here, -1, 0))
                inside = here > 0.0
                down_ref[i, rows(g), :] = jnp.where(inside, connect(here, under), 0.0)
                right = jnp.where(inside & (lane < 255), connect(here, roll(here, -1, 1)), 0.0)
                right_ref[i, rows(g), :] = right
                left_ref[i, rows(g), :] = roll(right, 1, 1)
            for g in range(GROUPS):
                here, before = down_ref[i, rows(g), :], down_ref[i, rows((g - 1) % GROUPS), :]
                up = jnp.where(sub == 0, roll(before, 1, 0), roll(here, 1, 0))
                up_ref[i, rows(g), :] = up
                diag = c_ref[d, rows(g), :] + up + here + left_ref[i, rows(g), :] + right_ref[i, rows(g), :]
                diag_ref[i, rows(g), :] = diag + VIA_CONDUCT * k_ref[d, rows(g), :]
    source = lax.broadcasted_iota(jnp.int32, (256, 384), 0) % 128
    column = lax.broadcasted_iota(jnp.int32, (256, 384), 1)
    column = jnp.where(column < 256, 16 + column // 8, jnp.where(column < 320, 48, 0) + (column - 256) // 8)
    for n in range(2):
        spread_ref[n] = jnp.where(source == column + 64 * n, 1.0, 0.0).astype(jnp.bfloat16)


def connect(center, neighbour):
    return jnp.where(neighbour > 0.0, 2.0 / (center + neighbour), 0.0)


def three_terms(k):
    if k == 0:
        return 1.0 - 1.0 / MIDDLE, 0.0, 1.0 / MIDDLE
    a, b = WEIGHTS[k - 1]
    return 1.0 + a - b, -a, b


def advance(k, value, previous, total):
    fore, back, gain = three_terms(k)
    out = total if gain == 1.0 else gain * total
    if fore != 0.0:
        out = out + fore * value
    return out + back * previous() if k else out


def base_solve(fields):
    sheet, state, arriving, bump = fields
    steps = [(1, 0), (-1, 0), (1, 1), (-1, 1)]
    inside = sheet > 0.0
    links = [jnp.where(inside, connect(sheet, roll(sheet, s, a)), 0.0) for s, a in steps]
    diagonal = BASE_CAPACITY + links[0] + links[1] + links[2] + links[3] + BUMP_CONDUCT * bump
    inverse = 1.0 / diagonal
    links = [inverse * link for link in links]
    results = []
    for t in range(STEPS):
        source = inverse * (BASE_CAPACITY * state + arriving[t])
        previous = None
        for k in range(SWEEPS):
            total = (links[0] * roll(state, 1, 0) + links[1] * roll(state, -1, 0)) + (
                links[2] * roll(state, 1, 1) + links[3] * roll(state, -1, 1)
            ) + source
            state, previous = advance(k, state, lambda: previous, total), state
        results.append(state)
    return results


def needed(halo):
    if halo > 8:
        return list(range(GROUPS))
    return list(range(8)) + ([8, 11] if halo > 0 else [])


def solve_kernel(
    s_ref, x_ref, c_ref, k_ref, one_ref, two_ref, up_ref, down_ref, left_ref, right_ref, diag_ref, spread_ref,
    wide_ref, even_ref, odd_ref, out_ref, base_out_ref,
    c_ext, k_ext, f_ext, bound, link_up, link_down, link_left, link_right, inv_ext, src, state, alt,
):
    lane = lane_iota()
    row, col = lax.axis_index("row"), lax.axis_index("col")
    has_left, has_right = col > 0, col < (lax.axis_size("col") - 1)
    even_col = col % 2 == 0

    def from_left(g):
        return jnp.where(even_col, odd_ref[rows(g), :], even_ref[rows(g), :])

    def from_right(g):
        return jnp.where(even_col, even_ref[rows(g), :], odd_ref[rows(g), :])

    start = 2 * GROUPS
    quarter = (lane % 64) // 16
    take_left, take_right = (quarter == 0) & has_left, (quarter == 3) & has_right
    fields = []
    for field in range(5):
        out = []
        for g in range(5):
            right_shift = (32, 16, 0, 48, 32)[field]
            left_shift = (-32, -48, 0, -16, -32)[field]
            group = g + 5 * (field == 4)
            value = jnp.where(take_right, roll(from_right(start + group), right_shift, 1), wide_ref[rows(5 * field + g), :])
            out.append(jnp.where(take_left, roll(from_left(start + group), left_shift, 1), value))
        fields.append(jnp.concatenate(out, axis=0))
    solved = base_solve((fields[0], fields[1], (fields[2], fields[3]), fields[4]))
    for t in range(STEPS):
        pieces = halves(solved[t])
        for n in range(2):
            bound[2 * t + n] = jnp.dot(pieces, spread_ref[n], preferred_element_type=F32)
    for n in range(2):
        base_out_ref[n] = roll(solved[1][0:8], -(64 * n + 16), 1)[:, 0:32]

    def third(part, chunk, g):
        right_ok, left_ok = has_right, has_left
        if g in (8, 9):
            right_ok, left_ok = right_ok & (row < (lax.axis_size("row") - 1)), left_ok & (row < (lax.axis_size("row") - 1))
        if g in (10, 11):
            right_ok, left_ok = right_ok & (row > 0), left_ok & (row > 0)
        right = jnp.where((lane // 16 == chunk) & right_ok, from_right(part * GROUPS + g), 0.0)
        value = jnp.where((lane // 16 == (chunk + 7) % 8) & left_ok, from_left(part * GROUPS + g), right)
        return roll(value, -16 * chunk, 1)

    sub, sub3 = sub_iota(), sub_iota(384)

    def above(value, before, index):
        return jnp.where(index == 0, roll(before, 1, 0), roll(value, 1, 0))

    def below(value, after, index):
        return jnp.where(index == 7, roll(after, -1, 0), roll(value, -1, 0))

    for i in range(4):
        d, n = i // 2, i % 2

        def wide(ref, g, extra, index=i):
            return jnp.concatenate([ref[index, rows(g), :], extra], axis=1)

        if n == 0:
            for g in range(GROUPS):
                c_ext[rows(g), :] = wide(c_ref, g, third(1, d, g), d)
                k_ext[rows(g), :] = wide(k_ref, g, third(1, 2 + d, g), d)
        @pl.when(row >= 0)
        def _():
            sheets = [third(0, i, g) for g in range(GROUPS)]
            for g in range(GROUPS):
                here = sheets[g]
                inside = here > 0.0
                low, high = s_ref[i, rows(g), pl.ds(0, 128)], s_ref[i, rows(g), pl.ds(128, 128)]
                after = roll(jnp.where(lane == 0, low, here), -1, 1)
                before = roll(jnp.where(lane == 127, high, here), 1, 1)
                right = jnp.where(inside, connect(here, after), 0.0)
                left = jnp.where(inside, connect(here, before), 0.0)
                down = jnp.where(inside, connect(here, below(here, sheets[(g + 1) % GROUPS], sub)), 0.0)
                up = jnp.where(inside, connect(here, above(here, sheets[(g - 1) % GROUPS], sub)), 0.0)
                first = jnp.where(lane == 0, roll(right, 1, 1), 0.0)
                final = jnp.where(lane == 127, roll(left, -1, 1), 0.0)
                diag = wide(diag_ref, g, 0.0 * here) + jnp.concatenate(
                    [first, final, c_ext[rows(g), pl.ds(256, 128)] + up + down + left + right
                     + VIA_CONDUCT * k_ext[rows(g), pl.ds(256, 128)]], axis=1)
                inverse = jnp.where(diag > 0.0, 1.0 / diag, 0.0)
                inv_ext[rows(g), :] = inverse
                zero = jnp.zeros_like(first)
                link_up[rows(g), :] = inverse * wide(up_ref, g, up)
                link_down[rows(g), :] = inverse * wide(down_ref, g, down)
                link_left[rows(g), :] = inverse * (wide(left_ref, g, left) + jnp.concatenate([first, zero, zero], axis=1))
                link_right[rows(g), :] = inverse * (wide(right_ref, g, right) + jnp.concatenate([zero, final, zero], axis=1))
                drop = third(0, 4 + i, g)
                state[rows(g), :] = wide(x_ref, g, drop)
                one = third(1, 4 + i, g)
                f_ext[0, rows(g), :] = wide(one_ref, g, c_ext[rows(g), pl.ds(256, 128)] * drop + one)
                if g not in (9, 10):
                    two = jnp.where(lane < 64, roll(one, -11, 1), roll(one, 11, 1))
                    f_ext[1, rows(g), :] = wide(two_ref, g, two)

        @pl.when(row >= 0)
        def _():
            for t in range(STEPS):
                for k in range(SWEEPS):
                    now, then = (alt, state) if k % 2 else (state, alt)
                    for g in needed(11 - 6 * t - k):
                        value = now[rows(g), :]
                        total = link_up[rows(g), :] * above(value, now[rows((g - 1) % GROUPS), :], sub3)
                        total = total + link_down[rows(g), :] * below(value, now[rows((g + 1) % GROUPS), :], sub3)
                        total = total + (
                            link_left[rows(g), :] * roll(value, 1, 1) + link_right[rows(g), :] * roll(value, -1, 1))
                        if k == 0:
                            spread = jnp.broadcast_to(bound[2 * t + n, pl.ds(base_row(g), 1), :], (8, 384))
                            source = f_ext[t, rows(g), :] + k_ext[rows(g), :] * spread
                            if t:
                                source = source + c_ext[rows(g), :] * value
                            source = inv_ext[rows(g), :] * source
                            src[rows(g), :] = source
                        else:
                            source = src[rows(g), :]
                        then[rows(g), :] = advance(k, value, lambda: then[rows(g), :], total + source)

        for g in range(8):
            out_ref[d, n, rows(g), :] = state[rows(g), pl.ds(0, 256)]


def base_row(g):
    return g if g < 10 else 28 + g


def spec(count):
    return [pl.BlockSpec(memory_space=pltpu.VMEM)] * count


def call(kernel, name, outs, ins, scratch=(), limit=24):
    return pl.pallas_call(
        kernel,
        out_shape=outs,
        in_specs=ins,
        out_specs=spec(len(outs)),
        scratch_shapes=list(scratch),
        compiler_params=pltpu.CompilerParams(vmem_limit_bytes=limit * 1024 * 1024),
        name=name,
        cost_estimate=HINTS.get(name),
    )


LONG = pl.CostEstimate(flops=10**9, bytes_accessed=10**7, transcendentals=0)
NONE = pl.CostEstimate(flops=0, bytes_accessed=0, transcendentals=0)
HINTS = {"spread_cells": NONE, "pack_early": NONE, "place_vias": LONG, "pack_relay": LONG}


def arr(*shape, dtype=F32):
    return jax.ShapeDtypeStruct(shape, dtype)


def swaps(count, offset):
    pairs = []
    for i in range(offset, count, 2):
        j = (i + 1) % count
        pairs += [(i, j), (j, i)]
    return pairs


def per_device(
    sheet_res, capacity, drop_start, load_cell, load_current, via_cell, via_current, base_sheet, base_start, bump_cell
):
    row_count = lax.axis_size("row")
    col_count = lax.axis_size("col")
    others = [(0, 1), (1, 0)]

    packed, send = call(pack_kernel, "pack_vias", (arr(2, VIAS, 8, 128), arr(VIAS + 1, 8, 128)), spec(1))(via_current)
    got = lax.ppermute(send, "die", others)
    def buffer(count):
        return arr(8 * count, 128)

    base = call(base_kernel, "pack_base", (buffer(BASE),), spec(4))(bump_cell, base_sheet, base_start, send)[0]
    first = lax.ppermute(base, "row", swaps(row_count, 0))
    early, between = call(chip_kernel, "pack_early", (buffer(EARLY), buffer(EARLY + 2 * BASE)), spec(5))(
        base, first, sheet_res, capacity, drop_start
    )
    between = lax.ppermute(between, "row", swaps(row_count, 1))
    cells, load_cells, loads, spread, counts = call(
        prepare_kernel, "spread_cells",
        (arr(4, VIAS, 8, 128), arr(4, 8, 128), arr(4, 4, 8, 128), arr(256, 1024, dtype=jnp.bfloat16), arr(4, 64, 128)),
        spec(3),
    )(via_cell, load_cell, load_current)

    field, even, odd, arriving = call(
        place_kernel, "place_vias", (arr(4, 4, 64, 128), buffer(LATE + EARLY), buffer(LATE), buffer(1)),
        spec(9), [pltpu.VMEM((4, 4, VIAS, 8, 128), F32)],
    )(packed, send, got, cells, load_cells, loads, spread, counts, early)

    late = lax.ppermute(odd, "row", swaps(row_count, 1))
    within = lax.ppermute(even, "row", swaps(row_count, 0))
    relay = call(relay_kernel, "pack_relay", (buffer(BASE),), spec(1))(between)[0]
    relayed = lax.ppermute(relay, "row", swaps(row_count, 0))
    shares = call(shares_kernel, "pack_shares", (buffer(4),), spec(3))(first, between, relayed)[0]
    shares = lax.ppermute(shares, "die", others)

    even, odd, wide = call(
        strip_kernel, "column_strips", (buffer(COL_GROUPS), buffer(COL_GROUPS), arr(200, 128)), spec(13)
    )(sheet_res, capacity, drop_start, counts, field, base, arriving, first, between, within, late, relayed, shares)
    even = lax.ppermute(even, "col", swaps(col_count, 0))
    odd = lax.ppermute(odd, "col", swaps(col_count, 1))

    image, pair = arr(4, 96, 256), arr(2, 96, 256)
    parts = call(
        assemble_kernel, "assemble",
        (image, image, pair, pair) + (image,) * 7 + (arr(2, 256, 384, dtype=jnp.bfloat16),), spec(8),
    )(sheet_res, capacity, drop_start, counts, field, within, between, late)

    ext = pltpu.VMEM((96, 384), F32)
    scratch = [ext, ext, pltpu.VMEM((2, 96, 384), F32), pltpu.VMEM((4, 40, 384), F32)] + [ext] * 8
    return call(solve_kernel, "solve", (arr(2, 2, 64, 256), arr(2, 8, 32)), spec(15), scratch)(
        *parts, wide, even, odd
    )


def solution(mesh):
    in_specs = (
        P("die", None, "row", "col"),
        P("die", "row", "col"),
        P("die", None, "row", "col"),
        P("die", "row", "col"),
        P(None, "die", None, "row", "col"),
        P("die", None, "row", "col"),
        P(None, "die", None, None, "row", "col"),
        P(None, "row", "col"),
        P(None, "row", "col"),
        P("row", "col"),
    )
    out_specs = (P("die", None, "row", "col"), P(None, "row", "col"))
    return jax.shard_map(
        per_device, mesh=mesh, in_specs=in_specs, out_specs=out_specs, check_vma=False
    )
```

```python
import jax
import jax.numpy as jnp
from jax import lax
from jax.experimental import pallas as pl
from jax.experimental.pallas import tpu as pltpu
from jax.sharding import PartitionSpec as P

SWEEPS = 6
STEPS = 2
VIAS = 32

VIA_CONDUCT = 1.0
VIA_RESIST = 4.0
BUMP_CONDUCT = 50.0
BASE_CAPACITY = 0.1
LOWER_BOUND = 0.1
UPPER_BOUND = 1.9

MIDDLE = 0.5 * (UPPER_BOUND + LOWER_BOUND)
HALF = 0.5 * (UPPER_BOUND - LOWER_BOUND)

GROUPS = 11
F32 = jnp.float32


def sweep_weights():
    scaled = MIDDLE / HALF
    ratio = 1.0 / scaled
    pairs = []
    for _ in range(SWEEPS - 1):
        following = 1.0 / (2.0 * scaled - ratio)
        pairs.append((following * ratio, 2.0 * following / HALF))
        ratio = following
    return pairs


WEIGHTS = sweep_weights()


def lane_iota():
    return lax.broadcasted_iota(jnp.int32, (8, 128), 1)


def sub_iota(width=128):
    return lax.broadcasted_iota(jnp.int32, (8, width), 0)


def roll(x, shift, axis):
    shift = shift % x.shape[axis]
    return pltpu.roll(x, shift, axis) if shift else x


def rows(g):
    return pl.ds(8 * g, 8)


def pack_kernel(via_ref, packed_ref, send_ref):
    later = lax.axis_index("die").astype(F32)
    total = jnp.zeros((8, 128), F32)
    for v in range(VIAS):
        parts = []
        for d in range(2):
            part = jnp.concatenate([via_ref[t, d, n, v] for t in range(2) for n in range(2)], axis=1)
            packed_ref[d, v] = part
            parts.append(part)
        both = parts[0] + parts[1]
        send_ref[v] = both + later * parts[0]
        total = total + both
    send_ref[VIAS] = total


def spread_nets(ref):
    gap = jnp.zeros((8, 16), F32)
    return jnp.concatenate([gap, ref[0], gap, gap, ref[1], gap], axis=1)


def shared(first, second, shift):
    return jnp.where(sub_iota() < shift, first, roll(second, shift, 0))


def shared_low(first, second, shift):
    return jnp.where(sub_iota() >= shift, first, roll(second, shift, 0))


class RowSender:
    def __init__(self, even, even_ref, odd_ref):
        self.even, self.even_ref, self.odd_ref, self.place = even, even_ref, odd_ref, 0

    def put(self, up, down):
        self.even_ref[rows(self.place), :] = jnp.where(self.even, down, up)
        self.odd_ref[rows(self.place), :] = jnp.where(self.even, up, down)
        self.place += 1

    def pair(self, first, second):
        self.put(first(0), first(7))
        self.put(second(0), second(7))
        self.put(shared(first(1), second(1), 4), shared_low(first(6), second(6), 4))


BASE = 4
EARLY = 30
LATE = 22


def base_kernel(bump_ref, sheet_ref, start_ref, send_ref, base_ref):
    lane, sub = lane_iota(), sub_iota()
    bump = jnp.zeros((8, 128), F32)
    column = lane % 64 - 16
    for k in range(4):
        bump = jnp.where((column // 8 == k) & (sub * 8 + column % 8 == bump_ref[0:1, k : k + 1]), 1.0, bump)
    for part, value in enumerate([spread_nets(sheet_ref), spread_nets(start_ref), bump, send_ref[VIAS]]):
        base_ref[rows(part), :] = value


def chip_kernel(base_ref, got_ref, sheet_ref, cap_ref, drop_ref, within_ref, between_ref):
    even = lax.axis_index("row") % 2 == 0
    sender = RowSender(even, within_ref, between_ref)
    for d in range(2):
        for half in range(2):
            lanes = pl.ds(half * 128, 128)
            for n in range(2):
                sender.pair(lambda g: sheet_ref[d, n, rows(g), lanes], lambda g: drop_ref[d, n, rows(g), lanes])
        sender.pair(lambda g: cap_ref[d, rows(g), pl.ds(0, 128)], lambda g: cap_ref[d, rows(g), pl.ds(128, 128)])
    for part in range(BASE):
        own, got = base_ref[rows(part), :], got_ref[rows(part), :]
        for slot, value in enumerate([jnp.where(even, own, got), jnp.where(even, got, own)]):
            between_ref[rows(EARLY + BASE * slot + part), :] = value


def relay_kernel(between_ref, relay_ref):
    even = lax.axis_index("row") % 2 == 0
    for part in range(BASE):
        a, b = between_ref[rows(EARLY + part), :], between_ref[rows(EARLY + BASE + part), :]
        relay_ref[rows(part), :] = jnp.where(even, b, a)


def shares_kernel(first_ref, between_ref, relayed_ref, shares_ref):
    shares_ref[rows(0), :] = first_ref[rows(3), :]
    for slot in range(2):
        shares_ref[rows(1 + slot), :] = between_ref[rows(EARLY + BASE * slot + 3), :]
    shares_ref[rows(3), :] = relayed_ref[rows(3), :]


def spread_matrix(height, width):
    row = lax.broadcasted_iota(jnp.int32, (height, width), 0) % 128
    column = lax.broadcasted_iota(jnp.int32, (height, width), 1)
    return jnp.where(row == column // 8, 1.0, 0.0).astype(jnp.bfloat16)


def halves(value):
    high = value.astype(jnp.bfloat16)
    low = (value - high.astype(F32)).astype(jnp.bfloat16)
    return jnp.concatenate([high, low], axis=1)


def prepare_kernel(cell_ref, load_cell_ref, load_ref, cells_ref, load_cells_ref, loads_ref, spread_ref, counts_ref):
    within = (lane_iota() % 8).astype(F32)
    spread = spread_matrix(32, 256)
    for d in range(2):
        cells = cell_ref[d].reshape(8 * VIAS, 32).astype(F32).astype(jnp.bfloat16)
        wide = jnp.dot(cells, spread, preferred_element_type=F32)
        load_cell = load_cell_ref[d].astype(F32).astype(jnp.bfloat16)
        load_cell = jnp.dot(load_cell, spread, preferred_element_type=F32)
        for half in range(2):
            lanes = slice(128 * half, 128 * half + 128)
            for v in range(VIAS):
                cells_ref[2 * d + half, v] = wide[8 * v : 8 * v + 8, lanes] - within
            load_cells_ref[2 * d + half] = load_cell[:, lanes] - within
    spread_ref[...] = spread_matrix(256, 1024)
    loads = jnp.concatenate([load_ref[t, d, n] for d in range(2) for t in range(2) for n in range(2)], axis=0)
    high = loads.astype(jnp.bfloat16)
    low = (loads - high.astype(F32)).astype(jnp.bfloat16)
    wide = jnp.dot(high, spread, preferred_element_type=F32) + jnp.dot(low, spread, preferred_element_type=F32)
    for d in range(2):
        for half in range(2):
            for m in range(4):
                loads_ref[2 * d + half, m] = wide[32 * d + 8 * m : 32 * d + 8 * m + 8, 128 * half : 128 * half + 128]

    def count(i, carry):
        state = [jnp.zeros((8, 128), F32) for _ in range(8)]
        for v in range(VIAS):
            cell = cells_ref[i, v]
            for oi in range(8):
                state[oi] = state[oi] + jnp.where(cell == 8.0 * oi, 1.0, 0.0)
        for oi in range(8):
            counts_ref[i, pl.ds(oi, 8, stride=8), :] = state[oi]
        return carry

    lax.fori_loop(0, 4, count, 0)


def place_kernel(
    packed_ref, send_ref, got_ref, cells_ref, load_cells_ref, loads_ref, spread_ref, counts_ref, early_ref,
    field_ref, even_ref, odd_ref, arriving_ref, values_ref,
):
    lane = lane_iota()
    later = lax.axis_index("die").astype(F32)
    even = lax.axis_index("row") % 2 == 0
    weights = (
        (VIA_RESIST * (4.0 - 2.0 * later), VIA_RESIST * (3.0 - 2.0 * later), VIA_RESIST * (1.0 + later)),
        (VIA_RESIST * (3.0 - 2.0 * later), VIA_RESIST * (3.0 - 2.0 * later), VIA_RESIST),
    )
    size = (8 * VIAS, 128)
    first, second, got = packed_ref[0].reshape(size), packed_ref[1].reshape(size), got_ref[0:VIAS].reshape(size)
    for d in range(2):
        mixed = weights[d][0] * first + weights[d][1] * second + weights[d][2] * got
        wide = jnp.dot(halves(mixed), spread_ref[...], preferred_element_type=F32)
        for half in range(2):
            for m in range(4):
                start = 256 * m + 128 * half
                values_ref[2 * d + half, m] = wide[:, start : start + 128].reshape(VIAS, 8, 128)

    def add(i, carry):
        cell = load_cells_ref[i]
        loads = [loads_ref[i, m] for m in range(4)]
        state = []
        for oi in range(8):
            hit = cell == 8.0 * oi
            state.append([jnp.where(hit, load, 0.0) for load in loads])
        for v in range(VIAS):
            cell = cells_ref[i, v]
            values = [values_ref[i, m, v] for m in range(4)]
            for oi in range(8):
                hit = cell == 8.0 * oi
                state[oi] = [old + jnp.where(hit, value, 0.0) for old, value in zip(state[oi], values)]
        for oi in range(8):
            for m in range(4):
                field_ref[m, i, pl.ds(oi, 8, stride=8), :] = state[oi][m]
        return carry

    lax.fori_loop(0, 4, add, 0)

    arriving_ref[...] = send_ref[VIAS] + got_ref[VIAS]
    for g in range(EARLY):
        even_ref[rows(LATE + g), :] = early_ref[rows(g), :]
    sender = RowSender(even, even_ref, odd_ref)
    for d in range(2):
        for half in range(2):
            for n in range(2):
                one = lambda g: field_ref[n, 2 * d + half, rows(g), :]
                two = lambda g: field_ref[2 + n, 2 * d + half, rows(g), :]
                sender.put(one(0), one(7))
                sender.put(shared(one(1), two(0), 3), shared_low(one(6), two(7), 5))
        sender.pair(lambda g: counts_ref[2 * d, rows(g), :], lambda g: counts_ref[2 * d + 1, rows(g), :])


SHEET, DROP, CAPACITY, COUNTS, FIRST, SECOND = range(6)


def near_rows(read, kind, d, half, n, upper):
    early, late = read
    if kind in (FIRST, SECOND):
        start = 11 * d + 4 * half + 2 * n
        if kind == SECOND:
            return roll(late(start + 1), -5 if upper else -3, 0), None
        return late(start), late(start + 1)
    if kind in (SHEET, DROP):
        take, start, second = early, 15 * d + 6 * half + 3 * n, kind == DROP
    elif kind == CAPACITY:
        take, start, second = early, 15 * d + 12, half == 1
    else:
        take, start, second = late, 11 * d + 8, half == 1
    last = take(start + 2)
    return (take(start + 1), roll(last, -4, 0)) if second else (take(start), last)


def column_groups(own, below, above, kind, d, half, n):
    low = near_rows(below, kind, d, half, n, False)
    high = near_rows(above, kind, d, half, n, True)
    both = None if low[1] is None else jnp.where(sub_iota() < 4, low[1], high[1])
    return [own(g) for g in range(8)] + [low[0], both, high[0]]


def readers(even, below, above, within_ref, between_ref, late_ref):
    def make(inside, near, skip, far_ref):
        def read(g):
            value = jnp.where(near, within_ref[rows(skip + g), :], far_ref[rows(g), :])
            return value if inside is None else jnp.where(inside, value, 0.0)
        return read

    odd = jnp.logical_not(even)
    return tuple(
        (make(inside, near, LATE, between_ref), make(inside, near, 0, late_ref)) for inside, near in ((below, even), (above, odd))
    )


COL_GROUPS = 2 * GROUPS + 6


def strip_kernel(
    sheet_ref, cap_ref, drop_ref, counts_ref, field_ref, base_ref, arriving_ref, first_ref, between_ref,
    within_ref, late_ref, relayed_ref, shares_ref, even_ref, odd_ref, wide_ref,
):
    lane = lane_iota()
    within = lane % 16
    row, last = lax.axis_index("row"), (lax.axis_size("row") - 1)
    even = row % 2 == 0
    below, above = readers(even, None, None, within_ref, between_ref, late_ref)
    even_col = lax.axis_index("col") % 2 == 0

    own = (lane % 64 >= 16) & (lane % 64 < 48)

    def spread_steps(value):
        out = []
        for t in range(2):
            moved = jnp.where(lane < 64, roll(value, 16 - 64 * t, 1), roll(value, 48 - 64 * t, 1))
            out.append(jnp.where(own, moved, 0.0))
        return out

    def block(ref, start, share):
        parts = [ref[rows(start + f), :] for f in range(BASE)]
        parts[3] = parts[3] + shares_ref[rows(share), :]
        return parts

    def choose(a, b, inside):
        return [jnp.where(inside, jnp.where(even, x, y), 0.0) for x, y in zip(a, b)]

    partner = block(first_ref, 0, 0)
    between = [block(between_ref, EARLY + BASE * slot, 1 + slot) for slot in range(2)]
    relayed = block(relayed_ref, 0, 3)
    groups = []
    for g, parts in enumerate([
        [base_ref[rows(f), :] for f in range(3)] + [arriving_ref[...]],
        choose(partner, between[0], row < last),
        choose(relayed, between[1], row + 2 <= last),
        choose(between[0], relayed, row >= 2),
        choose(between[1], partner, row > 0),
    ]):
        one, two = spread_steps(parts[3])
        groups.append([parts[0], parts[1], one, two, parts[2]])
        for f in range(5):
            wide_ref[rows(5 * f + g), :] = groups[g][f]

    def fields(part, half):
        lanes = pl.ds(half * 128, 128)
        images = [(d, n) for d in range(2) for n in range(2)]
        if part == 0:
            return [
                column_groups(lambda g: ref[d, n, rows(g), lanes], below, above, kind, d, half, n)
                for kind, ref in ((SHEET, sheet_ref), (DROP, drop_ref)) for d, n in images
            ]
        out = [column_groups(lambda g: cap_ref[d, rows(g), lanes], below, above, CAPACITY, d, half, 0) for d in range(2)]
        out += [
            column_groups(lambda g: counts_ref[2 * d + half, rows(g), :], below, above, COUNTS, d, half, 0)
            for d in range(2)
        ]
        for d, n in images:
            one = column_groups(lambda g: field_ref[n, 2 * d + half, rows(g), :], below, above, FIRST, d, half, n)
            two = column_groups(lambda g: field_ref[2 + n, 2 * d + half, rows(g), :], below, above, SECOND, d, half, n)
            merged = []
            for a, b in zip(one, two):
                if b is None:
                    merged.append(a)
                elif half == 0:
                    merged.append(jnp.where(within < 11, a, roll(b, 11, 1)))
                else:
                    merged.append(jnp.where(within >= 5, a, roll(b, -11, 1)))
            out.append(merged)
        return out

    def put(index, left, right):
        even_ref[rows(index), :] = jnp.where(even_col, right, left)
        odd_ref[rows(index), :] = jnp.where(even_col, left, right)

    for part in range(2):
        sides = [fields(part, half) for half in range(2)]
        for g in range(GROUPS):
            out = []
            for half, chunks in enumerate(sides):
                value = chunks[0][g]
                for k in range(1, 8):
                    value = jnp.where((lane // 16 + half) % 8 == k, roll(chunks[k][g], 16 * k, 1), value)
                out.append(value)
            put(part * GROUPS + g, *out)

    start = 2 * GROUPS
    quarter = (lane % 64) // 16
    for g in range(5):
        sheet, drop, one, two, _ = groups[g]
        left = jnp.where(
            quarter == 1, sheet,
            jnp.where(quarter == 2, roll(drop, 16, 1), jnp.where(quarter == 3, roll(one, 32, 1), roll(two, -16, 1))),
        )
        right = jnp.where(
            quarter == 2, sheet,
            jnp.where(quarter == 3, roll(drop, 16, 1), jnp.where(quarter == 1, roll(two, -16, 1), roll(one, -32, 1))),
        )
        put(start + g, left, right)
    bumps = []
    for origin in (16, 32):
        value = roll(groups[0][4], -origin, 1)
        for g in range(1, 5):
            value = jnp.where(lane // 16 == g, roll(groups[g][4], 16 * g - origin, 1), value)
        bumps.append(value)
    put(start + 5, *bumps)


def assemble_kernel(
    sheet_ref, cap_ref, drop_ref, counts_ref, field_ref, within_ref, between_ref, late_ref,
    s_ref, x_ref, c_ref, k_ref, one_ref, two_ref, up_ref, down_ref, left_ref, right_ref, diag_ref, spread_ref,
):
    row, last = lax.axis_index("row"), (lax.axis_size("row") - 1)
    sub, lane = sub_iota(256), lax.broadcasted_iota(jnp.int32, (8, 256), 1)
    below, above = readers(row % 2 == 0, row < last, row > 0, within_ref, between_ref, late_ref)

    def both(own, kind, d, n):
        sides = [column_groups(lambda g: own(half, g), below, above, kind, d, half, n) for half in range(2)]
        return [None if a is None else jnp.concatenate([a, b], axis=1) for a, b in zip(*sides)]

    for d in range(2):
        caps = both(lambda half, g: cap_ref[d, rows(g), pl.ds(half * 128, 128)], CAPACITY, d, 0)
        counts = both(lambda half, g: counts_ref[2 * d + half, rows(g), :], COUNTS, d, 0)
        for g in range(GROUPS):
            c_ref[d, rows(g), :] = caps[g]
            k_ref[d, rows(g), :] = counts[g]
        for n in range(2):
            i = 2 * d + n
            sheets = both(lambda half, g: sheet_ref[d, n, rows(g), pl.ds(half * 128, 128)], SHEET, d, n)
            drops = both(lambda half, g: drop_ref[d, n, rows(g), pl.ds(half * 128, 128)], DROP, d, n)
            ones = both(lambda half, g: field_ref[n, 2 * d + half, rows(g), :], FIRST, d, n)
            twos = both(lambda half, g: field_ref[2 + n, 2 * d + half, rows(g), :], SECOND, d, n)
            for g in range(GROUPS):
                s_ref[i, rows(g), :] = sheets[g]
                x_ref[i, rows(g), :] = drops[g]
                one_ref[i, rows(g), :] = c_ref[d, rows(g), :] * drops[g] + ones[g]
                if twos[g] is not None:
                    two_ref[i, rows(g), :] = twos[g]
            for g in range(GROUPS):
                here, after = s_ref[i, rows(g), :], s_ref[i, rows((g + 1) % GROUPS), :]
                under = jnp.where(sub == 7, roll(after, -1, 0), roll(here, -1, 0))
                inside = here > 0.0
                down_ref[i, rows(g), :] = jnp.where(inside, connect(here, under), 0.0)
                right = jnp.where(inside & (lane < 255), connect(here, roll(here, -1, 1)), 0.0)
                right_ref[i, rows(g), :] = right
                left_ref[i, rows(g), :] = roll(right, 1, 1)
            for g in range(GROUPS):
                here, before = down_ref[i, rows(g), :], down_ref[i, rows((g - 1) % GROUPS), :]
                up = jnp.where(sub == 0, roll(before, 1, 0), roll(here, 1, 0))
                up_ref[i, rows(g), :] = up
                diag = c_ref[d, rows(g), :] + up + here + left_ref[i, rows(g), :] + right_ref[i, rows(g), :]
                diag_ref[i, rows(g), :] = diag + VIA_CONDUCT * k_ref[d, rows(g), :]
    source = lax.broadcasted_iota(jnp.int32, (256, 384), 0) % 128
    column = lax.broadcasted_iota(jnp.int32, (256, 384), 1)
    column = jnp.where(column < 256, 16 + column // 8, jnp.where(column < 320, 48, 0) + (column - 256) // 8)
    for n in range(2):
        spread_ref[n] = jnp.where(source == column + 64 * n, 1.0, 0.0).astype(jnp.bfloat16)


def connect(center, neighbour):
    return jnp.where(neighbour > 0.0, 2.0 / (center + neighbour), 0.0)


def three_terms(k):
    if k == 0:
        return 1.0 - 1.0 / MIDDLE, 0.0, 1.0 / MIDDLE
    a, b = WEIGHTS[k - 1]
    return 1.0 + a - b, -a, b


def advance(k, value, previous, total):
    fore, back, gain = three_terms(k)
    out = total if gain == 1.0 else gain * total
    if fore != 0.0:
        out = out + fore * value
    return out + back * previous() if k else out


def base_solve(fields):
    sheet, state, arriving, bump = fields
    steps = [(1, 0), (-1, 0), (1, 1), (-1, 1)]
    inside = sheet > 0.0
    links = [jnp.where(inside, connect(sheet, roll(sheet, s, a)), 0.0) for s, a in steps]
    diagonal = BASE_CAPACITY + links[0] + links[1] + links[2] + links[3] + BUMP_CONDUCT * bump
    inverse = 1.0 / diagonal
    links = [inverse * link for link in links]
    results = []
    for t in range(STEPS):
        source = inverse * (BASE_CAPACITY * state + arriving[t])
        previous = None
        for k in range(SWEEPS):
            total = (links[0] * roll(state, 1, 0) + links[1] * roll(state, -1, 0)) + (
                links[2] * roll(state, 1, 1) + links[3] * roll(state, -1, 1)
            ) + source
            state, previous = advance(k, state, lambda: previous, total), state
        results.append(state)
    return results


def needed(halo):
    if halo > 8:
        return list(range(GROUPS))
    return list(range(8)) + ([8, 10] if halo > 0 else [])


def solve_kernel(
    s_ref, x_ref, c_ref, k_ref, one_ref, two_ref, up_ref, down_ref, left_ref, right_ref, diag_ref, spread_ref,
    wide_ref, even_ref, odd_ref, out_ref, base_out_ref,
    c_ext, k_ext, f_ext, bound, link_up, link_down, link_left, link_right, inv_ext, src, state, alt,
):
    lane = lane_iota()
    row, col = lax.axis_index("row"), lax.axis_index("col")
    has_left, has_right = col > 0, col < (lax.axis_size("col") - 1)
    even_col = col % 2 == 0

    def from_left(g):
        return jnp.where(even_col, odd_ref[rows(g), :], even_ref[rows(g), :])

    def from_right(g):
        return jnp.where(even_col, even_ref[rows(g), :], odd_ref[rows(g), :])

    start = 2 * GROUPS
    quarter = (lane % 64) // 16
    take_left, take_right = (quarter == 0) & has_left, (quarter == 3) & has_right
    fields = []
    for field in range(5):
        out = []
        for g in range(5):
            if field == 4:
                right, left = roll(from_right(start + 5), 48 - 16 * g, 1), roll(from_left(start + 5), -16 * g, 1)
                right = jnp.where(lane < 64, right, roll(right, 64, 1))
                left = jnp.where(lane < 64, left, roll(left, 64, 1))
            else:
                right = roll(from_right(start + g), (32, 16, 0, 48)[field], 1)
                left = roll(from_left(start + g), (-32, -48, 0, -16)[field], 1)
            value = jnp.where(take_right, right, wide_ref[rows(5 * field + g), :])
            out.append(jnp.where(take_left, left, value))
        fields.append(jnp.concatenate(out, axis=0))
    solved = base_solve((fields[0], fields[1], (fields[2], fields[3]), fields[4]))
    for t in range(STEPS):
        pieces = halves(solved[t])
        for n in range(2):
            bound[2 * t + n] = jnp.dot(pieces, spread_ref[n], preferred_element_type=F32)
    for n in range(2):
        base_out_ref[n] = roll(solved[1][0:8], -(64 * n + 16), 1)[:, 0:32]

    sub, sub3 = sub_iota(), sub_iota(384)
    last = lax.axis_size("row") - 1

    def third(part, chunk, g):
        right_ok, left_ok = has_right, has_left
        if g >= 8:
            inside = {8: row < last, 9: ((sub < 4) & (row < last)) | ((sub >= 4) & (row > 0)), 10: row > 0}[g]
            right_ok, left_ok = right_ok & inside, left_ok & inside
        right = jnp.where((lane // 16 == chunk) & right_ok, from_right(part * GROUPS + g), 0.0)
        value = jnp.where((lane // 16 == (chunk + 7) % 8) & left_ok, from_left(part * GROUPS + g), right)
        return roll(value, -16 * chunk, 1)

    def above(value, before, index):
        return jnp.where(index == 0, roll(before, 1, 0), roll(value, 1, 0))

    def below(value, after, index):
        return jnp.where(index == 7, roll(after, -1, 0), roll(value, -1, 0))

    for i in range(4):
        d, n = i // 2, i % 2

        def wide(ref, g, extra, index=i):
            return jnp.concatenate([ref[index, rows(g), :], extra], axis=1)

        if n == 0:
            for g in range(GROUPS):
                c_ext[rows(g), :] = wide(c_ref, g, third(1, d, g), d)
                k_ext[rows(g), :] = wide(k_ref, g, third(1, 2 + d, g), d)
        @pl.when(row >= 0)
        def _():
            sheets = [third(0, i, g) for g in range(GROUPS)]
            for g in range(GROUPS):
                here = sheets[g]
                inside = here > 0.0
                low, high = s_ref[i, rows(g), pl.ds(0, 128)], s_ref[i, rows(g), pl.ds(128, 128)]
                after = roll(jnp.where(lane == 0, low, here), -1, 1)
                before = roll(jnp.where(lane == 127, high, here), 1, 1)
                right = jnp.where(inside, connect(here, after), 0.0)
                left = jnp.where(inside, connect(here, before), 0.0)
                down = jnp.where(inside, connect(here, below(here, sheets[(g + 1) % GROUPS], sub)), 0.0)
                up = jnp.where(inside, connect(here, above(here, sheets[(g - 1) % GROUPS], sub)), 0.0)
                first = jnp.where(lane == 0, roll(right, 1, 1), 0.0)
                final = jnp.where(lane == 127, roll(left, -1, 1), 0.0)
                diag = wide(diag_ref, g, 0.0 * here) + jnp.concatenate(
                    [first, final, c_ext[rows(g), pl.ds(256, 128)] + up + down + left + right
                     + VIA_CONDUCT * k_ext[rows(g), pl.ds(256, 128)]], axis=1)
                inverse = jnp.where(diag > 0.0, 1.0 / diag, 0.0)
                inv_ext[rows(g), :] = inverse
                zero = jnp.zeros_like(first)
                link_up[rows(g), :] = inverse * wide(up_ref, g, up)
                link_down[rows(g), :] = inverse * wide(down_ref, g, down)
                link_left[rows(g), :] = inverse * (wide(left_ref, g, left) + jnp.concatenate([first, zero, zero], axis=1))
                link_right[rows(g), :] = inverse * (wide(right_ref, g, right) + jnp.concatenate([zero, final, zero], axis=1))
                drop = third(0, 4 + i, g)
                state[rows(g), :] = wide(x_ref, g, drop)
                one = third(1, 4 + i, g)
                f_ext[0, rows(g), :] = wide(one_ref, g, c_ext[rows(g), pl.ds(256, 128)] * drop + one)
                if g != 9:
                    two = jnp.where(lane < 64, roll(one, -11, 1), roll(one, 11, 1))
                    f_ext[1, rows(g), :] = wide(two_ref, g, two)

        @pl.when(row >= 0)
        def _():
            for t in range(STEPS):
                for k in range(SWEEPS):
                    now, then = (alt, state) if k % 2 else (state, alt)
                    for g in needed(11 - 6 * t - k):
                        value = now[rows(g), :]
                        total = link_up[rows(g), :] * above(value, now[rows((g - 1) % GROUPS), :], sub3)
                        total = total + link_down[rows(g), :] * below(value, now[rows((g + 1) % GROUPS), :], sub3)
                        total = total + (
                            link_left[rows(g), :] * roll(value, 1, 1) + link_right[rows(g), :] * roll(value, -1, 1))
                        if k == 0:
                            spread = jnp.broadcast_to(bound[2 * t + n, pl.ds(39 if g == 10 else g, 1), :], (8, 384))
                            if g == 9:
                                spread = jnp.where(sub3 < 4, spread, bound[2 * t + n, pl.ds(38, 1), :])
                            source = f_ext[t, rows(g), :] + k_ext[rows(g), :] * spread
                            if t:
                                source = source + c_ext[rows(g), :] * value
                            source = inv_ext[rows(g), :] * source
                            src[rows(g), :] = source
                        else:
                            source = src[rows(g), :]
                        then[rows(g), :] = advance(k, value, lambda: then[rows(g), :], total + source)

        for g in range(8):
            out_ref[d, n, rows(g), :] = state[rows(g), pl.ds(0, 256)]


def spec(count):
    return [pl.BlockSpec(memory_space=pltpu.VMEM)] * count


def call(kernel, name, outs, ins, scratch=(), limit=24):
    return pl.pallas_call(
        kernel,
        out_shape=outs,
        in_specs=ins,
        out_specs=spec(len(outs)),
        scratch_shapes=list(scratch),
        compiler_params=pltpu.CompilerParams(vmem_limit_bytes=limit * 1024 * 1024),
        name=name,
        cost_estimate=HINTS.get(name),
    )


LONG = pl.CostEstimate(flops=10**9, bytes_accessed=10**7, transcendentals=0)
NONE = pl.CostEstimate(flops=0, bytes_accessed=0, transcendentals=0)
HINTS = {"spread_cells": NONE, "pack_early": NONE, "place_vias": LONG, "pack_relay": LONG}


def arr(*shape, dtype=F32):
    return jax.ShapeDtypeStruct(shape, dtype)


def swaps(count, offset):
    pairs = []
    for die in range(2):
        partner = {}
        for i in range(offset, count - 1, 2):
            partner[i], partner[i + 1] = i + 1, i
        for i in range(count):
            target = die * count + partner[i] if i in partner else (1 - die) * count + i
            pairs.append((die * count + i, target))
    return pairs


def swap(value, axis, offset):
    return lax.ppermute(value, ("die", axis), swaps(lax.axis_size(axis), offset))


def per_device(
    sheet_res, capacity, drop_start, load_cell, load_current, via_cell, via_current, base_sheet, base_start, bump_cell
):
    others = [(0, 1), (1, 0)]

    packed, send = call(pack_kernel, "pack_vias", (arr(2, VIAS, 8, 128), arr(VIAS + 1, 8, 128)), spec(1))(via_current)
    got = lax.ppermute(send, "die", others)
    def buffer(count):
        return arr(8 * count, 128)

    base = call(base_kernel, "pack_base", (buffer(BASE),), spec(4))(bump_cell, base_sheet, base_start, send)[0]
    first = swap(base, "row", 0)
    early, between = call(chip_kernel, "pack_early", (buffer(EARLY), buffer(EARLY + 2 * BASE)), spec(5))(
        base, first, sheet_res, capacity, drop_start
    )
    between = swap(between, "row", 1)
    cells, load_cells, loads, spread, counts = call(
        prepare_kernel, "spread_cells",
        (arr(4, VIAS, 8, 128), arr(4, 8, 128), arr(4, 4, 8, 128), arr(256, 1024, dtype=jnp.bfloat16), arr(4, 64, 128)),
        spec(3),
    )(via_cell, load_cell, load_current)

    field, even, odd, arriving = call(
        place_kernel, "place_vias", (arr(4, 4, 64, 128), buffer(LATE + EARLY), buffer(LATE), buffer(1)),
        spec(9), [pltpu.VMEM((4, 4, VIAS, 8, 128), F32)],
    )(packed, send, got, cells, load_cells, loads, spread, counts, early)

    late = swap(odd, "row", 1)
    within = swap(even, "row", 0)
    relay = call(relay_kernel, "pack_relay", (buffer(BASE),), spec(1))(between)[0]
    relayed = swap(relay, "row", 0)
    shares = call(shares_kernel, "pack_shares", (buffer(4),), spec(3))(first, between, relayed)[0]
    shares = lax.ppermute(shares, "die", others)

    even, odd, wide = call(
        strip_kernel, "column_strips", (buffer(COL_GROUPS), buffer(COL_GROUPS), arr(200, 128)), spec(13)
    )(sheet_res, capacity, drop_start, counts, field, base, arriving, first, between, within, late, relayed, shares)
    even = swap(even, "col", 0)
    odd = swap(odd, "col", 1)

    image, pair = arr(4, 8 * GROUPS, 256), arr(2, 8 * GROUPS, 256)
    parts = call(
        assemble_kernel, "assemble",
        (image, image, pair, pair) + (image,) * 7 + (arr(2, 256, 384, dtype=jnp.bfloat16),), spec(8),
    )(sheet_res, capacity, drop_start, counts, field, within, between, late)

    ext = pltpu.VMEM((8 * GROUPS, 384), F32)
    scratch = [ext, ext, pltpu.VMEM((2, 8 * GROUPS, 384), F32), pltpu.VMEM((4, 40, 384), F32)] + [ext] * 8
    return call(solve_kernel, "solve", (arr(2, 2, 64, 256), arr(2, 8, 32)), spec(15), scratch)(
        *parts, wide, even, odd
    )


def solution(mesh):
    in_specs = (
        P("die", None, "row", "col"),
        P("die", "row", "col"),
        P("die", None, "row", "col"),
        P("die", "row", "col"),
        P(None, "die", None, "row", "col"),
        P("die", None, "row", "col"),
        P(None, "die", None, None, "row", "col"),
        P(None, "row", "col"),
        P(None, "row", "col"),
        P("row", "col"),
    )
    out_specs = (P("die", None, "row", "col"), P(None, "row", "col"))
    return jax.shard_map(
        per_device, mesh=mesh, in_specs=in_specs, out_specs=out_specs, check_vma=False
    )
```

```python
import jax
import jax.numpy as jnp
from jax import lax
from jax.experimental import pallas as pl
from jax.experimental.pallas import tpu as pltpu
from jax.sharding import PartitionSpec as P

SWEEPS = 6
STEPS = 2
VIAS = 32

VIA_CONDUCT = 1.0
VIA_RESIST = 4.0
BUMP_CONDUCT = 50.0
BASE_CAPACITY = 0.1
LOWER_BOUND = 0.1
UPPER_BOUND = 1.9

MIDDLE = 0.5 * (UPPER_BOUND + LOWER_BOUND)
HALF = 0.5 * (UPPER_BOUND - LOWER_BOUND)

GROUPS = 11
F32 = jnp.float32


def sweep_weights():
    scaled = MIDDLE / HALF
    ratio = 1.0 / scaled
    pairs = []
    for _ in range(SWEEPS - 1):
        following = 1.0 / (2.0 * scaled - ratio)
        pairs.append((following * ratio, 2.0 * following / HALF))
        ratio = following
    return pairs


WEIGHTS = sweep_weights()


def lane_iota():
    return lax.broadcasted_iota(jnp.int32, (8, 128), 1)


def sub_iota(width=128):
    return lax.broadcasted_iota(jnp.int32, (8, width), 0)


def roll(x, shift, axis):
    shift = shift % x.shape[axis]
    return pltpu.roll(x, shift, axis) if shift else x


def rows(g):
    return pl.ds(8 * g, 8)


def pack_kernel(via_ref, packed_ref, send_ref):
    later = lax.axis_index("die").astype(F32)
    total = jnp.zeros((8, 128), F32)
    for v in range(VIAS):
        parts = []
        for d in range(2):
            part = jnp.concatenate([via_ref[t, d, n, v] for t in range(2) for n in range(2)], axis=1)
            packed_ref[d, v] = part
            parts.append(part)
        both = parts[0] + parts[1]
        send_ref[v] = both + later * parts[0]
        total = total + both
    send_ref[VIAS] = total


def spread_nets(ref):
    gap = jnp.zeros((8, 16), F32)
    return jnp.concatenate([gap, ref[0], gap, gap, ref[1], gap], axis=1)


def shared(first, second, shift):
    return jnp.where(sub_iota() < shift, first, roll(second, shift, 0))


def shared_low(first, second, shift):
    return jnp.where(sub_iota() >= shift, first, roll(second, shift, 0))


class RowSender:
    def __init__(self, even, even_ref, odd_ref):
        self.even, self.even_ref, self.odd_ref, self.place = even, even_ref, odd_ref, 0

    def put(self, up, down):
        self.even_ref[rows(self.place), :] = jnp.where(self.even, down, up)
        self.odd_ref[rows(self.place), :] = jnp.where(self.even, up, down)
        self.place += 1

    def pair(self, first, second):
        self.put(first(0), first(7))
        self.put(second(0), second(7))
        self.put(shared(first(1), second(1), 4), shared_low(first(6), second(6), 4))


BASE = 4
EARLY = 36
LATE = 16


def base_kernel(bump_ref, sheet_ref, start_ref, send_ref, base_ref):
    lane, sub = lane_iota(), sub_iota()
    bump = jnp.zeros((8, 128), F32)
    column = lane % 64 - 16
    for k in range(4):
        bump = jnp.where((column // 8 == k) & (sub * 8 + column % 8 == bump_ref[0:1, k : k + 1]), 1.0, bump)
    for part, value in enumerate([spread_nets(sheet_ref), spread_nets(start_ref), bump, send_ref[VIAS]]):
        base_ref[rows(part), :] = value


def chip_kernel(base_ref, got_ref, sheet_ref, cap_ref, drop_ref, counts_ref, within_ref, between_ref):
    even = lax.axis_index("row") % 2 == 0
    sender = RowSender(even, within_ref, between_ref)
    for d in range(2):
        for half in range(2):
            lanes = pl.ds(half * 128, 128)
            for n in range(2):
                sender.pair(lambda g: sheet_ref[d, n, rows(g), lanes], lambda g: drop_ref[d, n, rows(g), lanes])
        sender.pair(lambda g: cap_ref[d, rows(g), pl.ds(0, 128)], lambda g: cap_ref[d, rows(g), pl.ds(128, 128)])
        sender.pair(lambda g: counts_ref[2 * d, rows(g), :], lambda g: counts_ref[2 * d + 1, rows(g), :])
    for part in range(BASE):
        own, got = base_ref[rows(part), :], got_ref[rows(part), :]
        for slot, value in enumerate([jnp.where(even, own, got), jnp.where(even, got, own)]):
            between_ref[rows(EARLY + BASE * slot + part), :] = value


def relay_kernel(between_ref, relay_ref):
    even = lax.axis_index("row") % 2 == 0
    for part in range(BASE):
        a, b = between_ref[rows(EARLY + part), :], between_ref[rows(EARLY + BASE + part), :]
        relay_ref[rows(part), :] = jnp.where(even, b, a)


def shares_kernel(first_ref, between_ref, relayed_ref, shares_ref):
    shares_ref[rows(0), :] = first_ref[rows(3), :]
    for slot in range(2):
        shares_ref[rows(1 + slot), :] = between_ref[rows(EARLY + BASE * slot + 3), :]
    shares_ref[rows(3), :] = relayed_ref[rows(3), :]


def spread_matrix(height, width):
    row = lax.broadcasted_iota(jnp.int32, (height, width), 0) % 128
    column = lax.broadcasted_iota(jnp.int32, (height, width), 1)
    return jnp.where(row == column // 8, 1.0, 0.0).astype(jnp.bfloat16)


def halves(value):
    high = value.astype(jnp.bfloat16)
    low = (value - high.astype(F32)).astype(jnp.bfloat16)
    return jnp.concatenate([high, low], axis=1)


def prepare_kernel(cell_ref, load_cell_ref, load_ref, cells_ref, load_cells_ref, loads_ref, spread_ref, counts_ref):
    within = (lane_iota() % 8).astype(F32)
    spread = spread_matrix(32, 256)
    for d in range(2):
        cells = cell_ref[d].reshape(8 * VIAS, 32).astype(F32).astype(jnp.bfloat16)
        wide = jnp.dot(cells, spread, preferred_element_type=F32)
        load_cell = load_cell_ref[d].astype(F32).astype(jnp.bfloat16)
        load_cell = jnp.dot(load_cell, spread, preferred_element_type=F32)
        for half in range(2):
            lanes = slice(128 * half, 128 * half + 128)
            for v in range(VIAS):
                cells_ref[2 * d + half, v] = wide[8 * v : 8 * v + 8, lanes] - within
            load_cells_ref[2 * d + half] = load_cell[:, lanes] - within
    spread_ref[...] = spread_matrix(256, 1024)
    loads = jnp.concatenate([load_ref[t, d, n] for d in range(2) for t in range(2) for n in range(2)], axis=0)
    high = loads.astype(jnp.bfloat16)
    low = (loads - high.astype(F32)).astype(jnp.bfloat16)
    wide = jnp.dot(high, spread, preferred_element_type=F32) + jnp.dot(low, spread, preferred_element_type=F32)
    for d in range(2):
        for half in range(2):
            for m in range(4):
                loads_ref[2 * d + half, m] = wide[32 * d + 8 * m : 32 * d + 8 * m + 8, 128 * half : 128 * half + 128]

    def count(i, carry):
        state = [jnp.zeros((8, 128), F32) for _ in range(8)]
        for v in range(VIAS):
            cell = cells_ref[i, v]
            for oi in range(8):
                state[oi] = state[oi] + jnp.where(cell == 8.0 * oi, 1.0, 0.0)
        for oi in range(8):
            counts_ref[i, pl.ds(oi, 8, stride=8), :] = state[oi]
        return carry

    lax.fori_loop(0, 4, count, 0)


def place_kernel(
    packed_ref, send_ref, got_ref, cells_ref, load_cells_ref, loads_ref, spread_ref, early_ref,
    field_ref, even_ref, odd_ref, arriving_ref, values_ref,
):
    lane = lane_iota()
    later = lax.axis_index("die").astype(F32)
    even = lax.axis_index("row") % 2 == 0
    weights = (
        (VIA_RESIST * (4.0 - 2.0 * later), VIA_RESIST * (3.0 - 2.0 * later), VIA_RESIST * (1.0 + later)),
        (VIA_RESIST * (3.0 - 2.0 * later), VIA_RESIST * (3.0 - 2.0 * later), VIA_RESIST),
    )
    size = (8 * VIAS, 128)
    first, second, got = packed_ref[0].reshape(size), packed_ref[1].reshape(size), got_ref[0:VIAS].reshape(size)
    for d in range(2):
        mixed = weights[d][0] * first + weights[d][1] * second + weights[d][2] * got
        wide = jnp.dot(halves(mixed), spread_ref[...], preferred_element_type=F32)
        for half in range(2):
            for m in range(4):
                start = 256 * m + 128 * half
                values_ref[2 * d + half, m] = wide[:, start : start + 128].reshape(VIAS, 8, 128)

    def add(i, carry):
        cell = load_cells_ref[i]
        loads = [loads_ref[i, m] for m in range(4)]
        state = []
        for oi in range(8):
            hit = cell == 8.0 * oi
            state.append([jnp.where(hit, load, 0.0) for load in loads])
        for v in range(VIAS):
            cell = cells_ref[i, v]
            values = [values_ref[i, m, v] for m in range(4)]
            for oi in range(8):
                hit = cell == 8.0 * oi
                state[oi] = [old + jnp.where(hit, value, 0.0) for old, value in zip(state[oi], values)]
        for oi in range(8):
            for m in range(4):
                field_ref[m, i, pl.ds(oi, 8, stride=8), :] = state[oi][m]
        return carry

    lax.fori_loop(0, 4, add, 0)

    arriving_ref[...] = send_ref[VIAS] + got_ref[VIAS]
    for g in range(EARLY):
        even_ref[rows(LATE + g), :] = early_ref[rows(g), :]
    sender = RowSender(even, even_ref, odd_ref)
    for d in range(2):
        for half in range(2):
            for n in range(2):
                one = lambda g: field_ref[n, 2 * d + half, rows(g), :]
                two = lambda g: field_ref[2 + n, 2 * d + half, rows(g), :]
                sender.put(one(0), one(7))
                sender.put(shared(one(1), two(0), 3), shared_low(one(6), two(7), 5))


SHEET, DROP, CAPACITY, COUNTS, FIRST, SECOND = range(6)


def near_rows(read, kind, d, half, n, upper):
    early, late = read
    if kind in (FIRST, SECOND):
        start = 8 * d + 4 * half + 2 * n
        if kind == SECOND:
            return roll(late(start + 1), -5 if upper else -3, 0), None
        return late(start), late(start + 1)
    if kind in (SHEET, DROP):
        start, second = 18 * d + 6 * half + 3 * n, kind == DROP
    else:
        start, second = 18 * d + (12 if kind == CAPACITY else 15), half == 1
    last = early(start + 2)
    return (early(start + 1), roll(last, -4, 0)) if second else (early(start), last)


def column_groups(own, below, above, kind, d, half, n):
    low = near_rows(below, kind, d, half, n, False)
    high = near_rows(above, kind, d, half, n, True)
    both = None if low[1] is None else jnp.where(sub_iota() < 4, low[1], high[1])
    return [own(g) for g in range(8)] + [low[0], both, high[0]]


def readers(even, below, above, within_ref, between_ref, late_ref):
    def make(inside, near, skip, far_ref):
        def read(g):
            value = jnp.where(near, within_ref[rows(skip + g), :], far_ref[rows(g), :])
            return value if inside is None else jnp.where(inside, value, 0.0)
        return read

    odd = jnp.logical_not(even)
    return tuple(
        (make(inside, near, LATE, between_ref), make(inside, near, 0, late_ref)) for inside, near in ((below, even), (above, odd))
    )


COL_GROUPS = 2 * GROUPS + 6


def strip_kernel(
    sheet_ref, cap_ref, drop_ref, counts_ref, field_ref, base_ref, arriving_ref, first_ref, between_ref,
    within_ref, late_ref, relayed_ref, shares_ref, even_ref, odd_ref, wide_ref,
):
    lane = lane_iota()
    within = lane % 16
    row, last = lax.axis_index("row"), (lax.axis_size("row") - 1)
    even = row % 2 == 0
    below, above = readers(even, None, None, within_ref, between_ref, late_ref)
    even_col = lax.axis_index("col") % 2 == 0

    own = (lane % 64 >= 16) & (lane % 64 < 48)

    def spread_steps(value):
        out = []
        for t in range(2):
            moved = jnp.where(lane < 64, roll(value, 16 - 64 * t, 1), roll(value, 48 - 64 * t, 1))
            out.append(jnp.where(own, moved, 0.0))
        return out

    def block(ref, start, share):
        parts = [ref[rows(start + f), :] for f in range(BASE)]
        parts[3] = parts[3] + shares_ref[rows(share), :]
        return parts

    def choose(a, b, inside):
        return [jnp.where(inside, jnp.where(even, x, y), 0.0) for x, y in zip(a, b)]

    partner = block(first_ref, 0, 0)
    between = [block(between_ref, EARLY + BASE * slot, 1 + slot) for slot in range(2)]
    relayed = block(relayed_ref, 0, 3)
    groups = []
    for g, parts in enumerate([
        [base_ref[rows(f), :] for f in range(3)] + [arriving_ref[...]],
        choose(partner, between[0], row < last),
        choose(relayed, between[1], row + 2 <= last),
        choose(between[0], relayed, row >= 2),
        choose(between[1], partner, row > 0),
    ]):
        one, two = spread_steps(parts[3])
        groups.append([parts[0], parts[1], one, two, parts[2]])
        for f in range(5):
            wide_ref[rows(5 * f + g), :] = groups[g][f]

    def fields(part, half):
        lanes = pl.ds(half * 128, 128)
        images = [(d, n) for d in range(2) for n in range(2)]
        if part == 0:
            return [
                column_groups(lambda g: ref[d, n, rows(g), lanes], below, above, kind, d, half, n)
                for kind, ref in ((SHEET, sheet_ref), (DROP, drop_ref)) for d, n in images
            ]
        out = [column_groups(lambda g: cap_ref[d, rows(g), lanes], below, above, CAPACITY, d, half, 0) for d in range(2)]
        out += [
            column_groups(lambda g: counts_ref[2 * d + half, rows(g), :], below, above, COUNTS, d, half, 0)
            for d in range(2)
        ]
        for d, n in images:
            one = column_groups(lambda g: field_ref[n, 2 * d + half, rows(g), :], below, above, FIRST, d, half, n)
            two = column_groups(lambda g: field_ref[2 + n, 2 * d + half, rows(g), :], below, above, SECOND, d, half, n)
            merged = []
            for a, b in zip(one, two):
                if b is None:
                    merged.append(a)
                elif half == 0:
                    merged.append(jnp.where(within < 11, a, roll(b, 11, 1)))
                else:
                    merged.append(jnp.where(within >= 5, a, roll(b, -11, 1)))
            out.append(merged)
        return out

    def put(index, left, right):
        even_ref[rows(index), :] = jnp.where(even_col, right, left)
        odd_ref[rows(index), :] = jnp.where(even_col, left, right)

    for part in range(2):
        sides = [fields(part, half) for half in range(2)]
        for g in range(GROUPS):
            out = []
            for half, chunks in enumerate(sides):
                value = chunks[0][g]
                for k in range(1, 8):
                    value = jnp.where((lane // 16 + half) % 8 == k, roll(chunks[k][g], 16 * k, 1), value)
                out.append(value)
            put(part * GROUPS + g, *out)

    start = 2 * GROUPS
    quarter = (lane % 64) // 16
    for g in range(5):
        sheet, drop, one, two, _ = groups[g]
        left = jnp.where(
            quarter == 1, sheet,
            jnp.where(quarter == 2, roll(drop, 16, 1), jnp.where(quarter == 3, roll(one, 32, 1), roll(two, -16, 1))),
        )
        right = jnp.where(
            quarter == 2, sheet,
            jnp.where(quarter == 3, roll(drop, 16, 1), jnp.where(quarter == 1, roll(two, -16, 1), roll(one, -32, 1))),
        )
        put(start + g, left, right)
    bumps = []
    for origin in (16, 32):
        value = roll(groups[0][4], -origin, 1)
        for g in range(1, 5):
            value = jnp.where(lane // 16 == g, roll(groups[g][4], 16 * g - origin, 1), value)
        bumps.append(value)
    put(start + 5, *bumps)


def assemble_kernel(
    sheet_ref, cap_ref, drop_ref, counts_ref, field_ref, within_ref, between_ref, late_ref,
    s_ref, x_ref, c_ref, k_ref, one_ref, two_ref, up_ref, down_ref, left_ref, right_ref, diag_ref, spread_ref,
):
    row, last = lax.axis_index("row"), (lax.axis_size("row") - 1)
    sub, lane = sub_iota(256), lax.broadcasted_iota(jnp.int32, (8, 256), 1)
    below, above = readers(row % 2 == 0, row < last, row > 0, within_ref, between_ref, late_ref)

    def both(own, kind, d, n):
        sides = [column_groups(lambda g: own(half, g), below, above, kind, d, half, n) for half in range(2)]
        return [None if a is None else jnp.concatenate([a, b], axis=1) for a, b in zip(*sides)]

    for d in range(2):
        caps = both(lambda half, g: cap_ref[d, rows(g), pl.ds(half * 128, 128)], CAPACITY, d, 0)
        counts = both(lambda half, g: counts_ref[2 * d + half, rows(g), :], COUNTS, d, 0)
        for g in range(GROUPS):
            c_ref[d, rows(g), :] = caps[g]
            k_ref[d, rows(g), :] = counts[g]
        for n in range(2):
            i = 2 * d + n
            sheets = both(lambda half, g: sheet_ref[d, n, rows(g), pl.ds(half * 128, 128)], SHEET, d, n)
            drops = both(lambda half, g: drop_ref[d, n, rows(g), pl.ds(half * 128, 128)], DROP, d, n)
            ones = both(lambda half, g: field_ref[n, 2 * d + half, rows(g), :], FIRST, d, n)
            twos = both(lambda half, g: field_ref[2 + n, 2 * d + half, rows(g), :], SECOND, d, n)
            for g in range(GROUPS):
                s_ref[i, rows(g), :] = sheets[g]
                x_ref[i, rows(g), :] = drops[g]
                one_ref[i, rows(g), :] = c_ref[d, rows(g), :] * drops[g] + ones[g]
                if twos[g] is not None:
                    two_ref[i, rows(g), :] = twos[g]
            for g in range(GROUPS):
                here, after = s_ref[i, rows(g), :], s_ref[i, rows((g + 1) % GROUPS), :]
                under = jnp.where(sub == 7, roll(after, -1, 0), roll(here, -1, 0))
                inside = here > 0.0
                down_ref[i, rows(g), :] = jnp.where(inside, connect(here, under), 0.0)
                right = jnp.where(inside & (lane < 255), connect(here, roll(here, -1, 1)), 0.0)
                right_ref[i, rows(g), :] = right
                left_ref[i, rows(g), :] = roll(right, 1, 1)
            for g in range(GROUPS):
                here, before = down_ref[i, rows(g), :], down_ref[i, rows((g - 1) % GROUPS), :]
                up = jnp.where(sub == 0, roll(before, 1, 0), roll(here, 1, 0))
                up_ref[i, rows(g), :] = up
                diag = c_ref[d, rows(g), :] + up + here + left_ref[i, rows(g), :] + right_ref[i, rows(g), :]
                diag_ref[i, rows(g), :] = diag + VIA_CONDUCT * k_ref[d, rows(g), :]
    source = lax.broadcasted_iota(jnp.int32, (256, 384), 0) % 128
    column = lax.broadcasted_iota(jnp.int32, (256, 384), 1)
    column = jnp.where(column < 256, 16 + column // 8, jnp.where(column < 320, 48, 0) + (column - 256) // 8)
    for n in range(2):
        spread_ref[n] = jnp.where(source == column + 64 * n, 1.0, 0.0).astype(jnp.bfloat16)


def connect(center, neighbour):
    return jnp.where(neighbour > 0.0, 2.0 / (center + neighbour), 0.0)


def three_terms(k):
    if k == 0:
        return 1.0 - 1.0 / MIDDLE, 0.0, 1.0 / MIDDLE
    a, b = WEIGHTS[k - 1]
    return 1.0 + a - b, -a, b


def advance(k, value, previous, total):
    fore, back, gain = three_terms(k)
    out = total if gain == 1.0 else gain * total
    if fore != 0.0:
        out = out + fore * value
    return out + back * previous() if k else out


def base_solve(fields):
    sheet, state, arriving, bump = fields
    steps = [(1, 0), (-1, 0), (1, 1), (-1, 1)]
    inside = sheet > 0.0
    links = [jnp.where(inside, connect(sheet, roll(sheet, s, a)), 0.0) for s, a in steps]
    diagonal = BASE_CAPACITY + links[0] + links[1] + links[2] + links[3] + BUMP_CONDUCT * bump
    inverse = 1.0 / diagonal
    links = [inverse * link for link in links]
    results = []
    for t in range(STEPS):
        source = inverse * (BASE_CAPACITY * state + arriving[t])
        previous = None
        for k in range(SWEEPS):
            total = (links[0] * roll(state, 1, 0) + links[1] * roll(state, -1, 0)) + (
                links[2] * roll(state, 1, 1) + links[3] * roll(state, -1, 1)
            ) + source
            state, previous = advance(k, state, lambda: previous, total), state
        results.append(state)
    return results


def needed(halo):
    if halo > 8:
        return list(range(GROUPS))
    return list(range(8)) + ([8, 10] if halo > 0 else [])


def solve_kernel(
    s_ref, x_ref, c_ref, k_ref, one_ref, two_ref, up_ref, down_ref, left_ref, right_ref, diag_ref, spread_ref,
    wide_ref, even_ref, odd_ref, out_ref, base_out_ref,
    c_ext, k_ext, f_ext, bound, link_up, link_down, link_left, link_right, inv_ext, src, state, alt,
):
    lane = lane_iota()
    row, col = lax.axis_index("row"), lax.axis_index("col")
    has_left, has_right = col > 0, col < (lax.axis_size("col") - 1)
    even_col = col % 2 == 0

    def from_left(g):
        return jnp.where(even_col, odd_ref[rows(g), :], even_ref[rows(g), :])

    def from_right(g):
        return jnp.where(even_col, even_ref[rows(g), :], odd_ref[rows(g), :])

    start = 2 * GROUPS
    quarter = (lane % 64) // 16
    take_left, take_right = (quarter == 0) & has_left, (quarter == 3) & has_right
    fields = []
    for field in range(5):
        out = []
        for g in range(5):
            if field == 4:
                right, left = roll(from_right(start + 5), 48 - 16 * g, 1), roll(from_left(start + 5), -16 * g, 1)
                right = jnp.where(lane < 64, right, roll(right, 64, 1))
                left = jnp.where(lane < 64, left, roll(left, 64, 1))
            else:
                right = roll(from_right(start + g), (32, 16, 0, 48)[field], 1)
                left = roll(from_left(start + g), (-32, -48, 0, -16)[field], 1)
            value = jnp.where(take_right, right, wide_ref[rows(5 * field + g), :])
            out.append(jnp.where(take_left, left, value))
        fields.append(jnp.concatenate(out, axis=0))
    solved = base_solve((fields[0], fields[1], (fields[2], fields[3]), fields[4]))
    for t in range(STEPS):
        pieces = halves(solved[t])
        for n in range(2):
            bound[2 * t + n] = jnp.dot(pieces, spread_ref[n], preferred_element_type=F32)
    for n in range(2):
        base_out_ref[n] = roll(solved[1][0:8], -(64 * n + 16), 1)[:, 0:32]

    sub, sub3 = sub_iota(), sub_iota(384)
    last = lax.axis_size("row") - 1

    def third(part, chunk, g):
        right_ok, left_ok = has_right, has_left
        if g >= 8:
            inside = {8: row < last, 9: ((sub < 4) & (row < last)) | ((sub >= 4) & (row > 0)), 10: row > 0}[g]
            right_ok, left_ok = right_ok & inside, left_ok & inside
        right = jnp.where((lane // 16 == chunk) & right_ok, from_right(part * GROUPS + g), 0.0)
        value = jnp.where((lane // 16 == (chunk + 7) % 8) & left_ok, from_left(part * GROUPS + g), right)
        return roll(value, -16 * chunk, 1)

    def above(value, before, index):
        return jnp.where(index == 0, roll(before, 1, 0), roll(value, 1, 0))

    def below(value, after, index):
        return jnp.where(index == 7, roll(after, -1, 0), roll(value, -1, 0))

    for i in range(4):
        d, n = i // 2, i % 2

        def wide(ref, g, extra, index=i):
            return jnp.concatenate([ref[index, rows(g), :], extra], axis=1)

        if n == 0:
            for g in range(GROUPS):
                c_ext[rows(g), :] = wide(c_ref, g, third(1, d, g), d)
                k_ext[rows(g), :] = wide(k_ref, g, third(1, 2 + d, g), d)
        @pl.when(row >= 0)
        def _():
            sheets = [third(0, i, g) for g in range(GROUPS)]
            for g in range(GROUPS):
                here = sheets[g]
                inside = here > 0.0
                low, high = s_ref[i, rows(g), pl.ds(0, 128)], s_ref[i, rows(g), pl.ds(128, 128)]
                after = roll(jnp.where(lane == 0, low, here), -1, 1)
                before = roll(jnp.where(lane == 127, high, here), 1, 1)
                right = jnp.where(inside, connect(here, after), 0.0)
                left = jnp.where(inside, connect(here, before), 0.0)
                down = jnp.where(inside, connect(here, below(here, sheets[(g + 1) % GROUPS], sub)), 0.0)
                up = jnp.where(inside, connect(here, above(here, sheets[(g - 1) % GROUPS], sub)), 0.0)
                first = jnp.where(lane == 0, roll(right, 1, 1), 0.0)
                final = jnp.where(lane == 127, roll(left, -1, 1), 0.0)
                diag = wide(diag_ref, g, 0.0 * here) + jnp.concatenate(
                    [first, final, c_ext[rows(g), pl.ds(256, 128)] + up + down + left + right
                     + VIA_CONDUCT * k_ext[rows(g), pl.ds(256, 128)]], axis=1)
                inverse = jnp.where(diag > 0.0, 1.0 / diag, 0.0)
                inv_ext[rows(g), :] = inverse
                zero = jnp.zeros_like(first)
                link_up[rows(g), :] = inverse * wide(up_ref, g, up)
                link_down[rows(g), :] = inverse * wide(down_ref, g, down)
                link_left[rows(g), :] = inverse * (wide(left_ref, g, left) + jnp.concatenate([first, zero, zero], axis=1))
                link_right[rows(g), :] = inverse * (wide(right_ref, g, right) + jnp.concatenate([zero, final, zero], axis=1))
                drop = third(0, 4 + i, g)
                state[rows(g), :] = wide(x_ref, g, drop)
                one = third(1, 4 + i, g)
                f_ext[0, rows(g), :] = wide(one_ref, g, c_ext[rows(g), pl.ds(256, 128)] * drop + one)
                if g != 9:
                    two = jnp.where(lane < 64, roll(one, -11, 1), roll(one, 11, 1))
                    f_ext[1, rows(g), :] = wide(two_ref, g, two)

        @pl.when(row >= 0)
        def _():
            for t in range(STEPS):
                for k in range(SWEEPS):
                    now, then = (alt, state) if k % 2 else (state, alt)
                    for g in needed(11 - 6 * t - k):
                        value = now[rows(g), :]
                        total = link_up[rows(g), :] * above(value, now[rows((g - 1) % GROUPS), :], sub3)
                        total = total + link_down[rows(g), :] * below(value, now[rows((g + 1) % GROUPS), :], sub3)
                        total = total + (
                            link_left[rows(g), :] * roll(value, 1, 1) + link_right[rows(g), :] * roll(value, -1, 1))
                        if k == 0:
                            spread = jnp.broadcast_to(bound[2 * t + n, pl.ds(39 if g == 10 else g, 1), :], (8, 384))
                            if g == 9:
                                spread = jnp.where(sub3 < 4, spread, bound[2 * t + n, pl.ds(38, 1), :])
                            source = f_ext[t, rows(g), :] + k_ext[rows(g), :] * spread
                            if t:
                                source = source + c_ext[rows(g), :] * value
                            source = inv_ext[rows(g), :] * source
                            src[rows(g), :] = source
                        else:
                            source = src[rows(g), :]
                        then[rows(g), :] = advance(k, value, lambda: then[rows(g), :], total + source)

        for g in range(8):
            out_ref[d, n, rows(g), :] = state[rows(g), pl.ds(0, 256)]


def spec(count):
    return [pl.BlockSpec(memory_space=pltpu.VMEM)] * count


def call(kernel, name, outs, ins, scratch=(), limit=24):
    return pl.pallas_call(
        kernel,
        out_shape=outs,
        in_specs=ins,
        out_specs=spec(len(outs)),
        scratch_shapes=list(scratch),
        compiler_params=pltpu.CompilerParams(vmem_limit_bytes=limit * 1024 * 1024),
        name=name,
        cost_estimate=HINTS.get(name),
    )


LONG = pl.CostEstimate(flops=10**9, bytes_accessed=10**7, transcendentals=0)
NONE = pl.CostEstimate(flops=0, bytes_accessed=0, transcendentals=0)
HINTS = {"spread_cells": NONE, "pack_early": NONE, "place_vias": LONG, "pack_relay": LONG}


def arr(*shape, dtype=F32):
    return jax.ShapeDtypeStruct(shape, dtype)


def swaps(count, offset):
    pairs = []
    for die in range(2):
        partner = {}
        for i in range(offset, count - 1, 2):
            partner[i], partner[i + 1] = i + 1, i
        for i in range(count):
            target = die * count + partner[i] if i in partner else (1 - die) * count + i
            pairs.append((die * count + i, target))
    return pairs


def swap(value, axis, offset):
    return lax.ppermute(value, ("die", axis), swaps(lax.axis_size(axis), offset))


def per_device(
    sheet_res, capacity, drop_start, load_cell, load_current, via_cell, via_current, base_sheet, base_start, bump_cell
):
    others = [(0, 1), (1, 0)]

    packed, send = call(pack_kernel, "pack_vias", (arr(2, VIAS, 8, 128), arr(VIAS + 1, 8, 128)), spec(1))(via_current)
    got = lax.ppermute(send, "die", others)
    def buffer(count):
        return arr(8 * count, 128)

    base = call(base_kernel, "pack_base", (buffer(BASE),), spec(4))(bump_cell, base_sheet, base_start, send)[0]
    first = swap(base, "row", 0)
    cells, load_cells, loads, spread, counts = call(
        prepare_kernel, "spread_cells",
        (arr(4, VIAS, 8, 128), arr(4, 8, 128), arr(4, 4, 8, 128), arr(256, 1024, dtype=jnp.bfloat16), arr(4, 64, 128)),
        spec(3),
    )(via_cell, load_cell, load_current)
    early, between = call(chip_kernel, "pack_early", (buffer(EARLY), buffer(EARLY + 2 * BASE)), spec(6))(
        base, first, sheet_res, capacity, drop_start, counts
    )
    between = swap(between, "row", 1)
    field, even, odd, arriving = call(
        place_kernel, "place_vias", (arr(4, 4, 64, 128), buffer(LATE + EARLY), buffer(LATE), buffer(1)),
        spec(8), [pltpu.VMEM((4, 4, VIAS, 8, 128), F32)],
    )(packed, send, got, cells, load_cells, loads, spread, early)

    late = swap(odd, "row", 1)
    within = swap(even, "row", 0)
    relay = call(relay_kernel, "pack_relay", (buffer(BASE),), spec(1))(between)[0]
    relayed = swap(relay, "row", 0)
    shares = call(shares_kernel, "pack_shares", (buffer(4),), spec(3))(first, between, relayed)[0]
    shares = lax.ppermute(shares, "die", others)

    even, odd, wide = call(
        strip_kernel, "column_strips", (buffer(COL_GROUPS), buffer(COL_GROUPS), arr(200, 128)), spec(13)
    )(sheet_res, capacity, drop_start, counts, field, base, arriving, first, between, within, late, relayed, shares)
    even = swap(even, "col", 0)
    odd = swap(odd, "col", 1)

    image, pair = arr(4, 8 * GROUPS, 256), arr(2, 8 * GROUPS, 256)
    parts = call(
        assemble_kernel, "assemble",
        (image, image, pair, pair) + (image,) * 7 + (arr(2, 256, 384, dtype=jnp.bfloat16),), spec(8),
    )(sheet_res, capacity, drop_start, counts, field, within, between, late)

    ext = pltpu.VMEM((8 * GROUPS, 384), F32)
    scratch = [ext, ext, pltpu.VMEM((2, 8 * GROUPS, 384), F32), pltpu.VMEM((4, 40, 384), F32)] + [ext] * 8
    return call(solve_kernel, "solve", (arr(2, 2, 64, 256), arr(2, 8, 32)), spec(15), scratch)(
        *parts, wide, even, odd
    )


def solution(mesh):
    in_specs = (
        P("die", None, "row", "col"),
        P("die", "row", "col"),
        P("die", None, "row", "col"),
        P("die", "row", "col"),
        P(None, "die", None, "row", "col"),
        P("die", None, "row", "col"),
        P(None, "die", None, None, "row", "col"),
        P(None, "row", "col"),
        P(None, "row", "col"),
        P("row", "col"),
    )
    out_specs = (P("die", None, "row", "col"), P(None, "row", "col"))
    return jax.shard_map(
        per_device, mesh=mesh, in_specs=in_specs, out_specs=out_specs, check_vma=False
    )
```

```python
import jax
import jax.numpy as jnp
from jax import lax
from jax.experimental import pallas as pl
from jax.experimental.pallas import tpu as pltpu
from jax.sharding import PartitionSpec as P

SWEEPS = 6
STEPS = 2
VIAS = 32

VIA_CONDUCT = 1.0
VIA_RESIST = 4.0
BUMP_CONDUCT = 50.0
BASE_CAPACITY = 0.1
LOWER_BOUND = 0.1
UPPER_BOUND = 1.9

MIDDLE = 0.5 * (UPPER_BOUND + LOWER_BOUND)
HALF = 0.5 * (UPPER_BOUND - LOWER_BOUND)

GROUPS = 11
F32 = jnp.float32


def sweep_weights():
    scaled = MIDDLE / HALF
    ratio = 1.0 / scaled
    pairs = []
    for _ in range(SWEEPS - 1):
        following = 1.0 / (2.0 * scaled - ratio)
        pairs.append((following * ratio, 2.0 * following / HALF))
        ratio = following
    return pairs


WEIGHTS = sweep_weights()


def lane_iota():
    return lax.broadcasted_iota(jnp.int32, (8, 128), 1)


def sub_iota(width=128):
    return lax.broadcasted_iota(jnp.int32, (8, width), 0)


def roll(x, shift, axis):
    shift = shift % x.shape[axis]
    return pltpu.roll(x, shift, axis) if shift else x


def rows(g):
    return pl.ds(8 * g, 8)


def pack_kernel(via_ref, packed_ref, send_ref):
    later = lax.axis_index("die").astype(F32)
    total = jnp.zeros((8, 128), F32)
    for v in range(VIAS):
        parts = []
        for d in range(2):
            part = jnp.concatenate([via_ref[t, d, n, v] for t in range(2) for n in range(2)], axis=1)
            packed_ref[d, v] = part
            parts.append(part)
        both = parts[0] + parts[1]
        send_ref[v] = both + later * parts[0]
        total = total + both
    send_ref[VIAS] = total


def spread_nets(ref):
    gap = jnp.zeros((8, 16), F32)
    return jnp.concatenate([gap, ref[0], gap, gap, ref[1], gap], axis=1)


def shared(first, second, shift):
    return jnp.where(sub_iota() < shift, first, roll(second, shift, 0))


def shared_low(first, second, shift):
    return jnp.where(sub_iota() >= shift, first, roll(second, shift, 0))


class RowSender:
    def __init__(self, even, even_ref, odd_ref):
        self.even, self.even_ref, self.odd_ref, self.place = even, even_ref, odd_ref, 0

    def put(self, up, down):
        self.even_ref[rows(self.place), :] = jnp.where(self.even, down, up)
        self.odd_ref[rows(self.place), :] = jnp.where(self.even, up, down)
        self.place += 1

    def pair(self, first, second):
        self.put(first(0), first(7))
        self.put(second(0), second(7))
        self.put(shared(first(1), second(1), 4), shared_low(first(6), second(6), 4))


BASE = 4
EARLY = 36
LATE = 16


def base_kernel(bump_ref, sheet_ref, start_ref, send_ref, base_ref):
    lane, sub = lane_iota(), sub_iota()
    bump = jnp.zeros((8, 128), F32)
    column = lane % 64 - 16
    for k in range(4):
        bump = jnp.where((column // 8 == k) & (sub * 8 + column % 8 == bump_ref[0:1, k : k + 1]), 1.0, bump)
    for part, value in enumerate([spread_nets(sheet_ref), spread_nets(start_ref), bump, send_ref[VIAS]]):
        base_ref[rows(part), :] = value


def chip_kernel(base_ref, got_ref, sheet_ref, cap_ref, drop_ref, counts_ref, within_ref, between_ref):
    even = lax.axis_index("row") % 2 == 0
    sender = RowSender(even, within_ref, between_ref)
    for d in range(2):
        for half in range(2):
            lanes = pl.ds(half * 128, 128)
            for n in range(2):
                sender.pair(lambda g: sheet_ref[d, n, rows(g), lanes], lambda g: drop_ref[d, n, rows(g), lanes])
        sender.pair(lambda g: cap_ref[d, rows(g), pl.ds(0, 128)], lambda g: cap_ref[d, rows(g), pl.ds(128, 128)])
        sender.pair(lambda g: counts_ref[2 * d, rows(g), :], lambda g: counts_ref[2 * d + 1, rows(g), :])
    for part in range(BASE):
        own, got = base_ref[rows(part), :], got_ref[rows(part), :]
        for slot, value in enumerate([jnp.where(even, own, got), jnp.where(even, got, own)]):
            between_ref[rows(EARLY + BASE * slot + part), :] = value


def relay_kernel(between_ref, relay_ref):
    even = lax.axis_index("row") % 2 == 0
    for part in range(BASE):
        a, b = between_ref[rows(EARLY + part), :], between_ref[rows(EARLY + BASE + part), :]
        relay_ref[rows(part), :] = jnp.where(even, b, a)


def shares_kernel(first_ref, between_ref, relayed_ref, shares_ref):
    shares_ref[rows(0), :] = first_ref[rows(3), :]
    for slot in range(2):
        shares_ref[rows(1 + slot), :] = between_ref[rows(EARLY + BASE * slot + 3), :]
    shares_ref[rows(3), :] = relayed_ref[rows(3), :]


def spread_matrix(height, width):
    row = lax.broadcasted_iota(jnp.int32, (height, width), 0) % 128
    column = lax.broadcasted_iota(jnp.int32, (height, width), 1)
    return jnp.where(row == column // 8, 1.0, 0.0).astype(jnp.bfloat16)


def halves(value):
    high = value.astype(jnp.bfloat16)
    low = (value - high.astype(F32)).astype(jnp.bfloat16)
    return jnp.concatenate([high, low], axis=1)


def prepare_kernel(cell_ref, load_cell_ref, load_ref, cells_ref, load_cells_ref, loads_ref, spread_ref, counts_ref):
    within = (lane_iota() % 8).astype(F32)
    spread = spread_matrix(32, 256)
    for d in range(2):
        cells = cell_ref[d].reshape(8 * VIAS, 32).astype(F32).astype(jnp.bfloat16)
        wide = jnp.dot(cells, spread, preferred_element_type=F32)
        load_cell = load_cell_ref[d].astype(F32).astype(jnp.bfloat16)
        load_cell = jnp.dot(load_cell, spread, preferred_element_type=F32)
        for half in range(2):
            lanes = slice(128 * half, 128 * half + 128)
            for v in range(VIAS):
                cells_ref[2 * d + half, v] = wide[8 * v : 8 * v + 8, lanes] - within
            load_cells_ref[2 * d + half] = load_cell[:, lanes] - within
    spread_ref[...] = spread_matrix(256, 1024)
    loads = jnp.concatenate([load_ref[t, d, n] for d in range(2) for t in range(2) for n in range(2)], axis=0)
    high = loads.astype(jnp.bfloat16)
    low = (loads - high.astype(F32)).astype(jnp.bfloat16)
    wide = jnp.dot(high, spread, preferred_element_type=F32) + jnp.dot(low, spread, preferred_element_type=F32)
    for d in range(2):
        for half in range(2):
            for m in range(4):
                loads_ref[2 * d + half, m] = wide[32 * d + 8 * m : 32 * d + 8 * m + 8, 128 * half : 128 * half + 128]

    def count(i, carry):
        state = [jnp.zeros((8, 128), F32) for _ in range(8)]
        for v in range(VIAS):
            cell = cells_ref[i, v]
            for oi in range(8):
                state[oi] = state[oi] + jnp.where(cell == 8.0 * oi, 1.0, 0.0)
        for oi in range(8):
            counts_ref[i, pl.ds(oi, 8, stride=8), :] = state[oi]
        return carry

    lax.fori_loop(0, 4, count, 0)


def place_kernel(
    packed_ref, send_ref, got_ref, cells_ref, load_cells_ref, loads_ref, spread_ref, early_ref,
    field_ref, even_ref, odd_ref, arriving_ref, values_ref,
):
    lane = lane_iota()
    later = lax.axis_index("die").astype(F32)
    even = lax.axis_index("row") % 2 == 0
    weights = (
        (VIA_RESIST * (4.0 - 2.0 * later), VIA_RESIST * (3.0 - 2.0 * later), VIA_RESIST * (1.0 + later)),
        (VIA_RESIST * (3.0 - 2.0 * later), VIA_RESIST * (3.0 - 2.0 * later), VIA_RESIST),
    )
    size = (8 * VIAS, 128)
    first, second, got = packed_ref[0].reshape(size), packed_ref[1].reshape(size), got_ref[0:VIAS].reshape(size)
    for d in range(2):
        mixed = weights[d][0] * first + weights[d][1] * second + weights[d][2] * got
        wide = jnp.dot(halves(mixed), spread_ref[...], preferred_element_type=F32)
        for half in range(2):
            for m in range(4):
                start = 256 * m + 128 * half
                values_ref[2 * d + half, m] = wide[:, start : start + 128].reshape(VIAS, 8, 128)

    def add(i, carry):
        cell = load_cells_ref[i]
        loads = [loads_ref[i, m] for m in range(4)]
        state = []
        for oi in range(8):
            hit = cell == 8.0 * oi
            state.append([jnp.where(hit, load, 0.0) for load in loads])
        for v in range(VIAS):
            cell = cells_ref[i, v]
            values = [values_ref[i, m, v] for m in range(4)]
            for oi in range(8):
                hit = cell == 8.0 * oi
                state[oi] = [old + jnp.where(hit, value, 0.0) for old, value in zip(state[oi], values)]
        for oi in range(8):
            for m in range(4):
                field_ref[m, i, pl.ds(oi, 8, stride=8), :] = state[oi][m]
        return carry

    lax.fori_loop(0, 4, add, 0)

    arriving_ref[...] = send_ref[VIAS] + got_ref[VIAS]
    for g in range(EARLY):
        even_ref[rows(LATE + g), :] = early_ref[rows(g), :]
    sender = RowSender(even, even_ref, odd_ref)
    for d in range(2):
        for half in range(2):
            for n in range(2):
                one = lambda g: field_ref[n, 2 * d + half, rows(g), :]
                two = lambda g: field_ref[2 + n, 2 * d + half, rows(g), :]
                sender.put(one(0), one(7))
                sender.put(shared(one(1), two(0), 3), shared_low(one(6), two(7), 5))


SHEET, DROP, CAPACITY, COUNTS, FIRST, SECOND = range(6)


def near_rows(read, kind, d, half, n, upper):
    early, late = read
    if kind in (FIRST, SECOND):
        start = 8 * d + 4 * half + 2 * n
        if kind == SECOND:
            return roll(late(start + 1), -5 if upper else -3, 0), None
        return late(start), late(start + 1)
    if kind in (SHEET, DROP):
        start, second = 18 * d + 6 * half + 3 * n, kind == DROP
    else:
        start, second = 18 * d + (12 if kind == CAPACITY else 15), half == 1
    last = early(start + 2)
    return (early(start + 1), roll(last, -4, 0)) if second else (early(start), last)


def column_groups(own, below, above, kind, d, half, n):
    low = near_rows(below, kind, d, half, n, False)
    high = near_rows(above, kind, d, half, n, True)
    both = None if low[1] is None else jnp.where(sub_iota() < 4, low[1], high[1])
    return [own(g) for g in range(8)] + [low[0], both, high[0]]


def readers(even, below, above, within_ref, between_ref, late_ref):
    def make(inside, near, skip, far_ref):
        def read(g):
            value = jnp.where(near, within_ref[rows(skip + g), :], far_ref[rows(g), :])
            return value if inside is None else jnp.where(inside, value, 0.0)
        return read

    odd = jnp.logical_not(even)
    return tuple(
        (make(inside, near, LATE, between_ref), make(inside, near, 0, late_ref)) for inside, near in ((below, even), (above, odd))
    )


COL_GROUPS = 2 * GROUPS + 6


def strip_kernel(
    sheet_ref, cap_ref, drop_ref, counts_ref, field_ref, base_ref, arriving_ref, first_ref, between_ref,
    within_ref, late_ref, relayed_ref, shares_ref, odd_ref, even_ref, wide_ref,
):
    lane = lane_iota()
    within = lane % 16
    row, last = lax.axis_index("row"), (lax.axis_size("row") - 1)
    even = row % 2 == 0
    below, above = readers(even, None, None, within_ref, between_ref, late_ref)
    even_col = lax.axis_index("col") % 2 == 0

    own = (lane % 64 >= 16) & (lane % 64 < 48)

    def spread_steps(value):
        out = []
        for t in range(2):
            moved = jnp.where(lane < 64, roll(value, 16 - 64 * t, 1), roll(value, 48 - 64 * t, 1))
            out.append(jnp.where(own, moved, 0.0))
        return out

    def block(ref, start, share):
        parts = [ref[rows(start + f), :] for f in range(BASE)]
        parts[3] = parts[3] + shares_ref[rows(share), :]
        return parts

    def choose(a, b, inside):
        return [jnp.where(inside, jnp.where(even, x, y), 0.0) for x, y in zip(a, b)]

    partner = block(first_ref, 0, 0)
    between = [block(between_ref, EARLY + BASE * slot, 1 + slot) for slot in range(2)]
    relayed = block(relayed_ref, 0, 3)
    groups = []
    for g, parts in enumerate([
        [base_ref[rows(f), :] for f in range(3)] + [arriving_ref[...]],
        choose(partner, between[0], row < last),
        choose(relayed, between[1], row + 2 <= last),
        choose(between[0], relayed, row >= 2),
        choose(between[1], partner, row > 0),
    ]):
        one, two = spread_steps(parts[3])
        groups.append([parts[0], parts[1], one, two, parts[2]])
        for f in range(5):
            wide_ref[rows(5 * f + g), :] = groups[g][f]

    def fields(part, half):
        lanes = pl.ds(half * 128, 128)
        images = [(d, n) for d in range(2) for n in range(2)]
        if part == 0:
            return [
                column_groups(lambda g: ref[d, n, rows(g), lanes], below, above, kind, d, half, n)
                for kind, ref in ((SHEET, sheet_ref), (DROP, drop_ref)) for d, n in images
            ]
        out = [column_groups(lambda g: cap_ref[d, rows(g), lanes], below, above, CAPACITY, d, half, 0) for d in range(2)]
        out += [
            column_groups(lambda g: counts_ref[2 * d + half, rows(g), :], below, above, COUNTS, d, half, 0)
            for d in range(2)
        ]
        for d, n in images:
            one = column_groups(lambda g: field_ref[n, 2 * d + half, rows(g), :], below, above, FIRST, d, half, n)
            two = column_groups(lambda g: field_ref[2 + n, 2 * d + half, rows(g), :], below, above, SECOND, d, half, n)
            merged = []
            for a, b in zip(one, two):
                if b is None:
                    merged.append(a)
                elif half == 0:
                    merged.append(jnp.where(within < 11, a, roll(b, 11, 1)))
                else:
                    merged.append(jnp.where(within >= 5, a, roll(b, -11, 1)))
            out.append(merged)
        return out

    def put(index, left, right):
        even_ref[rows(index), :] = jnp.where(even_col, right, left)
        odd_ref[rows(index), :] = jnp.where(even_col, left, right)

    for part in range(2):
        sides = [fields(part, half) for half in range(2)]
        for g in range(GROUPS):
            out = []
            for half, chunks in enumerate(sides):
                value = chunks[0][g]
                for k in range(1, 8):
                    value = jnp.where((lane // 16 + half) % 8 == k, roll(chunks[k][g], 16 * k, 1), value)
                out.append(value)
            put(part * GROUPS + g, *out)

    start = 2 * GROUPS
    quarter = (lane % 64) // 16
    for g in range(5):
        sheet, drop, one, two, _ = groups[g]
        left = jnp.where(
            quarter == 1, sheet,
            jnp.where(quarter == 2, roll(drop, 16, 1), jnp.where(quarter == 3, roll(one, 32, 1), roll(two, -16, 1))),
        )
        right = jnp.where(
            quarter == 2, sheet,
            jnp.where(quarter == 3, roll(drop, 16, 1), jnp.where(quarter == 1, roll(two, -16, 1), roll(one, -32, 1))),
        )
        put(start + g, left, right)
    bumps = []
    for origin in (16, 32):
        value = roll(groups[0][4], -origin, 1)
        for g in range(1, 5):
            value = jnp.where(lane // 16 == g, roll(groups[g][4], 16 * g - origin, 1), value)
        bumps.append(value)
    put(start + 5, *bumps)


def assemble_kernel(
    sheet_ref, cap_ref, drop_ref, counts_ref, field_ref, within_ref, between_ref, late_ref,
    s_ref, x_ref, c_ref, k_ref, one_ref, two_ref, up_ref, down_ref, left_ref, right_ref, diag_ref, spread_ref,
):
    row, last = lax.axis_index("row"), (lax.axis_size("row") - 1)
    sub, lane = sub_iota(256), lax.broadcasted_iota(jnp.int32, (8, 256), 1)
    below, above = readers(row % 2 == 0, row < last, row > 0, within_ref, between_ref, late_ref)

    def both(own, kind, d, n):
        sides = [column_groups(lambda g: own(half, g), below, above, kind, d, half, n) for half in range(2)]
        return [None if a is None else jnp.concatenate([a, b], axis=1) for a, b in zip(*sides)]

    for d in range(2):
        caps = both(lambda half, g: cap_ref[d, rows(g), pl.ds(half * 128, 128)], CAPACITY, d, 0)
        counts = both(lambda half, g: counts_ref[2 * d + half, rows(g), :], COUNTS, d, 0)
        for g in range(GROUPS):
            c_ref[d, rows(g), :] = caps[g]
            k_ref[d, rows(g), :] = counts[g]
        for n in range(2):
            i = 2 * d + n
            sheets = both(lambda half, g: sheet_ref[d, n, rows(g), pl.ds(half * 128, 128)], SHEET, d, n)
            drops = both(lambda half, g: drop_ref[d, n, rows(g), pl.ds(half * 128, 128)], DROP, d, n)
            ones = both(lambda half, g: field_ref[n, 2 * d + half, rows(g), :], FIRST, d, n)
            twos = both(lambda half, g: field_ref[2 + n, 2 * d + half, rows(g), :], SECOND, d, n)
            for g in range(GROUPS):
                s_ref[i, rows(g), :] = sheets[g]
                x_ref[i, rows(g), :] = drops[g]
                one_ref[i, rows(g), :] = c_ref[d, rows(g), :] * drops[g] + ones[g]
                if twos[g] is not None:
                    two_ref[i, rows(g), :] = twos[g]
            for g in range(GROUPS):
                here, after = s_ref[i, rows(g), :], s_ref[i, rows((g + 1) % GROUPS), :]
                under = jnp.where(sub == 7, roll(after, -1, 0), roll(here, -1, 0))
                inside = here > 0.0
                down_ref[i, rows(g), :] = jnp.where(inside, connect(here, under), 0.0)
                right = jnp.where(inside & (lane < 255), connect(here, roll(here, -1, 1)), 0.0)
                right_ref[i, rows(g), :] = right
                left_ref[i, rows(g), :] = roll(right, 1, 1)
            for g in range(GROUPS):
                here, before = down_ref[i, rows(g), :], down_ref[i, rows((g - 1) % GROUPS), :]
                up = jnp.where(sub == 0, roll(before, 1, 0), roll(here, 1, 0))
                up_ref[i, rows(g), :] = up
                diag = c_ref[d, rows(g), :] + up + here + left_ref[i, rows(g), :] + right_ref[i, rows(g), :]
                diag_ref[i, rows(g), :] = diag + VIA_CONDUCT * k_ref[d, rows(g), :]
    source = lax.broadcasted_iota(jnp.int32, (256, 384), 0) % 128
    column = lax.broadcasted_iota(jnp.int32, (256, 384), 1)
    column = jnp.where(column < 256, 16 + column // 8, jnp.where(column < 320, 48, 0) + (column - 256) // 8)
    for n in range(2):
        spread_ref[n] = jnp.where(source == column + 64 * n, 1.0, 0.0).astype(jnp.bfloat16)


def connect(center, neighbour):
    return jnp.where(neighbour > 0.0, 2.0 / (center + neighbour), 0.0)


def three_terms(k):
    if k == 0:
        return 1.0 - 1.0 / MIDDLE, 0.0, 1.0 / MIDDLE
    a, b = WEIGHTS[k - 1]
    return 1.0 + a - b, -a, b


def advance(k, value, previous, total):
    fore, back, gain = three_terms(k)
    out = total if gain == 1.0 else gain * total
    if fore != 0.0:
        out = out + fore * value
    return out + back * previous() if k else out


def base_solve(fields):
    sheet, state, arriving, bump = fields
    steps = [(1, 0), (-1, 0), (1, 1), (-1, 1)]
    inside = sheet > 0.0
    links = [jnp.where(inside, connect(sheet, roll(sheet, s, a)), 0.0) for s, a in steps]
    diagonal = BASE_CAPACITY + links[0] + links[1] + links[2] + links[3] + BUMP_CONDUCT * bump
    inverse = 1.0 / diagonal
    links = [inverse * link for link in links]
    results = []
    for t in range(STEPS):
        source = inverse * (BASE_CAPACITY * state + arriving[t])
        previous = None
        for k in range(SWEEPS):
            total = (links[0] * roll(state, 1, 0) + links[1] * roll(state, -1, 0)) + (
                links[2] * roll(state, 1, 1) + links[3] * roll(state, -1, 1)
            ) + source
            state, previous = advance(k, state, lambda: previous, total), state
        results.append(state)
    return results


def needed(halo):
    if halo > 8:
        return list(range(GROUPS))
    return list(range(8)) + ([8, 10] if halo > 0 else [])


def solve_kernel(
    s_ref, x_ref, c_ref, k_ref, one_ref, two_ref, up_ref, down_ref, left_ref, right_ref, diag_ref, spread_ref,
    wide_ref, odd_ref, even_ref, out_ref, base_out_ref,
    c_ext, k_ext, f_ext, bound, link_up, link_down, link_left, link_right, inv_ext, src, state, alt,
):
    lane = lane_iota()
    row, col = lax.axis_index("row"), lax.axis_index("col")
    has_left, has_right = col > 0, col < (lax.axis_size("col") - 1)
    even_col = col % 2 == 0

    def from_left(g):
        return jnp.where(even_col, odd_ref[rows(g), :], even_ref[rows(g), :])

    def from_right(g):
        return jnp.where(even_col, even_ref[rows(g), :], odd_ref[rows(g), :])

    start = 2 * GROUPS
    quarter = (lane % 64) // 16
    take_left, take_right = (quarter == 0) & has_left, (quarter == 3) & has_right
    fields = []
    for field in range(5):
        out = []
        for g in range(5):
            if field == 4:
                right, left = roll(from_right(start + 5), 48 - 16 * g, 1), roll(from_left(start + 5), -16 * g, 1)
                right = jnp.where(lane < 64, right, roll(right, 64, 1))
                left = jnp.where(lane < 64, left, roll(left, 64, 1))
            else:
                right = roll(from_right(start + g), (32, 16, 0, 48)[field], 1)
                left = roll(from_left(start + g), (-32, -48, 0, -16)[field], 1)
            value = jnp.where(take_right, right, wide_ref[rows(5 * field + g), :])
            out.append(jnp.where(take_left, left, value))
        fields.append(jnp.concatenate(out, axis=0))
    solved = base_solve((fields[0], fields[1], (fields[2], fields[3]), fields[4]))
    for t in range(STEPS):
        pieces = halves(solved[t])
        for n in range(2):
            bound[2 * t + n] = jnp.dot(pieces, spread_ref[n], preferred_element_type=F32)
    for n in range(2):
        base_out_ref[n] = roll(solved[1][0:8], -(64 * n + 16), 1)[:, 0:32]

    sub, sub3 = sub_iota(), sub_iota(384)
    last = lax.axis_size("row") - 1

    def third(part, chunk, g):
        right_ok, left_ok = has_right, has_left
        if g >= 8:
            inside = {8: row < last, 9: ((sub < 4) & (row < last)) | ((sub >= 4) & (row > 0)), 10: row > 0}[g]
            right_ok, left_ok = right_ok & inside, left_ok & inside
        right = jnp.where((lane // 16 == chunk) & right_ok, from_right(part * GROUPS + g), 0.0)
        value = jnp.where((lane // 16 == (chunk + 7) % 8) & left_ok, from_left(part * GROUPS + g), right)
        return roll(value, -16 * chunk, 1)

    def above(value, before, index):
        return jnp.where(index == 0, roll(before, 1, 0), roll(value, 1, 0))

    def below(value, after, index):
        return jnp.where(index == 7, roll(after, -1, 0), roll(value, -1, 0))

    for i in range(4):
        d, n = i // 2, i % 2

        def wide(ref, g, extra, index=i):
            return jnp.concatenate([ref[index, rows(g), :], extra], axis=1)

        if n == 0:
            for g in range(GROUPS):
                c_ext[rows(g), :] = wide(c_ref, g, third(1, d, g), d)
                k_ext[rows(g), :] = wide(k_ref, g, third(1, 2 + d, g), d)
        @pl.when(row >= 0)
        def _():
            sheets = [third(0, i, g) for g in range(GROUPS)]
            for g in range(GROUPS):
                here = sheets[g]
                inside = here > 0.0
                low, high = s_ref[i, rows(g), pl.ds(0, 128)], s_ref[i, rows(g), pl.ds(128, 128)]
                after = roll(jnp.where(lane == 0, low, here), -1, 1)
                before = roll(jnp.where(lane == 127, high, here), 1, 1)
                right = jnp.where(inside, connect(here, after), 0.0)
                left = jnp.where(inside, connect(here, before), 0.0)
                down = jnp.where(inside, connect(here, below(here, sheets[(g + 1) % GROUPS], sub)), 0.0)
                up = jnp.where(inside, connect(here, above(here, sheets[(g - 1) % GROUPS], sub)), 0.0)
                first = jnp.where(lane == 0, roll(right, 1, 1), 0.0)
                final = jnp.where(lane == 127, roll(left, -1, 1), 0.0)
                diag = wide(diag_ref, g, 0.0 * here) + jnp.concatenate(
                    [first, final, c_ext[rows(g), pl.ds(256, 128)] + up + down + left + right
                     + VIA_CONDUCT * k_ext[rows(g), pl.ds(256, 128)]], axis=1)
                inverse = jnp.where(diag > 0.0, 1.0 / diag, 0.0)
                inv_ext[rows(g), :] = inverse
                zero = jnp.zeros_like(first)
                link_up[rows(g), :] = inverse * wide(up_ref, g, up)
                link_down[rows(g), :] = inverse * wide(down_ref, g, down)
                link_left[rows(g), :] = inverse * (wide(left_ref, g, left) + jnp.concatenate([first, zero, zero], axis=1))
                link_right[rows(g), :] = inverse * (wide(right_ref, g, right) + jnp.concatenate([zero, final, zero], axis=1))
                drop = third(0, 4 + i, g)
                state[rows(g), :] = wide(x_ref, g, drop)
                one = third(1, 4 + i, g)
                f_ext[0, rows(g), :] = wide(one_ref, g, c_ext[rows(g), pl.ds(256, 128)] * drop + one)
                if g != 9:
                    two = jnp.where(lane < 64, roll(one, -11, 1), roll(one, 11, 1))
                    f_ext[1, rows(g), :] = wide(two_ref, g, two)

        @pl.when(row >= 0)
        def _():
            for t in range(STEPS):
                for k in range(SWEEPS):
                    now, then = (alt, state) if k % 2 else (state, alt)
                    for g in needed(11 - 6 * t - k):
                        value = now[rows(g), :]
                        total = link_up[rows(g), :] * above(value, now[rows((g - 1) % GROUPS), :], sub3)
                        total = total + link_down[rows(g), :] * below(value, now[rows((g + 1) % GROUPS), :], sub3)
                        total = total + (
                            link_left[rows(g), :] * roll(value, 1, 1) + link_right[rows(g), :] * roll(value, -1, 1))
                        if k == 0:
                            spread = jnp.broadcast_to(bound[2 * t + n, pl.ds(39 if g == 10 else g, 1), :], (8, 384))
                            if g == 9:
                                spread = jnp.where(sub3 < 4, spread, bound[2 * t + n, pl.ds(38, 1), :])
                            source = f_ext[t, rows(g), :] + k_ext[rows(g), :] * spread
                            if t:
                                source = source + c_ext[rows(g), :] * value
                            source = inv_ext[rows(g), :] * source
                            src[rows(g), :] = source
                        else:
                            source = src[rows(g), :]
                        then[rows(g), :] = advance(k, value, lambda: then[rows(g), :], total + source)

        for g in range(8):
            out_ref[d, n, rows(g), :] = state[rows(g), pl.ds(0, 256)]


def spec(count):
    return [pl.BlockSpec(memory_space=pltpu.VMEM)] * count


def call(kernel, name, outs, ins, scratch=(), limit=24):
    return pl.pallas_call(
        kernel,
        out_shape=outs,
        in_specs=ins,
        out_specs=spec(len(outs)),
        scratch_shapes=list(scratch),
        compiler_params=pltpu.CompilerParams(vmem_limit_bytes=limit * 1024 * 1024),
        name=name,
        cost_estimate=HINTS.get(name),
    )


LONG = pl.CostEstimate(flops=10**9, bytes_accessed=10**7, transcendentals=0)
NONE = pl.CostEstimate(flops=0, bytes_accessed=0, transcendentals=0)
HINTS = {"spread_cells": NONE, "pack_early": NONE, "place_vias": LONG, "pack_relay": LONG}


def arr(*shape, dtype=F32):
    return jax.ShapeDtypeStruct(shape, dtype)


def swaps(count, offset):
    pairs = []
    for die in range(2):
        partner = {}
        for i in range(offset, count - 1, 2):
            partner[i], partner[i + 1] = i + 1, i
        for i in range(count):
            target = die * count + partner[i] if i in partner else (1 - die) * count + i
            pairs.append((die * count + i, target))
    return pairs


def swap(value, axis, offset):
    return lax.ppermute(value, ("die", axis), swaps(lax.axis_size(axis), offset))


def per_device(
    sheet_res, capacity, drop_start, load_cell, load_current, via_cell, via_current, base_sheet, base_start, bump_cell
):
    others = [(0, 1), (1, 0)]

    packed, send = call(pack_kernel, "pack_vias", (arr(2, VIAS, 8, 128), arr(VIAS + 1, 8, 128)), spec(1))(via_current)
    got = lax.ppermute(send, "die", others)
    def buffer(count):
        return arr(8 * count, 128)

    base = call(base_kernel, "pack_base", (buffer(BASE),), spec(4))(bump_cell, base_sheet, base_start, send)[0]
    first = swap(base, "row", 0)
    cells, load_cells, loads, spread, counts = call(
        prepare_kernel, "spread_cells",
        (arr(4, VIAS, 8, 128), arr(4, 8, 128), arr(4, 4, 8, 128), arr(256, 1024, dtype=jnp.bfloat16), arr(4, 64, 128)),
        spec(3),
    )(via_cell, load_cell, load_current)
    early, between = call(chip_kernel, "pack_early", (buffer(EARLY), buffer(EARLY + 2 * BASE)), spec(6))(
        base, first, sheet_res, capacity, drop_start, counts
    )
    between = swap(between, "row", 1)
    field, even, odd, arriving = call(
        place_kernel, "place_vias", (arr(4, 4, 64, 128), buffer(LATE + EARLY), buffer(LATE), buffer(1)),
        spec(8), [pltpu.VMEM((4, 4, VIAS, 8, 128), F32)],
    )(packed, send, got, cells, load_cells, loads, spread, early)

    late = swap(odd, "row", 1)
    within = swap(even, "row", 0)
    relay = call(relay_kernel, "pack_relay", (buffer(BASE),), spec(1))(between)[0]
    relayed = swap(relay, "row", 0)
    shares = call(shares_kernel, "pack_shares", (buffer(4),), spec(3))(first, between, relayed)[0]
    shares = lax.ppermute(shares, "die", others)

    odd, even, wide = call(
        strip_kernel, "column_strips", (buffer(COL_GROUPS), buffer(COL_GROUPS), arr(200, 128)), spec(13)
    )(sheet_res, capacity, drop_start, counts, field, base, arriving, first, between, within, late, relayed, shares)
    odd = swap(odd, "col", 1)
    even = swap(even, "col", 0)

    image, pair = arr(4, 8 * GROUPS, 256), arr(2, 8 * GROUPS, 256)
    parts = call(
        assemble_kernel, "assemble",
        (image, image, pair, pair) + (image,) * 7 + (arr(2, 256, 384, dtype=jnp.bfloat16),), spec(8),
    )(sheet_res, capacity, drop_start, counts, field, within, between, late)

    ext = pltpu.VMEM((8 * GROUPS, 384), F32)
    scratch = [ext, ext, pltpu.VMEM((2, 8 * GROUPS, 384), F32), pltpu.VMEM((4, 40, 384), F32)] + [ext] * 8
    return call(solve_kernel, "solve", (arr(2, 2, 64, 256), arr(2, 8, 32)), spec(15), scratch)(
        *parts, wide, odd, even
    )


def solution(mesh):
    in_specs = (
        P("die", None, "row", "col"),
        P("die", "row", "col"),
        P("die", None, "row", "col"),
        P("die", "row", "col"),
        P(None, "die", None, "row", "col"),
        P("die", None, "row", "col"),
        P(None, "die", None, None, "row", "col"),
        P(None, "row", "col"),
        P(None, "row", "col"),
        P("row", "col"),
    )
    out_specs = (P("die", None, "row", "col"), P(None, "row", "col"))
    return jax.shard_map(
        per_device, mesh=mesh, in_specs=in_specs, out_specs=out_specs, check_vma=False
    )
```

```python
import jax
import jax.numpy as jnp
from jax import lax
from jax.experimental import pallas as pl
from jax.experimental.pallas import tpu as pltpu
from jax.sharding import PartitionSpec as P

SWEEPS = 6
STEPS = 2
VIAS = 32

VIA_CONDUCT = 1.0
VIA_RESIST = 4.0
BUMP_CONDUCT = 50.0
BASE_CAPACITY = 0.1
LOWER_BOUND = 0.1
UPPER_BOUND = 1.9

MIDDLE = 0.5 * (UPPER_BOUND + LOWER_BOUND)
HALF = 0.5 * (UPPER_BOUND - LOWER_BOUND)

GROUPS = 11
F32 = jnp.float32


def sweep_weights():
    scaled = MIDDLE / HALF
    ratio = 1.0 / scaled
    pairs = []
    for _ in range(SWEEPS - 1):
        following = 1.0 / (2.0 * scaled - ratio)
        pairs.append((following * ratio, 2.0 * following / HALF))
        ratio = following
    return pairs


WEIGHTS = sweep_weights()


def lane_iota():
    return lax.broadcasted_iota(jnp.int32, (8, 128), 1)


def sub_iota(width=128):
    return lax.broadcasted_iota(jnp.int32, (8, width), 0)


def roll(x, shift, axis):
    shift = shift % x.shape[axis]
    return pltpu.roll(x, shift, axis) if shift else x


def rows(g):
    return pl.ds(8 * g, 8)


def pack_kernel(via_ref, packed_ref, send_ref):
    later = lax.axis_index("die").astype(F32)
    total = jnp.zeros((8, 128), F32)
    for v in range(VIAS):
        parts = []
        for d in range(2):
            part = jnp.concatenate([via_ref[t, d, n, v] for t in range(2) for n in range(2)], axis=1)
            packed_ref[d, v] = part
            parts.append(part)
        both = parts[0] + parts[1]
        send_ref[v] = both + later * parts[0]
        total = total + both
    send_ref[VIAS] = total


def spread_nets(ref):
    gap = jnp.zeros((8, 16), F32)
    return jnp.concatenate([gap, ref[0], gap, gap, ref[1], gap], axis=1)


def shared(first, second, shift):
    return jnp.where(sub_iota() < shift, first, roll(second, shift, 0))


def shared_low(first, second, shift):
    return jnp.where(sub_iota() >= shift, first, roll(second, shift, 0))


class RowSender:
    def __init__(self, even, even_ref, odd_ref):
        self.even, self.even_ref, self.odd_ref, self.place = even, even_ref, odd_ref, 0

    def put(self, up, down):
        self.even_ref[rows(self.place), :] = jnp.where(self.even, down, up)
        self.odd_ref[rows(self.place), :] = jnp.where(self.even, up, down)
        self.place += 1

    def pair(self, first, second):
        self.put(first(0), first(7))
        self.put(second(0), second(7))
        self.put(shared(first(1), second(1), 4), shared_low(first(6), second(6), 4))


BASE = 4
EARLY = 36
LATE = 16


def base_kernel(bump_ref, sheet_ref, start_ref, send_ref, base_ref):
    lane, sub = lane_iota(), sub_iota()
    bump = jnp.zeros((8, 128), F32)
    column = lane % 64 - 16
    for k in range(4):
        bump = jnp.where((column // 8 == k) & (sub * 8 + column % 8 == bump_ref[0:1, k : k + 1]), 1.0, bump)
    for part, value in enumerate([spread_nets(sheet_ref), spread_nets(start_ref), bump, send_ref[VIAS]]):
        base_ref[rows(part), :] = value


def chip_kernel(base_ref, got_ref, sheet_ref, cap_ref, drop_ref, counts_ref, within_ref, between_ref):
    even = lax.axis_index("row") % 2 == 0
    sender = RowSender(even, within_ref, between_ref)
    for d in range(2):
        for half in range(2):
            lanes = pl.ds(half * 128, 128)
            for n in range(2):
                sender.pair(lambda g: sheet_ref[d, n, rows(g), lanes], lambda g: drop_ref[d, n, rows(g), lanes])
        sender.pair(lambda g: cap_ref[d, rows(g), pl.ds(0, 128)], lambda g: cap_ref[d, rows(g), pl.ds(128, 128)])
        sender.pair(lambda g: counts_ref[2 * d, rows(g), :], lambda g: counts_ref[2 * d + 1, rows(g), :])
    for part in range(BASE):
        own, got = base_ref[rows(part), :], got_ref[rows(part), :]
        for slot, value in enumerate([jnp.where(even, own, got), jnp.where(even, got, own)]):
            between_ref[rows(EARLY + BASE * slot + part), :] = value


def relay_kernel(between_ref, relay_ref):
    even = lax.axis_index("row") % 2 == 0
    for part in range(BASE):
        a, b = between_ref[rows(EARLY + part), :], between_ref[rows(EARLY + BASE + part), :]
        relay_ref[rows(part), :] = jnp.where(even, b, a)


def shares_kernel(first_ref, between_ref, relayed_ref, shares_ref):
    shares_ref[rows(0), :] = first_ref[rows(3), :]
    for slot in range(2):
        shares_ref[rows(1 + slot), :] = between_ref[rows(EARLY + BASE * slot + 3), :]
    shares_ref[rows(3), :] = relayed_ref[rows(3), :]


def spread_matrix(height, width):
    row = lax.broadcasted_iota(jnp.int32, (height, width), 0) % 128
    column = lax.broadcasted_iota(jnp.int32, (height, width), 1)
    return jnp.where(row == column // 8, 1.0, 0.0).astype(jnp.bfloat16)


def halves(value):
    high = value.astype(jnp.bfloat16)
    low = (value - high.astype(F32)).astype(jnp.bfloat16)
    return jnp.concatenate([high, low], axis=1)


def prepare_kernel(cell_ref, load_cell_ref, load_ref, cells_ref, load_cells_ref, loads_ref, spread_ref, counts_ref):
    within = (lane_iota() % 8).astype(F32)
    spread = spread_matrix(32, 256)
    for d in range(2):
        cells = cell_ref[d].reshape(8 * VIAS, 32).astype(F32).astype(jnp.bfloat16)
        wide = jnp.dot(cells, spread, preferred_element_type=F32)
        load_cell = load_cell_ref[d].astype(F32).astype(jnp.bfloat16)
        load_cell = jnp.dot(load_cell, spread, preferred_element_type=F32)
        for half in range(2):
            lanes = slice(128 * half, 128 * half + 128)
            for v in range(VIAS):
                cells_ref[2 * d + half, v] = wide[8 * v : 8 * v + 8, lanes] - within
            load_cells_ref[2 * d + half] = load_cell[:, lanes] - within
    spread_ref[...] = spread_matrix(256, 1024)
    loads = jnp.concatenate([load_ref[t, d, n] for d in range(2) for t in range(2) for n in range(2)], axis=0)
    high = loads.astype(jnp.bfloat16)
    low = (loads - high.astype(F32)).astype(jnp.bfloat16)
    wide = jnp.dot(high, spread, preferred_element_type=F32) + jnp.dot(low, spread, preferred_element_type=F32)
    for d in range(2):
        for half in range(2):
            for m in range(4):
                loads_ref[2 * d + half, m] = wide[32 * d + 8 * m : 32 * d + 8 * m + 8, 128 * half : 128 * half + 128]

    def count(i, carry):
        state = [jnp.zeros((8, 128), F32) for _ in range(8)]
        for v in range(VIAS):
            cell = cells_ref[i, v]
            for oi in range(8):
                state[oi] = state[oi] + jnp.where(cell == 8.0 * oi, 1.0, 0.0)
        for oi in range(8):
            counts_ref[i, pl.ds(oi, 8, stride=8), :] = state[oi]
        return carry

    lax.fori_loop(0, 4, count, 0)


def place_kernel(
    packed_ref, send_ref, got_ref, cells_ref, load_cells_ref, loads_ref, spread_ref, early_ref,
    field_ref, even_ref, odd_ref, arriving_ref, values_ref,
):
    lane = lane_iota()
    later = lax.axis_index("die").astype(F32)
    even = lax.axis_index("row") % 2 == 0
    weights = (
        (VIA_RESIST * (4.0 - 2.0 * later), VIA_RESIST * (3.0 - 2.0 * later), VIA_RESIST * (1.0 + later)),
        (VIA_RESIST * (3.0 - 2.0 * later), VIA_RESIST * (3.0 - 2.0 * later), VIA_RESIST),
    )
    size = (8 * VIAS, 128)
    first, second, got = packed_ref[0].reshape(size), packed_ref[1].reshape(size), got_ref[0:VIAS].reshape(size)
    for d in range(2):
        mixed = weights[d][0] * first + weights[d][1] * second + weights[d][2] * got
        wide = jnp.dot(halves(mixed), spread_ref[...], preferred_element_type=F32)
        for half in range(2):
            for m in range(4):
                start = 256 * m + 128 * half
                values_ref[2 * d + half, m] = wide[:, start : start + 128].reshape(VIAS, 8, 128)

    def add(i, carry):
        cell = load_cells_ref[i]
        loads = [loads_ref[i, m] for m in range(4)]
        state = []
        for oi in range(8):
            hit = cell == 8.0 * oi
            state.append([jnp.where(hit, load, 0.0) for load in loads])
        for v in range(VIAS):
            cell = cells_ref[i, v]
            values = [values_ref[i, m, v] for m in range(4)]
            for oi in range(8):
                hit = cell == 8.0 * oi
                state[oi] = [old + jnp.where(hit, value, 0.0) for old, value in zip(state[oi], values)]
        for oi in range(8):
            for m in range(4):
                field_ref[m, i, pl.ds(oi, 8, stride=8), :] = state[oi][m]
        return carry

    lax.fori_loop(0, 4, add, 0)

    arriving_ref[...] = send_ref[VIAS] + got_ref[VIAS]
    for g in range(EARLY):
        even_ref[rows(LATE + g), :] = early_ref[rows(g), :]
    sender = RowSender(even, even_ref, odd_ref)
    for d in range(2):
        for half in range(2):
            for n in range(2):
                one = lambda g: field_ref[n, 2 * d + half, rows(g), :]
                two = lambda g: field_ref[2 + n, 2 * d + half, rows(g), :]
                sender.put(one(0), one(7))
                sender.put(shared(one(1), two(0), 3), shared_low(one(6), two(7), 5))


SHEET, DROP, CAPACITY, COUNTS, FIRST, SECOND = range(6)


def near_rows(read, kind, d, half, n, upper):
    early, late = read
    if kind in (FIRST, SECOND):
        start = 8 * d + 4 * half + 2 * n
        if kind == SECOND:
            return roll(late(start + 1), -5 if upper else -3, 0), None
        return late(start), late(start + 1)
    if kind in (SHEET, DROP):
        start, second = 18 * d + 6 * half + 3 * n, kind == DROP
    else:
        start, second = 18 * d + (12 if kind == CAPACITY else 15), half == 1
    last = early(start + 2)
    return (early(start + 1), roll(last, -4, 0)) if second else (early(start), last)


def column_groups(own, below, above, kind, d, half, n):
    low = near_rows(below, kind, d, half, n, False)
    high = near_rows(above, kind, d, half, n, True)
    both = None if low[1] is None else jnp.where(sub_iota() < 4, low[1], high[1])
    return [own(g) for g in range(8)] + [low[0], both, high[0]]


def readers(even, below, above, within_ref, between_ref, late_ref):
    def make(inside, near, skip, far_ref):
        def read(g):
            value = jnp.where(near, within_ref[rows(skip + g), :], far_ref[rows(g), :])
            return value if inside is None else jnp.where(inside, value, 0.0)
        return read

    odd = jnp.logical_not(even)
    return tuple(
        (make(inside, near, LATE, between_ref), make(inside, near, 0, late_ref)) for inside, near in ((below, even), (above, odd))
    )


COL_GROUPS = 2 * GROUPS + 6


def strip_kernel(
    sheet_ref, cap_ref, drop_ref, counts_ref, field_ref, base_ref, arriving_ref, first_ref, between_ref,
    within_ref, late_ref, relayed_ref, shares_ref, even_ref, odd_ref, wide_ref,
):
    lane = lane_iota()
    within = lane % 16
    row, last = lax.axis_index("row"), (lax.axis_size("row") - 1)
    even = row % 2 == 0
    below, above = readers(even, None, None, within_ref, between_ref, late_ref)
    even_col = lax.axis_index("col") % 2 == 0

    own = (lane % 64 >= 16) & (lane % 64 < 48)

    def spread_steps(value):
        out = []
        for t in range(2):
            moved = jnp.where(lane < 64, roll(value, 16 - 64 * t, 1), roll(value, 48 - 64 * t, 1))
            out.append(jnp.where(own, moved, 0.0))
        return out

    def block(ref, start, share):
        parts = [ref[rows(start + f), :] for f in range(BASE)]
        parts[3] = parts[3] + shares_ref[rows(share), :]
        return parts

    def choose(a, b, inside):
        return [jnp.where(inside, jnp.where(even, x, y), 0.0) for x, y in zip(a, b)]

    partner = block(first_ref, 0, 0)
    between = [block(between_ref, EARLY + BASE * slot, 1 + slot) for slot in range(2)]
    relayed = block(relayed_ref, 0, 3)
    groups = []
    for g, parts in enumerate([
        [base_ref[rows(f), :] for f in range(3)] + [arriving_ref[...]],
        choose(partner, between[0], row < last),
        choose(relayed, between[1], row + 2 <= last),
        choose(between[0], relayed, row >= 2),
        choose(between[1], partner, row > 0),
    ]):
        one, two = spread_steps(parts[3])
        groups.append([parts[0], parts[1], one, two, parts[2]])
        for f in range(5):
            wide_ref[rows(5 * f + g), :] = groups[g][f]

    def fields(part, half):
        lanes = pl.ds(half * 128, 128)
        images = [(d, n) for d in range(2) for n in range(2)]
        if part == 0:
            return [
                column_groups(lambda g: ref[d, n, rows(g), lanes], below, above, kind, d, half, n)
                for kind, ref in ((SHEET, sheet_ref), (DROP, drop_ref)) for d, n in images
            ]
        out = [column_groups(lambda g: cap_ref[d, rows(g), lanes], below, above, CAPACITY, d, half, 0) for d in range(2)]
        out += [
            column_groups(lambda g: counts_ref[2 * d + half, rows(g), :], below, above, COUNTS, d, half, 0)
            for d in range(2)
        ]
        for d, n in images:
            one = column_groups(lambda g: field_ref[n, 2 * d + half, rows(g), :], below, above, FIRST, d, half, n)
            two = column_groups(lambda g: field_ref[2 + n, 2 * d + half, rows(g), :], below, above, SECOND, d, half, n)
            merged = []
            for a, b in zip(one, two):
                if b is None:
                    merged.append(a)
                elif half == 0:
                    merged.append(jnp.where(within < 11, a, roll(b, 11, 1)))
                else:
                    merged.append(jnp.where(within >= 5, a, roll(b, -11, 1)))
            out.append(merged)
        return out

    def put(index, left, right):
        even_ref[rows(index), :] = jnp.where(even_col, right, left)
        odd_ref[rows(index), :] = jnp.where(even_col, left, right)

    for part in range(2):
        sides = [fields(part, half) for half in range(2)]
        for g in range(GROUPS):
            out = []
            for half, chunks in enumerate(sides):
                value = chunks[0][g]
                for k in range(1, 8):
                    value = jnp.where((lane // 16 + half) % 8 == k, roll(chunks[k][g], 16 * k, 1), value)
                out.append(value)
            put(part * GROUPS + g, *out)

    start = 2 * GROUPS
    quarter = (lane % 64) // 16
    for g in range(5):
        sheet, drop, one, two, _ = groups[g]
        left = jnp.where(
            quarter == 1, sheet,
            jnp.where(quarter == 2, roll(drop, 16, 1), jnp.where(quarter == 3, roll(one, 32, 1), roll(two, -16, 1))),
        )
        right = jnp.where(
            quarter == 2, sheet,
            jnp.where(quarter == 3, roll(drop, 16, 1), jnp.where(quarter == 1, roll(two, -16, 1), roll(one, -32, 1))),
        )
        put(start + g, left, right)
    bumps = []
    for origin in (16, 32):
        value = roll(groups[0][4], -origin, 1)
        for g in range(1, 5):
            value = jnp.where(lane // 16 == g, roll(groups[g][4], 16 * g - origin, 1), value)
        bumps.append(value)
    put(start + 5, *bumps)


def assemble_kernel(
    sheet_ref, cap_ref, drop_ref, counts_ref, field_ref, within_ref, between_ref, late_ref,
    s_ref, x_ref, c_ref, k_ref, one_ref, two_ref, up_ref, down_ref, left_ref, right_ref, diag_ref, spread_ref,
):
    row, last = lax.axis_index("row"), (lax.axis_size("row") - 1)
    sub, lane = sub_iota(256), lax.broadcasted_iota(jnp.int32, (8, 256), 1)
    below, above = readers(row % 2 == 0, row < last, row > 0, within_ref, between_ref, late_ref)

    def both(own, kind, d, n):
        sides = [column_groups(lambda g: own(half, g), below, above, kind, d, half, n) for half in range(2)]
        return [None if a is None else jnp.concatenate([a, b], axis=1) for a, b in zip(*sides)]

    for d in range(2):
        caps = both(lambda half, g: cap_ref[d, rows(g), pl.ds(half * 128, 128)], CAPACITY, d, 0)
        counts = both(lambda half, g: counts_ref[2 * d + half, rows(g), :], COUNTS, d, 0)
        for g in range(GROUPS):
            c_ref[d, rows(g), :] = caps[g]
            k_ref[d, rows(g), :] = counts[g]
        for n in range(2):
            i = 2 * d + n
            sheets = both(lambda half, g: sheet_ref[d, n, rows(g), pl.ds(half * 128, 128)], SHEET, d, n)
            drops = both(lambda half, g: drop_ref[d, n, rows(g), pl.ds(half * 128, 128)], DROP, d, n)
            ones = both(lambda half, g: field_ref[n, 2 * d + half, rows(g), :], FIRST, d, n)
            twos = both(lambda half, g: field_ref[2 + n, 2 * d + half, rows(g), :], SECOND, d, n)
            for g in range(GROUPS):
                s_ref[i, rows(g), :] = sheets[g]
                x_ref[i, rows(g), :] = drops[g]
                one_ref[i, rows(g), :] = c_ref[d, rows(g), :] * drops[g] + ones[g]
                if twos[g] is not None:
                    two_ref[i, rows(g), :] = twos[g]
            for g in range(GROUPS):
                here, after = s_ref[i, rows(g), :], s_ref[i, rows((g + 1) % GROUPS), :]
                under = jnp.where(sub == 7, roll(after, -1, 0), roll(here, -1, 0))
                inside = here > 0.0
                down_ref[i, rows(g), :] = jnp.where(inside, connect(here, under), 0.0)
                right = jnp.where(inside & (lane < 255), connect(here, roll(here, -1, 1)), 0.0)
                right_ref[i, rows(g), :] = right
                left_ref[i, rows(g), :] = roll(right, 1, 1)
            for g in range(GROUPS):
                here, before = down_ref[i, rows(g), :], down_ref[i, rows((g - 1) % GROUPS), :]
                up = jnp.where(sub == 0, roll(before, 1, 0), roll(here, 1, 0))
                up_ref[i, rows(g), :] = up
                diag = c_ref[d, rows(g), :] + up + here + left_ref[i, rows(g), :] + right_ref[i, rows(g), :]
                diag_ref[i, rows(g), :] = diag + VIA_CONDUCT * k_ref[d, rows(g), :]
    source = lax.broadcasted_iota(jnp.int32, (256, 384), 0) % 128
    column = lax.broadcasted_iota(jnp.int32, (256, 384), 1)
    column = jnp.where(column < 256, 16 + column // 8, jnp.where(column < 320, 48, 0) + (column - 256) // 8)
    for n in range(2):
        spread_ref[n] = jnp.where(source == column + 64 * n, 1.0, 0.0).astype(jnp.bfloat16)


def connect(center, neighbour):
    return jnp.where(neighbour > 0.0, 2.0 / (center + neighbour), 0.0)


def three_terms(k):
    if k == 0:
        return 1.0 - 1.0 / MIDDLE, 0.0, 1.0 / MIDDLE
    a, b = WEIGHTS[k - 1]
    return 1.0 + a - b, -a, b


def advance(k, value, previous, total):
    fore, back, gain = three_terms(k)
    out = total if gain == 1.0 else gain * total
    if fore != 0.0:
        out = out + fore * value
    return out + back * previous() if k else out


def base_solve(fields):
    sheet, state, arriving, bump = fields
    steps = [(1, 0), (-1, 0), (1, 1), (-1, 1)]
    inside = sheet > 0.0
    links = [jnp.where(inside, connect(sheet, roll(sheet, s, a)), 0.0) for s, a in steps]
    diagonal = BASE_CAPACITY + links[0] + links[1] + links[2] + links[3] + BUMP_CONDUCT * bump
    inverse = 1.0 / diagonal
    links = [inverse * link for link in links]
    results = []
    for t in range(STEPS):
        source = inverse * (BASE_CAPACITY * state + arriving[t])
        previous = None
        for k in range(SWEEPS):
            total = (links[0] * roll(state, 1, 0) + links[1] * roll(state, -1, 0)) + (
                links[2] * roll(state, 1, 1) + links[3] * roll(state, -1, 1)
            ) + source
            state, previous = advance(k, state, lambda: previous, total), state
        results.append(state)
    return results


def needed(halo):
    if halo > 8:
        return list(range(GROUPS))
    return list(range(8)) + ([8, 10] if halo > 0 else [])


def solve_kernel(
    s_ref, x_ref, c_ref, k_ref, one_ref, two_ref, up_ref, down_ref, left_ref, right_ref, diag_ref, spread_ref,
    wide_ref, even_ref, odd_ref, out_ref, base_out_ref,
    c_ext, k_ext, f_ext, bound, link_up, link_down, link_left, link_right, inv_ext, src, state, alt,
):
    lane = lane_iota()
    row, col = lax.axis_index("row"), lax.axis_index("col")
    has_left, has_right = col > 0, col < (lax.axis_size("col") - 1)
    even_col = col % 2 == 0

    def from_left(g):
        return jnp.where(even_col, odd_ref[rows(g), :], even_ref[rows(g), :])

    def from_right(g):
        return jnp.where(even_col, even_ref[rows(g), :], odd_ref[rows(g), :])

    start = 2 * GROUPS
    quarter = (lane % 64) // 16
    take_left, take_right = (quarter == 0) & has_left, (quarter == 3) & has_right
    fields = []
    for field in range(5):
        out = []
        for g in range(5):
            if field == 4:
                right, left = roll(from_right(start + 5), 48 - 16 * g, 1), roll(from_left(start + 5), -16 * g, 1)
                right = jnp.where(lane < 64, right, roll(right, 64, 1))
                left = jnp.where(lane < 64, left, roll(left, 64, 1))
            else:
                right = roll(from_right(start + g), (32, 16, 0, 48)[field], 1)
                left = roll(from_left(start + g), (-32, -48, 0, -16)[field], 1)
            value = jnp.where(take_right, right, wide_ref[rows(5 * field + g), :])
            out.append(jnp.where(take_left, left, value))
        fields.append(jnp.concatenate(out, axis=0))
    sub, sub3 = sub_iota(), sub_iota(384)
    last = lax.axis_size("row") - 1

    def third(part, chunk, g):
        right_ok, left_ok = has_right, has_left
        if g >= 8:
            inside = {8: row < last, 9: ((sub < 4) & (row < last)) | ((sub >= 4) & (row > 0)), 10: row > 0}[g]
            right_ok, left_ok = right_ok & inside, left_ok & inside
        right = jnp.where((lane // 16 == chunk) & right_ok, from_right(part * GROUPS + g), 0.0)
        value = jnp.where((lane // 16 == (chunk + 7) % 8) & left_ok, from_left(part * GROUPS + g), right)
        return roll(value, -16 * chunk, 1)

    def above(value, before, index):
        return jnp.where(index == 0, roll(before, 1, 0), roll(value, 1, 0))

    def below(value, after, index):
        return jnp.where(index == 7, roll(after, -1, 0), roll(value, -1, 0))

    for i in range(4):
        d, n = i // 2, i % 2

        def wide(ref, g, extra, index=i):
            return jnp.concatenate([ref[index, rows(g), :], extra], axis=1)

        if n == 0:
            for g in range(GROUPS):
                c_ext[rows(g), :] = wide(c_ref, g, third(1, d, g), d)
                k_ext[rows(g), :] = wide(k_ref, g, third(1, 2 + d, g), d)
        @pl.when(row >= 0)
        def _():
            if i == 0:
                solved = base_solve((fields[0], fields[1], (fields[2], fields[3]), fields[4]))
                for t in range(STEPS):
                    pieces = halves(solved[t])
                    for n in range(2):
                        bound[2 * t + n] = jnp.dot(pieces, spread_ref[n], preferred_element_type=F32)
                for n in range(2):
                    base_out_ref[n] = roll(solved[1][0:8], -(64 * n + 16), 1)[:, 0:32]

            sheets = [third(0, i, g) for g in range(GROUPS)]
            for g in range(GROUPS):
                here = sheets[g]
                inside = here > 0.0
                low, high = s_ref[i, rows(g), pl.ds(0, 128)], s_ref[i, rows(g), pl.ds(128, 128)]
                after = roll(jnp.where(lane == 0, low, here), -1, 1)
                before = roll(jnp.where(lane == 127, high, here), 1, 1)
                right = jnp.where(inside, connect(here, after), 0.0)
                left = jnp.where(inside, connect(here, before), 0.0)
                down = jnp.where(inside, connect(here, below(here, sheets[(g + 1) % GROUPS], sub)), 0.0)
                up = jnp.where(inside, connect(here, above(here, sheets[(g - 1) % GROUPS], sub)), 0.0)
                first = jnp.where(lane == 0, roll(right, 1, 1), 0.0)
                final = jnp.where(lane == 127, roll(left, -1, 1), 0.0)
                diag = wide(diag_ref, g, 0.0 * here) + jnp.concatenate(
                    [first, final, c_ext[rows(g), pl.ds(256, 128)] + up + down + left + right
                     + VIA_CONDUCT * k_ext[rows(g), pl.ds(256, 128)]], axis=1)
                inverse = jnp.where(diag > 0.0, 1.0 / diag, 0.0)
                inv_ext[rows(g), :] = inverse
                zero = jnp.zeros_like(first)
                link_up[rows(g), :] = inverse * wide(up_ref, g, up)
                link_down[rows(g), :] = inverse * wide(down_ref, g, down)
                link_left[rows(g), :] = inverse * (wide(left_ref, g, left) + jnp.concatenate([first, zero, zero], axis=1))
                link_right[rows(g), :] = inverse * (wide(right_ref, g, right) + jnp.concatenate([zero, final, zero], axis=1))
                drop = third(0, 4 + i, g)
                state[rows(g), :] = wide(x_ref, g, drop)
                one = third(1, 4 + i, g)
                f_ext[0, rows(g), :] = wide(one_ref, g, c_ext[rows(g), pl.ds(256, 128)] * drop + one)
                if g != 9:
                    two = jnp.where(lane < 64, roll(one, -11, 1), roll(one, 11, 1))
                    f_ext[1, rows(g), :] = wide(two_ref, g, two)

        @pl.when(row >= 0)
        def _():
            for t in range(STEPS):
                for k in range(SWEEPS):
                    now, then = (alt, state) if k % 2 else (state, alt)
                    for g in needed(11 - 6 * t - k):
                        value = now[rows(g), :]
                        total = link_up[rows(g), :] * above(value, now[rows((g - 1) % GROUPS), :], sub3)
                        total = total + link_down[rows(g), :] * below(value, now[rows((g + 1) % GROUPS), :], sub3)
                        total = total + (
                            link_left[rows(g), :] * roll(value, 1, 1) + link_right[rows(g), :] * roll(value, -1, 1))
                        if k == 0:
                            spread = jnp.broadcast_to(bound[2 * t + n, pl.ds(39 if g == 10 else g, 1), :], (8, 384))
                            if g == 9:
                                spread = jnp.where(sub3 < 4, spread, bound[2 * t + n, pl.ds(38, 1), :])
                            source = f_ext[t, rows(g), :] + k_ext[rows(g), :] * spread
                            if t:
                                source = source + c_ext[rows(g), :] * value
                            source = inv_ext[rows(g), :] * source
                            src[rows(g), :] = source
                        else:
                            source = src[rows(g), :]
                        then[rows(g), :] = advance(k, value, lambda: then[rows(g), :], total + source)

        for g in range(8):
            out_ref[d, n, rows(g), :] = state[rows(g), pl.ds(0, 256)]


def spec(count):
    return [pl.BlockSpec(memory_space=pltpu.VMEM)] * count


def call(kernel, name, outs, ins, scratch=(), limit=24):
    return pl.pallas_call(
        kernel,
        out_shape=outs,
        in_specs=ins,
        out_specs=spec(len(outs)),
        scratch_shapes=list(scratch),
        compiler_params=pltpu.CompilerParams(vmem_limit_bytes=limit * 1024 * 1024),
        name=name,
        cost_estimate=HINTS.get(name),
    )


LONG = pl.CostEstimate(flops=10**9, bytes_accessed=10**7, transcendentals=0)
NONE = pl.CostEstimate(flops=0, bytes_accessed=0, transcendentals=0)
HINTS = {"spread_cells": NONE, "pack_early": NONE, "place_vias": LONG, "pack_relay": LONG}


def arr(*shape, dtype=F32):
    return jax.ShapeDtypeStruct(shape, dtype)


def swaps(count, offset):
    pairs = []
    for die in range(2):
        partner = {}
        for i in range(offset, count - 1, 2):
            partner[i], partner[i + 1] = i + 1, i
        for i in range(count):
            target = die * count + partner[i] if i in partner else (1 - die) * count + i
            pairs.append((die * count + i, target))
    return pairs


def swap(value, axis, offset):
    return lax.ppermute(value, ("die", axis), swaps(lax.axis_size(axis), offset))


def per_device(
    sheet_res, capacity, drop_start, load_cell, load_current, via_cell, via_current, base_sheet, base_start, bump_cell
):
    others = [(0, 1), (1, 0)]

    packed, send = call(pack_kernel, "pack_vias", (arr(2, VIAS, 8, 128), arr(VIAS + 1, 8, 128)), spec(1))(via_current)
    got = lax.ppermute(send, "die", others)
    def buffer(count):
        return arr(8 * count, 128)

    base = call(base_kernel, "pack_base", (buffer(BASE),), spec(4))(bump_cell, base_sheet, base_start, send)[0]
    first = swap(base, "row", 0)
    cells, load_cells, loads, spread, counts = call(
        prepare_kernel, "spread_cells",
        (arr(4, VIAS, 8, 128), arr(4, 8, 128), arr(4, 4, 8, 128), arr(256, 1024, dtype=jnp.bfloat16), arr(4, 64, 128)),
        spec(3),
    )(via_cell, load_cell, load_current)
    early, between = call(chip_kernel, "pack_early", (buffer(EARLY), buffer(EARLY + 2 * BASE)), spec(6))(
        base, first, sheet_res, capacity, drop_start, counts
    )
    between = swap(between, "row", 1)
    field, even, odd, arriving = call(
        place_kernel, "place_vias", (arr(4, 4, 64, 128), buffer(LATE + EARLY), buffer(LATE), buffer(1)),
        spec(8), [pltpu.VMEM((4, 4, VIAS, 8, 128), F32)],
    )(packed, send, got, cells, load_cells, loads, spread, early)

    late = swap(odd, "row", 1)
    within = swap(even, "row", 0)
    relay = call(relay_kernel, "pack_relay", (buffer(BASE),), spec(1))(between)[0]
    relayed = swap(relay, "row", 0)
    shares = call(shares_kernel, "pack_shares", (buffer(4),), spec(3))(first, between, relayed)[0]
    shares = lax.ppermute(shares, "die", others)

    even, odd, wide = call(
        strip_kernel, "column_strips", (buffer(COL_GROUPS), buffer(COL_GROUPS), arr(200, 128)), spec(13)
    )(sheet_res, capacity, drop_start, counts, field, base, arriving, first, between, within, late, relayed, shares)
    even = swap(even, "col", 0)
    odd = swap(odd, "col", 1)

    image, pair = arr(4, 8 * GROUPS, 256), arr(2, 8 * GROUPS, 256)
    parts = call(
        assemble_kernel, "assemble",
        (image, image, pair, pair) + (image,) * 7 + (arr(2, 256, 384, dtype=jnp.bfloat16),), spec(8),
    )(sheet_res, capacity, drop_start, counts, field, within, between, late)

    ext = pltpu.VMEM((8 * GROUPS, 384), F32)
    scratch = [ext, ext, pltpu.VMEM((2, 8 * GROUPS, 384), F32), pltpu.VMEM((4, 40, 384), F32)] + [ext] * 8
    return call(solve_kernel, "solve", (arr(2, 2, 64, 256), arr(2, 8, 32)), spec(15), scratch)(
        *parts, wide, even, odd
    )


def solution(mesh):
    in_specs = (
        P("die", None, "row", "col"),
        P("die", "row", "col"),
        P("die", None, "row", "col"),
        P("die", "row", "col"),
        P(None, "die", None, "row", "col"),
        P("die", None, "row", "col"),
        P(None, "die", None, None, "row", "col"),
        P(None, "row", "col"),
        P(None, "row", "col"),
        P("row", "col"),
    )
    out_specs = (P("die", None, "row", "col"), P(None, "row", "col"))
    return jax.shard_map(
        per_device, mesh=mesh, in_specs=in_specs, out_specs=out_specs, check_vma=False
    )
```
